32 devices in a mesh: frag: 2 (over y), pair: 4 (over x, core), aux: 4 (over z).
Axes of the slice: x: 2, y: 2, z: 4, core: 2. Of those that a mesh axis runs over, the one named last changes fastest.
Arguments:
- slabs: bfloat16 [128, 256, 4096], P(('frag', 'pair'), 'aux'), parts along dimension 0, may hold values from -6 to 6
- block_row: int32 [128], P(('frag', 'pair')), parts along dimension 0, may hold values from 0 to 63
- block_col: int32 [128], P(('frag', 'pair')), parts along dimension 0, may hold values from 0 to 63, as said below
- live_count: int32 [8], P(('frag', 'pair')), parts along dimension 0, may hold values from 1 to 16, as said below
- orbitals: bfloat16 [8192, 192], P('frag'), parts along dimension 0, may hold values from -0.09375 to 0.09375
- hcore: float32 [128, 64], P(('frag', 'pair')), parts along dimension 0, may hold values from -6 to 6
Outputs:
- active_vectors: float32 [512, 64, 64], P(('frag', 'aux'), 'pair'), parts along dimension 0
- fock: float32 [128, 64], P(('frag', 'pair')), parts along dimension 0
The draws below stay inside these ranges and needn't reach their ends.
There are 2 independent parts, one for each index of `frag`. The reference program is written for one: setup_inputs(seed, part) draws one part's arguments, and reference() takes and returns one part's arrays. A program takes and returns all parts, laid end to end along the dimension named above; each array names one. Nothing has to cross between parts.
Inputs may be any that keep to these rules, and one draw needn't show every extreme that they name: `block_col`: never above the same slab's block_row; a diagonal block holds half of each integral. `live_count`: a device's live slabs fill its first slots; exactly one device in every draw has all 16 live.
All inputs are finite; a program needn't handle non-finite values.
Results may differ from the reference program's by a relative error of at most 0.0029.
Values may be sent and summed in bfloat16 or wider, within the bound.
No kernel may reach another device: no remote copies, remote signals or barrier semaphores. Data moves between devices by JAX's collectives and lax.ppermute only.
A program may use at most 128 MiB of HBM per device.

```python
import jax
import jax.numpy as jnp
from jax import lax

NAO = 4096
BS = 64
NBLK = 64
NACT = 64
NCOL = 192
NQ = 256
SLAB_DEV = 16
NSLAB = 64


def pair_blocks(key):
    first = jax.random.randint(jax.random.fold_in(key, 21), (NSLAB,), 0, NBLK)
    second = jax.random.randint(jax.random.fold_in(key, 22), (NSLAB,), 0, NBLK)
    first = first.at[0].set(NBLK - 1)
    second = second.at[0].set(0)
    return (jnp.maximum(first, second), jnp.minimum(first, second))


def draw_block_row(key, part):
    upper, lower = pair_blocks(key)
    return upper.astype(jnp.int32)


def draw_block_col(key, part):
    upper, lower = pair_blocks(key)
    return lower.astype(jnp.int32)


def draw_live_count(key, part):
    key = jax.random.fold_in(key, 3)
    devices = NSLAB // SLAB_DEV
    counts = jax.random.randint(jax.random.fold_in(key, 1), (devices,), 1, SLAB_DEV)
    offset = jax.random.randint(jax.random.fold_in(key, 2), (), 0, devices // 2)
    busiest = (2 * offset + part) % devices
    filled = jnp.where(jnp.arange(devices) == busiest, SLAB_DEV, counts)
    return filled.astype(jnp.int32)


def block_levels(stream_key, dims, pieces, smallest, top_value):
    gain = 1.0
    for position, blocks in pieces:
        steps = jax.random.uniform(jax.random.fold_in(jax.random.fold_in(stream_key, 6), position), (blocks,), jnp.float32, smallest / len(pieces), top_value / len(pieces))
        gain = gain * jnp.repeat(jnp.exp(steps), dims[position] // blocks).reshape((-1,) + (1,) * (len(dims) - 1 - position))
    return gain


def gaussian(own_key, shape, deviation, most, cuts=(), kind=jnp.bfloat16):
    entries = jax.random.normal(own_key, shape, jnp.float32) * deviation
    if len(cuts) > 0:
        entries = block_levels(own_key, shape, cuts, -0.22, 0.18) * entries
    return jnp.clip(entries, min=-most, max=most).astype(kind)


def setup_inputs(seed: int = 0, part: int = 0) -> dict:
    keys = jax.random.split(jax.random.key(seed), 7)
    part_splits = jax.random.split(jax.random.fold_in(keys[6], part), 7)
    slabs = gaussian(part_splits[0], (NSLAB, NQ, BS * BS), 0.4, 6.0, ((0, 4), (1, 4)))
    block_row = draw_block_row(jax.random.fold_in(jax.random.fold_in(keys[6], part), 71), part)
    block_col = draw_block_col(jax.random.fold_in(jax.random.fold_in(keys[6], part), 71), part)
    live_count = draw_live_count(jax.random.fold_in(jax.random.fold_in(keys[6], part), 71), part)
    orbitals = gaussian(part_splits[4], (NAO, NCOL), NAO ** -0.5, 0.09375)
    hcore = gaussian(part_splits[5], (NACT, NACT), 1.0, 6.0, ((0, 4),), jnp.float32)
    return {"slabs": slabs, "block_row": block_row, "block_col": block_col, "live_count": live_count, "orbitals": orbitals, "hcore": hcore}


def slab_terms(values, left, right):
    half = jnp.einsum('mc,qmn->qnc', left.astype(jnp.float32), values.astype(jnp.float32))
    half = lax.optimization_barrier(half.astype(jnp.bfloat16)).astype(jnp.float32)
    rightf = right.astype(jnp.float32)
    first = jnp.einsum('qnt,nc->qtc', half[:, :, :NACT], rightf)
    second = jnp.einsum('qnc,nt->qtc', half, rightf[:, :NACT])
    trace = 2.0 * jnp.einsum('qni,ni->q', half[:, :, NACT:], rightf[:, NACT:])
    return first + second, trace


def reference(slabs, block_row, block_col, live_count, orbitals, hcore):
    slot_index = jnp.arange(NSLAB, dtype=jnp.int32)
    owner = slot_index // SLAB_DEV
    live = (slot_index % SLAB_DEV) < live_count[owner]

    def step(carry, item):
        values, row_blk, col_blk, flag = item

        def work(state):
            left = lax.dynamic_slice_in_dim(orbitals, (row_blk * BS).astype(jnp.int32), BS, 0)
            right = lax.dynamic_slice_in_dim(orbitals, (col_blk * BS).astype(jnp.int32), BS, 0)
            terms, trace = slab_terms(values.reshape(NQ, BS, BS), left, right)
            return (state[0] + terms, state[1] + trace)

        return lax.cond(flag, work, lambda state: state, carry), None

    init = (jnp.zeros((NQ, NACT, NCOL), jnp.float32), jnp.zeros((NQ,), jnp.float32))
    (vectors, density), _ = lax.scan(step, init, (slabs, block_row, block_col, live))
    active_vectors = vectors[:, :, :NACT]
    inactive = vectors[:, :, NACT:]
    exchange = jnp.einsum('qti,qui->tu', inactive, inactive, precision=lax.Precision.HIGHEST)
    coulomb = jnp.einsum('qtu,q->tu', active_vectors, density, precision=lax.Precision.HIGHEST)
    fock = hcore + 2.0 * coulomb - exchange
    return active_vectors, fock
```

```python
import functools

import jax
import jax.numpy as jnp
from jax import lax
from jax.experimental import pallas as pl
from jax.experimental.pallas import tpu as pltpu
from jax.sharding import PartitionSpec as P

BS = 64
NACT = 64
NCOL = 192
NIN = NCOL - NACT
LANES = 128
NBQ = 16
PAIRED = 2 * BS
BF = jnp.bfloat16
F32 = jnp.float32


def low_half(rows):
    return lax.broadcasted_iota(jnp.int32, (rows, LANES), 1) < BS


def orbital_blocks(rows, cols, live, ot_ref, lt_ref, r_ref):
    slabs = lt_ref.shape[0] * 2
    first = low_half(NCOL)

    def window(blk, slot, upper):
        base = pl.multiple_of((blk // 2) * PAIRED, PAIRED)
        w = ot_ref[:, pl.ds(base, PAIRED)].astype(F32)
        w = jnp.concatenate([w[NACT:], w[:NACT]], axis=0)
        moved = lax.rem(blk, 2) != (1 if upper else 0)
        w = jnp.where(moved, pltpu.roll(w, BS, 1), w)
        return jnp.where(slot < live, w, 0.0)

    for k in range(slabs // 2):
        a, b = 2 * k, 2 * k + 1
        left = jnp.where(first, window(rows[a], a, False), window(rows[b], b, True))
        lt_ref[k] = left.astype(BF)
        right = jnp.where(first, window(cols[a], a, False), window(cols[b], b, True))
        right = jnp.concatenate([right, right[NIN:]], axis=0)
        r_ref[pl.ds(k * PAIRED, PAIRED), :] = right.T.astype(BF)


def transform_block(sbuf, lt_ref, r_ref, pair_ref, half_ref, emit_pair):
    slabs = sbuf.shape[0]
    first = low_half(NBQ)
    first_s = low_half(BS)
    zero = jnp.zeros((BS, LANES), BF)

    def half_step(k, wait):
        wait(k)
        for j in range(sbuf.shape[2] // LANES):
            lanes = slice(j * LANES, (j + 1) * LANES)
            a = sbuf[2 * k, :, lanes].astype(F32)
            b = sbuf[2 * k + 1, :, lanes].astype(F32)
            even = jnp.where(first, a, pltpu.roll(b, BS, 1))
            odd = jnp.where(first, pltpu.roll(a, BS, 1), b)
            pair_ref[pl.ds(2 * j, NBQ, stride=BS), :] = even
            pair_ref[pl.ds(2 * j + 1, NBQ, stride=BS), :] = odd
        left = lt_ref[k]
        for q in range(0, NBQ, 2):
            cols = []
            for u in (q, q + 1):
                s = pair_ref[pl.ds(u * BS, BS), :].astype(BF)
                cols.append(
                    jnp.concatenate(
                        [jnp.where(first_s, s, zero), jnp.where(first_s, zero, s)], axis=0
                    )
                )
            half = jnp.dot(
                left, jnp.concatenate(cols, axis=1), preferred_element_type=F32
            ).astype(BF)
            at = pl.ds(pl.multiple_of(k * LANES, LANES), LANES)
            half_ref[q, :, at] = half[:, :LANES]
            half_ref[q + 1, :, at] = half[:, LANES:]

    def second_step(h):
        lhs = half_ref[pl.ds(2 * h, 2)].reshape(2 * NCOL, half_ref.shape[2])
        both = jnp.dot(lhs, r_ref[...], preferred_element_type=F32)
        w0, w1 = both[:NCOL], both[NCOL:]
        side = jnp.where(low_half(NCOL), w0[:, LANES:], w1[:, LANES:])
        across = side[:NIN].T
        in0 = w0[NIN:, :NIN] + across[:NACT]
        in1 = w1[NIN:, :NIN] + across[NACT:]
        square = jnp.concatenate([w0[NIN:, LANES:], w1[NIN:, LANES:]], axis=0).T
        act = side[NIN:] + square[:NACT]
        eye = lax.broadcasted_iota(jnp.int32, (NIN, NIN), 0) == lax.broadcasted_iota(
            jnp.int32, (NIN, NIN), 1
        )
        d0 = jnp.sum(jnp.where(eye, w0[:NIN, :NIN], 0.0), axis=0, keepdims=True)
        d1 = jnp.sum(jnp.where(eye, w1[:NIN, :NIN], 0.0), axis=0, keepdims=True)
        emit_pair(h, in0, in1, act, d0, d1)

    return half_step, second_step


def split_density(diag):
    d = 2.0 * jnp.sum(diag, axis=1, keepdims=True)
    d = jnp.broadcast_to(d, diag.shape)
    hi = d.astype(BF).astype(F32)
    return d, jnp.where(low_half(diag.shape[0]), hi, d - hi).astype(BF)


def load_slabs(slabs_ref, sbuf, sem, block, slot):
    copies = []
    for k in range(slabs_ref.shape[0] // 2):
        copies.append(
            pltpu.make_async_copy(
                slabs_ref.at[pl.ds(2 * k, 2), pl.ds(pl.multiple_of(block * NBQ, NBQ), NBQ), :],
                sbuf.at[slot, pl.ds(2 * k, 2)],
                sem.at[slot, k],
            )
        )
    return copies


def run_block(slabs_ref, sbuf, sem, block, slot, lt_ref, r_ref, pair_ref, half_ref, emit):
    def wait(k):
        pltpu.make_async_copy(
            slabs_ref.at[
                pl.ds(2 * k, 2), pl.ds(pl.multiple_of(block * NBQ, NBQ), NBQ), :
            ],
            sbuf.at[slot, pl.ds(2 * k, 2)],
            sem.at[slot, k],
        ).wait()

    half_step, second_step = transform_block(
        sbuf.at[slot], lt_ref, r_ref, pair_ref, half_ref, emit
    )
    lax.fori_loop(0, slabs_ref.shape[0] // 2, lambda k, c: (half_step(k, wait), c)[1], 0)
    lax.fori_loop(0, NBQ // 2, lambda h, c: (second_step(h), c)[1], 0)


def rows_of(h, first, count):
    return pl.ds(pl.multiple_of(first + h * count, 16), count)


def emit_active(h, act, core, x, send, keep, send_at, keep_at):
    quarter = NACT // 4
    for place in (0, 1):
        xx = (1 - x) if place == 0 else x
        for cc in (0, 1):
            block = act[: quarter]
            for idx in range(4):
                block = jnp.where(
                    2 * xx + cc == idx, act[idx * quarter : (idx + 1) * quarter], block
                ) if idx else act[:quarter]

            @pl.when(core == cc)
            def _():
                keep[place, rows_of(h, keep_at, quarter), :] = block

            @pl.when(core != cc)
            def _():
                send[rows_of(h, send_at[place], quarter), :] = block.astype(BF)


def first_kernel(
    where, rows, cols, live, slabs_ref, ot_ref, lt_out, r_out, msg, act_send, act_keep, dens,
    sbuf, pair_ref, half_ref, diag, sem,
):
    core, x = where[0], where[1]
    block = 2 * (1 - x) + (1 - core)
    for copy in load_slabs(slabs_ref, sbuf, sem, block, 0):
        copy.start()
    orbital_blocks(rows, cols, live[0], ot_ref, lt_out, r_out)

    def emit(h, in0, in1, act, d0, d1):
        msg[2 * h] = in0.astype(BF)
        msg[2 * h + 1] = in1.astype(BF)
        emit_active(h, act, core, x, act_send, act_keep, (0, 128), 0)
        diag[pl.ds(2 * h, 1), :] = d0
        diag[pl.ds(2 * h + 1, 1), :] = d1

    run_block(slabs_ref, sbuf, sem, block, 0, lt_out, r_out, pair_ref, half_ref, emit)
    dens[...] = 2.0 * diag[...]


def second_kernel(
    where, slabs_ref, lt_ref, r_ref, keep_in, act_send, act_keep, dens,
    sbuf, pair_ref, half_ref, diag, sem,
):
    core, x = where[0], where[1]
    block = 2 * (1 - x) + core
    for copy in load_slabs(slabs_ref, sbuf, sem, block, 0):
        copy.start()

    def emit(h, in0, in1, act, d0, d1):
        keep_in[2 * h] = in0
        keep_in[2 * h + 1] = in1
        emit_active(h, act, core, x, act_send, act_keep, (0, 128), 0)
        diag[pl.ds(2 * h, 1), :] = d0
        diag[pl.ds(2 * h + 1, 1), :] = d1

    run_block(slabs_ref, sbuf, sem, block, 0, lt_ref, r_ref, pair_ref, half_ref, emit)
    dens[...] = 2.0 * diag[...]


def third_kernel(
    where, slabs_ref, lt_ref, r_ref, send1, keep1, dens1, send2, keep2, dens2,
    msg, keep_in, act_keep, dens,
    sbuf, pair_ref, half_ref, diag, act_send, sem,
):
    core, x = where[0], where[1]
    blocks = (2 * x + (1 - core), 2 * x + core)
    for slot, block in enumerate(blocks):
        for copy in load_slabs(slabs_ref, sbuf, sem, block, slot):
            copy.start()

    inrows = NBQ * NACT
    per = NBQ // 2 * (NACT // 4)
    for slot, block in enumerate(blocks):

        def emit(h, in0, in1, act, d0, d1, slot=slot):
            if slot == 0:
                msg[rows_of(2 * h, 0, NACT), :] = in0.astype(BF)
                msg[rows_of(2 * h + 1, 0, NACT), :] = in1.astype(BF)
            else:
                keep_in[2 * h] = in0
                keep_in[2 * h + 1] = in1
            emit_active(
                h, act, core, x, msg, act_keep,
                (inrows + (3 - slot) * per, inrows + (7 - slot) * per), (2 + slot) * per,
            )
            diag[pl.ds(slot * NBQ + 2 * h, 1), :] = d0
            diag[pl.ds(slot * NBQ + 2 * h + 1, 1), :] = d1

        run_block(
            slabs_ref, sbuf, sem, block, slot, lt_ref, r_ref, pair_ref, half_ref, emit
        )
    for n, (send, keep) in enumerate(((send1, keep1), (send2, keep2))):
        for place in (0, 1):
            at = inrows + (4 * place + 1 - n) * per
            msg[pl.ds(at, per), :] = send[pl.ds(place * per, per), :]
            act_keep[place, pl.ds(n * per, per), :] = keep[place]
    for n, part in enumerate(
        (dens1[...] * 0.5, dens2[...] * 0.5, diag[:NBQ], diag[NBQ:])
    ):
        d, wire = split_density(part)
        dens[pl.ds(n * NBQ, NBQ), :] = d
        msg[pl.ds(inrows + 8 * per + (n ^ 1) * NBQ, NBQ), :] = wire


def exchange_kernel(mine, near, far, out):
    parts = []
    for q in range(NBQ):
        rows = pl.ds(q * NACT, NACT)
        parts.append(
            mine[q] + near[rows, :].astype(F32) + far[rows, :].astype(F32)
        )
    v = jnp.concatenate(parts, axis=1)
    hi = v.astype(BF)
    lo = (v - hi.astype(F32)).astype(BF)
    both = lax.dot_general(
        jnp.concatenate([hi, lo], axis=0), hi, (((1,), (1,)), ((), ())),
        preferred_element_type=F32,
    )
    out[...] = both[:NACT] + both[NACT:] + both[NACT:].T


def final_kernel(where, act, act_far, dens, dens_far, exch, own, partial):
    x = where[1]
    quarter = NACT // 4
    per = act.shape[0] // 4
    far = dens_far[...].astype(F32)
    far = far + pltpu.roll(far, BS, 1)
    d = dens[...] + far
    first = low_half(quarter)
    total = jnp.zeros((quarter, LANES), F32)
    halves = act.shape[0] // 2
    core = where[0]
    for n in range(4):
        xx = (1 - x) if n < 2 else x
        cc = (1 - core) if n % 2 == 0 else core
        base = NBQ * (2 * xx + cc)
        for h in range(NBQ // 2):
            a = act[pl.ds(n * per + h * quarter, quarter), :]
            m = (n + 2) % 4
            a = a + act_far[pl.ds(m * per + h * quarter, quarter), :].astype(F32)
            own[base + 2 * h] = a[:, :BS]
            own[base + 2 * h + 1] = a[:, BS:]
            q = n * NBQ + 2 * h
            scale = jnp.where(first, d[q : q + 1, :], d[q + 1 : q + 2, :])
            total = total + a * scale
    total = 2.0 * (total + pltpu.roll(total, BS, 1))
    partial[...] = -exch[...]
    at = pl.ds(pl.multiple_of((2 * x + core) * quarter, quarter), quarter)
    partial[at, :] = partial[at, :] + total[:, :BS]


VM = pl.BlockSpec(memory_space=pltpu.VMEM)
SM = pl.BlockSpec(memory_space=pltpu.SMEM)
HB = pl.BlockSpec(memory_space=pl.ANY)


def shape(dims, dtype):
    return jax.ShapeDtypeStruct(dims, dtype)


def slab_scratch(slabs, width, blocks):
    return [
        pltpu.VMEM((blocks, slabs, NBQ, width), BF),
        pltpu.VMEM((NBQ * BS, LANES), F32),
        pltpu.VMEM((NBQ, NCOL, slabs * BS), BF),
        pltpu.VMEM((blocks * NBQ, LANES), F32),
    ]


PARAMS = pltpu.CompilerParams(vmem_limit_bytes=48 * 1024 * 1024)


def paired_body(slabs, block_row, block_col, live_count, orbitals, hcore):
    nslab, batch, width = slabs.shape
    index = lax.axis_index("pair")
    core, x = lax.rem(index, 2), index // 2
    where = jnp.stack([core, x])
    swap_core = [(0, 1), (1, 0), (2, 3), (3, 2)]
    swap_x = [(0, 2), (2, 0), (1, 3), (3, 1)]
    inrows = NBQ * NACT
    per = NBQ // 2 * (NACT // 4)
    aos = nslab * BS
    small = (
        shape((2 * per, LANES), BF),
        shape((2, per, LANES), F32),
        shape((NBQ, LANES), F32),
    )
    lt, r, msg1, send1, keep1, dens1 = pl.pallas_call(
        first_kernel,
        name="slabs_first",
        in_specs=[SM, SM, SM, SM, HB, VM],
        out_specs=[VM] * 6,
        out_shape=(
            shape((nslab // 2, NCOL, PAIRED), BF),
            shape((aos, 2 * LANES), BF),
            shape((NBQ, NACT, NIN), BF),
        ) + small,
        scratch_shapes=slab_scratch(nslab, width, 1) + [pltpu.SemaphoreType.DMA((1, nslab // 2))],
        compiler_params=PARAMS,
    )(where, block_row, block_col, live_count, slabs, orbitals.T)
    near1 = lax.ppermute(msg1.reshape(inrows, LANES), "pair", swap_core)
    keep_in2, send2, keep2, dens2 = pl.pallas_call(
        second_kernel,
        name="slabs_second",
        in_specs=[SM, HB, VM, VM],
        out_specs=[VM] * 4,
        out_shape=(shape((NBQ, NACT, NIN), F32),) + small,
        scratch_shapes=slab_scratch(nslab, width, 1) + [pltpu.SemaphoreType.DMA((1, nslab // 2))],
        compiler_params=PARAMS,
        cost_estimate=pl.CostEstimate(flops=4 * 10**9, bytes_accessed=4 * 10**6, transcendentals=0),
    )(where, slabs, lt, r)
    out2 = (keep_in2.reshape(inrows, LANES) + near1.astype(F32)).astype(BF)
    far1 = lax.ppermute(out2, "pair", swap_x)
    msg3, keep_in3, act_keep, dens = pl.pallas_call(
        third_kernel,
        name="slabs_third",
        in_specs=[SM, HB] + [VM] * 8,
        out_specs=[VM] * 4,
        out_shape=(
            shape((inrows + 8 * per + 4 * NBQ, LANES), BF),
            shape((NBQ, NACT, NIN), F32),
            shape((2, 4 * per, LANES), F32),
            shape((4 * NBQ, LANES), F32),
        ),
        scratch_shapes=slab_scratch(nslab, width, 2)
        + [pltpu.VMEM((16, LANES), BF), pltpu.SemaphoreType.DMA((2, nslab // 2))],
        compiler_params=PARAMS,
        cost_estimate=pl.CostEstimate(flops=8 * 10**9, bytes_accessed=8 * 10**6, transcendentals=0),
    )(where, slabs, lt, r, send1, keep1, dens1, send2, keep2, dens2)
    near3 = lax.ppermute(msg3, "pair", swap_core)
    near_dens = near3[inrows + 8 * per :].astype(F32)
    near_dens = near_dens[:, :BS] + near_dens[:, BS:]
    dens = dens + jnp.concatenate([near_dens, near_dens], axis=1)
    act_other = act_keep[0] + near3[inrows : inrows + 4 * per].astype(F32)
    hi = dens.astype(BF).astype(F32)
    wire = jnp.where(lax.broadcasted_iota(jnp.int32, dens.shape, 1) < BS, hi, dens - hi)
    far3 = lax.ppermute(
        jnp.concatenate([act_other, wire], axis=0).astype(BF), "pair", swap_x
    )
    act_own = act_keep[1] + near3[inrows + 4 * per : inrows + 8 * per].astype(F32)
    exch = pl.pallas_call(
        exchange_kernel,
        name="exchange",
        in_specs=[VM] * 3,
        out_specs=VM,
        out_shape=shape((NACT, NACT), F32),
        compiler_params=PARAMS,
    )(keep_in3, near3[:inrows], far1)
    dens_far = far3[4 * per :]
    dens_far = jnp.concatenate([dens_far[2 * NBQ :], dens_far[: 2 * NBQ]], axis=0)
    own, partial = pl.pallas_call(
        final_kernel,
        name="active_and_coulomb",
        in_specs=[SM] + [VM] * 5,
        out_specs=[VM] * 2,
        out_shape=(
            shape((batch, NACT // 4, NACT), F32),
            shape((NACT, NACT), F32),
        ),
        compiler_params=PARAMS,
    )(where, act_own, far3[: 4 * per], dens, dens_far, exch)
    summed = lax.psum(partial, ("pair", "aux"))
    mine = lax.dynamic_slice_in_dim(summed, index * (NACT // 4), NACT // 4, 0)
    return (own, hcore + mine)


def slab_terms(values, left, right):
    half = jnp.einsum("mc,qmn->qnc", left, values, preferred_element_type=F32).astype(BF)
    first = jnp.einsum("qnt,nc->qtc", half[:, :, :NACT], right, preferred_element_type=F32)
    second = jnp.einsum("qnc,nt->qtc", half, right[:, :NACT], preferred_element_type=F32)
    trace = 2.0 * jnp.einsum(
        "qni,ni->q", half[:, :, NACT:], right[:, NACT:], preferred_element_type=F32
    )
    return (first + second, trace)


def general_body(slabs, block_row, block_col, live_count, orbitals, hcore):
    batch = slabs.shape[1]
    init = (jnp.zeros((batch, NACT, NCOL), F32), jnp.zeros((batch,), F32))

    def visit(k, state):
        values = lax.dynamic_index_in_dim(slabs, k, 0, keepdims=False)
        left = lax.dynamic_slice_in_dim(orbitals, block_row[k] * BS, BS, 0)
        right = lax.dynamic_slice_in_dim(orbitals, block_col[k] * BS, BS, 0)
        terms, trace = slab_terms(values.reshape(batch, BS, BS), left, right)
        return (state[0] + terms, state[1] + trace)

    vectors, density = lax.fori_loop(0, live_count[0], visit, init)
    density = lax.psum(density, "pair")
    owned = lax.psum_scatter(vectors, "pair", scatter_dimension=1, tiled=True)
    own_active, own_inactive = owned[:, :, :NACT], owned[:, :, NACT:]
    gathered = lax.all_gather(own_inactive.astype(BF), "pair", axis=1, tiled=True)
    exchange = jnp.einsum(
        "qti,qui->tu", own_inactive, gathered.astype(F32), precision=lax.Precision.HIGHEST
    )
    coulomb = jnp.einsum("qtu,q->tu", own_active, density, precision=lax.Precision.HIGHEST)
    return (own_active, hcore + lax.psum(2.0 * coulomb - exchange, "aux"))


def solution(mesh):
    placed = (
        P(("frag", "pair"), "aux", None),
        P(("frag", "pair")),
        P(("frag", "pair")),
        P(("frag", "pair")),
        P("frag", None),
        P(("frag", "pair"), None),
    )

    def body(slabs, *rest):
        fits = mesh.shape["pair"] == 4 and slabs.shape[1] == 4 * NBQ and slabs.shape[0] % 2 == 0
        return (paired_body if fits else general_body)(slabs, *rest)

    return jax.shard_map(
        body,
        mesh=mesh,
        in_specs=placed,
        out_specs=(P(("frag", "aux"), "pair", None), P(("frag", "pair"), None)),
        check_vma=False,
    )
```

```python
import jax
import jax.numpy as jnp
from jax import lax
from jax.experimental import pallas as pl
from jax.experimental.pallas import tpu as pltpu
from jax.sharding import PartitionSpec as P

BS = 64
NACT = 64
NCOL = 192
NIN = NCOL - NACT
LANES = 128
NBQ = 16
PAIRED = 2 * BS
QSTEP, MSTEP = 3, 49
BF = jnp.bfloat16
F32 = jnp.float32


def low_half(rows):
    return lax.broadcasted_iota(jnp.int32, (rows, LANES), 1) < BS


def orbital_blocks(rows, cols, live, ot_ref, lt_ref, r_ref):
    slabs = lt_ref.shape[0] * 2
    first = low_half(NCOL)

    def window(blk, slot, upper):
        base = pl.multiple_of((blk // 2) * PAIRED, PAIRED)
        w = ot_ref[:, pl.ds(base, PAIRED)].astype(F32)
        w = jnp.concatenate([w[NACT:], w[:NACT]], axis=0)
        moved = lax.rem(blk, 2) != (1 if upper else 0)
        w = jnp.where(moved, pltpu.roll(w, BS, 1), w)
        return jnp.where(slot < live, w, 0.0)

    for k in range(slabs // 2):
        a, b = 2 * k, 2 * k + 1
        left = jnp.where(first, window(rows[a], a, False), window(rows[b], b, True))
        lt_ref[k] = left.astype(BF)
        right = jnp.where(first, window(cols[a], a, False), window(cols[b], b, True))
        right = jnp.concatenate([right, right[NIN:]], axis=0)
        r_ref[pl.ds(k * PAIRED, PAIRED), :] = right.T.astype(BF)


def transform_block(sbuf, lt_ref, r_ref, pair_ref, half_ref, emit_pair):
    slabs = sbuf.shape[0]
    first = low_half(NBQ)
    first_s = low_half(BS)
    zero = jnp.zeros((BS, LANES), BF)

    def half_step(k, wait):
        wait(k)
        for j in range(sbuf.shape[2] // LANES):
            lanes = slice(j * LANES, (j + 1) * LANES)
            a = sbuf[2 * k, :, lanes].astype(F32)
            b = sbuf[2 * k + 1, :, lanes].astype(F32)
            even = jnp.where(first, a, pltpu.roll(b, BS, 1))
            odd = jnp.where(first, pltpu.roll(a, BS, 1), b)
            pair_ref[pl.ds(MSTEP * 2 * j, NBQ, stride=QSTEP), :] = even
            pair_ref[pl.ds(MSTEP * (2 * j + 1), NBQ, stride=QSTEP), :] = odd
        left = lt_ref[k]
        for q in range(0, NBQ, 2):
            cols = []
            for u in (q, q + 1):
                s = pair_ref[pl.ds(u * QSTEP, BS, stride=MSTEP), :].astype(BF)
                cols.append(
                    jnp.concatenate(
                        [jnp.where(first_s, s, zero), jnp.where(first_s, zero, s)], axis=0
                    )
                )
            half = jnp.dot(
                left, jnp.concatenate(cols, axis=1), preferred_element_type=F32
            ).astype(BF)
            at = pl.ds(pl.multiple_of(k * LANES, LANES), LANES)
            half_ref[q, :, at] = half[:, :LANES]
            half_ref[q + 1, :, at] = half[:, LANES:]

    def second_step(h):
        lhs = half_ref[pl.ds(2 * h, 2)].reshape(2 * NCOL, half_ref.shape[2])
        both = jnp.dot(lhs, r_ref[...], preferred_element_type=F32)
        w0, w1 = both[:NCOL], both[NCOL:]
        side = jnp.where(low_half(NCOL), w0[:, LANES:], w1[:, LANES:])
        across = side[:NIN].T
        in0 = w0[NIN:, :NIN] + across[:NACT]
        in1 = w1[NIN:, :NIN] + across[NACT:]
        square = jnp.concatenate([w0[NIN:, LANES:], w1[NIN:, LANES:]], axis=0).T
        act = side[NIN:] + square[:NACT]
        eye = lax.broadcasted_iota(jnp.int32, (NIN, NIN), 0) == lax.broadcasted_iota(
            jnp.int32, (NIN, NIN), 1
        )
        d0 = jnp.sum(jnp.where(eye, w0[:NIN, :NIN], 0.0), axis=0, keepdims=True)
        d1 = jnp.sum(jnp.where(eye, w1[:NIN, :NIN], 0.0), axis=0, keepdims=True)
        emit_pair(h, in0, in1, act, d0, d1)

    return half_step, second_step


def split_density(diag):
    d = 2.0 * jnp.sum(diag, axis=1, keepdims=True)
    d = jnp.broadcast_to(d, diag.shape)
    hi = d.astype(BF).astype(F32)
    return d, jnp.where(low_half(diag.shape[0]), hi, d - hi).astype(BF)


def load_slabs(slabs_ref, sbuf, sem, block, slot):
    copies = []
    for k in range(slabs_ref.shape[0] // 2):
        copies.append(
            pltpu.make_async_copy(
                slabs_ref.at[pl.ds(2 * k, 2), pl.ds(pl.multiple_of(block * NBQ, NBQ), NBQ), :],
                sbuf.at[slot, pl.ds(2 * k, 2)],
                sem.at[slot, k],
            )
        )
    return copies


def run_block(slabs_ref, sbuf, sem, block, slot, lt_ref, r_ref, pair_ref, half_ref, emit):
    def wait(k):
        pltpu.make_async_copy(
            slabs_ref.at[
                pl.ds(2 * k, 2), pl.ds(pl.multiple_of(block * NBQ, NBQ), NBQ), :
            ],
            sbuf.at[slot, pl.ds(2 * k, 2)],
            sem.at[slot, k],
        ).wait()

    half_step, second_step = transform_block(
        sbuf.at[slot], lt_ref, r_ref, pair_ref, half_ref, emit
    )
    lax.fori_loop(0, slabs_ref.shape[0] // 2, lambda k, c: (half_step(k, wait), c)[1], 0)
    lax.fori_loop(0, NBQ // 2, lambda h, c: (second_step(h), c)[1], 0)


def rows_of(h, first, count):
    return pl.ds(pl.multiple_of(first + h * count, 16), count)


def emit_active(h, act, core, x, send, keep, send_at, keep_at):
    quarter = NACT // 4
    for place in (0, 1):
        xx = (1 - x) if place == 0 else x
        for cc in (0, 1):
            block = act[: quarter]
            for idx in range(4):
                block = jnp.where(
                    2 * xx + cc == idx, act[idx * quarter : (idx + 1) * quarter], block
                ) if idx else act[:quarter]

            @pl.when(core == cc)
            def _():
                keep[place, rows_of(h, keep_at, quarter), :] = block

            @pl.when(core != cc)
            def _():
                send[rows_of(h, send_at[place], quarter), :] = block.astype(BF)


def first_kernel(
    where, rows, cols, live, slabs_ref, ot_ref, lt_out, r_out, msg, act_send, act_keep, dens,
    sbuf, pair_ref, half_ref, diag, sem,
):
    core, x = where[0], where[1]
    block = 2 * (1 - x) + (1 - core)
    for copy in load_slabs(slabs_ref, sbuf, sem, block, 0):
        copy.start()
    orbital_blocks(rows, cols, live[0], ot_ref, lt_out, r_out)

    def emit(h, in0, in1, act, d0, d1):
        msg[2 * h] = in0.astype(BF)
        msg[2 * h + 1] = in1.astype(BF)
        emit_active(h, act, core, x, act_send, act_keep, (0, 128), 0)
        diag[pl.ds(2 * h, 1), :] = d0
        diag[pl.ds(2 * h + 1, 1), :] = d1

    run_block(slabs_ref, sbuf, sem, block, 0, lt_out, r_out, pair_ref, half_ref, emit)
    dens[...] = 2.0 * diag[...]


def second_kernel(
    where, slabs_ref, lt_ref, r_ref, keep_in, act_send, act_keep, dens,
    sbuf, pair_ref, half_ref, diag, sem,
):
    core, x = where[0], where[1]
    block = 2 * (1 - x) + core
    for copy in load_slabs(slabs_ref, sbuf, sem, block, 0):
        copy.start()

    def emit(h, in0, in1, act, d0, d1):
        keep_in[2 * h] = in0
        keep_in[2 * h + 1] = in1
        emit_active(h, act, core, x, act_send, act_keep, (0, 128), 0)
        diag[pl.ds(2 * h, 1), :] = d0
        diag[pl.ds(2 * h + 1, 1), :] = d1

    run_block(slabs_ref, sbuf, sem, block, 0, lt_ref, r_ref, pair_ref, half_ref, emit)
    dens[...] = 2.0 * diag[...]


def third_kernel(
    where, slabs_ref, lt_ref, r_ref, send1, keep1, dens1, send2, keep2, dens2,
    msg, keep_in, act_keep, dens,
    sbuf, pair_ref, half_ref, diag, act_send, sem,
):
    core, x = where[0], where[1]
    blocks = (2 * x + (1 - core), 2 * x + core)
    for slot, block in enumerate(blocks):
        for copy in load_slabs(slabs_ref, sbuf, sem, block, slot):
            copy.start()

    inrows = NBQ * NACT
    per = NBQ // 2 * (NACT // 4)
    for slot, block in enumerate(blocks):

        def emit(h, in0, in1, act, d0, d1, slot=slot):
            if slot == 0:
                msg[rows_of(2 * h, 0, NACT), :] = in0.astype(BF)
                msg[rows_of(2 * h + 1, 0, NACT), :] = in1.astype(BF)
            else:
                keep_in[2 * h] = in0
                keep_in[2 * h + 1] = in1
            emit_active(
                h, act, core, x, msg, act_keep,
                (inrows + (3 - slot) * per, inrows + (7 - slot) * per), (2 + slot) * per,
            )
            diag[pl.ds(slot * NBQ + 2 * h, 1), :] = d0
            diag[pl.ds(slot * NBQ + 2 * h + 1, 1), :] = d1

        run_block(
            slabs_ref, sbuf, sem, block, slot, lt_ref, r_ref, pair_ref, half_ref, emit
        )
    for n, (send, keep) in enumerate(((send1, keep1), (send2, keep2))):
        for place in (0, 1):
            at = inrows + (4 * place + 1 - n) * per
            msg[pl.ds(at, per), :] = send[pl.ds(place * per, per), :]
            act_keep[place, pl.ds(n * per, per), :] = keep[place]
    for n, part in enumerate(
        (dens1[...] * 0.5, dens2[...] * 0.5, diag[:NBQ], diag[NBQ:])
    ):
        d, wire = split_density(part)
        dens[pl.ds(n * NBQ, NBQ), :] = d
        msg[pl.ds(inrows + 8 * per + (n ^ 1) * NBQ, NBQ), :] = wire


def exchange_kernel(mine, near, far, out):
    parts = []
    for q in range(NBQ):
        rows = pl.ds(q * NACT, NACT)
        parts.append(
            mine[q] + near[rows, :].astype(F32) + far[rows, :].astype(F32)
        )
    v = jnp.concatenate(parts, axis=1)
    hi = v.astype(BF)
    lo = (v - hi.astype(F32)).astype(BF)
    both = lax.dot_general(
        jnp.concatenate([hi, lo], axis=0), hi, (((1,), (1,)), ((), ())),
        preferred_element_type=F32,
    )
    out[...] = both[:NACT] + both[NACT:] + both[NACT:].T


def final_kernel(where, act, act_far, dens, dens_far, exch, e1, e2, e3, own, partial):
    x = where[1]
    quarter = NACT // 4
    per = act.shape[0] // 4
    far = dens_far[...].astype(F32)
    far = far + pltpu.roll(far, BS, 1)
    d = dens[...] + far
    first = low_half(quarter)
    total = jnp.zeros((quarter, LANES), F32)
    halves = act.shape[0] // 2
    core = where[0]
    for n in range(4):
        xx = (1 - x) if n < 2 else x
        cc = (1 - core) if n % 2 == 0 else core
        base = NBQ * (2 * xx + cc)
        for h in range(NBQ // 2):
            a = act[pl.ds(n * per + h * quarter, quarter), :]
            m = (n + 2) % 4
            a = a + act_far[pl.ds(m * per + h * quarter, quarter), :].astype(F32)
            own[base + 2 * h] = a[:, :BS]
            own[base + 2 * h + 1] = a[:, BS:]
            q = n * NBQ + 2 * h
            scale = jnp.where(first, d[q : q + 1, :], d[q + 1 : q + 2, :])
            total = total + a * scale
    total = 2.0 * (total + pltpu.roll(total, BS, 1))
    at = pl.ds(pl.multiple_of((2 * x + core) * quarter, quarter), quarter)
    partial[...] = total[:, :BS] - (exch[at, :] + e1[...] + e2[...] + e3[...])


VM = pl.BlockSpec(memory_space=pltpu.VMEM)
SM = pl.BlockSpec(memory_space=pltpu.SMEM)
HB = pl.BlockSpec(memory_space=pl.ANY)


def shape(dims, dtype):
    return jax.ShapeDtypeStruct(dims, dtype)


def slab_scratch(slabs, width, blocks):
    return [
        pltpu.VMEM((blocks, slabs, NBQ, width), BF),
        pltpu.VMEM((MSTEP * BS, LANES), F32),
        pltpu.VMEM((NBQ, NCOL, slabs * BS), BF),
        pltpu.VMEM((blocks * NBQ, LANES), F32),
    ]


PARAMS = pltpu.CompilerParams(vmem_limit_bytes=48 * 1024 * 1024)


def sum_over_aux(part):
    n = lax.axis_size("aux")
    if n != 4:
        return lax.psum(part, "aux")
    one, two, three = (
        lax.ppermute(part, "aux", [(z, (z + k) % n) for z in range(n)]) for k in (1, 2, 3)
    )
    return (part + two) + (one + three)


def paired_body(slabs, block_row, block_col, live_count, orbitals, hcore):
    nslab, batch, width = slabs.shape
    index = lax.axis_index("pair")
    core, x = lax.rem(index, 2), index // 2
    where = jnp.stack([core, x])
    swap_core = [(0, 1), (1, 0), (2, 3), (3, 2)]
    swap_x = [(0, 2), (2, 0), (1, 3), (3, 1)]
    inrows = NBQ * NACT
    per = NBQ // 2 * (NACT // 4)
    aos = nslab * BS
    small = (
        shape((2 * per, LANES), BF),
        shape((2, per, LANES), F32),
        shape((NBQ, LANES), F32),
    )
    lt, r, msg1, send1, keep1, dens1 = pl.pallas_call(
        first_kernel,
        name="slabs_first",
        in_specs=[SM, SM, SM, SM, HB, VM],
        out_specs=[VM] * 6,
        out_shape=(
            shape((nslab // 2, NCOL, PAIRED), BF),
            shape((aos, 2 * LANES), BF),
            shape((NBQ, NACT, NIN), BF),
        ) + small,
        scratch_shapes=slab_scratch(nslab, width, 1) + [pltpu.SemaphoreType.DMA((1, nslab // 2))],
        compiler_params=PARAMS,
    )(where, block_row, block_col, live_count, slabs, orbitals.T)
    near1 = lax.ppermute(msg1.reshape(inrows, LANES), "pair", swap_core)
    keep_in2, send2, keep2, dens2 = pl.pallas_call(
        second_kernel,
        name="slabs_second",
        in_specs=[SM, HB, VM, VM],
        out_specs=[VM] * 4,
        out_shape=(shape((NBQ, NACT, NIN), F32),) + small,
        scratch_shapes=slab_scratch(nslab, width, 1) + [pltpu.SemaphoreType.DMA((1, nslab // 2))],
        compiler_params=PARAMS,
        cost_estimate=pl.CostEstimate(flops=4 * 10**9, bytes_accessed=4 * 10**6, transcendentals=0),
    )(where, slabs, lt, r)
    out2 = (keep_in2.reshape(inrows, LANES) + near1.astype(F32)).astype(BF)
    far1 = lax.ppermute(out2, "pair", swap_x)
    msg3, keep_in3, act_keep, dens = pl.pallas_call(
        third_kernel,
        name="slabs_third",
        in_specs=[SM, HB] + [VM] * 8,
        out_specs=[VM] * 4,
        out_shape=(
            shape((inrows + 8 * per + 4 * NBQ, LANES), BF),
            shape((NBQ, NACT, NIN), F32),
            shape((2, 4 * per, LANES), F32),
            shape((4 * NBQ, LANES), F32),
        ),
        scratch_shapes=slab_scratch(nslab, width, 2)
        + [pltpu.VMEM((16, LANES), BF), pltpu.SemaphoreType.DMA((2, nslab // 2))],
        compiler_params=PARAMS,
        cost_estimate=pl.CostEstimate(flops=8 * 10**9, bytes_accessed=8 * 10**6, transcendentals=0),
    )(where, slabs, lt, r, send1, keep1, dens1, send2, keep2, dens2)
    near3 = lax.ppermute(msg3, "pair", swap_core)
    near_dens = near3[inrows + 8 * per :].astype(F32)
    near_dens = near_dens[:, :BS] + near_dens[:, BS:]
    dens = dens + jnp.concatenate([near_dens, near_dens], axis=1)
    act_other = act_keep[0] + near3[inrows : inrows + 4 * per].astype(F32)
    hi = dens.astype(BF).astype(F32)
    wire = jnp.where(lax.broadcasted_iota(jnp.int32, dens.shape, 1) < BS, hi, dens - hi)
    far3 = lax.ppermute(
        jnp.concatenate([act_other, wire], axis=0).astype(BF), "pair", swap_x
    )
    act_own = act_keep[1] + near3[inrows + 4 * per : inrows + 8 * per].astype(F32)
    exch = pl.pallas_call(
        exchange_kernel,
        name="exchange",
        in_specs=[VM] * 3,
        out_specs=VM,
        out_shape=shape((NACT, NACT), F32),
        compiler_params=PARAMS,
    )(keep_in3, near3[:inrows], far1)
    def rows_for(peer):
        return lax.dynamic_slice_in_dim(exch, peer * (NACT // 4), NACT // 4, 0)

    parts = [
        lax.ppermute(rows_for(index ^ k), "pair", [(p, p ^ k) for p in range(4)])
        for k in (1, 2, 3)
    ]
    dens_far = far3[4 * per :]
    dens_far = jnp.concatenate([dens_far[2 * NBQ :], dens_far[: 2 * NBQ]], axis=0)
    own, partial = pl.pallas_call(
        final_kernel,
        name="active_and_coulomb",
        in_specs=[SM] + [VM] * 8,
        out_specs=[VM] * 2,
        out_shape=(
            shape((batch, NACT // 4, NACT), F32),
            shape((NACT // 4, NACT), F32),
        ),
        compiler_params=PARAMS,
    )(where, act_own, far3[: 4 * per], dens, dens_far, exch, *parts)
    return (own, hcore + sum_over_aux(partial))


def slab_terms(values, left, right):
    half = jnp.einsum("mc,qmn->qnc", left, values, preferred_element_type=F32).astype(BF)
    first = jnp.einsum("qnt,nc->qtc", half[:, :, :NACT], right, preferred_element_type=F32)
    second = jnp.einsum("qnc,nt->qtc", half, right[:, :NACT], preferred_element_type=F32)
    trace = 2.0 * jnp.einsum(
        "qni,ni->q", half[:, :, NACT:], right[:, NACT:], preferred_element_type=F32
    )
    return (first + second, trace)


def general_body(slabs, block_row, block_col, live_count, orbitals, hcore):
    batch = slabs.shape[1]
    init = (jnp.zeros((batch, NACT, NCOL), F32), jnp.zeros((batch,), F32))

    def visit(k, state):
        values = lax.dynamic_index_in_dim(slabs, k, 0, keepdims=False)
        left = lax.dynamic_slice_in_dim(orbitals, block_row[k] * BS, BS, 0)
        right = lax.dynamic_slice_in_dim(orbitals, block_col[k] * BS, BS, 0)
        terms, trace = slab_terms(values.reshape(batch, BS, BS), left, right)
        return (state[0] + terms, state[1] + trace)

    vectors, density = lax.fori_loop(0, live_count[0], visit, init)
    density = lax.psum(density, "pair")
    owned = lax.psum_scatter(vectors, "pair", scatter_dimension=1, tiled=True)
    own_active, own_inactive = owned[:, :, :NACT], owned[:, :, NACT:]
    gathered = lax.all_gather(own_inactive.astype(BF), "pair", axis=1, tiled=True)
    exchange = jnp.einsum(
        "qti,qui->tu", own_inactive, gathered.astype(F32), precision=lax.Precision.HIGHEST
    )
    coulomb = jnp.einsum("qtu,q->tu", own_active, density, precision=lax.Precision.HIGHEST)
    return (own_active, hcore + lax.psum(2.0 * coulomb - exchange, "aux"))


def solution(mesh):
    placed = (
        P(("frag", "pair"), "aux", None),
        P(("frag", "pair")),
        P(("frag", "pair")),
        P(("frag", "pair")),
        P("frag", None),
        P(("frag", "pair"), None),
    )

    def body(slabs, *rest):
        fits = mesh.shape["pair"] == 4 and slabs.shape[1] == 4 * NBQ and slabs.shape[0] % 2 == 0
        return (paired_body if fits else general_body)(slabs, *rest)

    return jax.shard_map(
        body,
        mesh=mesh,
        in_specs=placed,
        out_specs=(P(("frag", "aux"), "pair", None), P(("frag", "pair"), None)),
        check_vma=False,
    )
```

```python
import jax
import jax.numpy as jnp
from jax import lax
from jax.experimental import pallas as pl
from jax.experimental.pallas import tpu as pltpu
from jax.sharding import PartitionSpec as P

BS = 64
NACT = 64
NCOL = 192
NIN = NCOL - NACT
LANES = 128
NBQ = 16
PAIRED = 2 * BS
QSTEP, MSTEP = 3, 49
BF = jnp.bfloat16
F32 = jnp.float32


def low_half(rows):
    return lax.broadcasted_iota(jnp.int32, (rows, LANES), 1) < BS


def orbital_blocks(scalars, slabs, windows, lt_ref, r_ref):
    first = low_half(NCOL)
    live = scalars[2 * slabs]

    def window(n, slot, upper):
        w = windows[n].astype(F32)
        w = jnp.concatenate([w[NACT:], w[:NACT]], axis=0)
        moved = lax.rem(scalars[n], 2) != (1 if upper else 0)
        w = jnp.where(moved, pltpu.roll(w, BS, 1), w)
        return jnp.where(slot < live, w, 0.0)

    for k in range(slabs // 2):
        a, b = 2 * k, 2 * k + 1
        left = jnp.where(first, window(a, a, False), window(b, b, True))
        lt_ref[k] = left.astype(BF)
        right = jnp.where(first, window(slabs + a, a, False), window(slabs + b, b, True))
        right = jnp.concatenate([right, right[NIN:]], axis=0)
        r_ref[pl.ds(k * PAIRED, PAIRED), :] = right.T.astype(BF)


def slab_copy(slabs_ref, sbuf, sem, block, k):
    last = slabs_ref.shape[0] // 2 - 1
    pair = min(k, last) if isinstance(k, int) else jnp.minimum(k, last)
    return pltpu.make_async_copy(
        slabs_ref.at[pl.ds(2 * pair, 2), pl.ds(pl.multiple_of(block * NBQ, NBQ), NBQ), :],
        sbuf.at[k],
        sem.at[k],
    )


def start_slabs(slabs_ref, sbuf, sem, block):
    for k in range(slabs_ref.shape[0] // 2 + 1):
        slab_copy(slabs_ref, sbuf, sem, block, k).start()


def run_block(slabs_ref, block, lt_ref, r_ref, scratch, emit):
    sbuf, even_ref, odd_ref, half_ref, diag, sem = scratch
    pairs = slabs_ref.shape[0] // 2
    first = low_half(NBQ)
    first_s = low_half(BS)
    zero = jnp.zeros((BS, LANES), BF)
    group = 4

    def wait(k):
        slab_copy(slabs_ref, sbuf, sem, block, k).wait()

    def relayout(k, out):
        for j in range(sbuf.shape[3] // LANES):
            lanes = slice(j * LANES, (j + 1) * LANES)
            a = sbuf[k, 0, :, lanes].astype(F32)
            b = sbuf[k, 1, :, lanes].astype(F32)
            out[pl.ds(MSTEP * 2 * j, NBQ, stride=QSTEP), :] = jnp.where(
                first, a, pltpu.roll(b, BS, 1)
            )
            out[pl.ds(MSTEP * (2 * j + 1), NBQ, stride=QSTEP), :] = jnp.where(
                first, pltpu.roll(a, BS, 1), b
            )

    def half_transform(k, rows):
        left = lt_ref[k]
        at = pl.ds(pl.multiple_of(k * LANES, LANES), LANES)
        for q in range(0, NBQ, group):
            cols = []
            for u in range(q, q + group):
                s = rows[pl.ds(u * QSTEP, BS, stride=MSTEP), :].astype(BF)
                cols.append(
                    jnp.concatenate(
                        [jnp.where(first_s, s, zero), jnp.where(first_s, zero, s)], axis=0
                    )
                )
            half = jnp.dot(left, jnp.concatenate(cols, axis=1), preferred_element_type=F32)
            half = half.astype(BF)
            for u in range(group):
                half_ref[q + u, :, at] = half[:, u * LANES : (u + 1) * LANES]

    def two_pairs(i, carry):
        wait(2 * i + 1)
        wait(2 * i + 2)
        relayout(2 * i + 1, odd_ref)
        half_transform(2 * i, even_ref)
        relayout(2 * i + 2, even_ref)
        half_transform(2 * i + 1, odd_ref)
        return carry

    def second_transform(g, carry):
        lhs = half_ref[pl.ds(group * g, group)].reshape(group * NCOL, half_ref.shape[2])
        whole = jnp.dot(lhs, r_ref[...], preferred_element_type=F32)
        eye = lax.broadcasted_iota(jnp.int32, (NIN, NIN), 0) == lax.broadcasted_iota(
            jnp.int32, (NIN, NIN), 1
        )
        for p in range(group // 2):
            w0 = whole[2 * p * NCOL : (2 * p + 1) * NCOL]
            w1 = whole[(2 * p + 1) * NCOL : (2 * p + 2) * NCOL]
            side = jnp.where(low_half(NCOL), w0[:, LANES:], w1[:, LANES:])
            across = side[:NIN].T
            square = jnp.concatenate([w0[NIN:, LANES:], w1[NIN:, LANES:]], axis=0).T
            h = group // 2 * g + p
            emit(
                h,
                w0[NIN:, :NIN] + across[:NACT],
                w1[NIN:, :NIN] + across[NACT:],
                side[NIN:] + square[:NACT],
            )
            for n, w in enumerate((w0, w1)):
                diag[pl.ds(2 * h + n, 1), :] = jnp.sum(
                    jnp.where(eye, w[:NIN, :NIN], 0.0), axis=0, keepdims=True
                )
        return carry

    wait(0)
    relayout(0, even_ref)
    lax.fori_loop(0, pairs // 2, two_pairs, 0)
    lax.fori_loop(0, NBQ // group, second_transform, 0)


def split_wire(d):
    hi = d.astype(BF).astype(F32)
    return jnp.where(low_half(d.shape[0]), hi, d - hi).astype(BF)


def joined(wire):
    w = wire.astype(F32)
    return w + pltpu.roll(w, BS, 1)


def density_of(diag):
    d = 2.0 * jnp.sum(diag, axis=1, keepdims=True)
    return jnp.broadcast_to(d, diag.shape)


QUARTER = NACT // 4
PER = NBQ // 2 * QUARTER
INROWS = NBQ * NACT


def emit_active(h, act, core, x, send, keep, send_at):
    for place in (0, 1):
        xx = (1 - x) if place == 0 else x
        for cc in (0, 1):
            block = act[:QUARTER]
            for idx in range(1, 4):
                block = jnp.where(
                    2 * xx + cc == idx, act[idx * QUARTER : (idx + 1) * QUARTER], block
                )
            off = place * PER + h * QUARTER

            @pl.when(core == cc)
            def _():
                keep[pl.ds(pl.multiple_of(off, QUARTER), QUARTER), :] = block

            @pl.when(core != cc)
            def _():
                send[pl.ds(pl.multiple_of(send_at + off, QUARTER), QUARTER), :] = block.astype(BF)


def pair_rows(h, n):
    return pl.ds(pl.multiple_of((2 * h + n) * NACT, NACT), NACT)


def first_kernel(
    scalars, slabs_ref, ot_ref, lt_out, r_out, msg, keep, dens, windows, wsem, *scratch
):
    slabs = slabs_ref.shape[0]
    core, x = scalars[2 * slabs + 1], scalars[2 * slabs + 2]
    block = 2 * (1 - x) + (1 - core)
    copies = []
    for n in range(2 * slabs):
        base = pl.multiple_of((scalars[n] // 2) * PAIRED, PAIRED)
        copies.append(
            pltpu.make_async_copy(ot_ref.at[:, pl.ds(base, PAIRED)], windows.at[n], wsem.at[n])
        )
        copies[-1].start()
    sbuf, sem, diag = scratch[0], scratch[5], scratch[4]
    start_slabs(slabs_ref, sbuf, sem, block)
    for copy in copies:
        copy.wait()
    orbital_blocks(scalars, slabs, windows, lt_out, r_out)

    def emit(h, in0, in1, act):
        msg[pair_rows(h, 0), :] = in0.astype(BF)
        msg[pair_rows(h, 1), :] = in1.astype(BF)
        emit_active(h, act, core, x, msg, keep, INROWS)

    run_block(slabs_ref, block, lt_out, r_out, scratch, emit)
    dens[...] = density_of(diag[...])
    msg[pl.ds(INROWS + 2 * PER, NBQ), :] = split_wire(dens[...])


def second_kernel(
    scalars, slabs_ref, lt_ref, r_ref, keep_in, send, keep, dens, *scratch
):
    slabs = slabs_ref.shape[0]
    core, x = scalars[2 * slabs + 1], scalars[2 * slabs + 2]
    block = 2 * (1 - x) + core
    start_slabs(slabs_ref, scratch[0], scratch[5], block)

    def emit(h, in0, in1, act):
        keep_in[pair_rows(h, 0), :] = in0
        keep_in[pair_rows(h, 1), :] = in1
        emit_active(h, act, core, x, send, keep, 0)

    run_block(slabs_ref, block, lt_ref, r_ref, scratch, emit)
    dens[...] = density_of(scratch[4][...])


def third_kernel(
    scalars, slabs_ref, lt_ref, r_ref, send2, dens2, msg, keep, dens, *scratch
):
    slabs = slabs_ref.shape[0]
    core, x = scalars[2 * slabs + 1], scalars[2 * slabs + 2]
    block = 2 * x + (1 - core)
    start_slabs(slabs_ref, scratch[0], scratch[5], block)

    def emit(h, in0, in1, act):
        msg[pair_rows(h, 0), :] = in0.astype(BF)
        msg[pair_rows(h, 1), :] = in1.astype(BF)
        emit_active(h, act, core, x, msg, keep, INROWS)

    run_block(slabs_ref, block, lt_ref, r_ref, scratch, emit)
    msg[pl.ds(INROWS + 2 * PER, 2 * PER), :] = send2[...]
    dens[...] = density_of(scratch[4][...])
    msg[pl.ds(INROWS + 4 * PER, NBQ), :] = split_wire(dens[...])
    msg[pl.ds(INROWS + 4 * PER + NBQ, NBQ), :] = split_wire(dens2[...])


def fourth_kernel(
    scalars, slabs_ref, lt_ref, r_ref, far1, msg, keep_in, keep, dens, *scratch
):
    slabs = slabs_ref.shape[0]
    core, x = scalars[2 * slabs + 1], scalars[2 * slabs + 2]
    block = 2 * x + core
    start_slabs(slabs_ref, scratch[0], scratch[5], block)

    def emit(h, in0, in1, act):
        for n, v in enumerate((in0, in1)):
            keep_in[pair_rows(h, n), :] = v + far1[pair_rows(h, n), :].astype(F32)
        emit_active(h, act, core, x, msg, keep, 0)

    run_block(slabs_ref, block, lt_ref, r_ref, scratch, emit)
    dens[...] = density_of(scratch[4][...])
    msg[pl.ds(2 * PER, NBQ), :] = split_wire(dens[...])


def exchange_kernel(scalars, mine, near3, own, e1, e2, e3, whole):
    parts = []
    for q in range(NBQ):
        rows = pl.ds(q * NACT, NACT)
        parts.append(mine[rows, :] + near3[rows, :].astype(F32))
    v = jnp.concatenate(parts, axis=1)
    hi = v.astype(BF)
    lo = (v - hi.astype(F32)).astype(BF)
    both = lax.dot_general(
        jnp.concatenate([hi, lo], axis=0), hi, (((1,), (1,)), ((), ())),
        preferred_element_type=F32,
    )
    whole[...] = both[:NACT] + both[NACT:] + both[NACT:].T
    last = scalars.shape[0] - 1
    index = 2 * scalars[last] + scalars[last - 1]
    for k, out in enumerate((own, e1, e2, e3)):
        at = pl.multiple_of((index ^ k) * QUARTER, QUARTER)
        out[...] = whole[pl.ds(at, QUARTER), :]


def gather_kernel(
    keep1, keep2, keep3, keep4, dens1, dens2, dens3, dens4, near1, near3, near4, far1,
    msg, own, dens,
):
    base = INROWS + 2 * PER
    here = (
        (keep1, near3, base, dens1, base + 2 * PER + NBQ),
        (keep2, near1, INROWS, dens2, base),
        (keep3, near4, 0, dens3, 2 * PER),
        (keep4, near3, INROWS, dens4, base + 2 * PER),
    )
    sent = 0
    for n, (keep, near, at, d, dens_at) in enumerate(here):
        if n != 1:
            other = keep[pl.ds(0, PER), :] + near[pl.ds(at, PER), :].astype(F32)
            msg[pl.ds(sent * PER, PER), :] = other.astype(BF)
            sent += 1
        mine = keep[pl.ds(PER, PER), :] + near[pl.ds(at + PER, PER), :].astype(F32)
        if n == 3:
            mine = mine + far1[pl.ds(INROWS, PER), :].astype(F32)
        own[pl.ds(n * PER, PER), :] = mine
        total = d[...] + joined(near[pl.ds(dens_at, NBQ), :])
        dens[pl.ds(n * NBQ, NBQ), :] = total
        msg[pl.ds(3 * PER + n * NBQ, NBQ), :] = split_wire(total)


FAR_ACTIVE = (1, 2, 0)


def coulomb_kernel(act, far, dens, own, e1, e2, e3, partial):
    first = low_half(QUARTER)
    total = jnp.zeros((QUARTER, LANES), F32)
    for n in range(4):
        d = dens[pl.ds(n * NBQ, NBQ), :] + joined(
            far[pl.ds(3 * PER + (n ^ 2) * NBQ, NBQ), :]
        )
        for h in range(NBQ // 2):
            a = act[pl.ds(n * PER + h * QUARTER, QUARTER), :]
            if n < 3:
                a = a + far[
                    pl.ds(FAR_ACTIVE[n] * PER + h * QUARTER, QUARTER), :
                ].astype(F32)
            total = total + a * jnp.where(first, d[2 * h : 2 * h + 1], d[2 * h + 1 : 2 * h + 2])
    total = 2.0 * (total + pltpu.roll(total, BS, 1))
    partial[...] = total[:, :BS] - (own[...] + e1[...] + e2[...] + e3[...])


def active_kernel(scalars, act, far, out):
    last = scalars.shape[0] - 1
    core, x = scalars[last - 1], scalars[last]
    for n in range(4):
        xx = (1 - x) if n < 2 else x
        cc = (1 - core) if n % 2 == 0 else core
        base = NBQ * (2 * xx + cc)
        for h in range(NBQ // 2):
            a = act[pl.ds(n * PER + h * QUARTER, QUARTER), :]
            if n < 3:
                a = a + far[
                    pl.ds(FAR_ACTIVE[n] * PER + h * QUARTER, QUARTER), :
                ].astype(F32)
            out[base + 2 * h] = a[:, :BS]
            out[base + 2 * h + 1] = a[:, BS:]


VM = pl.BlockSpec(memory_space=pltpu.VMEM)
SM = pl.BlockSpec(memory_space=pltpu.SMEM)
HB = pl.BlockSpec(memory_space=pl.ANY)
PARAMS = pltpu.CompilerParams(vmem_limit_bytes=48 * 1024 * 1024)


def shape(dims, dtype):
    return jax.ShapeDtypeStruct(dims, dtype)


def sum_over_aux(part):
    n = lax.axis_size("aux")
    if n != 4:
        return lax.psum(part, "aux")
    for k in (1, 2):
        part = part + lax.ppermute(part, "aux", [(z, z ^ k) for z in range(n)])
    return part


def paired_body(slabs, block_row, block_col, live_count, orbitals, hcore):
    nslab, batch, width = slabs.shape
    index = lax.axis_index("pair")
    where = jnp.stack([lax.rem(index, 2), index // 2])
    scalars = jnp.concatenate([block_row, block_col, live_count, where])
    swap_core = [(0, 1), (1, 0), (2, 3), (3, 2)]
    swap_x = [(0, 2), (2, 0), (1, 3), (3, 1)]
    aos = nslab * BS
    scratch = [
        pltpu.VMEM((nslab // 2 + 1, 2, NBQ, width), BF),
        pltpu.VMEM((MSTEP * BS, LANES), F32),
        pltpu.VMEM((MSTEP * BS, LANES), F32),
        pltpu.VMEM((NBQ, NCOL, aos), BF),
        pltpu.VMEM((NBQ, LANES), F32),
        pltpu.SemaphoreType.DMA((nslab // 2 + 1,)),
    ]
    cost = pl.CostEstimate(flops=6 * 10**9, bytes_accessed=10**7, transcendentals=0)
    keep, dens = shape((2 * PER, LANES), F32), shape((NBQ, LANES), F32)
    lt, r, msg1, keep1, dens1 = pl.pallas_call(
        first_kernel,
        name="slabs_first",
        in_specs=[SM, HB, HB],
        out_specs=[VM] * 5,
        out_shape=(
            shape((nslab // 2, NCOL, PAIRED), BF),
            shape((aos, 2 * LANES), BF),
            shape((INROWS + 2 * PER + NBQ, LANES), BF),
            keep,
            dens,
        ),
        scratch_shapes=[
            pltpu.VMEM((2 * nslab, NCOL, PAIRED), BF), pltpu.SemaphoreType.DMA((2 * nslab,)),
        ] + scratch,
        compiler_params=PARAMS,
        cost_estimate=cost,
    )(scalars, slabs, orbitals.T)
    near1 = lax.ppermute(msg1, "pair", swap_core)
    keep_in2, send2, keep2, dens2 = pl.pallas_call(
        second_kernel,
        name="slabs_second",
        in_specs=[SM, HB, VM, VM],
        out_specs=[VM] * 4,
        out_shape=(
            shape((INROWS, LANES), F32), shape((2 * PER, LANES), BF), keep, dens,
        ),
        scratch_shapes=scratch,
        compiler_params=PARAMS,
        cost_estimate=cost,
    )(scalars, slabs, lt, r)
    out2 = jnp.concatenate([keep_in2, keep2[:PER]], axis=0)
    out2 = (out2 + near1[: INROWS + PER].astype(F32)).astype(BF)
    out2, lt, r = lax.optimization_barrier((out2, lt, r))
    far1 = lax.ppermute(out2, "pair", swap_x)
    msg3, keep3, dens3 = pl.pallas_call(
        third_kernel,
        name="slabs_third",
        in_specs=[SM, HB] + [VM] * 4,
        out_specs=[VM] * 3,
        out_shape=(shape((INROWS + 4 * PER + 2 * NBQ, LANES), BF), keep, dens),
        scratch_shapes=scratch,
        compiler_params=PARAMS,
        cost_estimate=cost,
    )(scalars, slabs, lt, r, send2, dens2)
    near3 = lax.ppermute(msg3, "pair", swap_core)
    msg4, keep_in4, keep4, dens4 = pl.pallas_call(
        fourth_kernel,
        name="slabs_fourth",
        in_specs=[SM, HB] + [VM] * 3,
        out_specs=[VM] * 4,
        out_shape=(
            shape((2 * PER + NBQ, LANES), BF), shape((INROWS, LANES), F32), keep, dens,
        ),
        scratch_shapes=scratch,
        compiler_params=PARAMS,
        cost_estimate=cost,
    )(scalars, slabs, lt, r, far1)
    near4 = lax.ppermute(msg4, "pair", swap_core)
    rows = shape((QUARTER, NACT), F32)
    own, e1, e2, e3 = pl.pallas_call(
        exchange_kernel,
        name="exchange",
        in_specs=[SM] + [VM] * 2,
        out_specs=[VM] * 4,
        out_shape=(rows,) * 4,
        scratch_shapes=[pltpu.VMEM((NACT, NACT), F32)],
        compiler_params=PARAMS,
    )(scalars, keep_in4, near3)
    msg5, act, dens = pl.pallas_call(
        gather_kernel,
        name="active_of_chip",
        in_specs=[VM] * 12,
        out_specs=[VM] * 3,
        out_shape=(
            shape((3 * PER + 4 * NBQ, LANES), BF),
            shape((4 * PER, LANES), F32),
            shape((4 * NBQ, LANES), F32),
        ),
        compiler_params=PARAMS,
    )(keep1, keep2, keep3, keep4, dens1, dens2, dens3, dens4, near1, near3, near4, far1)
    far5 = lax.ppermute(msg5, "pair", swap_x)
    e1, e2, e3 = (
        lax.ppermute(e, "pair", [(p, p ^ k) for p in range(4)])
        for k, e in ((1, e1), (2, e2), (3, e3))
    )
    partial = pl.pallas_call(
        coulomb_kernel,
        name="coulomb",
        in_specs=[VM] * 7,
        out_specs=VM,
        out_shape=rows,
        compiler_params=PARAMS,
    )(act, far5, dens, own, e1, e2, e3)
    active = pl.pallas_call(
        active_kernel,
        name="own_active",
        in_specs=[SM, VM, VM],
        out_specs=VM,
        out_shape=shape((batch, QUARTER, NACT), F32),
        compiler_params=PARAMS,
        cost_estimate=pl.CostEstimate(flops=10**6, bytes_accessed=10**6, transcendentals=0),
    )(scalars, act, far5)
    return (active, hcore + sum_over_aux(partial))


def slab_terms(values, left, right):
    half = jnp.einsum("mc,qmn->qnc", left, values, preferred_element_type=F32).astype(BF)
    first = jnp.einsum("qnt,nc->qtc", half[:, :, :NACT], right, preferred_element_type=F32)
    second = jnp.einsum("qnc,nt->qtc", half, right[:, :NACT], preferred_element_type=F32)
    trace = 2.0 * jnp.einsum(
        "qni,ni->q", half[:, :, NACT:], right[:, NACT:], preferred_element_type=F32
    )
    return (first + second, trace)


def general_body(slabs, block_row, block_col, live_count, orbitals, hcore):
    batch = slabs.shape[1]
    init = (jnp.zeros((batch, NACT, NCOL), F32), jnp.zeros((batch,), F32))

    def visit(k, state):
        values = lax.dynamic_index_in_dim(slabs, k, 0, keepdims=False)
        left = lax.dynamic_slice_in_dim(orbitals, block_row[k] * BS, BS, 0)
        right = lax.dynamic_slice_in_dim(orbitals, block_col[k] * BS, BS, 0)
        terms, trace = slab_terms(values.reshape(batch, BS, BS), left, right)
        return (state[0] + terms, state[1] + trace)

    vectors, density = lax.fori_loop(0, live_count[0], visit, init)
    density = lax.psum(density, "pair")
    owned = lax.psum_scatter(vectors, "pair", scatter_dimension=1, tiled=True)
    own_active, own_inactive = owned[:, :, :NACT], owned[:, :, NACT:]
    gathered = lax.all_gather(own_inactive.astype(BF), "pair", axis=1, tiled=True)
    exchange = jnp.einsum(
        "qti,qui->tu", own_inactive, gathered.astype(F32), precision=lax.Precision.HIGHEST
    )
    coulomb = jnp.einsum("qtu,q->tu", own_active, density, precision=lax.Precision.HIGHEST)
    return (own_active, hcore + lax.psum(2.0 * coulomb - exchange, "aux"))


def solution(mesh):
    placed = (
        P(("frag", "pair"), "aux", None),
        P(("frag", "pair")),
        P(("frag", "pair")),
        P(("frag", "pair")),
        P("frag", None),
        P(("frag", "pair"), None),
    )

    def body(slabs, *rest):
        fits = mesh.shape["pair"] == 4 and slabs.shape[1] == 4 * NBQ and slabs.shape[0] % 4 == 0
        return (paired_body if fits else general_body)(slabs, *rest)

    return jax.shard_map(
        body,
        mesh=mesh,
        in_specs=placed,
        out_specs=(P(("frag", "aux"), "pair", None), P(("frag", "pair"), None)),
        check_vma=False,
    )
```

```python
import jax
import jax.numpy as jnp
from jax import lax
from jax.experimental import pallas as pl
from jax.experimental.pallas import tpu as pltpu
from jax.sharding import PartitionSpec as P

BS = 64
NACT = 64
NCOL = 192
NIN = NCOL - NACT
LANES = 128
NBQ = 16
PAIRED = 2 * BS
QSTEP, MSTEP = 3, 49
BF = jnp.bfloat16
F32 = jnp.float32


def low_half(rows):
    return lax.broadcasted_iota(jnp.int32, (rows, LANES), 1) < BS


def orbital_blocks(scalars, slabs, windows, lt_ref, r_ref):
    first = low_half(NCOL)
    live = scalars[2 * slabs]

    def window(n, slot, upper):
        w = windows[n].astype(F32)
        w = jnp.concatenate([w[NACT:], w[:NACT]], axis=0)
        moved = lax.rem(scalars[n], 2) != (1 if upper else 0)
        w = jnp.where(moved, pltpu.roll(w, BS, 1), w)
        return jnp.where(slot < live, w, 0.0)

    for k in range(slabs // 2):
        a, b = 2 * k, 2 * k + 1
        left = jnp.where(first, window(a, a, False), window(b, b, True))
        lt_ref[k] = left.astype(BF)
        right = jnp.where(first, window(slabs + a, a, False), window(slabs + b, b, True))
        right = jnp.concatenate([right, right[NIN:]], axis=0)
        r_ref[pl.ds(k * PAIRED, PAIRED), :] = right.T.astype(BF)


def slab_copy(slabs_ref, sbuf, sem, block, k):
    last = slabs_ref.shape[0] // 2 - 1
    pair = min(k, last) if isinstance(k, int) else jnp.minimum(k, last)
    return pltpu.make_async_copy(
        slabs_ref.at[pl.ds(2 * pair, 2), pl.ds(pl.multiple_of(block * NBQ, NBQ), NBQ), :],
        sbuf.at[k],
        sem.at[k],
    )


def start_slabs(slabs_ref, sbuf, sem, block):
    for k in range(slabs_ref.shape[0] // 2 + 1):
        slab_copy(slabs_ref, sbuf, sem, block, k).start()


def run_block(slabs_ref, block, lt_ref, r_ref, scratch, emit):
    sbuf, even_ref, odd_ref, half_ref, diag, sem = scratch
    pairs = slabs_ref.shape[0] // 2
    first = low_half(NBQ)
    first_s = low_half(BS)
    zero = jnp.zeros((BS, LANES), BF)
    wide, group = NBQ, 8

    def wait(k):
        slab_copy(slabs_ref, sbuf, sem, block, k).wait()

    def relayout(k, out):
        for j in range(sbuf.shape[3] // LANES):
            lanes = slice(j * LANES, (j + 1) * LANES)
            a = sbuf[k, 0, :, lanes].astype(F32)
            b = sbuf[k, 1, :, lanes].astype(F32)
            out[pl.ds(MSTEP * 2 * j, NBQ, stride=QSTEP), :] = jnp.where(
                first, a, pltpu.roll(b, BS, 1)
            )
            out[pl.ds(MSTEP * (2 * j + 1), NBQ, stride=QSTEP), :] = jnp.where(
                first, pltpu.roll(a, BS, 1), b
            )

    def half_transform(k, rows):
        left = lt_ref[k]
        at = pl.ds(pl.multiple_of(k * LANES, LANES), LANES)
        for q in range(0, NBQ, wide):
            cols = []
            for u in range(q, q + wide):
                s = rows[pl.ds(u * QSTEP, BS, stride=MSTEP), :].astype(BF)
                cols.append(
                    jnp.concatenate(
                        [jnp.where(first_s, s, zero), jnp.where(first_s, zero, s)], axis=0
                    )
                )
            half = jnp.dot(left, jnp.concatenate(cols, axis=1), preferred_element_type=F32)
            half = half.astype(BF)
            for u in range(wide):
                half_ref[q + u, :, at] = half[:, u * LANES : (u + 1) * LANES]

    def two_pairs(i, carry):
        wait(2 * i + 1)
        wait(2 * i + 2)
        relayout(2 * i + 1, odd_ref)
        half_transform(2 * i, even_ref)
        relayout(2 * i + 2, even_ref)
        half_transform(2 * i + 1, odd_ref)
        return carry

    def second_transform(g, carry):
        lhs = half_ref[pl.ds(group * g, group)].reshape(group * NCOL, half_ref.shape[2])
        whole = jnp.dot(lhs, r_ref[...], preferred_element_type=F32)
        eye = lax.broadcasted_iota(jnp.int32, (NIN, NIN), 0) == lax.broadcasted_iota(
            jnp.int32, (NIN, NIN), 1
        )
        for p in range(group // 2):
            w0 = whole[2 * p * NCOL : (2 * p + 1) * NCOL]
            w1 = whole[(2 * p + 1) * NCOL : (2 * p + 2) * NCOL]
            side = jnp.where(low_half(NCOL), w0[:, LANES:], w1[:, LANES:])
            across = side[:NIN].T
            square = jnp.concatenate([w0[NIN:, LANES:], w1[NIN:, LANES:]], axis=0).T
            h = group // 2 * g + p
            emit(
                h,
                w0[NIN:, :NIN] + across[:NACT],
                w1[NIN:, :NIN] + across[NACT:],
                side[NIN:] + square[:NACT],
            )
            for n, w in enumerate((w0, w1)):
                diag[pl.ds(2 * h + n, 1), :] = jnp.sum(
                    jnp.where(eye, w[:NIN, :NIN], 0.0), axis=0, keepdims=True
                )
        return carry

    wait(0)
    relayout(0, even_ref)
    lax.fori_loop(0, pairs // 2, two_pairs, 0)
    lax.fori_loop(0, NBQ // group, second_transform, 0)


def split_wire(d):
    hi = d.astype(BF).astype(F32)
    return jnp.where(low_half(d.shape[0]), hi, d - hi).astype(BF)


def joined(wire):
    w = wire.astype(F32)
    return w + pltpu.roll(w, BS, 1)


def density_of(diag):
    d = 2.0 * jnp.sum(diag, axis=1, keepdims=True)
    return jnp.broadcast_to(d, diag.shape)


QUARTER = NACT // 4
PER = NBQ // 2 * QUARTER
INROWS = NBQ * NACT


def emit_active(h, act, core, x, send, keep, send_at):
    for place in (0, 1):
        xx = (1 - x) if place == 0 else x
        for cc in (0, 1):
            block = act[:QUARTER]
            for idx in range(1, 4):
                block = jnp.where(
                    2 * xx + cc == idx, act[idx * QUARTER : (idx + 1) * QUARTER], block
                )
            off = place * PER + h * QUARTER

            @pl.when(core == cc)
            def _():
                keep[pl.ds(pl.multiple_of(off, QUARTER), QUARTER), :] = block

            @pl.when(core != cc)
            def _():
                send[pl.ds(pl.multiple_of(send_at + off, QUARTER), QUARTER), :] = block.astype(BF)


def pair_rows(h, n):
    return pl.ds(pl.multiple_of((2 * h + n) * NACT, NACT), NACT)


def first_kernel(
    scalars, slabs_ref, ot_ref, lt_out, r_out, msg, keep, dens, windows, wsem, *scratch
):
    slabs = slabs_ref.shape[0]
    core, x = scalars[2 * slabs + 1], scalars[2 * slabs + 2]
    block = 2 * (1 - x) + (1 - core)
    copies = []
    for n in range(2 * slabs):
        base = pl.multiple_of((scalars[n] // 2) * PAIRED, PAIRED)
        copies.append(
            pltpu.make_async_copy(ot_ref.at[:, pl.ds(base, PAIRED)], windows.at[n], wsem.at[n])
        )
        copies[-1].start()
    sbuf, sem, diag = scratch[0], scratch[5], scratch[4]
    start_slabs(slabs_ref, sbuf, sem, block)
    for copy in copies:
        copy.wait()
    orbital_blocks(scalars, slabs, windows, lt_out, r_out)

    def emit(h, in0, in1, act):
        msg[pair_rows(h, 0), :] = in0.astype(BF)
        msg[pair_rows(h, 1), :] = in1.astype(BF)
        emit_active(h, act, core, x, msg, keep, INROWS)

    run_block(slabs_ref, block, lt_out, r_out, scratch, emit)
    dens[...] = density_of(diag[...])
    msg[pl.ds(INROWS + 2 * PER, NBQ), :] = split_wire(dens[...])


def second_kernel(
    scalars, slabs_ref, lt_ref, r_ref, keep_in, send, keep, dens, *scratch
):
    slabs = slabs_ref.shape[0]
    core, x = scalars[2 * slabs + 1], scalars[2 * slabs + 2]
    block = 2 * (1 - x) + core
    start_slabs(slabs_ref, scratch[0], scratch[5], block)

    def emit(h, in0, in1, act):
        keep_in[pair_rows(h, 0), :] = in0
        keep_in[pair_rows(h, 1), :] = in1
        emit_active(h, act, core, x, send, keep, 0)

    run_block(slabs_ref, block, lt_ref, r_ref, scratch, emit)
    dens[...] = density_of(scratch[4][...])


def third_kernel(
    scalars, slabs_ref, lt_ref, r_ref, send2, dens2, msg, keep, dens, *scratch
):
    slabs = slabs_ref.shape[0]
    core, x = scalars[2 * slabs + 1], scalars[2 * slabs + 2]
    block = 2 * x + (1 - core)
    start_slabs(slabs_ref, scratch[0], scratch[5], block)

    def emit(h, in0, in1, act):
        msg[pair_rows(h, 0), :] = in0.astype(BF)
        msg[pair_rows(h, 1), :] = in1.astype(BF)
        emit_active(h, act, core, x, msg, keep, INROWS)

    run_block(slabs_ref, block, lt_ref, r_ref, scratch, emit)
    msg[pl.ds(INROWS + 2 * PER, 2 * PER), :] = send2[...]
    dens[...] = density_of(scratch[4][...])
    msg[pl.ds(INROWS + 4 * PER, NBQ), :] = split_wire(dens[...])
    msg[pl.ds(INROWS + 4 * PER + NBQ, NBQ), :] = split_wire(dens2[...])


def fourth_kernel(
    scalars, slabs_ref, lt_ref, r_ref, far1, msg, keep_in, keep, dens, *scratch
):
    slabs = slabs_ref.shape[0]
    core, x = scalars[2 * slabs + 1], scalars[2 * slabs + 2]
    block = 2 * x + core
    start_slabs(slabs_ref, scratch[0], scratch[5], block)

    def emit(h, in0, in1, act):
        for n, v in enumerate((in0, in1)):
            keep_in[pair_rows(h, n), :] = v + far1[pair_rows(h, n), :].astype(F32)
        emit_active(h, act, core, x, msg, keep, 0)

    run_block(slabs_ref, block, lt_ref, r_ref, scratch, emit)
    dens[...] = density_of(scratch[4][...])
    msg[pl.ds(2 * PER, NBQ), :] = split_wire(dens[...])


def exchange_kernel(scalars, mine, near3, msg4, msg, keep, whole):
    parts = []
    for q in range(NBQ):
        rows = pl.ds(q * NACT, NACT)
        parts.append(mine[rows, :] + near3[rows, :].astype(F32))
    v = jnp.concatenate(parts, axis=1)
    hi = v.astype(BF)
    lo = (v - hi.astype(F32)).astype(BF)
    both = lax.dot_general(
        jnp.concatenate([hi, lo], axis=0), hi, (((1,), (1,)), ((), ())),
        preferred_element_type=F32,
    )
    total = both[:NACT] + both[NACT:] + both[NACT:].T
    whole[...] = jnp.concatenate([total, total], axis=1)
    last = scalars.shape[0] - 1
    core, x = scalars[last - 1], scalars[last]
    size = msg4.shape[0]
    msg[pl.ds(0, size), :] = msg4[...]
    for place, xx in enumerate((1 - x, x)):
        there = pl.multiple_of((2 * xx + 1 - core) * QUARTER, QUARTER)
        here = pl.multiple_of((2 * xx + core) * QUARTER, QUARTER)
        msg[pl.ds(size + place * QUARTER, QUARTER), :] = split_wire(whole[pl.ds(there, QUARTER), :])
        keep[pl.ds(place * QUARTER, QUARTER), :] = whole[pl.ds(here, QUARTER), :]


def gather_kernel(
    keep1, keep2, keep3, keep4, dens1, dens2, dens3, dens4, exch, near1, near3, near4, far1,
    msg, own, dens, exch_own,
):
    base = INROWS + 2 * PER
    here = (
        (keep1, near3, base, dens1, base + 2 * PER + NBQ),
        (keep2, near1, INROWS, dens2, base),
        (keep3, near4, 0, dens3, 2 * PER),
        (keep4, near3, INROWS, dens4, base + 2 * PER),
    )
    sent = 0
    for n, (keep, near, at, d, dens_at) in enumerate(here):
        if n != 1:
            other = keep[pl.ds(0, PER), :] + near[pl.ds(at, PER), :].astype(F32)
            msg[pl.ds(sent * PER, PER), :] = other.astype(BF)
            sent += 1
        mine = keep[pl.ds(PER, PER), :] + near[pl.ds(at + PER, PER), :].astype(F32)
        if n == 3:
            mine = mine + far1[pl.ds(INROWS, PER), :].astype(F32)
        own[pl.ds(n * PER, PER), :] = mine
        total = d[...] + joined(near[pl.ds(dens_at, NBQ), :])
        dens[pl.ds(n * NBQ, NBQ), :] = total
        msg[pl.ds(3 * PER + n * NBQ, NBQ), :] = split_wire(total)
    rows = exch[...] + joined(near4[pl.ds(2 * PER + NBQ, 2 * QUARTER), :])
    msg[pl.ds(3 * PER + 4 * NBQ, QUARTER), :] = split_wire(rows[:QUARTER])
    exch_own[...] = rows[QUARTER:]


FAR_ACTIVE = (1, 2, 0)


def coulomb_kernel(act, far, dens, exch, partial):
    first = low_half(QUARTER)
    total = jnp.zeros((QUARTER, LANES), F32)
    for n in range(4):
        d = dens[pl.ds(n * NBQ, NBQ), :] + joined(
            far[pl.ds(3 * PER + (n ^ 2) * NBQ, NBQ), :]
        )
        for h in range(NBQ // 2):
            a = act[pl.ds(n * PER + h * QUARTER, QUARTER), :]
            if n < 3:
                a = a + far[
                    pl.ds(FAR_ACTIVE[n] * PER + h * QUARTER, QUARTER), :
                ].astype(F32)
            total = total + a * jnp.where(first, d[2 * h : 2 * h + 1], d[2 * h + 1 : 2 * h + 2])
    total = 2.0 * (total + pltpu.roll(total, BS, 1))
    total = total - exch[...] - joined(far[pl.ds(3 * PER + 4 * NBQ, QUARTER), :])
    partial[...] = total[:, :BS]


def active_kernel(scalars, act, far, out):
    last = scalars.shape[0] - 1
    core, x = scalars[last - 1], scalars[last]
    for n in range(4):
        xx = (1 - x) if n < 2 else x
        cc = (1 - core) if n % 2 == 0 else core
        base = NBQ * (2 * xx + cc)
        for h in range(NBQ // 2):
            a = act[pl.ds(n * PER + h * QUARTER, QUARTER), :]
            if n < 3:
                a = a + far[
                    pl.ds(FAR_ACTIVE[n] * PER + h * QUARTER, QUARTER), :
                ].astype(F32)
            out[base + 2 * h] = a[:, :BS]
            out[base + 2 * h + 1] = a[:, BS:]


VM = pl.BlockSpec(memory_space=pltpu.VMEM)
SM = pl.BlockSpec(memory_space=pltpu.SMEM)
HB = pl.BlockSpec(memory_space=pltpu.HBM)
PARAMS = pltpu.CompilerParams(vmem_limit_bytes=48 * 1024 * 1024)


def shape(dims, dtype):
    return jax.ShapeDtypeStruct(dims, dtype)


def sum_over_aux(part):
    n = lax.axis_size("aux")
    if n != 4:
        return lax.psum(part, "aux")
    one, two, three = (
        lax.ppermute(part, "aux", [(z, z ^ k) for z in range(n)]) for k in (1, 2, 3)
    )
    return (part + one) + (two + three)


def paired_body(slabs, block_row, block_col, live_count, orbitals, hcore):
    nslab, batch, width = slabs.shape
    index = lax.axis_index("pair")
    where = jnp.stack([lax.rem(index, 2), index // 2])
    scalars = jnp.concatenate([block_row, block_col, live_count, where])
    swap_core = [(0, 1), (1, 0), (2, 3), (3, 2)]
    swap_x = [(0, 2), (2, 0), (1, 3), (3, 1)]
    aos = nslab * BS
    scratch = [
        pltpu.VMEM((nslab // 2 + 1, 2, NBQ, width), BF),
        pltpu.VMEM((MSTEP * BS, LANES), F32),
        pltpu.VMEM((MSTEP * BS, LANES), F32),
        pltpu.VMEM((NBQ, NCOL, aos), BF),
        pltpu.VMEM((NBQ, LANES), F32),
        pltpu.SemaphoreType.DMA((nslab // 2 + 1,)),
    ]
    cost = pl.CostEstimate(flops=6 * 10**9, bytes_accessed=10**7, transcendentals=0)
    keep, dens = shape((2 * PER, LANES), F32), shape((NBQ, LANES), F32)
    lt, r, msg1, keep1, dens1 = pl.pallas_call(
        first_kernel,
        name="slabs_first",
        in_specs=[SM, HB, HB],
        out_specs=[VM] * 5,
        out_shape=(
            shape((nslab // 2, NCOL, PAIRED), BF),
            shape((aos, 2 * LANES), BF),
            shape((INROWS + 2 * PER + NBQ, LANES), BF),
            keep,
            dens,
        ),
        scratch_shapes=[
            pltpu.VMEM((2 * nslab, NCOL, PAIRED), BF), pltpu.SemaphoreType.DMA((2 * nslab,)),
        ] + scratch,
        compiler_params=PARAMS,
        cost_estimate=cost,
    )(scalars, slabs, orbitals.T)
    near1 = lax.ppermute(msg1, "pair", swap_core)
    keep_in2, send2, keep2, dens2 = pl.pallas_call(
        second_kernel,
        name="slabs_second",
        in_specs=[SM, HB, VM, VM],
        out_specs=[VM] * 4,
        out_shape=(
            shape((INROWS, LANES), F32), shape((2 * PER, LANES), BF), keep, dens,
        ),
        scratch_shapes=scratch,
        compiler_params=PARAMS,
        cost_estimate=cost,
    )(scalars, slabs, lt, r)
    out2 = jnp.concatenate([keep_in2, keep2[:PER]], axis=0)
    out2 = (out2 + near1[: INROWS + PER].astype(F32)).astype(BF)
    out2, lt, r = lax.optimization_barrier((out2, lt, r))
    far1 = lax.ppermute(out2, "pair", swap_x)
    msg3, keep3, dens3 = pl.pallas_call(
        third_kernel,
        name="slabs_third",
        in_specs=[SM, HB] + [VM] * 4,
        out_specs=[VM] * 3,
        out_shape=(shape((INROWS + 4 * PER + 2 * NBQ, LANES), BF), keep, dens),
        scratch_shapes=scratch,
        compiler_params=PARAMS,
        cost_estimate=cost,
    )(scalars, slabs, lt, r, send2, dens2)
    near3 = lax.ppermute(msg3, "pair", swap_core)
    msg4, keep_in4, keep4, dens4 = pl.pallas_call(
        fourth_kernel,
        name="slabs_fourth",
        in_specs=[SM, HB] + [VM] * 3,
        out_specs=[VM] * 4,
        out_shape=(
            shape((2 * PER + NBQ, LANES), BF), shape((INROWS, LANES), F32), keep, dens,
        ),
        scratch_shapes=scratch,
        compiler_params=PARAMS,
        cost_estimate=cost,
    )(scalars, slabs, lt, r, far1)
    msg4, exch = pl.pallas_call(
        exchange_kernel,
        name="exchange",
        in_specs=[SM] + [VM] * 3,
        out_specs=[VM] * 2,
        out_shape=(
            shape((2 * PER + NBQ + 2 * QUARTER, LANES), BF),
            shape((2 * QUARTER, LANES), F32),
        ),
        scratch_shapes=[pltpu.VMEM((NACT, LANES), F32)],
        compiler_params=PARAMS,
    )(scalars, keep_in4, near3, msg4)
    near4 = lax.ppermute(msg4, "pair", swap_core)
    msg5, act, dens, exch = pl.pallas_call(
        gather_kernel,
        name="active_of_chip",
        in_specs=[VM] * 13,
        out_specs=[VM] * 4,
        out_shape=(
            shape((3 * PER + 4 * NBQ + QUARTER, LANES), BF),
            shape((4 * PER, LANES), F32),
            shape((4 * NBQ, LANES), F32),
            shape((QUARTER, LANES), F32),
        ),
        compiler_params=PARAMS,
    )(keep1, keep2, keep3, keep4, dens1, dens2, dens3, dens4, exch, near1, near3, near4, far1)
    far5 = lax.ppermute(msg5, "pair", swap_x)
    partial = pl.pallas_call(
        coulomb_kernel,
        name="coulomb",
        in_specs=[VM] * 4,
        out_specs=VM,
        out_shape=shape((QUARTER, NACT), F32),
        compiler_params=PARAMS,
    )(act, far5, dens, exch)
    active = pl.pallas_call(
        active_kernel,
        name="own_active",
        in_specs=[SM, VM, VM],
        out_specs=VM,
        out_shape=shape((batch, QUARTER, NACT), F32),
        compiler_params=PARAMS,
        cost_estimate=pl.CostEstimate(flops=10**6, bytes_accessed=10**6, transcendentals=0),
    )(scalars, act, far5)
    return (active, hcore + sum_over_aux(partial))


def slab_terms(values, left, right):
    half = jnp.einsum("mc,qmn->qnc", left, values, preferred_element_type=F32).astype(BF)
    first = jnp.einsum("qnt,nc->qtc", half[:, :, :NACT], right, preferred_element_type=F32)
    second = jnp.einsum("qnc,nt->qtc", half, right[:, :NACT], preferred_element_type=F32)
    trace = 2.0 * jnp.einsum(
        "qni,ni->q", half[:, :, NACT:], right[:, NACT:], preferred_element_type=F32
    )
    return (first + second, trace)


def general_body(slabs, block_row, block_col, live_count, orbitals, hcore):
    batch = slabs.shape[1]
    init = (jnp.zeros((batch, NACT, NCOL), F32), jnp.zeros((batch,), F32))

    def visit(k, state):
        values = lax.dynamic_index_in_dim(slabs, k, 0, keepdims=False)
        left = lax.dynamic_slice_in_dim(orbitals, block_row[k] * BS, BS, 0)
        right = lax.dynamic_slice_in_dim(orbitals, block_col[k] * BS, BS, 0)
        terms, trace = slab_terms(values.reshape(batch, BS, BS), left, right)
        return (state[0] + terms, state[1] + trace)

    vectors, density = lax.fori_loop(0, live_count[0], visit, init)
    density = lax.psum(density, "pair")
    owned = lax.psum_scatter(vectors, "pair", scatter_dimension=1, tiled=True)
    own_active, own_inactive = owned[:, :, :NACT], owned[:, :, NACT:]
    gathered = lax.all_gather(own_inactive.astype(BF), "pair", axis=1, tiled=True)
    exchange = jnp.einsum(
        "qti,qui->tu", own_inactive, gathered.astype(F32), precision=lax.Precision.HIGHEST
    )
    coulomb = jnp.einsum("qtu,q->tu", own_active, density, precision=lax.Precision.HIGHEST)
    return (own_active, hcore + lax.psum(2.0 * coulomb - exchange, "aux"))


def solution(mesh):
    placed = (
        P(("frag", "pair"), "aux", None),
        P(("frag", "pair")),
        P(("frag", "pair")),
        P(("frag", "pair")),
        P("frag", None),
        P(("frag", "pair"), None),
    )

    def body(slabs, *rest):
        fits = mesh.shape["pair"] == 4 and slabs.shape[1] == 4 * NBQ and slabs.shape[0] % 4 == 0
        return (paired_body if fits else general_body)(slabs, *rest)

    return jax.shard_map(
        body,
        mesh=mesh,
        in_specs=placed,
        out_specs=(P(("frag", "aux"), "pair", None), P(("frag", "pair"), None)),
        check_vma=False,
    )
```

```python
import jax
import jax.numpy as jnp
from jax import lax
from jax.experimental import pallas as pl
from jax.experimental.pallas import tpu as pltpu
from jax.sharding import PartitionSpec as P

BS = 64
NACT = 64
NCOL = 192
NIN = NCOL - NACT
LANES = 128
NBQ = 16
PAIRED = 2 * BS
QSTEP, MSTEP = 3, 49
BF = jnp.bfloat16
F32 = jnp.float32


def low_half(rows):
    return lax.broadcasted_iota(jnp.int32, (rows, LANES), 1) < BS


def orbital_blocks(blocks, live, slabs, windows, lt_ref, r_ref):
    first = low_half(NCOL)

    def window(n, slot, upper):
        w = windows[n].astype(F32)
        w = jnp.concatenate([w[NACT:], w[:NACT]], axis=0)
        moved = lax.rem(blocks[n], 2) != (1 if upper else 0)
        w = jnp.where(moved, pltpu.roll(w, BS, 1), w)
        return jnp.where(slot < live, w, 0.0)

    for k in range(slabs // 2):
        a, b = 2 * k, 2 * k + 1
        left = jnp.where(first, window(a, a, False), window(b, b, True))
        lt_ref[k] = left.astype(BF)
        right = jnp.where(first, window(slabs + a, a, False), window(slabs + b, b, True))
        right = jnp.concatenate([right, right[NIN:]], axis=0)
        r_ref[pl.ds(k * PAIRED, PAIRED), :] = right.T.astype(BF)


def slab_copy(slabs_ref, sbuf, sem, block, k):
    last = slabs_ref.shape[0] // 2 - 1
    pair = min(k, last) if isinstance(k, int) else jnp.minimum(k, last)
    return pltpu.make_async_copy(
        slabs_ref.at[pl.ds(2 * pair, 2), pl.ds(pl.multiple_of(block * NBQ, NBQ), NBQ), :],
        sbuf.at[k],
        sem.at[k],
    )


def start_slabs(slabs_ref, sbuf, sem, block):
    for k in range(slabs_ref.shape[0] // 2 + 1):
        slab_copy(slabs_ref, sbuf, sem, block, k).start()


def run_block(slabs_ref, block, lt_ref, r_ref, scratch, emit, prepare=None):
    sbuf, even_ref, odd_ref, half_ref, diag, sem = scratch
    pairs = slabs_ref.shape[0] // 2
    first = low_half(NBQ)
    first_s = low_half(BS)
    zero = jnp.zeros((BS, LANES), BF)
    wide, group = NBQ, 4

    def wait(k):
        slab_copy(slabs_ref, sbuf, sem, block, k).wait()

    def relayout(k, out):
        for j in range(sbuf.shape[3] // LANES):
            lanes = slice(j * LANES, (j + 1) * LANES)
            a = sbuf[k, 0, :, lanes]
            b = sbuf[k, 1, :, lanes]
            out[pl.ds(MSTEP * 2 * j, NBQ, stride=QSTEP), :] = jnp.where(
                first, a, pltpu.roll(b, BS, 1)
            ).astype(F32)
            out[pl.ds(MSTEP * (2 * j + 1), NBQ, stride=QSTEP), :] = jnp.where(
                first, pltpu.roll(a, BS, 1), b
            ).astype(F32)

    def half_transform(k, rows):
        left = lt_ref[k]
        at = pl.ds(pl.multiple_of(k * LANES, LANES), LANES)
        for q in range(0, NBQ, wide):
            cols = []
            for u in range(q, q + wide):
                s = rows[pl.ds(u * QSTEP, BS, stride=MSTEP), :].astype(BF)
                cols.append(
                    jnp.concatenate(
                        [jnp.where(first_s, s, zero), jnp.where(first_s, zero, s)], axis=0
                    )
                )
            half = jnp.dot(left, jnp.concatenate(cols, axis=1), preferred_element_type=F32)
            half = half.astype(BF)
            for u in range(wide):
                half_ref[q + u, :, at] = half[:, u * LANES : (u + 1) * LANES]

    def two_pairs(i, carry):
        wait(2 * i + 1)
        wait(2 * i + 2)
        relayout(2 * i + 1, odd_ref)
        half_transform(2 * i, even_ref)
        relayout(2 * i + 2, even_ref)
        half_transform(2 * i + 1, odd_ref)
        return carry

    def second_transform(g):
        lhs = half_ref[pl.ds(group * g, group)].reshape(group * NCOL, half_ref.shape[2])
        return jnp.dot(lhs, r_ref[...], preferred_element_type=F32)

    def assemble(g, whole):
        eye = lax.broadcasted_iota(jnp.int32, (NIN, NIN), 0) == lax.broadcasted_iota(
            jnp.int32, (NIN, NIN), 1
        )
        for p in range(group // 2):
            w0 = whole[2 * p * NCOL : (2 * p + 1) * NCOL]
            w1 = whole[(2 * p + 1) * NCOL : (2 * p + 2) * NCOL]
            side = jnp.where(low_half(NCOL), w0[:, LANES:], w1[:, LANES:])
            across = side[:NIN].T
            square = jnp.concatenate([w0[NIN:, LANES:], w1[NIN:, LANES:]], axis=0).T
            h = group // 2 * g + p
            emit(
                h,
                w0[NIN:, :NIN] + across[:NACT],
                w1[NIN:, :NIN] + across[NACT:],
                side[NIN:] + square[:NACT],
            )
            for n, w in enumerate((w0, w1)):
                diag[pl.ds(2 * h + n, 1), :] = jnp.sum(
                    jnp.where(eye, w[:NIN, :NIN], 0.0), axis=0, keepdims=True
                )

    wait(0)
    relayout(0, even_ref)
    if prepare is not None:
        prepare()
    lax.fori_loop(0, pairs // 2, two_pairs, 0)
    whole = second_transform(0)
    for g in range(NBQ // group):
        following = second_transform(g + 1) if g + 1 < NBQ // group else None
        assemble(g, whole)
        whole = following


def split_wire(d):
    hi = d.astype(BF).astype(F32)
    return jnp.where(low_half(d.shape[0]), hi, d - hi).astype(BF)


def joined(wire):
    w = wire.astype(F32)
    return w + pltpu.roll(w, BS, 1)


def density_of(diag):
    d = 2.0 * jnp.sum(diag, axis=1, keepdims=True)
    return jnp.broadcast_to(d, diag.shape)


QUARTER = NACT // 4
PER = NBQ // 2 * QUARTER
INROWS = NBQ * NACT


def emit_active(h, act, core, x, send, keep, send_at):
    upper, lower = act[: 2 * QUARTER], act[2 * QUARTER :]
    parts = (jnp.where(x == 0, lower, upper), jnp.where(x == 0, upper, lower))
    for place, part in enumerate(parts):
        one, two = part[:QUARTER], part[QUARTER:]
        off = place * PER + h * QUARTER
        keep[pl.ds(off, QUARTER), :] = jnp.where(core == 0, one, two)
        send[pl.ds(send_at + off, QUARTER), :] = jnp.where(core == 0, two, one).astype(BF)


def pair_rows(h, n):
    return pl.ds((2 * h + n) * NACT, NACT)


def first_kernel(
    where, rows_ref, cols_ref, live, slabs_ref, ot_ref, lt_out, r_out, msg, keep, dens,
    rows, cols, ssem, windows, wsem, *scratch
):
    slabs = slabs_ref.shape[0]
    core, x = where[0], where[1]
    block = 2 * (1 - x) + (1 - core)
    sbuf, sem, diag = scratch[0], scratch[5], scratch[4]
    small = [
        pltpu.make_async_copy(src, dst, ssem.at[n])
        for n, (src, dst) in enumerate(((rows_ref, rows), (cols_ref, cols)))
    ]
    for copy in small:
        copy.start()
    start_slabs(slabs_ref, sbuf, sem, block)
    for copy in small:
        copy.wait()
    blocks = [rows[n] for n in range(slabs)] + [cols[n] for n in range(slabs)]
    copies = []
    for n, blk in enumerate(blocks):
        base = pl.multiple_of((blk // 2) * PAIRED, PAIRED)
        copies.append(
            pltpu.make_async_copy(ot_ref.at[:, pl.ds(base, PAIRED)], windows.at[n], wsem.at[n])
        )
        copies[-1].start()

    def prepare():
        for copy in copies:
            copy.wait()
        orbital_blocks(blocks, live[0], slabs, windows, lt_out, r_out)

    def emit(h, in0, in1, act):
        msg[pair_rows(h, 0), :] = in0.astype(BF)
        msg[pair_rows(h, 1), :] = in1.astype(BF)
        emit_active(h, act, core, x, msg, keep, INROWS)

    run_block(slabs_ref, block, lt_out, r_out, scratch, emit, prepare)
    dens[...] = density_of(diag[...])
    msg[pl.ds(INROWS + 2 * PER, NBQ), :] = split_wire(dens[...])


def second_kernel(
    where, slabs_ref, lt_ref, r_ref, keep_in, send, keep, dens, *scratch
):
    core, x = where[0], where[1]
    block = 2 * (1 - x) + core
    start_slabs(slabs_ref, scratch[0], scratch[5], block)

    def emit(h, in0, in1, act):
        keep_in[pair_rows(h, 0), :] = in0
        keep_in[pair_rows(h, 1), :] = in1
        emit_active(h, act, core, x, send, keep, 0)

    run_block(slabs_ref, block, lt_ref, r_ref, scratch, emit)
    dens[...] = density_of(scratch[4][...])


def third_kernel(
    where, slabs_ref, lt_ref, r_ref, send2, dens2, msg, keep, dens, *scratch
):
    core, x = where[0], where[1]
    block = 2 * x + (1 - core)
    start_slabs(slabs_ref, scratch[0], scratch[5], block)

    def emit(h, in0, in1, act):
        msg[pair_rows(h, 0), :] = in0.astype(BF)
        msg[pair_rows(h, 1), :] = in1.astype(BF)
        emit_active(h, act, core, x, msg, keep, INROWS)

    run_block(slabs_ref, block, lt_ref, r_ref, scratch, emit)
    msg[pl.ds(INROWS + 2 * PER, 2 * PER), :] = send2[...]
    dens[...] = density_of(scratch[4][...])
    msg[pl.ds(INROWS + 4 * PER, NBQ), :] = split_wire(dens[...])
    msg[pl.ds(INROWS + 4 * PER + NBQ, NBQ), :] = split_wire(dens2[...])


def fourth_kernel(
    where, slabs_ref, lt_ref, r_ref, far1, msg, keep_in, keep, dens, *scratch
):
    core, x = where[0], where[1]
    block = 2 * x + core
    start_slabs(slabs_ref, scratch[0], scratch[5], block)

    def emit(h, in0, in1, act):
        for n, v in enumerate((in0, in1)):
            keep_in[pair_rows(h, n), :] = v + far1[pair_rows(h, n), :].astype(F32)
        emit_active(h, act, core, x, msg, keep, 0)

    run_block(slabs_ref, block, lt_ref, r_ref, scratch, emit)
    dens[...] = density_of(scratch[4][...])
    msg[pl.ds(2 * PER, NBQ), :] = split_wire(dens[...])


def exchange_kernel(where, mine, near3, msg4, msg, keep, whole):
    parts = []
    for q in range(NBQ):
        rows = pl.ds(q * NACT, NACT)
        parts.append(mine[rows, :] + near3[rows, :].astype(F32))
    v = jnp.concatenate(parts, axis=1)
    hi = v.astype(BF)
    lo = (v - hi.astype(F32)).astype(BF)
    both = lax.dot_general(
        jnp.concatenate([hi, lo], axis=0), hi, (((1,), (1,)), ((), ())),
        preferred_element_type=F32,
    )
    total = both[:NACT] + both[NACT:] + both[NACT:].T
    whole[...] = jnp.concatenate([total, total], axis=1)
    core, x = where[0], where[1]
    size = msg4.shape[0]
    msg[pl.ds(0, size), :] = msg4[...]
    for place, xx in enumerate((1 - x, x)):
        there = pl.multiple_of((2 * xx + 1 - core) * QUARTER, QUARTER)
        here = pl.multiple_of((2 * xx + core) * QUARTER, QUARTER)
        msg[pl.ds(size + place * QUARTER, QUARTER), :] = split_wire(whole[pl.ds(there, QUARTER), :])
        keep[pl.ds(place * QUARTER, QUARTER), :] = whole[pl.ds(here, QUARTER), :]


def gather_kernel(
    keep1, keep2, keep3, keep4, dens1, dens2, dens3, dens4, exch, near1, near3, near4, far1,
    msg, own, dens, exch_own,
):
    base = INROWS + 2 * PER
    here = (
        (keep1, near3, base, dens1, base + 2 * PER + NBQ),
        (keep2, near1, INROWS, dens2, base),
        (keep3, near4, 0, dens3, 2 * PER),
        (keep4, near3, INROWS, dens4, base + 2 * PER),
    )
    sent = 0
    for n, (keep, near, at, d, dens_at) in enumerate(here):
        if n != 1:
            other = keep[pl.ds(0, PER), :] + near[pl.ds(at, PER), :].astype(F32)
            msg[pl.ds(sent * PER, PER), :] = other.astype(BF)
            sent += 1
        mine = keep[pl.ds(PER, PER), :] + near[pl.ds(at + PER, PER), :].astype(F32)
        if n == 3:
            mine = mine + far1[pl.ds(INROWS, PER), :].astype(F32)
        own[pl.ds(n * PER, PER), :] = mine
        total = d[...] + joined(near[pl.ds(dens_at, NBQ), :])
        dens[pl.ds(n * NBQ, NBQ), :] = total
        msg[pl.ds(3 * PER + n * NBQ, NBQ), :] = split_wire(total)
    rows = exch[...] + joined(near4[pl.ds(2 * PER + NBQ, 2 * QUARTER), :])
    msg[pl.ds(3 * PER + 4 * NBQ, QUARTER), :] = split_wire(rows[:QUARTER])
    exch_own[...] = rows[QUARTER:]


FAR_ACTIVE = (1, 2, 0)


def coulomb_kernel(act, far, dens, exch, partial):
    first = low_half(QUARTER)
    total = jnp.zeros((QUARTER, LANES), F32)
    for n in range(4):
        d = dens[pl.ds(n * NBQ, NBQ), :] + joined(
            far[pl.ds(3 * PER + (n ^ 2) * NBQ, NBQ), :]
        )
        for h in range(NBQ // 2):
            a = act[pl.ds(n * PER + h * QUARTER, QUARTER), :]
            if n < 3:
                a = a + far[
                    pl.ds(FAR_ACTIVE[n] * PER + h * QUARTER, QUARTER), :
                ].astype(F32)
            total = total + a * jnp.where(first, d[2 * h : 2 * h + 1], d[2 * h + 1 : 2 * h + 2])
    total = 2.0 * (total + pltpu.roll(total, BS, 1))
    total = total - exch[...] - joined(far[pl.ds(3 * PER + 4 * NBQ, QUARTER), :])
    partial[...] = total[:, :BS]


def active_kernel(where, act, far, out):
    core, x = where[0], where[1]
    for n in range(4):
        xx = (1 - x) if n < 2 else x
        cc = (1 - core) if n % 2 == 0 else core
        base = NBQ * (2 * xx + cc)
        for h in range(NBQ // 2):
            a = act[pl.ds(n * PER + h * QUARTER, QUARTER), :]
            if n < 3:
                a = a + far[
                    pl.ds(FAR_ACTIVE[n] * PER + h * QUARTER, QUARTER), :
                ].astype(F32)
            out[base + 2 * h] = a[:, :BS]
            out[base + 2 * h + 1] = a[:, BS:]


VM = pl.BlockSpec(memory_space=pltpu.VMEM)
SM = pl.BlockSpec(memory_space=pltpu.SMEM)
HB = pl.BlockSpec(memory_space=pltpu.HBM)
PARAMS = pltpu.CompilerParams(vmem_limit_bytes=48 * 1024 * 1024)


def in_hbm(array):
    return pltpu.with_memory_space_constraint(array, pltpu.HBM)


def shape(dims, dtype):
    return jax.ShapeDtypeStruct(dims, dtype)


def sum_over_aux(part):
    n = lax.axis_size("aux")
    if n != 4:
        return lax.psum(part, "aux")
    one, two, three = (
        lax.ppermute(part, "aux", [(z, z ^ k) for z in range(n)]) for k in (1, 2, 3)
    )
    return (part + one) + (two + three)


def paired_body(slabs, block_row, block_col, live_count, orbitals, hcore):
    nslab, batch, width = slabs.shape
    index = lax.axis_index("pair")
    where = jnp.stack([lax.rem(index, 2), index // 2])
    swap_core = [(0, 1), (1, 0), (2, 3), (3, 2)]
    swap_x = [(0, 2), (2, 0), (1, 3), (3, 1)]
    aos = nslab * BS
    scratch = [
        pltpu.VMEM((nslab // 2 + 1, 2, NBQ, width), BF),
        pltpu.VMEM((MSTEP * BS, LANES), F32),
        pltpu.VMEM((MSTEP * BS, LANES), F32),
        pltpu.VMEM((NBQ, NCOL, aos), BF),
        pltpu.VMEM((NBQ, LANES), F32),
        pltpu.SemaphoreType.DMA((nslab // 2 + 1,)),
    ]
    cost = pl.CostEstimate(flops=6 * 10**9, bytes_accessed=10**7, transcendentals=0)
    keep, dens = shape((2 * PER, LANES), F32), shape((NBQ, LANES), F32)
    lt, r, msg1, keep1, dens1 = pl.pallas_call(
        first_kernel,
        name="slabs_first",
        in_specs=[SM, HB, HB, SM, HB, HB],
        out_specs=[VM] * 5,
        out_shape=(
            shape((nslab // 2, NCOL, PAIRED), BF),
            shape((aos, 2 * LANES), BF),
            shape((INROWS + 2 * PER + NBQ, LANES), BF),
            keep,
            dens,
        ),
        scratch_shapes=[
            pltpu.SMEM((nslab,), jnp.int32), pltpu.SMEM((nslab,), jnp.int32),
            pltpu.SemaphoreType.DMA((2,)),
            pltpu.VMEM((2 * nslab, NCOL, PAIRED), BF), pltpu.SemaphoreType.DMA((2 * nslab,)),
        ] + scratch,
        compiler_params=PARAMS,
        cost_estimate=cost,
    )(
        where, in_hbm(block_row), in_hbm(block_col), live_count, slabs,
        in_hbm(orbitals.T),
    )
    near1 = lax.ppermute(msg1, "pair", swap_core)
    keep_in2, send2, keep2, dens2 = pl.pallas_call(
        second_kernel,
        name="slabs_second",
        in_specs=[SM, HB, VM, VM],
        out_specs=[VM] * 4,
        out_shape=(
            shape((INROWS, LANES), F32), shape((2 * PER, LANES), BF), keep, dens,
        ),
        scratch_shapes=scratch,
        compiler_params=PARAMS,
        cost_estimate=cost,
    )(where, slabs, lt, r)
    out2 = jnp.concatenate([keep_in2, keep2[:PER]], axis=0)
    out2 = (out2 + near1[: INROWS + PER].astype(F32)).astype(BF)
    out2, lt, r = lax.optimization_barrier((out2, lt, r))
    far1 = lax.ppermute(out2, "pair", swap_x)
    msg3, keep3, dens3 = pl.pallas_call(
        third_kernel,
        name="slabs_third",
        in_specs=[SM, HB] + [VM] * 4,
        out_specs=[VM] * 3,
        out_shape=(shape((INROWS + 4 * PER + 2 * NBQ, LANES), BF), keep, dens),
        scratch_shapes=scratch,
        compiler_params=PARAMS,
        cost_estimate=cost,
    )(where, slabs, lt, r, send2, dens2)
    near3 = lax.ppermute(msg3, "pair", swap_core)
    msg4, keep_in4, keep4, dens4 = pl.pallas_call(
        fourth_kernel,
        name="slabs_fourth",
        in_specs=[SM, HB] + [VM] * 3,
        out_specs=[VM] * 4,
        out_shape=(
            shape((2 * PER + NBQ, LANES), BF), shape((INROWS, LANES), F32), keep, dens,
        ),
        scratch_shapes=scratch,
        compiler_params=PARAMS,
        cost_estimate=cost,
    )(where, slabs, lt, r, far1)
    msg4, exch = pl.pallas_call(
        exchange_kernel,
        name="exchange",
        in_specs=[SM] + [VM] * 3,
        out_specs=[VM] * 2,
        out_shape=(
            shape((2 * PER + NBQ + 2 * QUARTER, LANES), BF),
            shape((2 * QUARTER, LANES), F32),
        ),
        scratch_shapes=[pltpu.VMEM((NACT, LANES), F32)],
        compiler_params=PARAMS,
    )(where, keep_in4, near3, msg4)
    near4 = lax.ppermute(msg4, "pair", swap_core)
    msg5, act, dens, exch = pl.pallas_call(
        gather_kernel,
        name="active_of_chip",
        in_specs=[VM] * 13,
        out_specs=[VM] * 4,
        out_shape=(
            shape((3 * PER + 4 * NBQ + QUARTER, LANES), BF),
            shape((4 * PER, LANES), F32),
            shape((4 * NBQ, LANES), F32),
            shape((QUARTER, LANES), F32),
        ),
        compiler_params=PARAMS,
    )(keep1, keep2, keep3, keep4, dens1, dens2, dens3, dens4, exch, near1, near3, near4, far1)
    far5 = lax.ppermute(msg5, "pair", swap_x)
    partial = pl.pallas_call(
        coulomb_kernel,
        name="coulomb",
        in_specs=[VM] * 4,
        out_specs=VM,
        out_shape=shape((QUARTER, NACT), F32),
        compiler_params=PARAMS,
    )(act, far5, dens, exch)
    active = pl.pallas_call(
        active_kernel,
        name="own_active",
        in_specs=[SM, VM, VM],
        out_specs=VM,
        out_shape=shape((batch, QUARTER, NACT), F32),
        compiler_params=PARAMS,
        cost_estimate=pl.CostEstimate(flops=10**6, bytes_accessed=10**6, transcendentals=0),
    )(where, act, far5)
    return (active, hcore + sum_over_aux(partial))


def slab_terms(values, left, right):
    half = jnp.einsum("mc,qmn->qnc", left, values, preferred_element_type=F32).astype(BF)
    first = jnp.einsum("qnt,nc->qtc", half[:, :, :NACT], right, preferred_element_type=F32)
    second = jnp.einsum("qnc,nt->qtc", half, right[:, :NACT], preferred_element_type=F32)
    trace = 2.0 * jnp.einsum(
        "qni,ni->q", half[:, :, NACT:], right[:, NACT:], preferred_element_type=F32
    )
    return (first + second, trace)


def general_body(slabs, block_row, block_col, live_count, orbitals, hcore):
    batch = slabs.shape[1]
    init = (jnp.zeros((batch, NACT, NCOL), F32), jnp.zeros((batch,), F32))

    def visit(k, state):
        values = lax.dynamic_index_in_dim(slabs, k, 0, keepdims=False)
        left = lax.dynamic_slice_in_dim(orbitals, block_row[k] * BS, BS, 0)
        right = lax.dynamic_slice_in_dim(orbitals, block_col[k] * BS, BS, 0)
        terms, trace = slab_terms(values.reshape(batch, BS, BS), left, right)
        return (state[0] + terms, state[1] + trace)

    vectors, density = lax.fori_loop(0, live_count[0], visit, init)
    density = lax.psum(density, "pair")
    owned = lax.psum_scatter(vectors, "pair", scatter_dimension=1, tiled=True)
    own_active, own_inactive = owned[:, :, :NACT], owned[:, :, NACT:]
    gathered = lax.all_gather(own_inactive.astype(BF), "pair", axis=1, tiled=True)
    exchange = jnp.einsum(
        "qti,qui->tu", own_inactive, gathered.astype(F32), precision=lax.Precision.HIGHEST
    )
    coulomb = jnp.einsum("qtu,q->tu", own_active, density, precision=lax.Precision.HIGHEST)
    return (own_active, hcore + lax.psum(2.0 * coulomb - exchange, "aux"))


def solution(mesh):
    placed = (
        P(("frag", "pair"), "aux", None),
        P(("frag", "pair")),
        P(("frag", "pair")),
        P(("frag", "pair")),
        P("frag", None),
        P(("frag", "pair"), None),
    )

    def body(slabs, *rest):
        fits = mesh.shape["pair"] == 4 and slabs.shape[1] == 4 * NBQ and slabs.shape[0] % 4 == 0
        return (paired_body if fits else general_body)(slabs, *rest)

    return jax.shard_map(
        body,
        mesh=mesh,
        in_specs=placed,
        out_specs=(P(("frag", "aux"), "pair", None), P(("frag", "pair"), None)),
        check_vma=False,
    )
```

```python
import jax
import jax.numpy as jnp
from jax import lax
from jax.experimental import pallas as pl
from jax.experimental.pallas import tpu as pltpu
from jax.sharding import PartitionSpec as P

BS = 64
NACT = 64
NCOL = 192
NIN = NCOL - NACT
LANES = 128
NBQ = 16
PAIRED = 2 * BS
QSTEP, MSTEP = 3, 49
BF = jnp.bfloat16
F32 = jnp.float32


def low_half(rows):
    return lax.broadcasted_iota(jnp.int32, (rows, LANES), 1) < BS


def orbital_pair(k, blocks, first_window, live, windows):
    halves = []
    for n in range(2):
        slot = 2 * k + n
        w = windows[first_window + slot]
        w = jnp.concatenate([w[NACT:], w[:NACT]], axis=0)
        w = jnp.where(lax.rem(blocks[slot], 2) != n, pltpu.roll(w, BS, 1), w)
        halves.append(jnp.where(slot < live, w, jnp.zeros_like(w)))
    return jnp.where(low_half(NCOL), halves[0], halves[1])


def slab_copies(slabs_ref, sbuf, sem, block):
    return [
        pltpu.make_async_copy(
            slabs_ref.at[pl.ds(2 * k, 2), pl.ds(pl.multiple_of(block * NBQ, NBQ), NBQ), :],
            sbuf.at[k],
            sem.at[k],
        )
        for k in range(slabs_ref.shape[0] // 2)
    ]


def run_block(sbuf, lt_ref, r_ref, scratch, emit, prepare=None, beside=None):
    even_ref, odd_ref, half_ref, diag = scratch
    pairs = sbuf.shape[0]
    first = low_half(NBQ)
    first_s = low_half(BS)
    zero = jnp.zeros((BS, LANES), BF)
    wide, group = NBQ, 4

    def relayout(k, out):
        for j in range(sbuf.shape[3] // LANES):
            lanes = slice(j * LANES, (j + 1) * LANES)
            a = sbuf[k, 0, :, lanes]
            b = sbuf[k, 1, :, lanes]
            out[pl.ds(MSTEP * 2 * j, NBQ, stride=QSTEP), :] = jnp.where(
                first, a, pltpu.roll(b, BS, 1)
            ).astype(F32)
            out[pl.ds(MSTEP * (2 * j + 1), NBQ, stride=QSTEP), :] = jnp.where(
                first, pltpu.roll(a, BS, 1), b
            ).astype(F32)

    def half_transform(k, rows):
        left = lt_ref[k]
        at = pl.ds(pl.multiple_of(k * LANES, LANES), LANES)
        for q in range(0, NBQ, wide):
            cols = []
            for u in range(q, q + wide):
                s = rows[pl.ds(u * QSTEP, BS, stride=MSTEP), :].astype(BF)
                cols.append(
                    jnp.concatenate(
                        [jnp.where(first_s, s, zero), jnp.where(first_s, zero, s)], axis=0
                    )
                )
            half = jnp.dot(left, jnp.concatenate(cols, axis=1), preferred_element_type=F32)
            half = half.astype(BF)
            for u in range(wide):
                half_ref[q + u, :, at] = half[:, u * LANES : (u + 1) * LANES]

    def two_pairs(i, carry):
        relayout(2 * i + 1, odd_ref)
        half_transform(2 * i, even_ref)
        relayout(jnp.minimum(2 * i + 2, pairs - 1), even_ref)
        half_transform(2 * i + 1, odd_ref)
        if beside is not None:
            beside(i)
        return carry

    def second_transform(g):
        lhs = half_ref[pl.ds(group * g, group)].reshape(group * NCOL, half_ref.shape[2])
        return jnp.dot(lhs, r_ref[...], preferred_element_type=F32)

    def assemble(g, whole):
        eye = lax.broadcasted_iota(jnp.int32, (NIN, NIN), 0) == lax.broadcasted_iota(
            jnp.int32, (NIN, NIN), 1
        )
        for p in range(group // 2):
            w0 = whole[2 * p * NCOL : (2 * p + 1) * NCOL]
            w1 = whole[(2 * p + 1) * NCOL : (2 * p + 2) * NCOL]
            side = jnp.where(low_half(NCOL), w0[:, LANES:], w1[:, LANES:])
            across = side[:NIN].T
            square = jnp.concatenate([w0[NIN:, LANES:], w1[NIN:, LANES:]], axis=0).T
            h = group // 2 * g + p
            emit(
                h,
                w0[NIN:, :NIN] + across[:NACT],
                w1[NIN:, :NIN] + across[NACT:],
                side[NIN:] + square[:NACT],
            )
            for n, w in enumerate((w0, w1)):
                diag[pl.ds(2 * h + n, 1), :] = jnp.sum(
                    jnp.where(eye, w[:NIN, :NIN], 0.0), axis=0, keepdims=True
                )

    relayout(0, even_ref)
    if prepare is not None:
        prepare()
    lax.fori_loop(0, pairs // 2, two_pairs, 0)
    whole = second_transform(0)
    for g in range(NBQ // group):
        following = second_transform(g + 1) if g + 1 < NBQ // group else None
        assemble(g, whole)
        whole = following


def split_wire(d):
    hi = d.astype(BF).astype(F32)
    return jnp.where(low_half(d.shape[0]), hi, d - hi).astype(BF)


def joined(wire):
    w = wire.astype(F32)
    return w + pltpu.roll(w, BS, 1)


def density_of(diag):
    d = 2.0 * jnp.sum(diag, axis=1, keepdims=True)
    return jnp.broadcast_to(d, diag.shape)


QUARTER = NACT // 4
PER = NBQ // 2 * QUARTER
INROWS = NBQ * NACT


def emit_active(h, act, core, x, send, keep, send_at):
    upper, lower = act[: 2 * QUARTER], act[2 * QUARTER :]
    parts = (jnp.where(x == 0, lower, upper), jnp.where(x == 0, upper, lower))
    for place, part in enumerate(parts):
        one, two = part[:QUARTER], part[QUARTER:]
        off = place * PER + h * QUARTER
        keep[pl.ds(off, QUARTER), :] = jnp.where(core == 0, one, two)
        send[pl.ds(send_at + off, QUARTER), :] = jnp.where(core == 0, two, one).astype(BF)


def pair_rows(h, n):
    return pl.ds((2 * h + n) * NACT, NACT)


def first_kernel(
    where, rows_ref, cols_ref, live, slabs_ref, ot_ref, lt_out, r_out, msg, keep, dens, after,
    rows, cols, ssem, windows, wsem, sbuf, bsem, sem, *scratch
):
    slabs = slabs_ref.shape[0]
    pairs = slabs // 2
    core, x = where[0], where[1]
    small = [
        pltpu.make_async_copy(src, dst, ssem.at[n])
        for n, (src, dst) in enumerate(((rows_ref, rows), (cols_ref, cols)))
    ]
    for copy in small:
        copy.start()
    now = slab_copies(slabs_ref, sbuf, bsem, 2 * (1 - x) + (1 - core))
    for copy in now:
        copy.start()
    for copy in small:
        copy.wait()
    copies = []
    for n in range(2 * slabs):
        blk = rows[n] if n < slabs else cols[n - slabs]
        base = pl.multiple_of((blk // 2) * PAIRED, PAIRED)
        copies.append(
            pltpu.make_async_copy(ot_ref.at[:, pl.ds(base, PAIRED)], windows.at[n], wsem.at[n])
        )
        copies[-1].start()
    ahead = slab_copies(slabs_ref, after, sem, 2 * (1 - x) + core)
    for copy in ahead:
        copy.start()
    now[0].wait()

    def left(k):
        lt_out[k] = orbital_pair(k, rows, 0, live[0], windows)

    def prepare():
        for copy in copies + now[1:]:
            copy.wait()
        left(0)
        left(1)

    def beside(i):
        for k in (2 * i, 2 * i + 1):
            right = orbital_pair(k, cols, slabs, live[0], windows).astype(F32)
            right = jnp.concatenate([right, right[NIN:]], axis=0)
            r_out[pl.ds(pl.multiple_of(k * PAIRED, PAIRED), PAIRED), :] = right.T.astype(BF)
            left(jnp.minimum(k + 2, pairs - 1))

    def emit(h, in0, in1, act):
        msg[pair_rows(h, 0), :] = in0.astype(BF)
        msg[pair_rows(h, 1), :] = in1.astype(BF)
        emit_active(h, act, core, x, msg, keep, INROWS)

    run_block(sbuf, lt_out, r_out, scratch, emit, prepare, beside)
    dens[...] = density_of(scratch[3][...])
    msg[pl.ds(INROWS + 2 * PER, NBQ), :] = split_wire(dens[...])
    for copy in ahead:
        copy.wait()


def second_kernel(
    where, slabs_ref, sbuf, lt_ref, r_ref, keep_in, send, keep, dens, after, sem, *scratch
):
    core, x = where[0], where[1]
    ahead = slab_copies(slabs_ref, after, sem, 2 * x + (1 - core))
    for copy in ahead:
        copy.start()

    def emit(h, in0, in1, act):
        keep_in[pair_rows(h, 0), :] = in0
        keep_in[pair_rows(h, 1), :] = in1
        emit_active(h, act, core, x, send, keep, 0)

    run_block(sbuf, lt_ref, r_ref, scratch, emit)
    dens[...] = density_of(scratch[3][...])
    for copy in ahead:
        copy.wait()


def third_kernel(
    where, slabs_ref, sbuf, lt_ref, r_ref, send2, dens2, msg, keep, dens, after, sem, *scratch
):
    core, x = where[0], where[1]
    ahead = slab_copies(slabs_ref, after, sem, 2 * x + core)
    for copy in ahead:
        copy.start()

    def emit(h, in0, in1, act):
        msg[pair_rows(h, 0), :] = in0.astype(BF)
        msg[pair_rows(h, 1), :] = in1.astype(BF)
        emit_active(h, act, core, x, msg, keep, INROWS)

    run_block(sbuf, lt_ref, r_ref, scratch, emit)
    msg[pl.ds(INROWS + 2 * PER, 2 * PER), :] = send2[...]
    dens[...] = density_of(scratch[3][...])
    msg[pl.ds(INROWS + 4 * PER, NBQ), :] = split_wire(dens[...])
    msg[pl.ds(INROWS + 4 * PER + NBQ, NBQ), :] = split_wire(dens2[...])
    for copy in ahead:
        copy.wait()


def fourth_kernel(where, sbuf, lt_ref, r_ref, far1, msg, keep_in, keep, dens, *scratch):
    core, x = where[0], where[1]

    def emit(h, in0, in1, act):
        for n, v in enumerate((in0, in1)):
            keep_in[pair_rows(h, n), :] = v + far1[pair_rows(h, n), :].astype(F32)
        emit_active(h, act, core, x, msg, keep, 0)

    run_block(sbuf, lt_ref, r_ref, scratch, emit)
    dens[...] = density_of(scratch[3][...])
    msg[pl.ds(2 * PER, NBQ), :] = split_wire(dens[...])


def exchange_kernel(where, mine, near3, msg4, msg, keep, whole):
    parts = []
    for q in range(NBQ):
        rows = pl.ds(q * NACT, NACT)
        parts.append(mine[rows, :] + near3[rows, :].astype(F32))
    v = jnp.concatenate(parts, axis=1)
    v = v.astype(BF)
    total = lax.dot_general(v, v, (((1,), (1,)), ((), ())), preferred_element_type=F32)
    whole[...] = jnp.concatenate([total, total], axis=1)
    core, x = where[0], where[1]
    size = msg4.shape[0]
    msg[pl.ds(0, size), :] = msg4[...]
    for place, xx in enumerate((1 - x, x)):
        there = pl.multiple_of((2 * xx + 1 - core) * QUARTER, QUARTER)
        here = pl.multiple_of((2 * xx + core) * QUARTER, QUARTER)
        msg[pl.ds(size + place * QUARTER, QUARTER), :] = split_wire(whole[pl.ds(there, QUARTER), :])
        keep[pl.ds(place * QUARTER, QUARTER), :] = whole[pl.ds(here, QUARTER), :]


def gather_kernel(
    keep1, keep2, keep3, keep4, dens1, dens2, dens3, dens4, exch, near1, near3, near4, far1,
    msg, own, dens, exch_own,
):
    base = INROWS + 2 * PER
    here = (
        (keep1, near3, base, dens1, base + 2 * PER + NBQ),
        (keep2, near1, INROWS, dens2, base),
        (keep3, near4, 0, dens3, 2 * PER),
        (keep4, near3, INROWS, dens4, base + 2 * PER),
    )
    sent = 0
    for n, (keep, near, at, d, dens_at) in enumerate(here):
        if n != 1:
            other = keep[pl.ds(0, PER), :] + near[pl.ds(at, PER), :].astype(F32)
            msg[pl.ds(sent * PER, PER), :] = other.astype(BF)
            sent += 1
        mine = keep[pl.ds(PER, PER), :] + near[pl.ds(at + PER, PER), :].astype(F32)
        if n == 3:
            mine = mine + far1[pl.ds(INROWS, PER), :].astype(F32)
        own[pl.ds(n * PER, PER), :] = mine
        total = d[...] + joined(near[pl.ds(dens_at, NBQ), :])
        dens[pl.ds(n * NBQ, NBQ), :] = total
        msg[pl.ds(3 * PER + n * NBQ, NBQ), :] = split_wire(total)
    rows = exch[...] + joined(near4[pl.ds(2 * PER + NBQ, 2 * QUARTER), :])
    msg[pl.ds(3 * PER + 4 * NBQ, QUARTER), :] = split_wire(rows[:QUARTER])
    exch_own[...] = rows[QUARTER:]


FAR_ACTIVE = (1, 2, 0)


def coulomb_kernel(act, far, dens, exch, partial):
    first = low_half(QUARTER)
    total = jnp.zeros((QUARTER, LANES), F32)
    for n in range(4):
        d = dens[pl.ds(n * NBQ, NBQ), :] + joined(
            far[pl.ds(3 * PER + (n ^ 2) * NBQ, NBQ), :]
        )
        for h in range(NBQ // 2):
            a = act[pl.ds(n * PER + h * QUARTER, QUARTER), :]
            if n < 3:
                a = a + far[
                    pl.ds(FAR_ACTIVE[n] * PER + h * QUARTER, QUARTER), :
                ].astype(F32)
            total = total + a * jnp.where(first, d[2 * h : 2 * h + 1], d[2 * h + 1 : 2 * h + 2])
    total = 2.0 * (total + pltpu.roll(total, BS, 1))
    total = total - exch[...] - joined(far[pl.ds(3 * PER + 4 * NBQ, QUARTER), :])
    partial[...] = total[:, :BS]


def active_kernel(where, act, far, out):
    core, x = where[0], where[1]
    for n in range(4):
        xx = (1 - x) if n < 2 else x
        cc = (1 - core) if n % 2 == 0 else core
        base = NBQ * (2 * xx + cc)
        for h in range(NBQ // 2):
            a = act[pl.ds(n * PER + h * QUARTER, QUARTER), :]
            if n < 3:
                a = a + far[
                    pl.ds(FAR_ACTIVE[n] * PER + h * QUARTER, QUARTER), :
                ].astype(F32)
            out[base + 2 * h] = a[:, :BS]
            out[base + 2 * h + 1] = a[:, BS:]


VM = pl.BlockSpec(memory_space=pltpu.VMEM)
SM = pl.BlockSpec(memory_space=pltpu.SMEM)
HB = pl.BlockSpec(memory_space=pltpu.HBM)
PARAMS = pltpu.CompilerParams(vmem_limit_bytes=48 * 1024 * 1024)


def in_hbm(array):
    return pltpu.with_memory_space_constraint(array, pltpu.HBM)


def shape(dims, dtype):
    return jax.ShapeDtypeStruct(dims, dtype)


def sum_over_aux(part):
    n = lax.axis_size("aux")
    if n != 4:
        return lax.psum(part, "aux")
    three, two, one = (
        lax.ppermute(part, "aux", [(z, z ^ k) for z in range(n)]) for k in (3, 2, 1)
    )
    return (three + two) + (one + part)


def paired_body(slabs, block_row, block_col, live_count, orbitals, hcore):
    nslab, batch, width = slabs.shape
    index = lax.axis_index("pair")
    where = jnp.stack([lax.rem(index, 2), index // 2])
    swap_core = [(0, 1), (1, 0), (2, 3), (3, 2)]
    swap_x = [(0, 2), (2, 0), (1, 3), (3, 1)]
    aos = nslab * BS
    loaded = shape((nslab // 2, 2, NBQ, width), BF)
    copies = pltpu.SemaphoreType.DMA((nslab // 2,))
    scratch = [
        pltpu.VMEM((MSTEP * BS, LANES), F32),
        pltpu.VMEM((MSTEP * BS, LANES), F32),
        pltpu.VMEM((NBQ, NCOL, aos), BF),
        pltpu.VMEM((NBQ, LANES), F32),
    ]
    cost = pl.CostEstimate(flops=6 * 10**9, bytes_accessed=10**7, transcendentals=0)
    keep, dens = shape((2 * PER, LANES), F32), shape((NBQ, LANES), F32)
    lt, r, msg1, keep1, dens1, slabs2 = pl.pallas_call(
        first_kernel,
        name="slabs_first",
        in_specs=[SM, HB, HB, SM, HB, HB],
        out_specs=[VM] * 6,
        out_shape=(
            shape((nslab // 2, NCOL, PAIRED), BF),
            shape((aos, 2 * LANES), BF),
            shape((INROWS + 2 * PER + NBQ, LANES), BF),
            keep,
            dens,
            loaded,
        ),
        scratch_shapes=[
            pltpu.SMEM((nslab,), jnp.int32), pltpu.SMEM((nslab,), jnp.int32),
            pltpu.SemaphoreType.DMA((2,)),
            pltpu.VMEM((2 * nslab, NCOL, PAIRED), BF), pltpu.SemaphoreType.DMA((2 * nslab,)),
            pltpu.VMEM(loaded.shape, BF), copies, copies,
        ] + scratch,
        compiler_params=PARAMS,
        cost_estimate=cost,
    )(
        where, in_hbm(block_row), in_hbm(block_col), live_count, slabs,
        in_hbm(orbitals.T),
    )
    near1 = lax.ppermute(msg1, "pair", swap_core)
    keep_in2, send2, keep2, dens2, slabs3 = pl.pallas_call(
        second_kernel,
        name="slabs_second",
        in_specs=[SM, HB] + [VM] * 3,
        out_specs=[VM] * 5,
        out_shape=(
            shape((INROWS, LANES), F32), shape((2 * PER, LANES), BF), keep, dens, loaded,
        ),
        scratch_shapes=[copies] + scratch,
        compiler_params=PARAMS,
        cost_estimate=cost,
    )(where, slabs, slabs2, lt, r)
    out2 = jnp.concatenate([keep_in2, keep2[:PER]], axis=0)
    out2 = (out2 + near1[: INROWS + PER].astype(F32)).astype(BF)
    out2, lt, r = lax.optimization_barrier((out2, lt, r))
    far1 = lax.ppermute(out2, "pair", swap_x)
    msg3, keep3, dens3, slabs4 = pl.pallas_call(
        third_kernel,
        name="slabs_third",
        in_specs=[SM, HB] + [VM] * 5,
        out_specs=[VM] * 4,
        out_shape=(shape((INROWS + 4 * PER + 2 * NBQ, LANES), BF), keep, dens, loaded),
        scratch_shapes=[copies] + scratch,
        compiler_params=PARAMS,
        cost_estimate=cost,
    )(where, slabs, slabs3, lt, r, send2, dens2)
    near3 = lax.ppermute(msg3, "pair", swap_core)
    msg4, keep_in4, keep4, dens4 = pl.pallas_call(
        fourth_kernel,
        name="slabs_fourth",
        in_specs=[SM] + [VM] * 4,
        out_specs=[VM] * 4,
        out_shape=(
            shape((2 * PER + NBQ, LANES), BF), shape((INROWS, LANES), F32), keep, dens,
        ),
        scratch_shapes=scratch,
        compiler_params=PARAMS,
        cost_estimate=cost,
    )(where, slabs4, lt, r, far1)
    msg4, exch = pl.pallas_call(
        exchange_kernel,
        name="exchange",
        in_specs=[SM] + [VM] * 3,
        out_specs=[VM] * 2,
        out_shape=(
            shape((2 * PER + NBQ + 2 * QUARTER, LANES), BF),
            shape((2 * QUARTER, LANES), F32),
        ),
        scratch_shapes=[pltpu.VMEM((NACT, LANES), F32)],
        compiler_params=PARAMS,
    )(where, keep_in4, near3, msg4)
    near4 = lax.ppermute(msg4, "pair", swap_core)
    msg5, act, dens, exch = pl.pallas_call(
        gather_kernel,
        name="active_of_chip",
        in_specs=[VM] * 13,
        out_specs=[VM] * 4,
        out_shape=(
            shape((3 * PER + 4 * NBQ + QUARTER, LANES), BF),
            shape((4 * PER, LANES), F32),
            shape((4 * NBQ, LANES), F32),
            shape((QUARTER, LANES), F32),
        ),
        compiler_params=PARAMS,
    )(keep1, keep2, keep3, keep4, dens1, dens2, dens3, dens4, exch, near1, near3, near4, far1)
    far5 = lax.ppermute(msg5, "pair", swap_x)
    partial = pl.pallas_call(
        coulomb_kernel,
        name="coulomb",
        in_specs=[VM] * 4,
        out_specs=VM,
        out_shape=shape((QUARTER, NACT), F32),
        compiler_params=PARAMS,
    )(act, far5, dens, exch)
    active = pl.pallas_call(
        active_kernel,
        name="own_active",
        in_specs=[SM, VM, VM],
        out_specs=VM,
        out_shape=shape((batch, QUARTER, NACT), F32),
        compiler_params=PARAMS,
        cost_estimate=pl.CostEstimate(flops=10**6, bytes_accessed=10**6, transcendentals=0),
    )(where, act, far5)
    return (active, sum_over_aux(partial) + hcore)


def slab_terms(values, left, right):
    half = jnp.einsum("mc,qmn->qnc", left, values, preferred_element_type=F32).astype(BF)
    first = jnp.einsum("qnt,nc->qtc", half[:, :, :NACT], right, preferred_element_type=F32)
    second = jnp.einsum("qnc,nt->qtc", half, right[:, :NACT], preferred_element_type=F32)
    trace = 2.0 * jnp.einsum(
        "qni,ni->q", half[:, :, NACT:], right[:, NACT:], preferred_element_type=F32
    )
    return (first + second, trace)


def general_body(slabs, block_row, block_col, live_count, orbitals, hcore):
    batch = slabs.shape[1]
    init = (jnp.zeros((batch, NACT, NCOL), F32), jnp.zeros((batch,), F32))

    def visit(k, state):
        values = lax.dynamic_index_in_dim(slabs, k, 0, keepdims=False)
        left = lax.dynamic_slice_in_dim(orbitals, block_row[k] * BS, BS, 0)
        right = lax.dynamic_slice_in_dim(orbitals, block_col[k] * BS, BS, 0)
        terms, trace = slab_terms(values.reshape(batch, BS, BS), left, right)
        return (state[0] + terms, state[1] + trace)

    vectors, density = lax.fori_loop(0, live_count[0], visit, init)
    density = lax.psum(density, "pair")
    owned = lax.psum_scatter(vectors, "pair", scatter_dimension=1, tiled=True)
    own_active, own_inactive = owned[:, :, :NACT], owned[:, :, NACT:]
    gathered = lax.all_gather(own_inactive.astype(BF), "pair", axis=1, tiled=True)
    exchange = jnp.einsum(
        "qti,qui->tu", own_inactive, gathered.astype(F32), precision=lax.Precision.HIGHEST
    )
    coulomb = jnp.einsum("qtu,q->tu", own_active, density, precision=lax.Precision.HIGHEST)
    return (own_active, hcore + lax.psum(2.0 * coulomb - exchange, "aux"))


def solution(mesh):
    placed = (
        P(("frag", "pair"), "aux", None),
        P(("frag", "pair")),
        P(("frag", "pair")),
        P(("frag", "pair")),
        P("frag", None),
        P(("frag", "pair"), None),
    )

    def body(slabs, *rest):
        fits = mesh.shape["pair"] == 4 and slabs.shape[1] == 4 * NBQ and slabs.shape[0] % 4 == 0
        return (paired_body if fits else general_body)(slabs, *rest)

    return jax.shard_map(
        body,
        mesh=mesh,
        in_specs=placed,
        out_specs=(P(("frag", "aux"), "pair", None), P(("frag", "pair"), None)),
        check_vma=False,
    )
```

```python
import jax
import jax.numpy as jnp
from jax import lax
from jax.experimental import pallas as pl
from jax.experimental.pallas import tpu as pltpu
from jax.sharding import PartitionSpec as P

BS = 64
NACT = 64
NCOL = 192
NIN = NCOL - NACT
LANES = 128
NBQ = 16
PAIRED = 2 * BS
QSTEP, MSTEP = 3, 49
BF = jnp.bfloat16
F32 = jnp.float32


def low_half(rows):
    return lax.broadcasted_iota(jnp.int32, (rows, LANES), 1) < BS


def orbital_pair(k, blocks, live, orbitals):
    halves = []
    for n in range(2):
        slot = 2 * k + n
        base = pl.multiple_of((blocks[slot] // 2) * PAIRED, PAIRED)
        w = orbitals[:, pl.ds(base, PAIRED)]
        w = jnp.concatenate([w[NACT:], w[:NACT]], axis=0)
        w = jnp.where(lax.rem(blocks[slot], 2) != n, pltpu.roll(w, BS, 1), w)
        halves.append(jnp.where(slot < live, w, jnp.zeros_like(w)))
    return jnp.where(low_half(NCOL), halves[0], halves[1])


def slab_copies(slabs_ref, sbuf, sem, block):
    return [
        pltpu.make_async_copy(
            slabs_ref.at[pl.ds(2 * k, 2), pl.ds(pl.multiple_of(block * NBQ, NBQ), NBQ), :],
            sbuf.at[k],
            sem.at[k],
        )
        for k in range(slabs_ref.shape[0] // 2)
    ]


def run_block(sbuf, lt_ref, r_ref, scratch, emit, prepare=None, beside=None):
    even_ref, odd_ref, half_ref, diag = scratch
    pairs = sbuf.shape[0]
    first = low_half(NBQ)
    first_s = low_half(BS)
    zero = jnp.zeros((BS, LANES), BF)
    wide, group = NBQ, 4

    def relayout(k, out):
        for j in range(sbuf.shape[3] // LANES):
            lanes = slice(j * LANES, (j + 1) * LANES)
            a = sbuf[k, 0, :, lanes]
            b = sbuf[k, 1, :, lanes]
            out[pl.ds(MSTEP * 2 * j, NBQ, stride=QSTEP), :] = jnp.where(
                first, a, pltpu.roll(b, BS, 1)
            ).astype(F32)
            out[pl.ds(MSTEP * (2 * j + 1), NBQ, stride=QSTEP), :] = jnp.where(
                first, pltpu.roll(a, BS, 1), b
            ).astype(F32)

    def half_transform(k, rows):
        left = lt_ref[k]
        at = pl.ds(pl.multiple_of(k * LANES, LANES), LANES)
        for q in range(0, NBQ, wide):
            cols = []
            for u in range(q, q + wide):
                s = rows[pl.ds(u * QSTEP, BS, stride=MSTEP), :].astype(BF)
                cols.append(
                    jnp.concatenate(
                        [jnp.where(first_s, s, zero), jnp.where(first_s, zero, s)], axis=0
                    )
                )
            half = jnp.dot(left, jnp.concatenate(cols, axis=1), preferred_element_type=F32)
            half = half.astype(BF)
            for u in range(wide):
                half_ref[q + u, :, at] = half[:, u * LANES : (u + 1) * LANES]

    def two_pairs(i, carry):
        relayout(2 * i + 1, odd_ref)
        half_transform(2 * i, even_ref)
        relayout(jnp.minimum(2 * i + 2, pairs - 1), even_ref)
        half_transform(2 * i + 1, odd_ref)
        if beside is not None:
            beside(i)
        return carry

    def second_transform(g):
        lhs = half_ref[pl.ds(group * g, group)].reshape(group * NCOL, half_ref.shape[2])
        return jnp.dot(lhs, r_ref[...], preferred_element_type=F32)

    def assemble(g, whole):
        eye = lax.broadcasted_iota(jnp.int32, (NIN, NIN), 0) == lax.broadcasted_iota(
            jnp.int32, (NIN, NIN), 1
        )
        for p in range(group // 2):
            w0 = whole[2 * p * NCOL : (2 * p + 1) * NCOL]
            w1 = whole[(2 * p + 1) * NCOL : (2 * p + 2) * NCOL]
            side = jnp.where(low_half(NCOL), w0[:, LANES:], w1[:, LANES:])
            across = side[:NIN].T
            square = jnp.concatenate([w0[NIN:, LANES:], w1[NIN:, LANES:]], axis=0).T
            h = group // 2 * g + p
            emit(
                h,
                w0[NIN:, :NIN] + across[:NACT],
                w1[NIN:, :NIN] + across[NACT:],
                side[NIN:] + square[:NACT],
            )
            for n, w in enumerate((w0, w1)):
                diag[pl.ds(2 * h + n, 1), :] = jnp.sum(
                    jnp.where(eye, w[:NIN, :NIN], 0.0), axis=0, keepdims=True
                )

    relayout(0, even_ref)
    if prepare is not None:
        prepare()
    lax.fori_loop(0, pairs // 2, two_pairs, 0)
    whole = second_transform(0)
    for g in range(NBQ // group):
        following = second_transform(g + 1) if g + 1 < NBQ // group else None
        assemble(g, whole)
        whole = following


def split_wire(d):
    hi = d.astype(BF).astype(F32)
    return jnp.where(low_half(d.shape[0]), hi, d - hi).astype(BF)


def joined(wire):
    w = wire.astype(F32)
    return w + pltpu.roll(w, BS, 1)


def density_of(diag):
    d = 2.0 * jnp.sum(diag, axis=1, keepdims=True)
    return jnp.broadcast_to(d, diag.shape)


QUARTER = NACT // 4
PER = NBQ // 2 * QUARTER
INROWS = NBQ * NACT


def emit_active(h, act, core, x, send, keep, send_at):
    upper, lower = act[: 2 * QUARTER], act[2 * QUARTER :]
    parts = (jnp.where(x == 0, lower, upper), jnp.where(x == 0, upper, lower))
    for place, part in enumerate(parts):
        one, two = part[:QUARTER], part[QUARTER:]
        off = place * PER + h * QUARTER
        keep[pl.ds(off, QUARTER), :] = jnp.where(core == 0, one, two)
        send[pl.ds(send_at + off, QUARTER), :] = jnp.where(core == 0, two, one).astype(BF)


def pair_rows(h, n):
    return pl.ds((2 * h + n) * NACT, NACT)


def first_kernel(
    where, rows_ref, cols_ref, live, slabs_ref, ot_ref, lt_out, r_out, msg, keep, dens, after,
    rows, cols, orbitals, ssem, sbuf, bsem, sem, *scratch
):
    pairs = slabs_ref.shape[0] // 2
    core, x = where[0], where[1]
    small = [
        pltpu.make_async_copy(src, dst, ssem.at[n])
        for n, (src, dst) in enumerate(((rows_ref, rows), (cols_ref, cols), (ot_ref, orbitals)))
    ]
    now = slab_copies(slabs_ref, sbuf, bsem, 2 * (1 - x) + (1 - core))
    for copy in [small[0], now[0], small[1], small[2]] + now[1:]:
        copy.start()
    ahead = slab_copies(slabs_ref, after, sem, 2 * (1 - x) + core)
    now[0].wait()

    def left(k):
        lt_out[k] = orbital_pair(k, rows, live[0], orbitals)

    def prepare():
        for copy in small:
            copy.wait()
        left(0)
        left(1)
        for copy in now[1:]:
            copy.wait()
        for copy in ahead:
            copy.start()

    def beside(i):
        for k in (2 * i, 2 * i + 1):
            right = orbital_pair(k, cols, live[0], orbitals).astype(F32)
            right = jnp.concatenate([right, right[NIN:]], axis=0)
            r_out[pl.ds(pl.multiple_of(k * PAIRED, PAIRED), PAIRED), :] = right.T.astype(BF)
            left(jnp.minimum(k + 2, pairs - 1))

    def emit(h, in0, in1, act):
        msg[pair_rows(h, 0), :] = in0.astype(BF)
        msg[pair_rows(h, 1), :] = in1.astype(BF)
        emit_active(h, act, core, x, msg, keep, INROWS)

    run_block(sbuf, lt_out, r_out, scratch, emit, prepare, beside)
    dens[...] = density_of(scratch[3][...])
    msg[pl.ds(INROWS + 2 * PER, NBQ), :] = split_wire(dens[...])
    for copy in ahead:
        copy.wait()


def second_kernel(
    where, slabs_ref, sbuf, lt_ref, r_ref, keep_in, send, keep, dens, after, sem, *scratch
):
    core, x = where[0], where[1]
    ahead = slab_copies(slabs_ref, after, sem, 2 * x + (1 - core))
    for copy in ahead:
        copy.start()

    def emit(h, in0, in1, act):
        keep_in[pair_rows(h, 0), :] = in0
        keep_in[pair_rows(h, 1), :] = in1
        emit_active(h, act, core, x, send, keep, 0)

    run_block(sbuf, lt_ref, r_ref, scratch, emit)
    dens[...] = density_of(scratch[3][...])
    for copy in ahead:
        copy.wait()


def third_kernel(
    where, slabs_ref, sbuf, lt_ref, r_ref, send2, dens2, msg, keep, dens, after, sem, *scratch
):
    core, x = where[0], where[1]
    ahead = slab_copies(slabs_ref, after, sem, 2 * x + core)
    for copy in ahead:
        copy.start()

    def emit(h, in0, in1, act):
        msg[pair_rows(h, 0), :] = in0.astype(BF)
        msg[pair_rows(h, 1), :] = in1.astype(BF)
        emit_active(h, act, core, x, msg, keep, INROWS)

    run_block(sbuf, lt_ref, r_ref, scratch, emit)
    msg[pl.ds(INROWS + 2 * PER, 2 * PER), :] = send2[...]
    dens[...] = density_of(scratch[3][...])
    msg[pl.ds(INROWS + 4 * PER, NBQ), :] = split_wire(dens[...])
    msg[pl.ds(INROWS + 4 * PER + NBQ, NBQ), :] = split_wire(dens2[...])
    for copy in ahead:
        copy.wait()


def fourth_kernel(where, sbuf, lt_ref, r_ref, msg, keep_in, keep, dens, *scratch):
    core, x = where[0], where[1]

    def emit(h, in0, in1, act):
        for n, v in enumerate((in0, in1)):
            keep_in[pair_rows(h, n), :] = v
        emit_active(h, act, core, x, msg, keep, 0)

    run_block(sbuf, lt_ref, r_ref, scratch, emit)
    dens[...] = density_of(scratch[3][...])
    msg[pl.ds(2 * PER, NBQ), :] = split_wire(dens[...])


def exchange_kernel(where, mine, near3, far1a, far1b, msg4, msg, keep, whole):
    parts = []
    for q in range(NBQ):
        rows = pl.ds(q * NACT, NACT)
        at = q * NACT - far1a.shape[0]
        far = far1a[rows, :] if at < 0 else far1b[pl.ds(at, NACT), :]
        parts.append(mine[rows, :] + near3[rows, :].astype(F32) + far.astype(F32))
    v = jnp.concatenate(parts, axis=1)
    v = v.astype(BF)
    total = lax.dot_general(v, v, (((1,), (1,)), ((), ())), preferred_element_type=F32)
    whole[...] = jnp.concatenate([total, total], axis=1)
    core, x = where[0], where[1]
    size = msg4.shape[0]
    msg[pl.ds(0, size), :] = msg4[...]
    for place, xx in enumerate((1 - x, x)):
        there = pl.multiple_of((2 * xx + 1 - core) * QUARTER, QUARTER)
        here = pl.multiple_of((2 * xx + core) * QUARTER, QUARTER)
        msg[pl.ds(size + place * QUARTER, QUARTER), :] = split_wire(whole[pl.ds(there, QUARTER), :])
        keep[pl.ds(place * QUARTER, QUARTER), :] = whole[pl.ds(here, QUARTER), :]


def gather_kernel(
    keep1, keep2, keep3, keep4, dens1, dens2, dens3, dens4, exch, near1, near3, near4, far1,
    msg, own, dens, exch_own,
):
    base = INROWS + 2 * PER
    here = (
        (keep1, near3, base, dens1, base + 2 * PER + NBQ),
        (keep2, near1, INROWS, dens2, base),
        (keep3, near4, 0, dens3, 2 * PER),
        (keep4, near3, INROWS, dens4, base + 2 * PER),
    )
    sent = 0
    for n, (keep, near, at, d, dens_at) in enumerate(here):
        if n != 1:
            other = keep[pl.ds(0, PER), :] + near[pl.ds(at, PER), :].astype(F32)
            msg[pl.ds(sent * PER, PER), :] = other.astype(BF)
            sent += 1
        mine = keep[pl.ds(PER, PER), :] + near[pl.ds(at + PER, PER), :].astype(F32)
        if n == 3:
            mine = mine + far1[pl.ds(far1.shape[0] - PER, PER), :].astype(F32)
        own[pl.ds(n * PER, PER), :] = mine
        total = d[...] + joined(near[pl.ds(dens_at, NBQ), :])
        dens[pl.ds(n * NBQ, NBQ), :] = total
        msg[pl.ds(3 * PER + n * NBQ, NBQ), :] = split_wire(total)
    rows = exch[...] + joined(near4[pl.ds(2 * PER + NBQ, 2 * QUARTER), :])
    msg[pl.ds(3 * PER + 4 * NBQ, QUARTER), :] = split_wire(rows[:QUARTER])
    exch_own[...] = rows[QUARTER:]


FAR_ACTIVE = (1, 2, 0)


def coulomb_kernel(act, far, dens, exch, partial):
    first = low_half(QUARTER)
    total = jnp.zeros((QUARTER, LANES), F32)
    for n in range(4):
        d = dens[pl.ds(n * NBQ, NBQ), :] + joined(
            far[pl.ds(3 * PER + (n ^ 2) * NBQ, NBQ), :]
        )
        for h in range(NBQ // 2):
            a = act[pl.ds(n * PER + h * QUARTER, QUARTER), :]
            if n < 3:
                a = a + far[
                    pl.ds(FAR_ACTIVE[n] * PER + h * QUARTER, QUARTER), :
                ].astype(F32)
            total = total + a * jnp.where(first, d[2 * h : 2 * h + 1], d[2 * h + 1 : 2 * h + 2])
    total = 2.0 * (total + pltpu.roll(total, BS, 1))
    total = total - exch[...] - joined(far[pl.ds(3 * PER + 4 * NBQ, QUARTER), :])
    partial[...] = total[:, :BS]


def active_kernel(where, act, far, out):
    core, x = where[0], where[1]
    for n in range(4):
        xx = (1 - x) if n < 2 else x
        cc = (1 - core) if n % 2 == 0 else core
        base = NBQ * (2 * xx + cc)
        for h in range(NBQ // 2):
            a = act[pl.ds(n * PER + h * QUARTER, QUARTER), :]
            if n < 3:
                a = a + far[
                    pl.ds(FAR_ACTIVE[n] * PER + h * QUARTER, QUARTER), :
                ].astype(F32)
            out[base + 2 * h] = a[:, :BS]
            out[base + 2 * h + 1] = a[:, BS:]


VM = pl.BlockSpec(memory_space=pltpu.VMEM)
SM = pl.BlockSpec(memory_space=pltpu.SMEM)
HB = pl.BlockSpec(memory_space=pltpu.HBM)
PARAMS = pltpu.CompilerParams(vmem_limit_bytes=48 * 1024 * 1024)


def in_hbm(array):
    return pltpu.with_memory_space_constraint(array, pltpu.HBM)


def shape(dims, dtype):
    return jax.ShapeDtypeStruct(dims, dtype)


def sum_over_aux(part, active):
    n = lax.axis_size("aux")
    if n != 4:
        return lax.psum(part, "aux"), active
    down, up = {}, {}
    for k in range(1, n):
        down[k] = lax.ppermute(part, "aux", [(z, z - k) for z in range(k, n)])
    part, active = lax.optimization_barrier((part, active))
    for k in range(1, n):
        up[k] = lax.ppermute(part, "aux", [(z, z + k) for z in range(n - k)])
    z = lax.axis_index("aux")

    def from_device(s):
        value = part
        for other in range(n):
            if other != s:
                value = jnp.where(z == other, down[s - other] if s > other else up[other - s], value)
        return value

    return (from_device(0) + from_device(1)) + (from_device(2) + from_device(3)), active


def paired_body(slabs, block_row, block_col, live_count, orbitals, hcore):
    nslab, batch, width = slabs.shape
    index = lax.axis_index("pair")
    where = jnp.stack([lax.rem(index, 2), index // 2])
    swap_core = [(0, 1), (1, 0), (2, 3), (3, 2)]
    swap_x = [(0, 2), (2, 0), (1, 3), (3, 1)]
    aos = nslab * BS
    loaded = shape((nslab // 2, 2, NBQ, width), BF)
    copies = pltpu.SemaphoreType.DMA((nslab // 2,))
    scratch = [
        pltpu.VMEM((MSTEP * BS, LANES), F32),
        pltpu.VMEM((MSTEP * BS, LANES), F32),
        pltpu.VMEM((NBQ, NCOL, aos), BF),
        pltpu.VMEM((NBQ, LANES), F32),
    ]
    cost = pl.CostEstimate(flops=6 * 10**9, bytes_accessed=10**7, transcendentals=0)
    keep, dens = shape((2 * PER, LANES), F32), shape((NBQ, LANES), F32)
    lt, r, msg1, keep1, dens1, slabs2 = pl.pallas_call(
        first_kernel,
        name="slabs_first",
        in_specs=[SM, HB, HB, SM, HB, HB],
        out_specs=[VM] * 6,
        out_shape=(
            shape((nslab // 2, NCOL, PAIRED), BF),
            shape((aos, 2 * LANES), BF),
            shape((INROWS + 2 * PER + NBQ, LANES), BF),
            keep,
            dens,
            loaded,
        ),
        scratch_shapes=[
            pltpu.SMEM((nslab,), jnp.int32), pltpu.SMEM((nslab,), jnp.int32),
            pltpu.VMEM(orbitals.T.shape, BF), pltpu.SemaphoreType.DMA((3,)),
            pltpu.VMEM(loaded.shape, BF), copies, copies,
        ] + scratch,
        compiler_params=PARAMS,
        cost_estimate=cost,
    )(
        where, in_hbm(block_row), in_hbm(block_col), live_count, slabs,
        in_hbm(orbitals.T),
    )
    near1 = lax.ppermute(msg1, "pair", swap_core)
    keep_in2, send2, keep2, dens2, slabs3 = pl.pallas_call(
        second_kernel,
        name="slabs_second",
        in_specs=[SM, HB] + [VM] * 3,
        out_specs=[VM] * 5,
        out_shape=(
            shape((INROWS, LANES), F32), shape((2 * PER, LANES), BF), keep, dens, loaded,
        ),
        scratch_shapes=[copies] + scratch,
        compiler_params=PARAMS,
        cost_estimate=cost,
    )(where, slabs, slabs2, lt, r)
    out2 = jnp.concatenate([keep_in2, keep2[:PER]], axis=0)
    out2 = (out2 + near1[: INROWS + PER].astype(F32)).astype(BF)
    out2, lt, r = lax.optimization_barrier((out2, lt, r))
    cut = INROWS // 2 + NACT
    far1a = lax.ppermute(out2[:cut], "pair", swap_x)
    far1b = lax.ppermute(out2[cut:], "pair", swap_x)
    msg3, keep3, dens3, slabs4 = pl.pallas_call(
        third_kernel,
        name="slabs_third",
        in_specs=[SM, HB] + [VM] * 5,
        out_specs=[VM] * 4,
        out_shape=(shape((INROWS + 4 * PER + 2 * NBQ, LANES), BF), keep, dens, loaded),
        scratch_shapes=[copies] + scratch,
        compiler_params=PARAMS,
        cost_estimate=cost,
    )(where, slabs, slabs3, lt, r, send2, dens2)
    near3 = lax.ppermute(msg3, "pair", swap_core)
    far1a, lt, r = lax.optimization_barrier((far1a, lt, r))
    msg4, keep_in4, keep4, dens4 = pl.pallas_call(
        fourth_kernel,
        name="slabs_fourth",
        in_specs=[SM] + [VM] * 3,
        out_specs=[VM] * 4,
        out_shape=(
            shape((2 * PER + NBQ, LANES), BF), shape((INROWS, LANES), F32), keep, dens,
        ),
        scratch_shapes=scratch,
        compiler_params=PARAMS,
        cost_estimate=cost,
    )(where, slabs4, lt, r)
    msg4, exch = pl.pallas_call(
        exchange_kernel,
        name="exchange",
        in_specs=[SM] + [VM] * 5,
        out_specs=[VM] * 2,
        out_shape=(
            shape((2 * PER + NBQ + 2 * QUARTER, LANES), BF),
            shape((2 * QUARTER, LANES), F32),
        ),
        scratch_shapes=[pltpu.VMEM((NACT, LANES), F32)],
        compiler_params=PARAMS,
    )(where, keep_in4, near3, far1a, far1b, msg4)
    near4 = lax.ppermute(msg4, "pair", swap_core)
    msg5, act, dens, exch = pl.pallas_call(
        gather_kernel,
        name="active_of_chip",
        in_specs=[VM] * 13,
        out_specs=[VM] * 4,
        out_shape=(
            shape((3 * PER + 4 * NBQ + QUARTER, LANES), BF),
            shape((4 * PER, LANES), F32),
            shape((4 * NBQ, LANES), F32),
            shape((QUARTER, LANES), F32),
        ),
        compiler_params=PARAMS,
    )(keep1, keep2, keep3, keep4, dens1, dens2, dens3, dens4, exch, near1, near3, near4, far1b)
    far5 = lax.ppermute(msg5, "pair", swap_x)
    partial = pl.pallas_call(
        coulomb_kernel,
        name="coulomb",
        in_specs=[VM] * 4,
        out_specs=VM,
        out_shape=shape((QUARTER, NACT), F32),
        compiler_params=PARAMS,
    )(act, far5, dens, exch)
    active = pl.pallas_call(
        active_kernel,
        name="own_active",
        in_specs=[SM, VM, VM],
        out_specs=VM,
        out_shape=shape((batch, QUARTER, NACT), F32),
        compiler_params=PARAMS,
        cost_estimate=pl.CostEstimate(flops=10**6, bytes_accessed=10**6, transcendentals=0),
    )(where, act, far5)
    total, active = sum_over_aux(partial, active)
    return (active, total + hcore)


def slab_terms(values, left, right):
    half = jnp.einsum("mc,qmn->qnc", left, values, preferred_element_type=F32).astype(BF)
    first = jnp.einsum("qnt,nc->qtc", half[:, :, :NACT], right, preferred_element_type=F32)
    second = jnp.einsum("qnc,nt->qtc", half, right[:, :NACT], preferred_element_type=F32)
    trace = 2.0 * jnp.einsum(
        "qni,ni->q", half[:, :, NACT:], right[:, NACT:], preferred_element_type=F32
    )
    return (first + second, trace)


def general_body(slabs, block_row, block_col, live_count, orbitals, hcore):
    batch = slabs.shape[1]
    init = (jnp.zeros((batch, NACT, NCOL), F32), jnp.zeros((batch,), F32))

    def visit(k, state):
        values = lax.dynamic_index_in_dim(slabs, k, 0, keepdims=False)
        left = lax.dynamic_slice_in_dim(orbitals, block_row[k] * BS, BS, 0)
        right = lax.dynamic_slice_in_dim(orbitals, block_col[k] * BS, BS, 0)
        terms, trace = slab_terms(values.reshape(batch, BS, BS), left, right)
        return (state[0] + terms, state[1] + trace)

    vectors, density = lax.fori_loop(0, live_count[0], visit, init)
    density = lax.psum(density, "pair")
    owned = lax.psum_scatter(vectors, "pair", scatter_dimension=1, tiled=True)
    own_active, own_inactive = owned[:, :, :NACT], owned[:, :, NACT:]
    gathered = lax.all_gather(own_inactive.astype(BF), "pair", axis=1, tiled=True)
    exchange = jnp.einsum(
        "qti,qui->tu", own_inactive, gathered.astype(F32), precision=lax.Precision.HIGHEST
    )
    coulomb = jnp.einsum("qtu,q->tu", own_active, density, precision=lax.Precision.HIGHEST)
    return (own_active, hcore + lax.psum(2.0 * coulomb - exchange, "aux"))


def solution(mesh):
    placed = (
        P(("frag", "pair"), "aux", None),
        P(("frag", "pair")),
        P(("frag", "pair")),
        P(("frag", "pair")),
        P("frag", None),
        P(("frag", "pair"), None),
    )

    def body(slabs, *rest):
        fits = mesh.shape["pair"] == 4 and slabs.shape[1] == 4 * NBQ and slabs.shape[0] % 4 == 0
        return (paired_body if fits else general_body)(slabs, *rest)

    return jax.shard_map(
        body,
        mesh=mesh,
        in_specs=placed,
        out_specs=(P(("frag", "aux"), "pair", None), P(("frag", "pair"), None)),
        check_vma=False,
    )
```

```python
import jax
import jax.numpy as jnp
from jax import lax
from jax.experimental import pallas as pl
from jax.experimental.pallas import tpu as pltpu
from jax.sharding import PartitionSpec as P

BS = 64
NACT = 64
NCOL = 192
NIN = NCOL - NACT
LANES = 128
NBQ = 16
PAIRED = 2 * BS
QSTEP, MSTEP = 3, 49
BF = jnp.bfloat16
F32 = jnp.float32


def low_half(rows):
    return lax.broadcasted_iota(jnp.int32, (rows, LANES), 1) < BS


def orbital_pair(k, blocks, live, orbitals):
    halves = []
    for n in range(2):
        slot = 2 * k + n
        base = pl.multiple_of((blocks[slot] // 2) * PAIRED, PAIRED)
        w = orbitals[:, pl.ds(base, PAIRED)]
        w = jnp.concatenate([w[NACT:], w[:NACT]], axis=0)
        w = jnp.where(lax.rem(blocks[slot], 2) != n, pltpu.roll(w, BS, 1), w)
        halves.append(jnp.where(slot < live, w, jnp.zeros_like(w)))
    return jnp.where(low_half(NCOL), halves[0], halves[1])


def slab_copies(slabs_ref, sbuf, sem, block):
    return [
        pltpu.make_async_copy(
            slabs_ref.at[pl.ds(2 * k, 2), pl.ds(pl.multiple_of(block * NBQ, NBQ), NBQ), :],
            sbuf.at[k],
            sem.at[k],
        )
        for k in range(slabs_ref.shape[0] // 2)
    ]


def run_block(sbuf, lt_ref, r_ref, scratch, emit, prepare=None, beside=None):
    even_ref, odd_ref, half_ref, diag = scratch
    pairs = sbuf.shape[0]
    first = low_half(NBQ)
    first_s = low_half(BS)
    zero = jnp.zeros((BS, LANES), BF)
    wide, group = NBQ, 4

    def relayout(k, out):
        for j in range(sbuf.shape[3] // LANES):
            lanes = slice(j * LANES, (j + 1) * LANES)
            a = sbuf[k, 0, :, lanes]
            b = sbuf[k, 1, :, lanes]
            out[pl.ds(MSTEP * 2 * j, NBQ, stride=QSTEP), :] = jnp.where(
                first, a, pltpu.roll(b, BS, 1)
            ).astype(F32)
            out[pl.ds(MSTEP * (2 * j + 1), NBQ, stride=QSTEP), :] = jnp.where(
                first, pltpu.roll(a, BS, 1), b
            ).astype(F32)

    def half_transform(k, rows):
        left = lt_ref[k]
        at = pl.ds(k * LANES, LANES)
        for q in range(0, NBQ, wide):
            cols = []
            for u in range(q, q + wide):
                s = rows[pl.ds(u * QSTEP, BS, stride=MSTEP), :].astype(BF)
                cols.append(
                    jnp.concatenate(
                        [jnp.where(first_s, s, zero), jnp.where(first_s, zero, s)], axis=0
                    )
                )
            half = jnp.dot(left, jnp.concatenate(cols, axis=1), preferred_element_type=F32)
            half = half.astype(BF)
            for u in range(wide):
                half_ref[q + u, :, at] = half[:, u * LANES : (u + 1) * LANES]

    def two_pairs(i):
        relayout(2 * i + 1, odd_ref)
        half_transform(2 * i, even_ref)
        if 2 * i + 2 < pairs:
            relayout(2 * i + 2, even_ref)
        half_transform(2 * i + 1, odd_ref)
        if beside is not None:
            beside(i)

    def second_transform(g):
        lhs = half_ref[pl.ds(group * g, group)].reshape(group * NCOL, half_ref.shape[2])
        return jnp.dot(lhs, r_ref[...], preferred_element_type=F32)

    def assemble(g, whole):
        eye = lax.broadcasted_iota(jnp.int32, (NIN, NIN), 0) == lax.broadcasted_iota(
            jnp.int32, (NIN, NIN), 1
        )
        for p in range(group // 2):
            w0 = whole[2 * p * NCOL : (2 * p + 1) * NCOL]
            w1 = whole[(2 * p + 1) * NCOL : (2 * p + 2) * NCOL]
            side = jnp.where(low_half(NCOL), w0[:, LANES:], w1[:, LANES:])
            across = side[:NIN].T
            square = jnp.concatenate([w0[NIN:, LANES:], w1[NIN:, LANES:]], axis=0).T
            h = group // 2 * g + p
            emit(
                h,
                w0[NIN:, :NIN] + across[:NACT],
                w1[NIN:, :NIN] + across[NACT:],
                side[NIN:] + square[:NACT],
            )
            for n, w in enumerate((w0, w1)):
                diag[pl.ds(2 * h + n, 1), :] = jnp.sum(
                    jnp.where(eye, w[:NIN, :NIN], 0.0), axis=0, keepdims=True
                )

    relayout(0, even_ref)
    if prepare is not None:
        prepare()
    for i in range(pairs // 2):
        two_pairs(i)
    whole = second_transform(0)
    for g in range(NBQ // group):
        following = second_transform(g + 1) if g + 1 < NBQ // group else None
        assemble(g, whole)
        whole = following


def split_wire(d):
    hi = d.astype(BF).astype(F32)
    return jnp.where(low_half(d.shape[0]), hi, d - hi).astype(BF)


def joined(wire):
    w = wire.astype(F32)
    return w + pltpu.roll(w, BS, 1)


def density_of(diag):
    d = 2.0 * jnp.sum(diag, axis=1, keepdims=True)
    return jnp.broadcast_to(d, diag.shape)


QUARTER = NACT // 4
PER = NBQ // 2 * QUARTER
INROWS = NBQ * NACT


def emit_active(h, act, core, x, send, keep, send_at):
    upper, lower = act[: 2 * QUARTER], act[2 * QUARTER :]
    parts = (jnp.where(x == 0, lower, upper), jnp.where(x == 0, upper, lower))
    for place, part in enumerate(parts):
        one, two = part[:QUARTER], part[QUARTER:]
        off = place * PER + h * QUARTER
        keep[pl.ds(off, QUARTER), :] = jnp.where(core == 0, one, two)
        send[pl.ds(send_at + off, QUARTER), :] = jnp.where(core == 0, two, one).astype(BF)


def pair_rows(h, n):
    return pl.ds((2 * h + n) * NACT, NACT)


def first_kernel(
    where, rows_ref, cols_ref, live, slabs_ref, ot_ref, lt_out, r_out, msg, keep, dens, after,
    rows, cols, orbitals, ssem, sbuf, bsem, sem, *scratch
):
    pairs = slabs_ref.shape[0] // 2
    core, x = where[0], where[1]
    small = [
        pltpu.make_async_copy(src, dst, ssem.at[n])
        for n, (src, dst) in enumerate(((rows_ref, rows), (cols_ref, cols), (ot_ref, orbitals)))
    ]
    now = slab_copies(slabs_ref, sbuf, bsem, 2 * (1 - x) + (1 - core))
    for copy in [small[0], now[0], small[1], small[2]] + now[1:]:
        copy.start()
    ahead = slab_copies(slabs_ref, after, sem, 2 * (1 - x) + core)
    now[0].wait()

    def left(k):
        lt_out[k] = orbital_pair(k, rows, live[0], orbitals)

    def prepare():
        for copy in small:
            copy.wait()
        left(0)
        left(1)
        for copy in now[1:]:
            copy.wait()
        for copy in ahead:
            copy.start()

    def beside(i):
        for k in (2 * i, 2 * i + 1):
            right = orbital_pair(k, cols, live[0], orbitals).astype(F32)
            right = jnp.concatenate([right, right[NIN:]], axis=0)
            r_out[pl.ds(k * PAIRED, PAIRED), :] = right.T.astype(BF)
            if k + 2 < pairs:
                left(k + 2)

    def emit(h, in0, in1, act):
        msg[pair_rows(h, 0), :] = in0.astype(BF)
        msg[pair_rows(h, 1), :] = in1.astype(BF)
        emit_active(h, act, core, x, msg, keep, INROWS)

    run_block(sbuf, lt_out, r_out, scratch, emit, prepare, beside)
    dens[...] = density_of(scratch[3][...])
    msg[pl.ds(INROWS + 2 * PER, NBQ), :] = split_wire(dens[...])
    for copy in ahead:
        copy.wait()


def second_kernel(
    where, slabs_ref, sbuf, lt_ref, r_ref, keep_in, send, keep, dens, after, sem, *scratch
):
    core, x = where[0], where[1]
    ahead = slab_copies(slabs_ref, after, sem, 2 * x + (1 - core))
    for copy in ahead:
        copy.start()

    def emit(h, in0, in1, act):
        keep_in[pair_rows(h, 0), :] = in0
        keep_in[pair_rows(h, 1), :] = in1
        emit_active(h, act, core, x, send, keep, 0)

    run_block(sbuf, lt_ref, r_ref, scratch, emit)
    dens[...] = density_of(scratch[3][...])
    for copy in ahead:
        copy.wait()


def third_kernel(
    where, slabs_ref, sbuf, lt_ref, r_ref, send2, dens2, msg, keep, dens, after, sem, *scratch
):
    core, x = where[0], where[1]
    ahead = slab_copies(slabs_ref, after, sem, 2 * x + core)
    for copy in ahead:
        copy.start()

    def emit(h, in0, in1, act):
        msg[pair_rows(h, 0), :] = in0.astype(BF)
        msg[pair_rows(h, 1), :] = in1.astype(BF)
        emit_active(h, act, core, x, msg, keep, INROWS)

    run_block(sbuf, lt_ref, r_ref, scratch, emit)
    msg[pl.ds(INROWS + 2 * PER, 2 * PER), :] = send2[...]
    dens[...] = density_of(scratch[3][...])
    msg[pl.ds(INROWS + 4 * PER, NBQ), :] = split_wire(dens[...])
    msg[pl.ds(INROWS + 4 * PER + NBQ, NBQ), :] = split_wire(dens2[...])
    for copy in ahead:
        copy.wait()


def fourth_kernel(where, sbuf, lt_ref, r_ref, msg, keep_in, keep, dens, *scratch):
    core, x = where[0], where[1]

    def emit(h, in0, in1, act):
        for n, v in enumerate((in0, in1)):
            keep_in[pair_rows(h, n), :] = v
        emit_active(h, act, core, x, msg, keep, 0)

    run_block(sbuf, lt_ref, r_ref, scratch, emit)
    dens[...] = density_of(scratch[3][...])
    msg[pl.ds(2 * PER, NBQ), :] = split_wire(dens[...])


def exchange_kernel(where, mine, near3, far1a, far1b, msg4, msg, keep, whole):
    parts = []
    for q in range(NBQ):
        rows = pl.ds(q * NACT, NACT)
        at = q * NACT - far1a.shape[0]
        far = far1a[rows, :] if at < 0 else far1b[pl.ds(at, NACT), :]
        parts.append(mine[rows, :] + near3[rows, :].astype(F32) + far.astype(F32))
    v = jnp.concatenate(parts, axis=1)
    v = v.astype(BF)
    total = lax.dot_general(v, v, (((1,), (1,)), ((), ())), preferred_element_type=F32)
    whole[...] = jnp.concatenate([total, total], axis=1)
    core, x = where[0], where[1]
    size = msg4.shape[0]
    msg[pl.ds(0, size), :] = msg4[...]
    for place, xx in enumerate((1 - x, x)):
        there = pl.multiple_of((2 * xx + 1 - core) * QUARTER, QUARTER)
        here = pl.multiple_of((2 * xx + core) * QUARTER, QUARTER)
        msg[pl.ds(size + place * QUARTER, QUARTER), :] = split_wire(whole[pl.ds(there, QUARTER), :])
        keep[pl.ds(place * QUARTER, QUARTER), :] = whole[pl.ds(here, QUARTER), :]


def gather_kernel(
    keep1, keep2, keep3, keep4, dens1, dens2, dens3, dens4, exch, near1, near3, near4, far1,
    msg, own, dens, exch_own,
):
    base = INROWS + 2 * PER
    here = (
        (keep1, near3, base, dens1, base + 2 * PER + NBQ),
        (keep2, near1, INROWS, dens2, base),
        (keep3, near4, 0, dens3, 2 * PER),
        (keep4, near3, INROWS, dens4, base + 2 * PER),
    )
    sent = 0
    for n, (keep, near, at, d, dens_at) in enumerate(here):
        if n != 1:
            other = keep[pl.ds(0, PER), :] + near[pl.ds(at, PER), :].astype(F32)
            msg[pl.ds(sent * PER, PER), :] = other.astype(BF)
            sent += 1
        mine = keep[pl.ds(PER, PER), :] + near[pl.ds(at + PER, PER), :].astype(F32)
        if n == 3:
            mine = mine + far1[pl.ds(far1.shape[0] - PER, PER), :].astype(F32)
        own[pl.ds(n * PER, PER), :] = mine
        total = d[...] + joined(near[pl.ds(dens_at, NBQ), :])
        dens[pl.ds(n * NBQ, NBQ), :] = total
        msg[pl.ds(3 * PER + n * NBQ, NBQ), :] = split_wire(total)
    rows = exch[...] + joined(near4[pl.ds(2 * PER + NBQ, 2 * QUARTER), :])
    msg[pl.ds(3 * PER + 4 * NBQ, QUARTER), :] = split_wire(rows[:QUARTER])
    exch_own[...] = rows[QUARTER:]


FAR_ACTIVE = (1, 2, 0)


def coulomb_kernel(act, far, dens, exch, partial):
    first = low_half(QUARTER)
    total = jnp.zeros((QUARTER, LANES), F32)
    for n in range(4):
        d = dens[pl.ds(n * NBQ, NBQ), :] + joined(
            far[pl.ds(3 * PER + (n ^ 2) * NBQ, NBQ), :]
        )
        for h in range(NBQ // 2):
            a = act[pl.ds(n * PER + h * QUARTER, QUARTER), :]
            if n < 3:
                a = a + far[
                    pl.ds(FAR_ACTIVE[n] * PER + h * QUARTER, QUARTER), :
                ].astype(F32)
            total = total + a * jnp.where(first, d[2 * h : 2 * h + 1], d[2 * h + 1 : 2 * h + 2])
    total = 2.0 * (total + pltpu.roll(total, BS, 1))
    total = total - exch[...] - joined(far[pl.ds(3 * PER + 4 * NBQ, QUARTER), :])
    partial[...] = total[:, :BS]


def active_kernel(where, act, far, out):
    core, x = where[0], where[1]
    for n in range(4):
        xx = (1 - x) if n < 2 else x
        cc = (1 - core) if n % 2 == 0 else core
        base = NBQ * (2 * xx + cc)
        for h in range(NBQ // 2):
            a = act[pl.ds(n * PER + h * QUARTER, QUARTER), :]
            if n < 3:
                a = a + far[
                    pl.ds(FAR_ACTIVE[n] * PER + h * QUARTER, QUARTER), :
                ].astype(F32)
            out[base + 2 * h] = a[:, :BS]
            out[base + 2 * h + 1] = a[:, BS:]


VM = pl.BlockSpec(memory_space=pltpu.VMEM)
SM = pl.BlockSpec(memory_space=pltpu.SMEM)
HB = pl.BlockSpec(memory_space=pltpu.HBM)
PARAMS = pltpu.CompilerParams(vmem_limit_bytes=48 * 1024 * 1024)


def in_hbm(array):
    return pltpu.with_memory_space_constraint(array, pltpu.HBM)


def shape(dims, dtype):
    return jax.ShapeDtypeStruct(dims, dtype)


def sum_over_aux(part):
    n = lax.axis_size("aux")
    if n != 4:
        return lax.psum(part, "aux")
    for k in (1, 2):
        part = part + lax.ppermute(part, "aux", [(z, z ^ k) for z in range(n)])
    return part


def paired_body(slabs, block_row, block_col, live_count, orbitals, hcore):
    nslab, batch, width = slabs.shape
    index = lax.axis_index("pair")
    where = jnp.stack([lax.rem(index, 2), index // 2])
    swap_core = [(0, 1), (1, 0), (2, 3), (3, 2)]
    swap_x = [(0, 2), (2, 0), (1, 3), (3, 1)]
    aos = nslab * BS
    loaded = shape((nslab // 2, 2, NBQ, width), BF)
    copies = pltpu.SemaphoreType.DMA((nslab // 2,))
    scratch = [
        pltpu.VMEM((MSTEP * BS, LANES), F32),
        pltpu.VMEM((MSTEP * BS, LANES), F32),
        pltpu.VMEM((NBQ, NCOL, aos), BF),
        pltpu.VMEM((NBQ, LANES), F32),
    ]
    cost = pl.CostEstimate(flops=6 * 10**9, bytes_accessed=10**7, transcendentals=0)
    keep, dens = shape((2 * PER, LANES), F32), shape((NBQ, LANES), F32)
    lt, r, msg1, keep1, dens1, slabs2 = pl.pallas_call(
        first_kernel,
        name="slabs_first",
        in_specs=[SM, HB, HB, SM, HB, HB],
        out_specs=[VM] * 6,
        out_shape=(
            shape((nslab // 2, NCOL, PAIRED), BF),
            shape((aos, 2 * LANES), BF),
            shape((INROWS + 2 * PER + NBQ, LANES), BF),
            keep,
            dens,
            loaded,
        ),
        scratch_shapes=[
            pltpu.SMEM((nslab,), jnp.int32), pltpu.SMEM((nslab,), jnp.int32),
            pltpu.VMEM(orbitals.T.shape, BF), pltpu.SemaphoreType.DMA((3,)),
            pltpu.VMEM(loaded.shape, BF), copies, copies,
        ] + scratch,
        compiler_params=PARAMS,
        cost_estimate=cost,
    )(
        where, in_hbm(block_row), in_hbm(block_col), live_count, slabs,
        in_hbm(orbitals.T),
    )
    near1 = lax.ppermute(msg1, "pair", swap_core)
    keep_in2, send2, keep2, dens2, slabs3 = pl.pallas_call(
        second_kernel,
        name="slabs_second",
        in_specs=[SM, HB] + [VM] * 3,
        out_specs=[VM] * 5,
        out_shape=(
            shape((INROWS, LANES), F32), shape((2 * PER, LANES), BF), keep, dens, loaded,
        ),
        scratch_shapes=[copies] + scratch,
        compiler_params=PARAMS,
        cost_estimate=cost,
    )(where, slabs, slabs2, lt, r)
    out2 = jnp.concatenate([keep_in2, keep2[:PER]], axis=0)
    out2 = (out2 + near1[: INROWS + PER].astype(F32)).astype(BF)
    out2, lt, r = lax.optimization_barrier((out2, lt, r))
    cut = INROWS // 2 + NACT
    far1a = lax.ppermute(out2[:cut], "pair", swap_x)
    far1b = lax.ppermute(out2[cut:], "pair", swap_x)
    msg3, keep3, dens3, slabs4 = pl.pallas_call(
        third_kernel,
        name="slabs_third",
        in_specs=[SM, HB] + [VM] * 5,
        out_specs=[VM] * 4,
        out_shape=(shape((INROWS + 4 * PER + 2 * NBQ, LANES), BF), keep, dens, loaded),
        scratch_shapes=[copies] + scratch,
        compiler_params=PARAMS,
        cost_estimate=cost,
    )(where, slabs, slabs3, lt, r, send2, dens2)
    near3 = lax.ppermute(msg3, "pair", swap_core)
    far1a, lt, r = lax.optimization_barrier((far1a, lt, r))
    msg4, keep_in4, keep4, dens4 = pl.pallas_call(
        fourth_kernel,
        name="slabs_fourth",
        in_specs=[SM] + [VM] * 3,
        out_specs=[VM] * 4,
        out_shape=(
            shape((2 * PER + NBQ, LANES), BF), shape((INROWS, LANES), F32), keep, dens,
        ),
        scratch_shapes=scratch,
        compiler_params=PARAMS,
        cost_estimate=cost,
    )(where, slabs4, lt, r)
    msg4, exch = pl.pallas_call(
        exchange_kernel,
        name="exchange",
        in_specs=[SM] + [VM] * 5,
        out_specs=[VM] * 2,
        out_shape=(
            shape((2 * PER + NBQ + 2 * QUARTER, LANES), BF),
            shape((2 * QUARTER, LANES), F32),
        ),
        scratch_shapes=[pltpu.VMEM((NACT, LANES), F32)],
        compiler_params=PARAMS,
    )(where, keep_in4, near3, far1a, far1b, msg4)
    near4 = lax.ppermute(msg4, "pair", swap_core)
    msg5, act, dens, exch = pl.pallas_call(
        gather_kernel,
        name="active_of_chip",
        in_specs=[VM] * 13,
        out_specs=[VM] * 4,
        out_shape=(
            shape((3 * PER + 4 * NBQ + QUARTER, LANES), BF),
            shape((4 * PER, LANES), F32),
            shape((4 * NBQ, LANES), F32),
            shape((QUARTER, LANES), F32),
        ),
        compiler_params=PARAMS,
    )(keep1, keep2, keep3, keep4, dens1, dens2, dens3, dens4, exch, near1, near3, near4, far1b)
    far5 = lax.ppermute(msg5, "pair", swap_x)
    partial = pl.pallas_call(
        coulomb_kernel,
        name="coulomb",
        in_specs=[VM] * 4,
        out_specs=VM,
        out_shape=shape((QUARTER, NACT), F32),
        compiler_params=PARAMS,
    )(act, far5, dens, exch)
    active = pl.pallas_call(
        active_kernel,
        name="own_active",
        in_specs=[SM, VM, VM],
        out_specs=VM,
        out_shape=shape((batch, QUARTER, NACT), F32),
        compiler_params=PARAMS,
        cost_estimate=pl.CostEstimate(flops=10**6, bytes_accessed=10**6, transcendentals=0),
    )(where, act, far5)
    return (active, hcore + sum_over_aux(partial))


def slab_terms(values, left, right):
    half = jnp.einsum("mc,qmn->qnc", left, values, preferred_element_type=F32).astype(BF)
    first = jnp.einsum("qnt,nc->qtc", half[:, :, :NACT], right, preferred_element_type=F32)
    second = jnp.einsum("qnc,nt->qtc", half, right[:, :NACT], preferred_element_type=F32)
    trace = 2.0 * jnp.einsum(
        "qni,ni->q", half[:, :, NACT:], right[:, NACT:], preferred_element_type=F32
    )
    return (first + second, trace)


def general_body(slabs, block_row, block_col, live_count, orbitals, hcore):
    batch = slabs.shape[1]
    init = (jnp.zeros((batch, NACT, NCOL), F32), jnp.zeros((batch,), F32))

    def visit(k, state):
        values = lax.dynamic_index_in_dim(slabs, k, 0, keepdims=False)
        left = lax.dynamic_slice_in_dim(orbitals, block_row[k] * BS, BS, 0)
        right = lax.dynamic_slice_in_dim(orbitals, block_col[k] * BS, BS, 0)
        terms, trace = slab_terms(values.reshape(batch, BS, BS), left, right)
        return (state[0] + terms, state[1] + trace)

    vectors, density = lax.fori_loop(0, live_count[0], visit, init)
    density = lax.psum(density, "pair")
    owned = lax.psum_scatter(vectors, "pair", scatter_dimension=1, tiled=True)
    own_active, own_inactive = owned[:, :, :NACT], owned[:, :, NACT:]
    gathered = lax.all_gather(own_inactive.astype(BF), "pair", axis=1, tiled=True)
    exchange = jnp.einsum(
        "qti,qui->tu", own_inactive, gathered.astype(F32), precision=lax.Precision.HIGHEST
    )
    coulomb = jnp.einsum("qtu,q->tu", own_active, density, precision=lax.Precision.HIGHEST)
    return (own_active, hcore + lax.psum(2.0 * coulomb - exchange, "aux"))


def solution(mesh):
    placed = (
        P(("frag", "pair"), "aux", None),
        P(("frag", "pair")),
        P(("frag", "pair")),
        P(("frag", "pair")),
        P("frag", None),
        P(("frag", "pair"), None),
    )

    def body(slabs, *rest):
        fits = mesh.shape["pair"] == 4 and slabs.shape[1] == 4 * NBQ and slabs.shape[0] % 4 == 0
        return (paired_body if fits else general_body)(slabs, *rest)

    return jax.shard_map(
        body,
        mesh=mesh,
        in_specs=placed,
        out_specs=(P(("frag", "aux"), "pair", None), P(("frag", "pair"), None)),
        check_vma=False,
    )
```

```python
import jax
import jax.numpy as jnp
from jax import lax
from jax.experimental import pallas as pl
from jax.experimental.pallas import tpu as pltpu
from jax.sharding import PartitionSpec as P

BS = 64
NACT = 64
NCOL = 192
NIN = NCOL - NACT
LANES = 128
NBQ = 16
PAIRED = 2 * BS
QSTEP, MSTEP = 3, 49
BF = jnp.bfloat16
F32 = jnp.float32


def low_half(rows):
    return lax.broadcasted_iota(jnp.int32, (rows, LANES), 1) < BS


def orbital_pair(k, blocks, live, orbitals):
    halves = []
    for n in range(2):
        slot = 2 * k + n
        base = pl.multiple_of((blocks[slot] // 2) * PAIRED, PAIRED)
        w = orbitals[:, pl.ds(base, PAIRED)]
        w = jnp.concatenate([w[NACT:], w[:NACT]], axis=0)
        w = jnp.where(lax.rem(blocks[slot], 2) != n, pltpu.roll(w, BS, 1), w)
        halves.append(jnp.where(slot < live, w, jnp.zeros_like(w)))
    return jnp.where(low_half(NCOL), halves[0], halves[1])


def slab_copies(slabs_ref, sbuf, sem, block):
    return [
        pltpu.make_async_copy(
            slabs_ref.at[pl.ds(2 * k, 2), pl.ds(pl.multiple_of(block * NBQ, NBQ), NBQ), :],
            sbuf.at[k],
            sem.at[k],
        )
        for k in range(slabs_ref.shape[0] // 2)
    ]


def run_block(sbuf, weights, scratch, emit, ready=None, midway=None):
    lt_ref, r_ref, bd_ref, d_ref = weights
    pt_ref, q_ref, diag = scratch[4:]
    quads = sbuf.shape[0] // 2
    first = low_half(NBQ)
    first_s = low_half(BS)
    zero = jnp.zeros((BS, LANES), BF)
    group = 8

    def relayout(k, out):
        for j in range(sbuf.shape[3] // LANES):
            lanes = slice(j * LANES, (j + 1) * LANES)
            a = sbuf[k, 0, :, lanes]
            b = sbuf[k, 1, :, lanes]
            out[pl.ds(MSTEP * 2 * j, NBQ, stride=QSTEP), :] = jnp.where(
                first, a, pltpu.roll(b, BS, 1)
            ).astype(F32)
            out[pl.ds(MSTEP * (2 * j + 1), NBQ, stride=QSTEP), :] = jnp.where(
                first, pltpu.roll(a, BS, 1), b
            ).astype(F32)

    def transform(g, bufs):
        dens = [d_ref[2 * g + n] for n in range(2)]
        for q in range(0, NBQ, group):
            slabs = [[], []]
            for u in range(q, q + group):
                total = None
                for n in range(2):
                    s = bufs[n][pl.ds(u * QSTEP, BS, stride=MSTEP), :]
                    part = jnp.sum((s * dens[n]).reshape(BS // 8, 8, LANES), axis=0)
                    total = part if total is None else total + part
                    slabs[n].append(s.astype(BF))
                diag[u] = total if g == 0 else diag[u] + total
            for n in range(2):
                k = 2 * g + n
                cols = [
                    jnp.concatenate(
                        [jnp.where(first_s, s, zero), jnp.where(first_s, zero, s)], axis=0
                    )
                    for s in slabs[n]
                ]
                p = jnp.dot(
                    lt_ref[NIN:, k * LANES : (k + 1) * LANES],
                    jnp.concatenate(cols, axis=1),
                    preferred_element_type=F32,
                ).astype(BF)
                for u in range(group):
                    pt_ref[q + u, :, k * LANES : (k + 1) * LANES] = p[
                        :, u * LANES : (u + 1) * LANES
                    ]
            rows = jnp.concatenate(
                [jnp.concatenate([s0, s1], axis=1) for s0, s1 in zip(*slabs)], axis=0
            )
            out = jnp.dot(rows, bd_ref[g], preferred_element_type=F32).astype(BF)
            for u in range(0, group, 2):
                for n in range(2):
                    lanes = slice(n * LANES, (n + 1) * LANES)
                    q0 = out[u * BS : (u + 1) * BS, lanes]
                    q1 = out[(u + 1) * BS : (u + 2) * BS, lanes]
                    at = slice((q + u) * BS, (q + u + 2) * BS)
                    row = (4 * g + 2 * n) * BS
                    q_ref[row : row + BS, at] = jnp.where(first_s, q0, pltpu.roll(q1, BS, 1))
                    q_ref[row + BS : row + 2 * BS, at] = jnp.where(
                        first_s, pltpu.roll(q0, BS, 1), q1
                    )

    def second_transform(g):
        rows = pt_ref[4 * g : 4 * g + 4].reshape(4 * NACT, pt_ref.shape[2])
        one = jnp.dot(rows, r_ref[...], preferred_element_type=F32)
        two = jnp.dot(
            lt_ref[...], q_ref[:, 4 * g * BS : (4 * g + 4) * BS], preferred_element_type=F32
        )
        return one, two

    def assemble(g, both):
        one, two = both
        for p in range(2):
            w0 = one[2 * p * NACT : (2 * p + 1) * NACT]
            w1 = one[(2 * p + 1) * NACT : (2 * p + 2) * NACT]
            turned = two[:, p * LANES : (p + 1) * LANES]
            across = turned[:NIN].T
            square = jnp.concatenate([turned[NIN:], turned[NIN:]], axis=0).T
            emit(
                2 * g + p,
                w0[:, :NIN] + across[:NACT],
                w1[:, :NIN] + across[NACT:],
                jnp.where(first_s, w0[:, NIN:] + square[:NACT], w1[:, NIN:] + square[NACT:]),
            )

    def load(g):
        for n in range(2):
            if ready is not None:
                ready(2 * g + n)
            relayout(2 * g + n, scratch[2 * (g % 2) + n])

    load(0)
    for g in range(quads):
        if g + 1 < quads:
            load(g + 1)
        transform(g, scratch[2 * (g % 2) : 2 * (g % 2) + 2])
    if midway is not None:
        midway()
    whole = second_transform(0)
    for g in range(NBQ // 4):
        following = second_transform(g + 1) if g + 1 < NBQ // 4 else None
        assemble(g, whole)
        whole = following


def split_wire(d):
    hi = d.astype(BF).astype(F32)
    return jnp.where(low_half(d.shape[0]), hi, d - hi).astype(BF)


def joined(wire):
    w = wire.astype(F32)
    return w + pltpu.roll(w, BS, 1)


def density_of(diag):
    d = 2.0 * jnp.sum(jnp.sum(diag, axis=1), axis=1, keepdims=True)
    return jnp.broadcast_to(d, (NBQ, LANES))


QUARTER = NACT // 4
PER = NBQ // 2 * QUARTER
INROWS = NBQ * NACT


def emit_active(h, act, core, x, send, keep, send_at):
    upper, lower = act[: 2 * QUARTER], act[2 * QUARTER :]
    parts = (jnp.where(x == 0, lower, upper), jnp.where(x == 0, upper, lower))
    for place, part in enumerate(parts):
        one, two = part[:QUARTER], part[QUARTER:]
        off = place * PER + h * QUARTER
        keep[pl.ds(off, QUARTER), :] = jnp.where(core == 0, one, two)
        send[pl.ds(send_at + off, QUARTER), :] = jnp.where(core == 0, two, one).astype(BF)


def pair_rows(h, n):
    return pl.ds((2 * h + n) * NACT, NACT)


def first_kernel(
    where, rows_ref, cols_ref, live, slabs_ref, ot_ref,
    lt_out, r_out, bd_out, d_out, msg, keep, dens, after,
    rows, cols, orbitals, ssem, sbuf, bsem, sem, *scratch
):
    pairs = slabs_ref.shape[0] // 2
    core, x = where[0], where[1]
    part = NACT // 2
    small = [
        pltpu.make_async_copy(src, dst, ssem.at[n])
        for n, (src, dst) in enumerate(((rows_ref, rows), (cols_ref, cols)))
    ] + [
        pltpu.make_async_copy(
            ot_ref.at[pl.ds(n * part, part)], orbitals.at[pl.ds(n * part, part)], ssem.at[2 + n]
        )
        for n in range(NCOL // part)
    ]
    now = slab_copies(slabs_ref, sbuf, bsem, 2 * (1 - x) + (1 - core))
    for copy in now[:2] + small + now[2:]:
        copy.start()
    ahead = slab_copies(slabs_ref, after, sem, 2 * (1 - x) + core)
    bd_out[...] = jnp.zeros_like(bd_out)

    def prepare(k):
        left = orbital_pair(k, rows, live[0], orbitals)
        right = orbital_pair(k, cols, live[0], orbitals)
        at = slice(k * PAIRED, (k + 1) * PAIRED)
        lt_out[:, at] = left
        turned = jnp.concatenate([right, right[NIN:]], axis=0).astype(F32).T.astype(BF)
        r_out[at, :] = turned
        inner = (lax.broadcasted_iota(jnp.int32, (PAIRED, LANES), 0) < BS) == low_half(PAIRED)
        place = slice((k % 2) * PAIRED, (k % 2 + 1) * PAIRED)
        bd_out[k // 2, place, place] = jnp.where(
            inner, turned[:, NIN:], jnp.zeros((PAIRED, LANES), BF)
        )
        both = jnp.dot(
            left[:NIN].astype(F32).T.astype(BF), right[:NIN], preferred_element_type=F32
        )
        d_out[k] = jnp.where(low_half(BS), both[:BS], both[BS:])

    def ready(k):
        now[k].wait()
        if k == 1:
            for copy in small:
                copy.wait()
        if k % 2 == 1:
            prepare(k - 1)
            prepare(k)

    def midway():
        for copy in ahead:
            copy.start()

    def emit(h, in0, in1, act):
        msg[pair_rows(h, 0), :] = in0.astype(BF)
        msg[pair_rows(h, 1), :] = in1.astype(BF)
        emit_active(h, act, core, x, msg, keep, INROWS)

    run_block(sbuf, (lt_out, r_out, bd_out, d_out), scratch, emit, ready, midway)
    dens[...] = density_of(scratch[6][...])
    msg[pl.ds(INROWS + 2 * PER, NBQ), :] = split_wire(dens[...])
    for copy in ahead:
        copy.wait()


def second_kernel(
    where, slabs_ref, sbuf, lt_ref, r_ref, bd_ref, d_ref, keep_in, send, keep, dens, after,
    sem, *scratch
):
    core, x = where[0], where[1]
    ahead = slab_copies(slabs_ref, after, sem, 2 * x + (1 - core))

    def midway():
        for copy in ahead:
            copy.start()

    def emit(h, in0, in1, act):
        keep_in[pair_rows(h, 0), :] = in0
        keep_in[pair_rows(h, 1), :] = in1
        emit_active(h, act, core, x, send, keep, 0)

    run_block(sbuf, (lt_ref, r_ref, bd_ref, d_ref), scratch, emit, None, midway)
    dens[...] = density_of(scratch[6][...])
    for copy in ahead:
        copy.wait()


def third_kernel(
    where, slabs_ref, sbuf, lt_ref, r_ref, bd_ref, d_ref, send2, dens2, msg, keep, dens, after,
    sem, *scratch
):
    core, x = where[0], where[1]
    ahead = slab_copies(slabs_ref, after, sem, 2 * x + core)

    def midway():
        for copy in ahead:
            copy.start()

    def emit(h, in0, in1, act):
        msg[pair_rows(h, 0), :] = in0.astype(BF)
        msg[pair_rows(h, 1), :] = in1.astype(BF)
        emit_active(h, act, core, x, msg, keep, INROWS)

    run_block(sbuf, (lt_ref, r_ref, bd_ref, d_ref), scratch, emit, None, midway)
    msg[pl.ds(INROWS + 2 * PER, 2 * PER), :] = send2[...]
    dens[...] = density_of(scratch[6][...])
    msg[pl.ds(INROWS + 4 * PER, NBQ), :] = split_wire(dens[...])
    msg[pl.ds(INROWS + 4 * PER + NBQ, NBQ), :] = split_wire(dens2[...])
    for copy in ahead:
        copy.wait()


def fourth_kernel(
    where, sbuf, lt_ref, r_ref, bd_ref, d_ref, msg, keep_in, keep, dens, *scratch
):
    core, x = where[0], where[1]

    def emit(h, in0, in1, act):
        keep_in[pair_rows(h, 0), :] = in0
        keep_in[pair_rows(h, 1), :] = in1
        emit_active(h, act, core, x, msg, keep, 0)

    run_block(sbuf, (lt_ref, r_ref, bd_ref, d_ref), scratch, emit)
    dens[...] = density_of(scratch[6][...])
    msg[pl.ds(2 * PER, NBQ), :] = split_wire(dens[...])


def exchange_kernel(where, mine, near3, far1a, far1b, msg4, msg, keep, whole):
    parts = []
    for q in range(NBQ):
        rows = pl.ds(q * NACT, NACT)
        at = q * NACT - far1a.shape[0]
        far = far1a[rows, :] if at < 0 else far1b[pl.ds(at, NACT), :]
        parts.append(mine[rows, :] + near3[rows, :].astype(F32) + far.astype(F32))
    v = jnp.concatenate(parts, axis=1)
    v = v.astype(BF)
    total = lax.dot_general(v, v, (((1,), (1,)), ((), ())), preferred_element_type=F32)
    whole[...] = jnp.concatenate([total, total], axis=1)
    core, x = where[0], where[1]
    size = msg4.shape[0]
    msg[pl.ds(0, size), :] = msg4[...]
    for place, xx in enumerate((1 - x, x)):
        there = pl.multiple_of((2 * xx + 1 - core) * QUARTER, QUARTER)
        here = pl.multiple_of((2 * xx + core) * QUARTER, QUARTER)
        msg[pl.ds(size + place * QUARTER, QUARTER), :] = split_wire(whole[pl.ds(there, QUARTER), :])
        keep[pl.ds(place * QUARTER, QUARTER), :] = whole[pl.ds(here, QUARTER), :]


def gather_kernel(
    keep1, keep2, keep3, keep4, dens1, dens2, dens3, dens4, exch, near1, near3, near4, far1,
    msg, own, dens, exch_own,
):
    base = INROWS + 2 * PER
    here = (
        (keep1, near3, base, dens1, base + 2 * PER + NBQ),
        (keep2, near1, INROWS, dens2, base),
        (keep3, near4, 0, dens3, 2 * PER),
        (keep4, near3, INROWS, dens4, base + 2 * PER),
    )
    sent = 0
    for n, (keep, near, at, d, dens_at) in enumerate(here):
        if n != 1:
            other = keep[pl.ds(0, PER), :] + near[pl.ds(at, PER), :].astype(F32)
            msg[pl.ds(sent * PER, PER), :] = other.astype(BF)
            sent += 1
        mine = keep[pl.ds(PER, PER), :] + near[pl.ds(at + PER, PER), :].astype(F32)
        if n == 3:
            mine = mine + far1[pl.ds(far1.shape[0] - PER, PER), :].astype(F32)
        own[pl.ds(n * PER, PER), :] = mine
        total = d[...] + joined(near[pl.ds(dens_at, NBQ), :])
        dens[pl.ds(n * NBQ, NBQ), :] = total
        msg[pl.ds(3 * PER + n * NBQ, NBQ), :] = split_wire(total)
    rows = exch[...] + joined(near4[pl.ds(2 * PER + NBQ, 2 * QUARTER), :])
    msg[pl.ds(3 * PER + 4 * NBQ, QUARTER), :] = split_wire(rows[:QUARTER])
    exch_own[...] = rows[QUARTER:]


FAR_ACTIVE = (1, 2, 0)


def coulomb_kernel(act, far, dens, exch, partial):
    first = low_half(QUARTER)
    total = jnp.zeros((QUARTER, LANES), F32)
    for n in range(4):
        d = dens[pl.ds(n * NBQ, NBQ), :] + joined(
            far[pl.ds(3 * PER + (n ^ 2) * NBQ, NBQ), :]
        )
        for h in range(NBQ // 2):
            a = act[pl.ds(n * PER + h * QUARTER, QUARTER), :]
            if n < 3:
                a = a + far[
                    pl.ds(FAR_ACTIVE[n] * PER + h * QUARTER, QUARTER), :
                ].astype(F32)
            total = total + a * jnp.where(first, d[2 * h : 2 * h + 1], d[2 * h + 1 : 2 * h + 2])
    total = 2.0 * (total + pltpu.roll(total, BS, 1))
    total = total - exch[...] - joined(far[pl.ds(3 * PER + 4 * NBQ, QUARTER), :])
    partial[...] = total[:, :BS]


def active_kernel(where, act, far, out):
    core, x = where[0], where[1]
    for n in range(4):
        xx = (1 - x) if n < 2 else x
        cc = (1 - core) if n % 2 == 0 else core
        base = NBQ * (2 * xx + cc)
        for h in range(NBQ // 2):
            a = act[pl.ds(n * PER + h * QUARTER, QUARTER), :]
            if n < 3:
                a = a + far[
                    pl.ds(FAR_ACTIVE[n] * PER + h * QUARTER, QUARTER), :
                ].astype(F32)
            out[base + 2 * h] = a[:, :BS]
            out[base + 2 * h + 1] = a[:, BS:]


VM = pl.BlockSpec(memory_space=pltpu.VMEM)
SM = pl.BlockSpec(memory_space=pltpu.SMEM)
HB = pl.BlockSpec(memory_space=pltpu.HBM)
PARAMS = pltpu.CompilerParams(vmem_limit_bytes=32 * 1024 * 1024)


def in_hbm(array):
    return pltpu.with_memory_space_constraint(array, pltpu.HBM)


def shape(dims, dtype):
    return jax.ShapeDtypeStruct(dims, dtype)


def sum_over_aux(part):
    n = lax.axis_size("aux")
    if n != 4:
        return lax.psum(part, "aux")
    for k in (1, 2):
        part = part + lax.ppermute(part, "aux", [(z, z ^ k) for z in range(n)])
    return part


def paired_body(slabs, block_row, block_col, live_count, orbitals, hcore):
    nslab, batch, width = slabs.shape
    index = lax.axis_index("pair")
    where = jnp.stack([lax.rem(index, 2), index // 2])
    swap_core = [(0, 1), (1, 0), (2, 3), (3, 2)]
    swap_x = [(0, 2), (2, 0), (1, 3), (3, 1)]
    aos = nslab * BS
    loaded = shape((nslab // 2, 2, NBQ, width), BF)
    copies = pltpu.SemaphoreType.DMA((nslab // 2,))
    scratch = [pltpu.VMEM((MSTEP * BS, LANES), F32)] * 4 + [
        pltpu.VMEM((NBQ, NACT, aos), BF),
        pltpu.VMEM((aos, NBQ * BS), BF),
        pltpu.VMEM((NBQ, 8, LANES), F32),
    ]
    weights = (
        shape((NCOL, aos), BF),
        shape((aos, 2 * LANES), BF),
        shape((nslab // 4, 2 * PAIRED, 2 * PAIRED), BF),
        shape((nslab // 2, BS, PAIRED), F32),
    )
    cost = pl.CostEstimate(flops=6 * 10**9, bytes_accessed=10**7, transcendentals=0)
    keep, dens = shape((2 * PER, LANES), F32), shape((NBQ, LANES), F32)
    lt, r, bd, d, msg1, keep1, dens1, slabs2 = pl.pallas_call(
        first_kernel,
        name="slabs_first",
        in_specs=[SM, HB, HB, SM, HB, HB],
        out_specs=[VM] * 8,
        out_shape=weights + (
            shape((INROWS + 2 * PER + NBQ, LANES), BF), keep, dens, loaded,
        ),
        scratch_shapes=[
            pltpu.SMEM((nslab,), jnp.int32), pltpu.SMEM((nslab,), jnp.int32),
            pltpu.VMEM(orbitals.T.shape, BF), pltpu.SemaphoreType.DMA((8,)),
            pltpu.VMEM(loaded.shape, BF), copies, copies,
        ] + scratch,
        compiler_params=PARAMS,
        cost_estimate=cost,
    )(
        where, in_hbm(block_row), in_hbm(block_col), live_count, slabs,
        in_hbm(orbitals.T),
    )
    near1 = lax.ppermute(msg1, "pair", swap_core)
    keep_in2, send2, keep2, dens2, slabs3 = pl.pallas_call(
        second_kernel,
        name="slabs_second",
        in_specs=[SM, HB] + [VM] * 5,
        out_specs=[VM] * 5,
        out_shape=(
            shape((INROWS, LANES), F32), shape((2 * PER, LANES), BF), keep, dens, loaded,
        ),
        scratch_shapes=[copies] + scratch,
        compiler_params=PARAMS,
        cost_estimate=cost,
    )(where, slabs, slabs2, lt, r, bd, d)
    out2 = jnp.concatenate([keep_in2, keep2[:PER]], axis=0)
    out2 = (out2 + near1[: INROWS + PER].astype(F32)).astype(BF)
    out2, lt = lax.optimization_barrier((out2, lt))
    cut = INROWS // 2 + NACT
    far1a = lax.ppermute(out2[:cut], "pair", swap_x)
    msg3, keep3, dens3, slabs4 = pl.pallas_call(
        third_kernel,
        name="slabs_third",
        in_specs=[SM, HB] + [VM] * 7,
        out_specs=[VM] * 4,
        out_shape=(shape((INROWS + 4 * PER + 2 * NBQ, LANES), BF), keep, dens, loaded),
        scratch_shapes=[copies] + scratch,
        compiler_params=PARAMS,
        cost_estimate=cost,
    )(where, slabs, slabs3, lt, r, bd, d, send2, dens2)
    near3 = lax.ppermute(msg3, "pair", swap_core)
    rest, msg3 = lax.optimization_barrier((out2[cut:], msg3))
    far1b = lax.ppermute(rest, "pair", swap_x)
    far1a, lt = lax.optimization_barrier((far1a, lt))
    msg4, keep_in4, keep4, dens4 = pl.pallas_call(
        fourth_kernel,
        name="slabs_fourth",
        in_specs=[SM] + [VM] * 5,
        out_specs=[VM] * 4,
        out_shape=(
            shape((2 * PER + NBQ, LANES), BF), shape((INROWS, LANES), F32), keep, dens,
        ),
        scratch_shapes=scratch,
        compiler_params=PARAMS,
        cost_estimate=cost,
    )(where, slabs4, lt, r, bd, d)
    msg4, exch = pl.pallas_call(
        exchange_kernel,
        name="exchange",
        in_specs=[SM] + [VM] * 5,
        out_specs=[VM] * 2,
        out_shape=(
            shape((2 * PER + NBQ + 2 * QUARTER, LANES), BF),
            shape((2 * QUARTER, LANES), F32),
        ),
        scratch_shapes=[pltpu.VMEM((NACT, LANES), F32)],
        compiler_params=PARAMS,
    )(where, keep_in4, near3, far1a, far1b, msg4)
    near4 = lax.ppermute(msg4, "pair", swap_core)
    msg5, act, dens, exch = pl.pallas_call(
        gather_kernel,
        name="active_of_chip",
        in_specs=[VM] * 13,
        out_specs=[VM] * 4,
        out_shape=(
            shape((3 * PER + 4 * NBQ + QUARTER, LANES), BF),
            shape((4 * PER, LANES), F32),
            shape((4 * NBQ, LANES), F32),
            shape((QUARTER, LANES), F32),
        ),
        compiler_params=PARAMS,
    )(keep1, keep2, keep3, keep4, dens1, dens2, dens3, dens4, exch, near1, near3, near4, far1b)
    far5 = lax.ppermute(msg5, "pair", swap_x)
    partial = pl.pallas_call(
        coulomb_kernel,
        name="coulomb",
        in_specs=[VM] * 4,
        out_specs=VM,
        out_shape=shape((QUARTER, NACT), F32),
        compiler_params=PARAMS,
    )(act, far5, dens, exch)
    active = pl.pallas_call(
        active_kernel,
        name="own_active",
        in_specs=[SM, VM, VM],
        out_specs=VM,
        out_shape=shape((batch, QUARTER, NACT), F32),
        compiler_params=PARAMS,
        cost_estimate=pl.CostEstimate(flops=10**6, bytes_accessed=10**6, transcendentals=0),
    )(where, act, far5)
    return (active, hcore + sum_over_aux(partial))


def slab_terms(values, left, right):
    half = jnp.einsum("mc,qmn->qnc", left, values, preferred_element_type=F32).astype(BF)
    first = jnp.einsum("qnt,nc->qtc", half[:, :, :NACT], right, preferred_element_type=F32)
    second = jnp.einsum("qnc,nt->qtc", half, right[:, :NACT], preferred_element_type=F32)
    trace = 2.0 * jnp.einsum(
        "qni,ni->q", half[:, :, NACT:], right[:, NACT:], preferred_element_type=F32
    )
    return (first + second, trace)


def general_body(slabs, block_row, block_col, live_count, orbitals, hcore):
    batch = slabs.shape[1]
    init = (jnp.zeros((batch, NACT, NCOL), F32), jnp.zeros((batch,), F32))

    def visit(k, state):
        values = lax.dynamic_index_in_dim(slabs, k, 0, keepdims=False)
        left = lax.dynamic_slice_in_dim(orbitals, block_row[k] * BS, BS, 0)
        right = lax.dynamic_slice_in_dim(orbitals, block_col[k] * BS, BS, 0)
        terms, trace = slab_terms(values.reshape(batch, BS, BS), left, right)
        return (state[0] + terms, state[1] + trace)

    vectors, density = lax.fori_loop(0, live_count[0], visit, init)
    density = lax.psum(density, "pair")
    owned = lax.psum_scatter(vectors, "pair", scatter_dimension=1, tiled=True)
    own_active, own_inactive = owned[:, :, :NACT], owned[:, :, NACT:]
    gathered = lax.all_gather(own_inactive.astype(BF), "pair", axis=1, tiled=True)
    exchange = jnp.einsum(
        "qti,qui->tu", own_inactive, gathered.astype(F32), precision=lax.Precision.HIGHEST
    )
    coulomb = jnp.einsum("qtu,q->tu", own_active, density, precision=lax.Precision.HIGHEST)
    return (own_active, hcore + lax.psum(2.0 * coulomb - exchange, "aux"))


def solution(mesh):
    placed = (
        P(("frag", "pair"), "aux", None),
        P(("frag", "pair")),
        P(("frag", "pair")),
        P(("frag", "pair")),
        P("frag", None),
        P(("frag", "pair"), None),
    )

    def body(slabs, *rest):
        fits = mesh.shape["pair"] == 4 and slabs.shape[1] == 4 * NBQ and slabs.shape[0] % 4 == 0
        return (paired_body if fits else general_body)(slabs, *rest)

    return jax.shard_map(
        body,
        mesh=mesh,
        in_specs=placed,
        out_specs=(P(("frag", "aux"), "pair", None), P(("frag", "pair"), None)),
        check_vma=False,
    )
```

```python
import jax
import jax.numpy as jnp
from jax import lax
from jax.experimental import pallas as pl
from jax.experimental.pallas import tpu as pltpu
from jax.sharding import PartitionSpec as P

BS = 64
NACT = 64
NCOL = 192
NIN = NCOL - NACT
LANES = 128
NBQ = 16
PAIRED = 2 * BS
QSTEP, MSTEP = 3, 49
BF = jnp.bfloat16
F32 = jnp.float32


def low_half(rows):
    return lax.broadcasted_iota(jnp.int32, (rows, LANES), 1) < BS


def orbital_pair(k, blocks, live, orbitals):
    halves = []
    for n in range(2):
        slot = 2 * k + n
        base = pl.multiple_of((blocks[slot] // 2) * PAIRED, PAIRED)
        w = orbitals[:, pl.ds(base, PAIRED)]
        w = jnp.concatenate([w[NACT:], w[:NACT]], axis=0)
        w = jnp.where(lax.rem(blocks[slot], 2) != n, pltpu.roll(w, BS, 1), w)
        halves.append(jnp.where(slot < live, w, jnp.zeros_like(w)))
    return jnp.where(low_half(NCOL), halves[0], halves[1])


def slab_copies(slabs_ref, sbuf, sem, block):
    return [
        pltpu.make_async_copy(
            slabs_ref.at[pl.ds(2 * k, 2), pl.ds(pl.multiple_of(block * NBQ, NBQ), NBQ), :],
            sbuf.at[k],
            sem.at[k],
        )
        for k in range(slabs_ref.shape[0] // 2)
    ]


def run_block(sbuf, weights, scratch, emit, ready=None, midway=None):
    lt_ref, r_ref, bd_ref, d_ref = weights
    pt_ref, q_ref, diag = scratch[4:]
    quads = sbuf.shape[0] // 2
    first = low_half(NBQ)
    first_s = low_half(BS)
    zero = jnp.zeros((BS, LANES), BF)
    group = 8

    def relayout(k, out):
        for j in range(sbuf.shape[3] // LANES):
            lanes = slice(j * LANES, (j + 1) * LANES)
            a = sbuf[k, 0, :, lanes]
            b = sbuf[k, 1, :, lanes]
            out[pl.ds(MSTEP * 2 * j, NBQ, stride=QSTEP), :] = jnp.where(
                first, a, pltpu.roll(b, BS, 1)
            ).astype(F32)
            out[pl.ds(MSTEP * (2 * j + 1), NBQ, stride=QSTEP), :] = jnp.where(
                first, pltpu.roll(a, BS, 1), b
            ).astype(F32)

    def transform(g, bufs):
        dens = [d_ref[2 * g + n] for n in range(2)]
        for q in range(0, NBQ, group):
            slabs = [[], []]
            for u in range(q, q + group):
                total = None
                for n in range(2):
                    s = bufs[n][pl.ds(u * QSTEP, BS, stride=MSTEP), :]
                    part = jnp.sum((s * dens[n]).reshape(BS // 8, 8, LANES), axis=0)
                    total = part if total is None else total + part
                    slabs[n].append(s.astype(BF))
                diag[u] = total if g == 0 else diag[u] + total
            for n in range(2):
                k = 2 * g + n
                cols = [
                    jnp.concatenate(
                        [jnp.where(first_s, s, zero), jnp.where(first_s, zero, s)], axis=0
                    )
                    for s in slabs[n]
                ]
                p = jnp.dot(
                    lt_ref[NIN:, k * LANES : (k + 1) * LANES],
                    jnp.concatenate(cols, axis=1),
                    preferred_element_type=F32,
                ).astype(BF)
                for u in range(group):
                    pt_ref[q + u, :, k * LANES : (k + 1) * LANES] = p[
                        :, u * LANES : (u + 1) * LANES
                    ]
            rows = jnp.concatenate(
                [jnp.concatenate([s0, s1], axis=1) for s0, s1 in zip(*slabs)], axis=0
            )
            out = jnp.dot(rows, bd_ref[g], preferred_element_type=F32).astype(BF)
            for u in range(0, group, 2):
                for n in range(2):
                    lanes = slice(n * LANES, (n + 1) * LANES)
                    q0 = out[u * BS : (u + 1) * BS, lanes]
                    q1 = out[(u + 1) * BS : (u + 2) * BS, lanes]
                    at = slice((q + u) * BS, (q + u + 2) * BS)
                    row = (4 * g + 2 * n) * BS
                    q_ref[row : row + BS, at] = jnp.where(first_s, q0, pltpu.roll(q1, BS, 1))
                    q_ref[row + BS : row + 2 * BS, at] = jnp.where(
                        first_s, pltpu.roll(q0, BS, 1), q1
                    )

    def second_transform(g):
        rows = pt_ref[4 * g : 4 * g + 4].reshape(4 * NACT, pt_ref.shape[2])
        one = jnp.dot(rows, r_ref[...], preferred_element_type=F32)
        two = jnp.dot(
            lt_ref[...], q_ref[:, 4 * g * BS : (4 * g + 4) * BS], preferred_element_type=F32
        )
        return one, two

    def assemble(g, both):
        one, two = both
        for p in range(2):
            w0 = one[2 * p * NACT : (2 * p + 1) * NACT]
            w1 = one[(2 * p + 1) * NACT : (2 * p + 2) * NACT]
            turned = two[:, p * LANES : (p + 1) * LANES]
            across = turned[:NIN].T
            square = jnp.concatenate([turned[NIN:], turned[NIN:]], axis=0).T
            emit(
                2 * g + p,
                w0[:, :NIN] + across[:NACT],
                w1[:, :NIN] + across[NACT:],
                jnp.where(first_s, w0[:, NIN:] + square[:NACT], w1[:, NIN:] + square[NACT:]),
            )

    def load(g):
        for n in range(2):
            if ready is not None:
                ready(2 * g + n)
            relayout(2 * g + n, scratch[2 * (g % 2) + n])

    load(0)
    for g in range(quads):
        if g + 1 < quads:
            load(g + 1)
        transform(g, scratch[2 * (g % 2) : 2 * (g % 2) + 2])
    if midway is not None:
        midway()
    whole = second_transform(0)
    for g in range(NBQ // 4):
        following = second_transform(g + 1) if g + 1 < NBQ // 4 else None
        assemble(g, whole)
        whole = following


def split_wire(d):
    hi = d.astype(BF).astype(F32)
    return jnp.where(low_half(d.shape[0]), hi, d - hi).astype(BF)


def joined(wire):
    w = wire.astype(F32)
    return w + pltpu.roll(w, BS, 1)


def density_of(diag):
    d = 2.0 * jnp.sum(jnp.sum(diag, axis=1), axis=1, keepdims=True)
    return jnp.broadcast_to(d, (NBQ, LANES))


QUARTER = NACT // 4
PER = NBQ // 2 * QUARTER
INROWS = NBQ * NACT


def emit_active(h, act, core, x, keep, sends):
    upper, lower = act[: 2 * QUARTER], act[2 * QUARTER :]
    near, far = jnp.where(x == 0, upper, lower), jnp.where(x == 0, lower, upper)
    at = pl.ds(h * QUARTER, QUARTER)
    for part, own, other in ((near, keep, sends.at[0]), (far, sends.at[1], sends.at[2])):
        one, two = part[:QUARTER], part[QUARTER:]
        own[at, :] = jnp.where(core == 0, one, two).astype(own.dtype)
        other[at, :] = jnp.where(core == 0, two, one).astype(BF)


def pair_rows(h, n):
    return pl.ds((2 * h + n) * NACT, NACT)


def first_kernel(
    where, rows_ref, cols_ref, live, slabs_ref, ot_ref,
    lt_out, r_out, bd_out, d_out, msg, keep, sends, dens, after,
    rows, cols, orbitals, ssem, sbuf, bsem, sem, *scratch
):
    pairs = slabs_ref.shape[0] // 2
    core, x = where[0], where[1]
    part = NACT // 2
    small = [
        pltpu.make_async_copy(src, dst, ssem.at[n])
        for n, (src, dst) in enumerate(((rows_ref, rows), (cols_ref, cols)))
    ] + [
        pltpu.make_async_copy(
            ot_ref.at[pl.ds(n * part, part)], orbitals.at[pl.ds(n * part, part)], ssem.at[2 + n]
        )
        for n in range(NCOL // part)
    ]
    now = slab_copies(slabs_ref, sbuf, bsem, 2 * (1 - x) + (1 - core))
    for copy in now[:2] + small + now[2:]:
        copy.start()
    ahead = slab_copies(slabs_ref, after, sem, 2 * (1 - x) + core)
    bd_out[...] = jnp.zeros_like(bd_out)

    def prepare(k):
        left = orbital_pair(k, rows, live[0], orbitals)
        right = orbital_pair(k, cols, live[0], orbitals)
        at = slice(k * PAIRED, (k + 1) * PAIRED)
        lt_out[:, at] = left
        turned = jnp.concatenate([right, right[NIN:]], axis=0).astype(F32).T.astype(BF)
        r_out[at, :] = turned
        inner = (lax.broadcasted_iota(jnp.int32, (PAIRED, LANES), 0) < BS) == low_half(PAIRED)
        place = slice((k % 2) * PAIRED, (k % 2 + 1) * PAIRED)
        bd_out[k // 2, place, place] = jnp.where(
            inner, turned[:, NIN:], jnp.zeros((PAIRED, LANES), BF)
        )
        both = jnp.dot(
            left[:NIN].astype(F32).T.astype(BF), right[:NIN], preferred_element_type=F32
        )
        d_out[k] = jnp.where(low_half(BS), both[:BS], both[BS:])

    def ready(k):
        if k < 2:
            now[k].wait()
        if k == 1:
            for copy in small + now[2:]:
                copy.wait()
        if k % 2 == 1:
            prepare(k - 1)
            prepare(k)

    def midway():
        for copy in ahead:
            copy.start()

    def emit(h, in0, in1, act):
        msg[pair_rows(h, 0), :] = in0.astype(BF)
        msg[pair_rows(h, 1), :] = in1.astype(BF)
        emit_active(h, act, core, x, keep, sends)

    run_block(sbuf, (lt_out, r_out, bd_out, d_out), scratch, emit, ready, midway)
    dens[...] = density_of(scratch[6][...])
    for copy in ahead:
        copy.wait()


def second_kernel(
    where, slabs_ref, sbuf, lt_ref, r_ref, bd_ref, d_ref, keep_in, keep, sends, dens, after,
    sem, *scratch
):
    core, x = where[0], where[1]
    ahead = slab_copies(slabs_ref, after, sem, 2 * x + (1 - core))

    def midway():
        for copy in ahead:
            copy.start()

    def emit(h, in0, in1, act):
        keep_in[pair_rows(h, 0), :] = in0
        keep_in[pair_rows(h, 1), :] = in1
        emit_active(h, act, core, x, keep, sends)

    run_block(sbuf, (lt_ref, r_ref, bd_ref, d_ref), scratch, emit, None, midway)
    dens[...] = density_of(scratch[6][...])
    for copy in ahead:
        copy.wait()


def third_kernel(
    where, slabs_ref, sbuf, lt_ref, r_ref, bd_ref, d_ref, sends1, sends2, dens1, dens2,
    near, far, cross, keep, dens, after, sem, sends, *scratch
):
    core, x = where[0], where[1]
    ahead = slab_copies(slabs_ref, after, sem, 2 * x + core)

    def midway():
        for copy in ahead:
            copy.start()

    def emit(h, in0, in1, act):
        near[pair_rows(h, 0), :] = in0.astype(BF)
        near[pair_rows(h, 1), :] = in1.astype(BF)
        emit_active(h, act, core, x, keep, sends)

    run_block(sbuf, (lt_ref, r_ref, bd_ref, d_ref), scratch, emit, None, midway)
    dens[...] = density_of(scratch[6][...])
    wires = [split_wire(d[...]) for d in (dens1, dens2, dens)]
    for k, (msg, base) in enumerate(((near, INROWS), (far, 0), (cross, 0))):
        for n, source in enumerate((sends1, sends2, sends)):
            msg[pl.ds(base + n * PER, PER), :] = source[k]
            msg[pl.ds(base + 3 * PER + n * NBQ, NBQ), :] = wires[n]
    for copy in ahead:
        copy.wait()


def fourth_kernel(
    where, sbuf, lt_ref, r_ref, bd_ref, d_ref, keep_in, keep, sends, dens, *scratch
):
    core, x = where[0], where[1]

    def emit(h, in0, in1, act):
        keep_in[pair_rows(h, 0), :] = in0
        keep_in[pair_rows(h, 1), :] = in1
        emit_active(h, act, core, x, keep, sends)

    run_block(sbuf, (lt_ref, r_ref, bd_ref, d_ref), scratch, emit)
    dens[...] = density_of(scratch[6][...])


def exchange_kernel(
    where, mine, near3, far1a, far1b, sends, dens, near, far, cross, keep, whole
):
    parts = []
    for q in range(NBQ):
        rows = pl.ds(q * NACT, NACT)
        at = q * NACT - far1a.shape[0]
        other = far1a[rows, :] if at < 0 else far1b[pl.ds(at, NACT), :]
        parts.append(mine[rows, :] + near3[rows, :].astype(F32) + other.astype(F32))
    v = jnp.concatenate(parts, axis=1)
    v = v.astype(BF)
    total = lax.dot_general(v, v, (((1,), (1,)), ((), ())), preferred_element_type=F32)
    whole[...] = jnp.concatenate([total, total], axis=1)
    index = 2 * where[1] + where[0]
    keep[...] = whole[pl.ds(pl.multiple_of(index * QUARTER, QUARTER), QUARTER), :]
    wire = split_wire(dens[...])
    for k, msg in enumerate((near, far, cross)):
        msg[pl.ds(0, PER), :] = sends[k]
        msg[pl.ds(PER, NBQ), :] = wire
        at = pl.multiple_of((index ^ (k + 1)) * QUARTER, QUARTER)
        msg[pl.ds(PER + NBQ, QUARTER), :] = split_wire(whole[pl.ds(at, QUARTER), :])


def coulomb_kernel(
    keep1, keep2, keep3, keep4, dens1, dens2, dens3, dens4, exch,
    near3, far3, cross3, near4, far4, cross4, act, partial,
):
    first = low_half(QUARTER)
    early, late = (near3, far3, cross3), (near4, far4, cross4)
    total = jnp.zeros((QUARTER, LANES), F32)
    for m, (keep, dens) in enumerate(
        ((keep1, dens1), (keep2, dens2), (keep3, dens3), (keep4, dens4))
    ):
        rows, d = keep[...], dens[...]
        for k in (1, 2, 3):
            n = m ^ k
            msg = late[k - 1] if n == 3 else early[k - 1]
            base = INROWS if n < 3 and k == 1 else 0
            at, dens_at = (0, PER) if n == 3 else (base + n * PER, base + 3 * PER + n * NBQ)
            rows = rows + msg[pl.ds(at, PER), :].astype(F32)
            d = d + joined(msg[pl.ds(dens_at, NBQ), :])
        act[pl.ds(m * PER, PER), :] = rows
        for h in range(NBQ // 2):
            total = total + rows[h * QUARTER : (h + 1) * QUARTER] * jnp.where(
                first, d[2 * h : 2 * h + 1], d[2 * h + 1 : 2 * h + 2]
            )
    total = 2.0 * (total + pltpu.roll(total, BS, 1)) - exch[...]
    for msg in late:
        total = total - joined(msg[pl.ds(PER + NBQ, QUARTER), :])
    partial[...] = total[:, :BS]


def active_kernel(where, act, out):
    core, x = where[0], where[1]
    for n in range(4):
        xx = (1 - x) if n < 2 else x
        cc = (1 - core) if n % 2 == 0 else core
        base = NBQ * (2 * xx + cc)
        for h in range(NBQ // 2):
            a = act[pl.ds(n * PER + h * QUARTER, QUARTER), :]
            out[base + 2 * h] = a[:, :BS]
            out[base + 2 * h + 1] = a[:, BS:]


VM = pl.BlockSpec(memory_space=pltpu.VMEM)
SM = pl.BlockSpec(memory_space=pltpu.SMEM)
HB = pl.BlockSpec(memory_space=pltpu.HBM)

PARAMS = pltpu.CompilerParams(vmem_limit_bytes=32 * 1024 * 1024)


def in_hbm(array):
    return pltpu.with_memory_space_constraint(array, pltpu.HBM)


def shape(dims, dtype):
    return jax.ShapeDtypeStruct(dims, dtype)


def sum_over_aux(part):
    n = lax.axis_size("aux")
    if n != 4:
        return lax.psum(part, "aux")
    for k in (1, 2):
        part = part + lax.ppermute(part, "aux", [(z, z ^ k) for z in range(n)])
    return part


def call(kernel, name, inputs, out_shape, scratch, args, work=0):
    return pl.pallas_call(
        kernel,
        name=name,
        in_specs=inputs,
        out_specs=[VM] * len(out_shape),
        out_shape=out_shape,
        scratch_shapes=scratch,
        compiler_params=PARAMS,
        cost_estimate=pl.CostEstimate(flops=work, bytes_accessed=10**5, transcendentals=0),
    )(*args)


def paired_body(slabs, block_row, block_col, live_count, orbitals, hcore):
    nslab, batch, width = slabs.shape
    index = lax.axis_index("pair")
    where = jnp.stack([lax.rem(index, 2), index // 2])
    aos = nslab * BS
    slabs = in_hbm(slabs)

    def to_peer(k, array):
        return lax.ppermute(array, "pair", [(p, p ^ k) for p in range(4)])

    loaded = shape((nslab // 2, 2, NBQ, width), BF)
    copies = pltpu.SemaphoreType.DMA((nslab // 2,))
    scratch = [pltpu.VMEM((MSTEP * BS, LANES), F32)] * 4 + [
        pltpu.VMEM((NBQ, NACT, aos), BF),
        pltpu.VMEM((aos, NBQ * BS), BF),
        pltpu.VMEM((NBQ, 8, LANES), F32),
    ]
    weights = (
        shape((NCOL, aos), BF),
        shape((aos, 2 * LANES), BF),
        shape((nslab // 4, 2 * PAIRED, 2 * PAIRED), BF),
        shape((nslab // 2, BS, PAIRED), F32),
    )
    kept = (
        shape((PER, LANES), F32), shape((3, PER, LANES), BF), shape((NBQ, LANES), F32),
    )
    work = 5 * 10**9
    lt, r, bd, d, msg1, keep1, sends1, dens1, slabs2 = call(
        first_kernel,
        "slabs_first",
        [SM, HB, HB, SM, HB, HB],
        weights + (shape((INROWS, LANES), BF),) + kept + (loaded,),
        [
            pltpu.SMEM((nslab,), jnp.int32), pltpu.SMEM((nslab,), jnp.int32),
            pltpu.VMEM(orbitals.T.shape, BF), pltpu.SemaphoreType.DMA((8,)),
            pltpu.VMEM(loaded.shape, BF), copies, copies,
        ] + scratch,
        (
            where, in_hbm(block_row), in_hbm(block_col), live_count, slabs,
            in_hbm(orbitals.T),
        ),
        work,
    )
    near1 = to_peer(1, msg1)
    keep_in2, keep2, sends2, dens2, slabs3 = call(
        second_kernel,
        "slabs_second",
        [SM, HB] + [VM] * 5,
        (shape((INROWS, LANES), F32),) + kept + (loaded,),
        [copies] + scratch,
        (where, slabs, slabs2, lt, r, bd, d),
        work,
    )
    out2 = (keep_in2 + near1.astype(F32)).astype(BF)
    out2, lt = lax.optimization_barrier((out2, lt))
    cut = INROWS // 4
    far1a = to_peer(2, out2[:cut])
    news = 3 * PER + 3 * NBQ
    msg3, msg3x, msg3c, keep3, dens3, slabs4 = call(
        third_kernel,
        "slabs_third",
        [SM, HB] + [VM] * 9,
        (
            shape((INROWS + news, LANES), BF), shape((news, LANES), BF),
            shape((news, LANES), BF), kept[0], kept[2], loaded,
        ),
        [copies, pltpu.VMEM((3, PER, LANES), BF)] + scratch,
        (where, slabs, slabs3, lt, r, bd, d, sends1, sends2, dens1, dens2),
        work,
    )
    near3 = to_peer(1, msg3)
    far1b = to_peer(2, out2[cut:])
    far3, cross3 = to_peer(2, msg3x), to_peer(3, msg3c)
    far1a, lt = lax.optimization_barrier((far1a, lt))
    keep_in4, keep4, sends4, dens4 = call(
        fourth_kernel,
        "slabs_fourth",
        [SM] + [VM] * 5,
        (shape((INROWS, LANES), F32),) + kept,
        scratch,
        (where, slabs4, lt, r, bd, d),
        work,
    )
    last = shape((PER + NBQ + QUARTER, LANES), BF)
    near4, far4, cross4, exch = call(
        exchange_kernel,
        "exchange",
        [SM] + [VM] * 6,
        (last,) * 3 + (shape((QUARTER, LANES), F32),),
        [pltpu.VMEM((NACT, LANES), F32)],
        (where, keep_in4, near3, far1a, far1b, sends4, dens4),
    )
    far4, cross4, near4 = to_peer(2, far4), to_peer(3, cross4), to_peer(1, near4)
    act, partial = call(
        coulomb_kernel,
        "coulomb",
        [VM] * 15,
        (shape((4 * PER, LANES), F32), shape((QUARTER, NACT), F32)),
        [],
        (
            keep1, keep2, keep3, keep4, dens1, dens2, dens3, dens4, exch,
            near3, far3, cross3, near4, far4, cross4,
        ),
    )
    (active,) = call(
        active_kernel,
        "own_active",
        [SM, VM],
        (shape((batch, QUARTER, NACT), F32),),
        [],
        (where, act),
        10**6,
    )
    return (active, hcore + sum_over_aux(partial))


def slab_terms(values, left, right):
    half = jnp.einsum("mc,qmn->qnc", left, values, preferred_element_type=F32).astype(BF)
    first = jnp.einsum("qnt,nc->qtc", half[:, :, :NACT], right, preferred_element_type=F32)
    second = jnp.einsum("qnc,nt->qtc", half, right[:, :NACT], preferred_element_type=F32)
    trace = 2.0 * jnp.einsum(
        "qni,ni->q", half[:, :, NACT:], right[:, NACT:], preferred_element_type=F32
    )
    return (first + second, trace)


def general_body(slabs, block_row, block_col, live_count, orbitals, hcore):
    batch = slabs.shape[1]
    init = (jnp.zeros((batch, NACT, NCOL), F32), jnp.zeros((batch,), F32))

    def visit(k, state):
        values = lax.dynamic_index_in_dim(slabs, k, 0, keepdims=False)
        left = lax.dynamic_slice_in_dim(orbitals, block_row[k] * BS, BS, 0)
        right = lax.dynamic_slice_in_dim(orbitals, block_col[k] * BS, BS, 0)
        terms, trace = slab_terms(values.reshape(batch, BS, BS), left, right)
        return (state[0] + terms, state[1] + trace)

    vectors, density = lax.fori_loop(0, live_count[0], visit, init)
    density = lax.psum(density, "pair")
    owned = lax.psum_scatter(vectors, "pair", scatter_dimension=1, tiled=True)
    own_active, own_inactive = owned[:, :, :NACT], owned[:, :, NACT:]
    gathered = lax.all_gather(own_inactive.astype(BF), "pair", axis=1, tiled=True)
    exchange = jnp.einsum(
        "qti,qui->tu", own_inactive, gathered.astype(F32), precision=lax.Precision.HIGHEST
    )
    coulomb = jnp.einsum("qtu,q->tu", own_active, density, precision=lax.Precision.HIGHEST)
    return (own_active, hcore + lax.psum(2.0 * coulomb - exchange, "aux"))


def solution(mesh):
    placed = (
        P(("frag", "pair"), "aux", None),
        P(("frag", "pair")),
        P(("frag", "pair")),
        P(("frag", "pair")),
        P("frag", None),
        P(("frag", "pair"), None),
    )

    def body(slabs, *rest):
        fits = mesh.shape["pair"] == 4 and slabs.shape[1] == 4 * NBQ and slabs.shape[0] % 4 == 0
        return (paired_body if fits else general_body)(slabs, *rest)

    return jax.shard_map(
        body,
        mesh=mesh,
        in_specs=placed,
        out_specs=(P(("frag", "aux"), "pair", None), P(("frag", "pair"), None)),
        check_vma=False,
    )
```

```python
import jax
import jax.numpy as jnp
from jax import lax
from jax.experimental import pallas as pl
from jax.experimental.pallas import tpu as pltpu
from jax.sharding import PartitionSpec as P

BS = 64
NACT = 64
NCOL = 192
NIN = NCOL - NACT
LANES = 128
NBQ = 16
PAIRED = 2 * BS
QSTEP, MSTEP = 3, 49
BF = jnp.bfloat16
F32 = jnp.float32


def low_half(rows):
    return lax.broadcasted_iota(jnp.int32, (rows, LANES), 1) < BS


def orbital_pair(k, blocks, live, orbitals):
    halves = []
    for n in range(2):
        slot = 2 * k + n
        base = pl.multiple_of((blocks[slot] // 2) * PAIRED, PAIRED)
        w = orbitals[:, pl.ds(base, PAIRED)]
        w = jnp.concatenate([w[NACT:], w[:NACT]], axis=0)
        w = jnp.where(lax.rem(blocks[slot], 2) != n, pltpu.roll(w, BS, 1), w)
        halves.append(jnp.where(slot < live, w, jnp.zeros_like(w)))
    return jnp.where(low_half(NCOL), halves[0], halves[1])


def slab_copies(slabs_ref, sbuf, sem, block):
    return [
        pltpu.make_async_copy(
            slabs_ref.at[pl.ds(2 * k, 2), pl.ds(pl.multiple_of(block * NBQ, NBQ), NBQ), :],
            sbuf.at[k],
            sem.at[k],
        )
        for k in range(slabs_ref.shape[0] // 2)
    ]


def run_block(sbuf, weights, scratch, emit, ready=None, ahead=()):
    lt_ref, r_ref, bd_ref, d_ref = weights
    pt_ref, q_ref, diag = scratch[4:]
    quads = sbuf.shape[0] // 2
    first = low_half(NBQ)
    first_s = low_half(BS)
    zero = jnp.zeros((BS, LANES), BF)
    group = 8

    def relayout(k, out):
        for j in range(sbuf.shape[3] // LANES):
            lanes = slice(j * LANES, (j + 1) * LANES)
            a = sbuf[k, 0, :, lanes]
            b = sbuf[k, 1, :, lanes]
            out[pl.ds(MSTEP * 2 * j, NBQ, stride=QSTEP), :] = jnp.where(
                first, a, pltpu.roll(b, BS, 1)
            ).astype(F32)
            out[pl.ds(MSTEP * (2 * j + 1), NBQ, stride=QSTEP), :] = jnp.where(
                first, pltpu.roll(a, BS, 1), b
            ).astype(F32)

    def transform(g, bufs):
        dens = [d_ref[2 * g + n] for n in range(2)]
        for q in range(0, NBQ, group):
            slabs = [[], []]
            for u in range(q, q + group):
                total = None
                for n in range(2):
                    s = bufs[n][pl.ds(u * QSTEP, BS, stride=MSTEP), :]
                    part = jnp.sum((s * dens[n]).reshape(BS // 8, 8, LANES), axis=0)
                    total = part if total is None else total + part
                    slabs[n].append(s.astype(BF))
                diag[u] = total if g == 0 else diag[u] + total
            for n in range(2):
                k = 2 * g + n
                cols = [
                    jnp.concatenate(
                        [jnp.where(first_s, s, zero), jnp.where(first_s, zero, s)], axis=0
                    )
                    for s in slabs[n]
                ]
                p = jnp.dot(
                    lt_ref[NIN:, k * LANES : (k + 1) * LANES],
                    jnp.concatenate(cols, axis=1),
                    preferred_element_type=F32,
                ).astype(BF)
                for u in range(group):
                    pt_ref[q + u, :, k * LANES : (k + 1) * LANES] = p[
                        :, u * LANES : (u + 1) * LANES
                    ]
            rows = jnp.concatenate(
                [jnp.concatenate([s0, s1], axis=1) for s0, s1 in zip(*slabs)], axis=0
            )
            out = jnp.dot(rows, bd_ref[g], preferred_element_type=F32).astype(BF)
            for u in range(0, group, 2):
                for n in range(2):
                    lanes = slice(n * LANES, (n + 1) * LANES)
                    q0 = out[u * BS : (u + 1) * BS, lanes]
                    q1 = out[(u + 1) * BS : (u + 2) * BS, lanes]
                    at = slice((q + u) * BS, (q + u + 2) * BS)
                    row = (4 * g + 2 * n) * BS
                    q_ref[row : row + BS, at] = jnp.where(first_s, q0, pltpu.roll(q1, BS, 1))
                    q_ref[row + BS : row + 2 * BS, at] = jnp.where(
                        first_s, pltpu.roll(q0, BS, 1), q1
                    )

    def second_transform(g):
        rows = pt_ref[4 * g : 4 * g + 4].reshape(4 * NACT, pt_ref.shape[2])
        one = jnp.dot(rows, r_ref[...], preferred_element_type=F32)
        two = jnp.dot(
            lt_ref[...], q_ref[:, 4 * g * BS : (4 * g + 4) * BS], preferred_element_type=F32
        )
        return one, two

    def assemble(g, both):
        one, two = both
        for p in range(2):
            w0 = one[2 * p * NACT : (2 * p + 1) * NACT]
            w1 = one[(2 * p + 1) * NACT : (2 * p + 2) * NACT]
            turned = two[:, p * LANES : (p + 1) * LANES]
            across = turned[:NIN].T
            square = jnp.concatenate([turned[NIN:], turned[NIN:]], axis=0).T
            emit(
                2 * g + p,
                w0[:, :NIN] + across[:NACT],
                w1[:, :NIN] + across[NACT:],
                jnp.where(first_s, w0[:, NIN:] + square[:NACT], w1[:, NIN:] + square[NACT:]),
            )

    def load(g):
        for n in range(2):
            if ready is not None:
                ready(2 * g + n)
            relayout(2 * g + n, scratch[2 * (g % 2) + n])

    load(0)
    for g in range(quads):
        if g + 1 < quads:
            load(g + 1)
        transform(g, scratch[2 * (g % 2) : 2 * (g % 2) + 2])
        for copy in ahead[2 * g : 2 * g + 2]:
            copy.start()
    whole = second_transform(0)
    for g in range(NBQ // 4):
        following = second_transform(g + 1) if g + 1 < NBQ // 4 else None
        assemble(g, whole)
        whole = following


def split_wire(d):
    hi = d.astype(BF).astype(F32)
    return jnp.where(low_half(d.shape[0]), hi, d - hi).astype(BF)


def joined(wire):
    w = wire.astype(F32)
    return w + pltpu.roll(w, BS, 1)


def density_of(diag):
    d = 2.0 * jnp.sum(jnp.sum(diag, axis=1), axis=1, keepdims=True)
    return jnp.broadcast_to(d, (NBQ, LANES))


QUARTER = NACT // 4
PER = NBQ // 2 * QUARTER
INROWS = NBQ * NACT


def emit_active(h, act, core, x, keep, sends):
    upper, lower = act[: 2 * QUARTER], act[2 * QUARTER :]
    near, far = jnp.where(x == 0, upper, lower), jnp.where(x == 0, lower, upper)
    at = pl.ds(h * QUARTER, QUARTER)
    for part, own, other in ((near, keep, sends.at[0]), (far, sends.at[1], sends.at[2])):
        one, two = part[:QUARTER], part[QUARTER:]
        own[at, :] = jnp.where(core == 0, one, two).astype(own.dtype)
        other[at, :] = jnp.where(core == 0, two, one).astype(BF)


def pair_rows(h, n):
    return pl.ds((2 * h + n) * NACT, NACT)


def first_kernel(
    where, rows_ref, cols_ref, live, slabs_ref, ot_ref,
    lt_out, r_out, bd_out, d_out, msg, keep, sends, dens, after,
    rows, cols, orbitals, ssem, sbuf, bsem, sem, *scratch
):
    pairs = slabs_ref.shape[0] // 2
    core, x = where[0], where[1]
    part = NACT // 2
    small = [
        pltpu.make_async_copy(src, dst, ssem.at[n])
        for n, (src, dst) in enumerate(((rows_ref, rows), (cols_ref, cols)))
    ] + [
        pltpu.make_async_copy(
            ot_ref.at[pl.ds(n * part, part)], orbitals.at[pl.ds(n * part, part)], ssem.at[2 + n]
        )
        for n in range(NCOL // part)
    ]
    now = slab_copies(slabs_ref, sbuf, bsem, 2 * (1 - x) + (1 - core))
    for copy in small[:2] + now[:2] + small[2:]:
        copy.start()
    ahead = slab_copies(slabs_ref, after, sem, 2 * (1 - x) + core)
    bd_out[...] = jnp.zeros_like(bd_out)

    def prepare(k):
        left = orbital_pair(k, rows, live[0], orbitals)
        right = orbital_pair(k, cols, live[0], orbitals)
        at = slice(k * PAIRED, (k + 1) * PAIRED)
        lt_out[:, at] = left
        turned = jnp.concatenate([right, right[NIN:]], axis=0).T
        r_out[at, :] = turned
        inner = (lax.broadcasted_iota(jnp.int32, (PAIRED, LANES), 0) < BS) == low_half(PAIRED)
        place = slice((k % 2) * PAIRED, (k % 2 + 1) * PAIRED)
        bd_out[k // 2, place, place] = jnp.where(
            inner, turned[:, NIN:], jnp.zeros((PAIRED, LANES), BF)
        )
        both = jnp.dot(
            left[:NIN].T, right[:NIN], preferred_element_type=F32
        )
        d_out[k] = jnp.where(low_half(BS), both[:BS], both[BS:])

    def ready(k):
        if k % 2 == 0:
            now[k].wait()
            now[k + 1].wait()
            for copy in now[k + 2 : k + 4]:
                copy.start()
        if k == 1:
            for copy in small:
                copy.wait()
        if k % 2 == 1:
            prepare(k - 1)
            prepare(k)

    def emit(h, in0, in1, act):
        msg[pair_rows(h, 0), :] = in0.astype(BF)
        msg[pair_rows(h, 1), :] = in1.astype(BF)
        emit_active(h, act, core, x, keep, sends)

    run_block(sbuf, (lt_out, r_out, bd_out, d_out), scratch, emit, ready, ahead)
    dens[...] = density_of(scratch[6][...])
    for copy in ahead:
        copy.wait()


def second_kernel(
    where, slabs_ref, sbuf, lt_ref, r_ref, bd_ref, d_ref, keep_in, keep, sends, dens, after,
    sem, *scratch
):
    core, x = where[0], where[1]
    ahead = slab_copies(slabs_ref, after, sem, 2 * x + (1 - core))

    def emit(h, in0, in1, act):
        keep_in[pair_rows(h, 0), :] = in0
        keep_in[pair_rows(h, 1), :] = in1
        emit_active(h, act, core, x, keep, sends)

    run_block(sbuf, (lt_ref, r_ref, bd_ref, d_ref), scratch, emit, None, ahead)
    dens[...] = density_of(scratch[6][...])
    for copy in ahead:
        copy.wait()


def third_kernel(
    where, slabs_ref, sbuf, lt_ref, r_ref, bd_ref, d_ref, sends1, sends2, dens1, dens2,
    near, far, cross, keep, dens, after, sem, sends, *scratch
):
    core, x = where[0], where[1]
    ahead = slab_copies(slabs_ref, after, sem, 2 * x + core)

    def emit(h, in0, in1, act):
        near[pair_rows(h, 0), :] = in0.astype(BF)
        near[pair_rows(h, 1), :] = in1.astype(BF)
        emit_active(h, act, core, x, keep, sends)

    run_block(sbuf, (lt_ref, r_ref, bd_ref, d_ref), scratch, emit, None, ahead)
    dens[...] = density_of(scratch[6][...])
    wires = [split_wire(d[...]) for d in (dens1, dens2, dens)]
    for k, (msg, base) in enumerate(((near, INROWS), (far, 0), (cross, 0))):
        for n, source in enumerate((sends1, sends2, sends)):
            msg[pl.ds(base + n * PER, PER), :] = source[k]
            msg[pl.ds(base + 3 * PER + n * NBQ, NBQ), :] = wires[n]
    for copy in ahead:
        copy.wait()


def fourth_kernel(
    where, sbuf, lt_ref, r_ref, bd_ref, d_ref, keep_in, keep, sends, dens, *scratch
):
    core, x = where[0], where[1]

    def emit(h, in0, in1, act):
        keep_in[pair_rows(h, 0), :] = in0
        keep_in[pair_rows(h, 1), :] = in1
        emit_active(h, act, core, x, keep, sends)

    run_block(sbuf, (lt_ref, r_ref, bd_ref, d_ref), scratch, emit)
    dens[...] = density_of(scratch[6][...])


def exchange_kernel(
    where, mine, near3, far1a, far1b, sends, dens, near, far, cross, keep, whole
):
    parts = []
    for q in range(NBQ):
        rows = pl.ds(q * NACT, NACT)
        at = q * NACT - far1a.shape[0]
        other = far1a[rows, :] if at < 0 else far1b[pl.ds(at, NACT), :]
        parts.append(mine[rows, :] + near3[rows, :].astype(F32) + other.astype(F32))
    v = jnp.concatenate(parts, axis=1)
    v = v.astype(BF)
    total = lax.dot_general(v, v, (((1,), (1,)), ((), ())), preferred_element_type=F32)
    whole[...] = jnp.concatenate([total, total], axis=1)
    index = 2 * where[1] + where[0]
    keep[...] = whole[pl.ds(pl.multiple_of(index * QUARTER, QUARTER), QUARTER), :]
    wire = split_wire(dens[...])
    for k, msg in enumerate((near, far, cross)):
        msg[pl.ds(0, PER), :] = sends[k]
        msg[pl.ds(PER, NBQ), :] = wire
        at = pl.multiple_of((index ^ (k + 1)) * QUARTER, QUARTER)
        msg[pl.ds(PER + NBQ, QUARTER), :] = split_wire(whole[pl.ds(at, QUARTER), :])


def coulomb_kernel(
    keep1, keep2, keep3, keep4, dens1, dens2, dens3, dens4, exch,
    near3, far3, cross3, near4, far4, cross4, act, partial,
):
    first = low_half(QUARTER)
    early, late = (near3, far3, cross3), (near4, far4, cross4)
    total = jnp.zeros((QUARTER, LANES), F32)
    for m, (keep, dens) in enumerate(
        ((keep1, dens1), (keep2, dens2), (keep3, dens3), (keep4, dens4))
    ):
        rows, d = keep[...], dens[...]
        for k in (1, 2, 3):
            n = m ^ k
            msg = late[k - 1] if n == 3 else early[k - 1]
            base = INROWS if n < 3 and k == 1 else 0
            at, dens_at = (0, PER) if n == 3 else (base + n * PER, base + 3 * PER + n * NBQ)
            rows = rows + msg[pl.ds(at, PER), :].astype(F32)
            d = d + joined(msg[pl.ds(dens_at, NBQ), :])
        act[pl.ds(m * PER, PER), :] = rows
        for h in range(NBQ // 2):
            total = total + rows[h * QUARTER : (h + 1) * QUARTER] * jnp.where(
                first, d[2 * h : 2 * h + 1], d[2 * h + 1 : 2 * h + 2]
            )
    total = 2.0 * (total + pltpu.roll(total, BS, 1)) - exch[...]
    for msg in late:
        total = total - joined(msg[pl.ds(PER + NBQ, QUARTER), :])
    partial[...] = total[:, :BS]


def active_kernel(where, act, out):
    core, x = where[0], where[1]
    for n in range(4):
        xx = (1 - x) if n < 2 else x
        cc = (1 - core) if n % 2 == 0 else core
        base = NBQ * (2 * xx + cc)
        for h in range(NBQ // 2):
            a = act[pl.ds(n * PER + h * QUARTER, QUARTER), :]
            out[base + 2 * h] = a[:, :BS]
            out[base + 2 * h + 1] = a[:, BS:]


VM = pl.BlockSpec(memory_space=pltpu.VMEM)
SM = pl.BlockSpec(memory_space=pltpu.SMEM)
HB = pl.BlockSpec(memory_space=pltpu.HBM)

PARAMS = pltpu.CompilerParams(vmem_limit_bytes=32 * 1024 * 1024)


def in_hbm(array):
    return pltpu.with_memory_space_constraint(array, pltpu.HBM)


def shape(dims, dtype):
    return jax.ShapeDtypeStruct(dims, dtype)


def sum_over_aux(part):
    n = lax.axis_size("aux")
    if n != 4:
        return lax.psum(part, "aux")
    for k in (1, 2):
        part = part + lax.ppermute(part, "aux", [(z, z ^ k) for z in range(n)])
    return part


def call(kernel, name, inputs, out_shape, scratch, args, work=0):
    return pl.pallas_call(
        kernel,
        name=name,
        in_specs=inputs,
        out_specs=[VM] * len(out_shape),
        out_shape=out_shape,
        scratch_shapes=scratch,
        compiler_params=PARAMS,
        cost_estimate=pl.CostEstimate(flops=work, bytes_accessed=10**5, transcendentals=0),
    )(*args)


def paired_body(slabs, block_row, block_col, live_count, orbitals, hcore):
    nslab, batch, width = slabs.shape
    index = lax.axis_index("pair")
    where = jnp.stack([lax.rem(index, 2), index // 2])
    aos = nslab * BS
    slabs = in_hbm(slabs)

    def to_peer(k, array):
        return lax.ppermute(array, "pair", [(p, p ^ k) for p in range(4)])

    loaded = shape((nslab // 2, 2, NBQ, width), BF)
    copies = pltpu.SemaphoreType.DMA((nslab // 2,))
    scratch = [pltpu.VMEM((MSTEP * BS, LANES), F32)] * 4 + [
        pltpu.VMEM((NBQ, NACT, aos), BF),
        pltpu.VMEM((aos, NBQ * BS), BF),
        pltpu.VMEM((NBQ, 8, LANES), F32),
    ]
    weights = (
        shape((NCOL, aos), BF),
        shape((aos, 2 * LANES), BF),
        shape((nslab // 4, 2 * PAIRED, 2 * PAIRED), BF),
        shape((nslab // 2, BS, PAIRED), F32),
    )
    kept = (
        shape((PER, LANES), F32), shape((3, PER, LANES), BF), shape((NBQ, LANES), F32),
    )
    work = 5 * 10**9
    lt, r, bd, d, msg1, keep1, sends1, dens1, slabs2 = call(
        first_kernel,
        "slabs_first",
        [SM, HB, HB, SM, HB, HB],
        weights + (shape((INROWS, LANES), BF),) + kept + (loaded,),
        [
            pltpu.SMEM((nslab,), jnp.int32), pltpu.SMEM((nslab,), jnp.int32),
            pltpu.VMEM(orbitals.T.shape, BF), pltpu.SemaphoreType.DMA((8,)),
            pltpu.VMEM(loaded.shape, BF), copies, copies,
        ] + scratch,
        (
            where, in_hbm(block_row), in_hbm(block_col), live_count, slabs,
            in_hbm(orbitals.T),
        ),
        work,
    )
    near1 = to_peer(1, msg1)
    keep_in2, keep2, sends2, dens2, slabs3 = call(
        second_kernel,
        "slabs_second",
        [SM, HB] + [VM] * 5,
        (shape((INROWS, LANES), F32),) + kept + (loaded,),
        [copies] + scratch,
        (where, slabs, slabs2, lt, r, bd, d),
        work,
    )
    out2 = (keep_in2 + near1.astype(F32)).astype(BF)
    out2, lt = lax.optimization_barrier((out2, lt))
    cut = INROWS // 4
    far1a = to_peer(2, out2[:cut])
    news = 3 * PER + 3 * NBQ
    msg3, msg3x, msg3c, keep3, dens3, slabs4 = call(
        third_kernel,
        "slabs_third",
        [SM, HB] + [VM] * 9,
        (
            shape((INROWS + news, LANES), BF), shape((news, LANES), BF),
            shape((news, LANES), BF), kept[0], kept[2], loaded,
        ),
        [copies, pltpu.VMEM((3, PER, LANES), BF)] + scratch,
        (where, slabs, slabs3, lt, r, bd, d, sends1, sends2, dens1, dens2),
        work,
    )
    near3 = to_peer(1, msg3)
    far1b = to_peer(2, out2[cut:])
    far3, cross3 = to_peer(2, msg3x), to_peer(3, msg3c)
    far1a, lt = lax.optimization_barrier((far1a, lt))
    keep_in4, keep4, sends4, dens4 = call(
        fourth_kernel,
        "slabs_fourth",
        [SM] + [VM] * 5,
        (shape((INROWS, LANES), F32),) + kept,
        scratch,
        (where, slabs4, lt, r, bd, d),
        work,
    )
    last = shape((PER + NBQ + QUARTER, LANES), BF)
    near4, far4, cross4, exch = call(
        exchange_kernel,
        "exchange",
        [SM] + [VM] * 6,
        (last,) * 3 + (shape((QUARTER, LANES), F32),),
        [pltpu.VMEM((NACT, LANES), F32)],
        (where, keep_in4, near3, far1a, far1b, sends4, dens4),
    )
    far4, cross4, near4 = to_peer(2, far4), to_peer(3, cross4), to_peer(1, near4)
    act, partial = call(
        coulomb_kernel,
        "coulomb",
        [VM] * 15,
        (shape((4 * PER, LANES), F32), shape((QUARTER, NACT), F32)),
        [],
        (
            keep1, keep2, keep3, keep4, dens1, dens2, dens3, dens4, exch,
            near3, far3, cross3, near4, far4, cross4,
        ),
    )
    (active,) = call(
        active_kernel,
        "own_active",
        [SM, VM],
        (shape((batch, QUARTER, NACT), F32),),
        [],
        (where, act),
        10**6,
    )
    return (active, hcore + sum_over_aux(partial))


def slab_terms(values, left, right):
    half = jnp.einsum("mc,qmn->qnc", left, values, preferred_element_type=F32).astype(BF)
    first = jnp.einsum("qnt,nc->qtc", half[:, :, :NACT], right, preferred_element_type=F32)
    second = jnp.einsum("qnc,nt->qtc", half, right[:, :NACT], preferred_element_type=F32)
    trace = 2.0 * jnp.einsum(
        "qni,ni->q", half[:, :, NACT:], right[:, NACT:], preferred_element_type=F32
    )
    return (first + second, trace)


def general_body(slabs, block_row, block_col, live_count, orbitals, hcore):
    batch = slabs.shape[1]
    init = (jnp.zeros((batch, NACT, NCOL), F32), jnp.zeros((batch,), F32))

    def visit(k, state):
        values = lax.dynamic_index_in_dim(slabs, k, 0, keepdims=False)
        left = lax.dynamic_slice_in_dim(orbitals, block_row[k] * BS, BS, 0)
        right = lax.dynamic_slice_in_dim(orbitals, block_col[k] * BS, BS, 0)
        terms, trace = slab_terms(values.reshape(batch, BS, BS), left, right)
        return (state[0] + terms, state[1] + trace)

    vectors, density = lax.fori_loop(0, live_count[0], visit, init)
    density = lax.psum(density, "pair")
    owned = lax.psum_scatter(vectors, "pair", scatter_dimension=1, tiled=True)
    own_active, own_inactive = owned[:, :, :NACT], owned[:, :, NACT:]
    gathered = lax.all_gather(own_inactive.astype(BF), "pair", axis=1, tiled=True)
    exchange = jnp.einsum(
        "qti,qui->tu", own_inactive, gathered.astype(F32), precision=lax.Precision.HIGHEST
    )
    coulomb = jnp.einsum("qtu,q->tu", own_active, density, precision=lax.Precision.HIGHEST)
    return (own_active, hcore + lax.psum(2.0 * coulomb - exchange, "aux"))


def solution(mesh):
    placed = (
        P(("frag", "pair"), "aux", None),
        P(("frag", "pair")),
        P(("frag", "pair")),
        P(("frag", "pair")),
        P("frag", None),
        P(("frag", "pair"), None),
    )

    def body(slabs, *rest):
        fits = mesh.shape["pair"] == 4 and slabs.shape[1] == 4 * NBQ and slabs.shape[0] % 4 == 0
        return (paired_body if fits else general_body)(slabs, *rest)

    return jax.shard_map(
        body,
        mesh=mesh,
        in_specs=placed,
        out_specs=(P(("frag", "aux"), "pair", None), P(("frag", "pair"), None)),
        check_vma=False,
    )
```

```python
import jax
import jax.numpy as jnp
from jax import lax
from jax.experimental import pallas as pl
from jax.experimental.pallas import tpu as pltpu
from jax.sharding import PartitionSpec as P

BS = 64
NACT = 64
NCOL = 192
NIN = NCOL - NACT
LANES = 128
NBQ = 16
PAIRED = 2 * BS
QSTEP, MSTEP = 3, 49
BF = jnp.bfloat16
F32 = jnp.float32


def low_half(rows):
    return lax.broadcasted_iota(jnp.int32, (rows, LANES), 1) < BS


def orbital_pair(k, blocks, live, orbitals):
    halves = []
    for n in range(2):
        slot = 2 * k + n
        base = pl.multiple_of((blocks[slot] // 2) * PAIRED, PAIRED)
        w = orbitals[:, pl.ds(base, PAIRED)]
        w = jnp.concatenate([w[NACT:], w[:NACT]], axis=0)
        w = jnp.where(lax.rem(blocks[slot], 2) != n, pltpu.roll(w, BS, 1), w)
        halves.append(jnp.where(slot < live, w, jnp.zeros_like(w)))
    return jnp.where(low_half(NCOL), halves[0], halves[1])


def slab_copies(slabs_ref, sbuf, sem, block):
    return [
        pltpu.make_async_copy(
            slabs_ref.at[pl.ds(2 * k, 2), pl.ds(pl.multiple_of(block * NBQ, NBQ), NBQ), :],
            sbuf.at[k],
            sem.at[k],
        )
        for k in range(slabs_ref.shape[0] // 2)
    ]


def run_block(sbuf, weights, scratch, emit, prepare=None):
    lt_ref, r_ref, bd_ref, d_ref = weights
    pt_ref, q_ref, diag = scratch[4:]
    quads = sbuf.shape[0] // 2
    first = low_half(NBQ)
    first_s = low_half(BS)
    zero = jnp.zeros((BS, LANES), BF)
    group = 8

    def relayout(k, out):
        for j in range(sbuf.shape[3] // LANES):
            lanes = slice(j * LANES, (j + 1) * LANES)
            a = sbuf[k, 0, :, lanes]
            b = sbuf[k, 1, :, lanes]
            out[pl.ds(MSTEP * 2 * j, NBQ, stride=QSTEP), :] = jnp.where(
                first, a, pltpu.roll(b, BS, 1)
            ).astype(F32)
            out[pl.ds(MSTEP * (2 * j + 1), NBQ, stride=QSTEP), :] = jnp.where(
                first, pltpu.roll(a, BS, 1), b
            ).astype(F32)

    def transform(g, bufs):
        dens = [d_ref[2 * g + n] for n in range(2)]
        left = [
            lt_ref[NIN:, pl.ds(pl.multiple_of((2 * g + n) * LANES, LANES), LANES)]
            for n in range(2)
        ]
        for q in range(0, NBQ, group):
            slabs = [[], []]
            for u in range(q, q + group):
                total = diag[u]
                for n in range(2):
                    s = bufs[n][pl.ds(u * QSTEP, BS, stride=MSTEP), :]
                    total = total + jnp.sum((s * dens[n]).reshape(BS // 8, 8, LANES), axis=0)
                    slabs[n].append(s.astype(BF))
                diag[u] = total
            for n in range(2):
                at = pl.ds(pl.multiple_of((2 * g + n) * LANES, LANES), LANES)
                cols = [
                    jnp.concatenate(
                        [jnp.where(first_s, s, zero), jnp.where(first_s, zero, s)], axis=0
                    )
                    for s in slabs[n]
                ]
                p = jnp.dot(
                    left[n], jnp.concatenate(cols, axis=1), preferred_element_type=F32
                ).astype(BF)
                for u in range(group):
                    pt_ref[q + u, :, at] = p[:, u * LANES : (u + 1) * LANES]
            rows = jnp.concatenate(
                [jnp.concatenate([s0, s1], axis=1) for s0, s1 in zip(*slabs)], axis=0
            )
            out = jnp.dot(rows, bd_ref[g], preferred_element_type=F32).astype(BF)
            for u in range(0, group, 2):
                for n in range(2):
                    lanes = slice(n * LANES, (n + 1) * LANES)
                    q0 = out[u * BS : (u + 1) * BS, lanes]
                    q1 = out[(u + 1) * BS : (u + 2) * BS, lanes]
                    at = slice((q + u) * BS, (q + u + 2) * BS)
                    row = pl.multiple_of((4 * g + 2 * n) * BS, 2 * BS)
                    q_ref[pl.ds(row, BS), at] = jnp.where(first_s, q0, pltpu.roll(q1, BS, 1))
                    q_ref[pl.ds(row + BS, BS), at] = jnp.where(
                        first_s, pltpu.roll(q0, BS, 1), q1
                    )

    def second_transform(g):
        rows = pt_ref[4 * g : 4 * g + 4].reshape(4 * NACT, pt_ref.shape[2])
        one = jnp.dot(rows, r_ref[...], preferred_element_type=F32)
        two = jnp.dot(
            lt_ref[...], q_ref[:, 4 * g * BS : (4 * g + 4) * BS], preferred_element_type=F32
        )
        return one, two

    def assemble(g, both):
        one, two = both
        for p in range(2):
            w0 = one[2 * p * NACT : (2 * p + 1) * NACT]
            w1 = one[(2 * p + 1) * NACT : (2 * p + 2) * NACT]
            turned = two[:, p * LANES : (p + 1) * LANES]
            across = turned[:NIN].T
            square = jnp.concatenate([turned[NIN:], turned[NIN:]], axis=0).T
            emit(
                2 * g + p,
                w0[:, :NIN] + across[:NACT],
                w1[:, :NIN] + across[NACT:],
                jnp.where(first_s, w0[:, NIN:] + square[:NACT], w1[:, NIN:] + square[NACT:]),
            )

    def load(g, bufs):
        for n in range(2):
            relayout(2 * g + n, bufs[n])

    def two_quads(i, carry):
        one, two = scratch[:2], scratch[2:4]
        after = jnp.minimum(2 * i + 2, quads - 1)
        if prepare is not None:
            prepare(2 * i + 1)
        load(2 * i + 1, two)
        transform(2 * i, one)
        if prepare is not None:
            prepare(after)
        load(after, one)
        transform(2 * i + 1, two)
        return carry

    diag[...] = jnp.zeros_like(diag)
    load(0, scratch[:2])
    if prepare is not None:
        prepare(0)
    lax.fori_loop(0, quads // 2, two_quads, 0)
    whole = second_transform(0)
    for g in range(NBQ // 4):
        following = second_transform(g + 1) if g + 1 < NBQ // 4 else None
        assemble(g, whole)
        whole = following


def split_wire(d):
    hi = d.astype(BF).astype(F32)
    return jnp.where(low_half(d.shape[0]), hi, d - hi).astype(BF)


def joined(wire):
    w = wire.astype(F32)
    return w + pltpu.roll(w, BS, 1)


def density_of(diag):
    d = 2.0 * jnp.sum(jnp.sum(diag, axis=1), axis=1, keepdims=True)
    return jnp.broadcast_to(d, (NBQ, LANES))


QUARTER = NACT // 4
PER = NBQ // 2 * QUARTER
INROWS = NBQ * NACT


def emit_active(h, act, core, x, keep, sends):
    upper, lower = act[: 2 * QUARTER], act[2 * QUARTER :]
    near, far = jnp.where(x == 0, upper, lower), jnp.where(x == 0, lower, upper)
    at = pl.ds(h * QUARTER, QUARTER)
    for part, own, other in ((near, keep, sends.at[0]), (far, sends.at[1], sends.at[2])):
        one, two = part[:QUARTER], part[QUARTER:]
        own[at, :] = jnp.where(core == 0, one, two).astype(own.dtype)
        other[at, :] = jnp.where(core == 0, two, one).astype(BF)


def pair_rows(h, n):
    return pl.ds((2 * h + n) * NACT, NACT)


def first_kernel(
    where, rows_ref, cols_ref, live, slabs_ref, ot_ref,
    lt_out, r_out, bd_out, d_out, msg, keep, sends, dens, after,
    rows, cols, orbitals, ssem, sbuf, bsem, sem, *scratch
):
    pairs = slabs_ref.shape[0] // 2
    core, x = where[0], where[1]
    part = NACT // 2
    small = [
        pltpu.make_async_copy(src, dst, ssem.at[n])
        for n, (src, dst) in enumerate(((rows_ref, rows), (cols_ref, cols)))
    ] + [
        pltpu.make_async_copy(
            ot_ref.at[pl.ds(n * part, part)], orbitals.at[pl.ds(n * part, part)], ssem.at[2 + n]
        )
        for n in range(NCOL // part)
    ]
    now = slab_copies(slabs_ref, sbuf, bsem, 2 * (1 - x) + (1 - core))
    for copy in now[:2] + small + now[2:]:
        copy.start()
    ahead = slab_copies(slabs_ref, after, sem, 2 * (1 - x) + core)
    bd_out[...] = jnp.zeros_like(bd_out)

    for copy in now + small:
        copy.wait()
    for copy in ahead:
        copy.start()

    def prepare(g):
        for n in range(2):
            k = 2 * g + n
            left = orbital_pair(k, rows, live[0], orbitals)
            right = orbital_pair(k, cols, live[0], orbitals)
            at = pl.ds(pl.multiple_of(k * PAIRED, PAIRED), PAIRED)
            lt_out[:, at] = left
            turned = jnp.concatenate([right, right[NIN:]], axis=0).astype(F32).T.astype(BF)
            r_out[at, :] = turned
            inner = (lax.broadcasted_iota(jnp.int32, (PAIRED, LANES), 0) < BS) == low_half(PAIRED)
            place = slice(n * PAIRED, (n + 1) * PAIRED)
            bd_out[g, place, place] = jnp.where(
                inner, turned[:, NIN:], jnp.zeros((PAIRED, LANES), BF)
            )
            both = jnp.dot(
                left[:NIN].astype(F32).T.astype(BF), right[:NIN], preferred_element_type=F32
            )
            d_out[k] = jnp.where(low_half(BS), both[:BS], both[BS:])

    def emit(h, in0, in1, act):
        msg[pair_rows(h, 0), :] = in0.astype(BF)
        msg[pair_rows(h, 1), :] = in1.astype(BF)
        emit_active(h, act, core, x, keep, sends)

    run_block(sbuf, (lt_out, r_out, bd_out, d_out), scratch, emit, prepare)
    dens[...] = density_of(scratch[6][...])
    for copy in ahead:
        copy.wait()


def second_kernel(
    where, slabs_ref, sbuf, lt_ref, r_ref, bd_ref, d_ref, keep_in, keep, sends, dens, after,
    sem, *scratch
):
    core, x = where[0], where[1]
    ahead = slab_copies(slabs_ref, after, sem, 2 * x + (1 - core))

    for copy in ahead:
        copy.start()

    def emit(h, in0, in1, act):
        keep_in[pair_rows(h, 0), :] = in0
        keep_in[pair_rows(h, 1), :] = in1
        emit_active(h, act, core, x, keep, sends)

    run_block(sbuf, (lt_ref, r_ref, bd_ref, d_ref), scratch, emit)
    dens[...] = density_of(scratch[6][...])
    for copy in ahead:
        copy.wait()


def third_kernel(
    where, slabs_ref, sbuf, lt_ref, r_ref, bd_ref, d_ref, sends1, sends2, dens1, dens2,
    near, far, cross, keep, dens, after, sem, sends, *scratch
):
    core, x = where[0], where[1]
    ahead = slab_copies(slabs_ref, after, sem, 2 * x + core)

    for copy in ahead:
        copy.start()

    def emit(h, in0, in1, act):
        near[pair_rows(h, 0), :] = in0.astype(BF)
        near[pair_rows(h, 1), :] = in1.astype(BF)
        emit_active(h, act, core, x, keep, sends)

    run_block(sbuf, (lt_ref, r_ref, bd_ref, d_ref), scratch, emit)
    dens[...] = density_of(scratch[6][...])
    wires = [split_wire(d[...]) for d in (dens1, dens2, dens)]
    for k, (msg, base) in enumerate(((near, INROWS), (far, 0), (cross, 0))):
        for n, source in enumerate((sends1, sends2, sends)):
            msg[pl.ds(base + n * PER, PER), :] = source[k]
            msg[pl.ds(base + 3 * PER + n * NBQ, NBQ), :] = wires[n]
    for copy in ahead:
        copy.wait()


def fourth_kernel(
    where, sbuf, lt_ref, r_ref, bd_ref, d_ref, keep_in, keep, sends, dens, *scratch
):
    core, x = where[0], where[1]

    def emit(h, in0, in1, act):
        keep_in[pair_rows(h, 0), :] = in0
        keep_in[pair_rows(h, 1), :] = in1
        emit_active(h, act, core, x, keep, sends)

    run_block(sbuf, (lt_ref, r_ref, bd_ref, d_ref), scratch, emit)
    dens[...] = density_of(scratch[6][...])


def exchange_kernel(
    where, mine, near3, far1a, far1b, sends, dens, near, far, cross, keep, whole
):
    parts = []
    for q in range(NBQ):
        rows = pl.ds(q * NACT, NACT)
        at = q * NACT - far1a.shape[0]
        other = far1a[rows, :] if at < 0 else far1b[pl.ds(at, NACT), :]
        parts.append(mine[rows, :] + near3[rows, :].astype(F32) + other.astype(F32))
    v = jnp.concatenate(parts, axis=1)
    v = v.astype(BF)
    total = lax.dot_general(v, v, (((1,), (1,)), ((), ())), preferred_element_type=F32)
    whole[...] = jnp.concatenate([total, total], axis=1)
    index = 2 * where[1] + where[0]
    keep[...] = whole[pl.ds(pl.multiple_of(index * QUARTER, QUARTER), QUARTER), :]
    wire = split_wire(dens[...])
    for k, msg in enumerate((near, far, cross)):
        msg[pl.ds(0, PER), :] = sends[k]
        msg[pl.ds(PER, NBQ), :] = wire
        at = pl.multiple_of((index ^ (k + 1)) * QUARTER, QUARTER)
        msg[pl.ds(PER + NBQ, QUARTER), :] = split_wire(whole[pl.ds(at, QUARTER), :])


def coulomb_kernel(
    keep1, keep2, keep3, keep4, dens1, dens2, dens3, dens4, exch,
    near3, far3, cross3, near4, far4, cross4, act, partial,
):
    first = low_half(QUARTER)
    early, late = (near3, far3, cross3), (near4, far4, cross4)
    total = jnp.zeros((QUARTER, LANES), F32)
    for m, (keep, dens) in enumerate(
        ((keep1, dens1), (keep2, dens2), (keep3, dens3), (keep4, dens4))
    ):
        rows, d = keep[...], dens[...]
        for k in (1, 2, 3):
            n = m ^ k
            msg = late[k - 1] if n == 3 else early[k - 1]
            base = INROWS if n < 3 and k == 1 else 0
            at, dens_at = (0, PER) if n == 3 else (base + n * PER, base + 3 * PER + n * NBQ)
            rows = rows + msg[pl.ds(at, PER), :].astype(F32)
            d = d + joined(msg[pl.ds(dens_at, NBQ), :])
        act[pl.ds(m * PER, PER), :] = rows
        for h in range(NBQ // 2):
            total = total + rows[h * QUARTER : (h + 1) * QUARTER] * jnp.where(
                first, d[2 * h : 2 * h + 1], d[2 * h + 1 : 2 * h + 2]
            )
    total = 2.0 * (total + pltpu.roll(total, BS, 1)) - exch[...]
    for msg in late:
        total = total - joined(msg[pl.ds(PER + NBQ, QUARTER), :])
    partial[...] = total[:, :BS]


def active_kernel(where, act, out):
    core, x = where[0], where[1]
    for n in range(4):
        xx = (1 - x) if n < 2 else x
        cc = (1 - core) if n % 2 == 0 else core
        base = NBQ * (2 * xx + cc)
        for h in range(NBQ // 2):
            a = act[pl.ds(n * PER + h * QUARTER, QUARTER), :]
            out[base + 2 * h] = a[:, :BS]
            out[base + 2 * h + 1] = a[:, BS:]


VM = pl.BlockSpec(memory_space=pltpu.VMEM)
SM = pl.BlockSpec(memory_space=pltpu.SMEM)
HB = pl.BlockSpec(memory_space=pltpu.HBM)

PARAMS = pltpu.CompilerParams(vmem_limit_bytes=32 * 1024 * 1024)


def in_hbm(array):
    return pltpu.with_memory_space_constraint(array, pltpu.HBM)


def shape(dims, dtype):
    return jax.ShapeDtypeStruct(dims, dtype)


def sum_over_aux(part):
    n = lax.axis_size("aux")
    if n != 4:
        return lax.psum(part, "aux")
    for k in (1, 2):
        part = part + lax.ppermute(part, "aux", [(z, z ^ k) for z in range(n)])
    return part


def call(kernel, name, inputs, out_shape, scratch, args, work=0):
    return pl.pallas_call(
        kernel,
        name=name,
        in_specs=inputs,
        out_specs=[VM] * len(out_shape),
        out_shape=out_shape,
        scratch_shapes=scratch,
        compiler_params=PARAMS,
        cost_estimate=pl.CostEstimate(flops=work, bytes_accessed=10**5, transcendentals=0),
    )(*args)


def paired_body(slabs, block_row, block_col, live_count, orbitals, hcore):
    nslab, batch, width = slabs.shape
    index = lax.axis_index("pair")
    where = jnp.stack([lax.rem(index, 2), index // 2])
    aos = nslab * BS
    slabs = in_hbm(slabs)

    def to_peer(k, array):
        return lax.ppermute(array, "pair", [(p, p ^ k) for p in range(4)])

    loaded = shape((nslab // 2, 2, NBQ, width), BF)
    copies = pltpu.SemaphoreType.DMA((nslab // 2,))
    scratch = [pltpu.VMEM((MSTEP * BS, LANES), F32)] * 4 + [
        pltpu.VMEM((NBQ, NACT, aos), BF),
        pltpu.VMEM((aos, NBQ * BS), BF),
        pltpu.VMEM((NBQ, 8, LANES), F32),
    ]
    weights = (
        shape((NCOL, aos), BF),
        shape((aos, 2 * LANES), BF),
        shape((nslab // 4, 2 * PAIRED, 2 * PAIRED), BF),
        shape((nslab // 2, BS, PAIRED), F32),
    )
    kept = (
        shape((PER, LANES), F32), shape((3, PER, LANES), BF), shape((NBQ, LANES), F32),
    )
    work = 5 * 10**9
    lt, r, bd, d, msg1, keep1, sends1, dens1, slabs2 = call(
        first_kernel,
        "slabs_first",
        [SM, HB, HB, SM, HB, HB],
        weights + (shape((INROWS, LANES), BF),) + kept + (loaded,),
        [
            pltpu.SMEM((nslab,), jnp.int32), pltpu.SMEM((nslab,), jnp.int32),
            pltpu.VMEM(orbitals.T.shape, BF), pltpu.SemaphoreType.DMA((8,)),
            pltpu.VMEM(loaded.shape, BF), copies, copies,
        ] + scratch,
        (
            where, in_hbm(block_row), in_hbm(block_col), live_count, slabs,
            in_hbm(orbitals.T),
        ),
        work,
    )
    near1 = to_peer(1, msg1)
    keep_in2, keep2, sends2, dens2, slabs3 = call(
        second_kernel,
        "slabs_second",
        [SM, HB] + [VM] * 5,
        (shape((INROWS, LANES), F32),) + kept + (loaded,),
        [copies] + scratch,
        (where, slabs, slabs2, lt, r, bd, d),
        work,
    )
    out2 = (keep_in2 + near1.astype(F32)).astype(BF)
    out2, lt = lax.optimization_barrier((out2, lt))
    cut = INROWS // 4
    far1a = to_peer(2, out2[:cut])
    news = 3 * PER + 3 * NBQ
    msg3, msg3x, msg3c, keep3, dens3, slabs4 = call(
        third_kernel,
        "slabs_third",
        [SM, HB] + [VM] * 9,
        (
            shape((INROWS + news, LANES), BF), shape((news, LANES), BF),
            shape((news, LANES), BF), kept[0], kept[2], loaded,
        ),
        [copies, pltpu.VMEM((3, PER, LANES), BF)] + scratch,
        (where, slabs, slabs3, lt, r, bd, d, sends1, sends2, dens1, dens2),
        work,
    )
    near3 = to_peer(1, msg3)
    far1b = to_peer(2, out2[cut:])
    far3, cross3 = to_peer(2, msg3x), to_peer(3, msg3c)
    far1a, lt = lax.optimization_barrier((far1a, lt))
    keep_in4, keep4, sends4, dens4 = call(
        fourth_kernel,
        "slabs_fourth",
        [SM] + [VM] * 5,
        (shape((INROWS, LANES), F32),) + kept,
        scratch,
        (where, slabs4, lt, r, bd, d),
        work,
    )
    last = shape((PER + NBQ + QUARTER, LANES), BF)
    near4, far4, cross4, exch = call(
        exchange_kernel,
        "exchange",
        [SM] + [VM] * 6,
        (last,) * 3 + (shape((QUARTER, LANES), F32),),
        [pltpu.VMEM((NACT, LANES), F32)],
        (where, keep_in4, near3, far1a, far1b, sends4, dens4),
    )
    far4, cross4, near4 = to_peer(2, far4), to_peer(3, cross4), to_peer(1, near4)
    act, partial = call(
        coulomb_kernel,
        "coulomb",
        [VM] * 15,
        (shape((4 * PER, LANES), F32), shape((QUARTER, NACT), F32)),
        [],
        (
            keep1, keep2, keep3, keep4, dens1, dens2, dens3, dens4, exch,
            near3, far3, cross3, near4, far4, cross4,
        ),
    )
    (active,) = call(
        active_kernel,
        "own_active",
        [SM, VM],
        (shape((batch, QUARTER, NACT), F32),),
        [],
        (where, act),
        10**6,
    )
    return (active, hcore + sum_over_aux(partial))


def slab_terms(values, left, right):
    half = jnp.einsum("mc,qmn->qnc", left, values, preferred_element_type=F32).astype(BF)
    first = jnp.einsum("qnt,nc->qtc", half[:, :, :NACT], right, preferred_element_type=F32)
    second = jnp.einsum("qnc,nt->qtc", half, right[:, :NACT], preferred_element_type=F32)
    trace = 2.0 * jnp.einsum(
        "qni,ni->q", half[:, :, NACT:], right[:, NACT:], preferred_element_type=F32
    )
    return (first + second, trace)


def general_body(slabs, block_row, block_col, live_count, orbitals, hcore):
    batch = slabs.shape[1]
    init = (jnp.zeros((batch, NACT, NCOL), F32), jnp.zeros((batch,), F32))

    def visit(k, state):
        values = lax.dynamic_index_in_dim(slabs, k, 0, keepdims=False)
        left = lax.dynamic_slice_in_dim(orbitals, block_row[k] * BS, BS, 0)
        right = lax.dynamic_slice_in_dim(orbitals, block_col[k] * BS, BS, 0)
        terms, trace = slab_terms(values.reshape(batch, BS, BS), left, right)
        return (state[0] + terms, state[1] + trace)

    vectors, density = lax.fori_loop(0, live_count[0], visit, init)
    density = lax.psum(density, "pair")
    owned = lax.psum_scatter(vectors, "pair", scatter_dimension=1, tiled=True)
    own_active, own_inactive = owned[:, :, :NACT], owned[:, :, NACT:]
    gathered = lax.all_gather(own_inactive.astype(BF), "pair", axis=1, tiled=True)
    exchange = jnp.einsum(
        "qti,qui->tu", own_inactive, gathered.astype(F32), precision=lax.Precision.HIGHEST
    )
    coulomb = jnp.einsum("qtu,q->tu", own_active, density, precision=lax.Precision.HIGHEST)
    return (own_active, hcore + lax.psum(2.0 * coulomb - exchange, "aux"))


def solution(mesh):
    placed = (
        P(("frag", "pair"), "aux", None),
        P(("frag", "pair")),
        P(("frag", "pair")),
        P(("frag", "pair")),
        P("frag", None),
        P(("frag", "pair"), None),
    )

    def body(slabs, *rest):
        fits = mesh.shape["pair"] == 4 and slabs.shape[1] == 4 * NBQ and slabs.shape[0] % 4 == 0
        return (paired_body if fits else general_body)(slabs, *rest)

    return jax.shard_map(
        body,
        mesh=mesh,
        in_specs=placed,
        out_specs=(P(("frag", "aux"), "pair", None), P(("frag", "pair"), None)),
        check_vma=False,
    )
```

```python
import jax
import jax.numpy as jnp
from jax import lax
from jax.experimental import pallas as pl
from jax.experimental.pallas import tpu as pltpu
from jax.sharding import PartitionSpec as P

BS = 64
NACT = 64
NCOL = 192
NIN = NCOL - NACT
LANES = 128
NBQ = 16
PAIRED = 2 * BS
QSTEP, MSTEP = 3, 49
BF = jnp.bfloat16
F32 = jnp.float32


def low_half(rows):
    return lax.broadcasted_iota(jnp.int32, (rows, LANES), 1) < BS


def orbital_pair(k, blocks, live, orbitals):
    halves = []
    for n in range(2):
        slot = 2 * k + n
        base = pl.multiple_of((blocks[slot] // 2) * PAIRED, PAIRED)
        w = orbitals[:, pl.ds(base, PAIRED)]
        w = jnp.concatenate([w[NACT:], w[:NACT]], axis=0)
        w = jnp.where(lax.rem(blocks[slot], 2) != n, pltpu.roll(w, BS, 1), w)
        halves.append(jnp.where(slot < live, w, jnp.zeros_like(w)))
    return jnp.where(low_half(NCOL), halves[0], halves[1])


def slab_copies(slabs_ref, sbuf, sem, block):
    return [
        pltpu.make_async_copy(
            slabs_ref.at[pl.ds(2 * k, 2), pl.ds(pl.multiple_of(block * NBQ, NBQ), NBQ), :],
            sbuf.at[k],
            sem.at[k],
        )
        for k in range(slabs_ref.shape[0] // 2)
    ]


def lanes_of(k):
    return pl.ds(k * PAIRED if isinstance(k, int) else pl.multiple_of(k * PAIRED, PAIRED), PAIRED)


def run_block(sbuf, weights, scratch, emit, prepare=None):
    lt_ref, r_ref, bd_ref, d_ref = weights
    pt_ref, q_ref, diag = scratch[4:]
    quads = sbuf.shape[0] // 2
    first = low_half(NBQ)
    first_s = low_half(BS)
    zero = jnp.zeros((BS, LANES), BF)
    group = 8

    def relayout(k, out):
        for j in range(sbuf.shape[3] // LANES):
            lanes = slice(j * LANES, (j + 1) * LANES)
            a = sbuf[k, 0, :, lanes]
            b = sbuf[k, 1, :, lanes]
            out[pl.ds(MSTEP * 2 * j, NBQ, stride=QSTEP), :] = jnp.where(
                first, a, pltpu.roll(b, BS, 1)
            ).astype(F32)
            out[pl.ds(MSTEP * (2 * j + 1), NBQ, stride=QSTEP), :] = jnp.where(
                first, pltpu.roll(a, BS, 1), b
            ).astype(F32)

    def transform(g, bufs):
        dens = [d_ref[2 * g + n] for n in range(2)]
        left = [lt_ref[NIN:, lanes_of(2 * g + n)] for n in range(2)]
        for q in range(0, NBQ, group):
            slabs = [[], []]
            for u in range(q, q + group):
                total = diag[u]
                for n in range(2):
                    s = bufs[n][pl.ds(u * QSTEP, BS, stride=MSTEP), :]
                    total = total + jnp.sum((s * dens[n]).reshape(BS // 8, 8, LANES), axis=0)
                    slabs[n].append(s.astype(BF))
                diag[u] = total
            for n in range(2):
                at = lanes_of(2 * g + n)
                cols = [
                    jnp.concatenate(
                        [jnp.where(first_s, s, zero), jnp.where(first_s, zero, s)], axis=0
                    )
                    for s in slabs[n]
                ]
                p = jnp.dot(
                    left[n], jnp.concatenate(cols, axis=1), preferred_element_type=F32
                ).astype(BF)
                for u in range(group):
                    pt_ref[q + u, :, at] = p[:, u * LANES : (u + 1) * LANES]
            rows = jnp.concatenate(
                [jnp.concatenate([s0, s1], axis=1) for s0, s1 in zip(*slabs)], axis=0
            )
            out = jnp.dot(rows, bd_ref[g], preferred_element_type=F32).astype(BF)
            for u in range(0, group, 2):
                for n in range(2):
                    lanes = slice(n * LANES, (n + 1) * LANES)
                    q0 = out[u * BS : (u + 1) * BS, lanes]
                    q1 = out[(u + 1) * BS : (u + 2) * BS, lanes]
                    at = slice((q + u) * BS, (q + u + 2) * BS)
                    row = lanes_of(2 * g + n).start
                    q_ref[pl.ds(row, BS), at] = jnp.where(first_s, q0, pltpu.roll(q1, BS, 1))
                    q_ref[pl.ds(row + BS, BS), at] = jnp.where(
                        first_s, pltpu.roll(q0, BS, 1), q1
                    )

    def second_transform(g):
        rows = pt_ref[4 * g : 4 * g + 4].reshape(4 * NACT, pt_ref.shape[2])
        one = jnp.dot(rows, r_ref[...], preferred_element_type=F32)
        two = jnp.dot(
            lt_ref[...], q_ref[:, 4 * g * BS : (4 * g + 4) * BS], preferred_element_type=F32
        )
        return one, two

    def assemble(g, both):
        one, two = both
        for p in range(2):
            w0 = one[2 * p * NACT : (2 * p + 1) * NACT]
            w1 = one[(2 * p + 1) * NACT : (2 * p + 2) * NACT]
            turned = two[:, p * LANES : (p + 1) * LANES]
            across = turned[:NIN].T
            square = jnp.concatenate([turned[NIN:], turned[NIN:]], axis=0).T
            emit(
                2 * g + p,
                w0[:, :NIN] + across[:NACT],
                w1[:, :NIN] + across[NACT:],
                jnp.where(first_s, w0[:, NIN:] + square[:NACT], w1[:, NIN:] + square[NACT:]),
            )

    def load(g, bufs):
        for n in range(2):
            relayout(2 * g + n, bufs[n])

    def two_quads(i, carry):
        one, two = scratch[:2], scratch[2:4]
        after = jnp.minimum(2 * i + 2, quads - 1)
        prepare(2 * i + 1)
        load(2 * i + 1, two)
        transform(2 * i, one)
        prepare(after)
        load(after, one)
        transform(2 * i + 1, two)
        return carry

    diag[...] = jnp.zeros_like(diag)
    load(0, scratch[:2])
    if prepare is not None:
        prepare(0)
        lax.fori_loop(0, quads // 2, two_quads, 0)
    else:
        for g in range(quads):
            if g + 1 < quads:
                load(g + 1, scratch[2 * ((g + 1) % 2) : 2 * ((g + 1) % 2) + 2])
            transform(g, scratch[2 * (g % 2) : 2 * (g % 2) + 2])
    whole = second_transform(0)
    for g in range(NBQ // 4):
        following = second_transform(g + 1) if g + 1 < NBQ // 4 else None
        assemble(g, whole)
        whole = following


def split_wire(d):
    hi = d.astype(BF).astype(F32)
    return jnp.where(low_half(d.shape[0]), hi, d - hi).astype(BF)


def joined(wire):
    w = wire.astype(F32)
    return w + pltpu.roll(w, BS, 1)


def density_of(diag):
    d = 2.0 * jnp.sum(jnp.sum(diag, axis=1), axis=1, keepdims=True)
    return jnp.broadcast_to(d, (NBQ, LANES))


QUARTER = NACT // 4
PER = NBQ // 2 * QUARTER
INROWS = NBQ * NACT


def emit_active(h, act, core, x, keep, sends):
    upper, lower = act[: 2 * QUARTER], act[2 * QUARTER :]
    near, far = jnp.where(x == 0, upper, lower), jnp.where(x == 0, lower, upper)
    at = pl.ds(h * QUARTER, QUARTER)
    for part, own, other in ((near, keep, sends.at[0]), (far, sends.at[1], sends.at[2])):
        one, two = part[:QUARTER], part[QUARTER:]
        own[at, :] = jnp.where(core == 0, one, two).astype(own.dtype)
        other[at, :] = jnp.where(core == 0, two, one).astype(BF)


def pair_rows(h, n):
    return pl.ds((2 * h + n) * NACT, NACT)


def first_kernel(
    where, rows_ref, cols_ref, live, slabs_ref, ot_ref,
    lt_out, r_out, bd_out, d_out, msg, keep, sends, dens, after2, after3, after4,
    rows, cols, orbitals, ssem, sbuf, sem, *scratch
):
    core, x = where[0], where[1]
    part = NACT // 2
    small = [
        pltpu.make_async_copy(src, dst, ssem.at[n])
        for n, (src, dst) in enumerate(((rows_ref, rows), (cols_ref, cols)))
    ] + [
        pltpu.make_async_copy(
            ot_ref.at[pl.ds(n * part, part)], orbitals.at[pl.ds(n * part, part)], ssem.at[2 + n]
        )
        for n in range(NCOL // part)
    ]
    blocks = (2 * (1 - x) + (1 - core), 2 * (1 - x) + core, 2 * x + (1 - core), 2 * x + core)
    now, *later = [
        slab_copies(slabs_ref, ref, sem.at[n], block)
        for n, (ref, block) in enumerate(zip((sbuf, after2, after3, after4), blocks))
    ]
    ahead = [copy for copies in later for copy in copies]
    for copy in now[:2] + small + now[2:]:
        copy.start()
    bd_out[...] = jnp.zeros_like(bd_out)
    for copy in now[:2]:
        copy.wait()

    def prepare(g):
        if isinstance(g, int):
            for copy in small + now[2:]:
                copy.wait()
            for copy in ahead:
                copy.start()
        for n in range(2):
            k = 2 * g + n
            left = orbital_pair(k, rows, live[0], orbitals)
            right = orbital_pair(k, cols, live[0], orbitals)
            at = lanes_of(k)
            lt_out[:, at] = left
            turned = jnp.concatenate([right, right[NIN:]], axis=0).astype(F32).T.astype(BF)
            r_out[at, :] = turned
            inner = (lax.broadcasted_iota(jnp.int32, (PAIRED, LANES), 0) < BS) == low_half(PAIRED)
            place = slice(n * PAIRED, (n + 1) * PAIRED)
            bd_out[g, place, place] = jnp.where(
                inner, turned[:, NIN:], jnp.zeros((PAIRED, LANES), BF)
            )
            both = jnp.dot(
                left[:NIN].astype(F32).T.astype(BF), right[:NIN], preferred_element_type=F32
            )
            d_out[k] = jnp.where(low_half(BS), both[:BS], both[BS:])

    def emit(h, in0, in1, act):
        msg[pair_rows(h, 0), :] = in0.astype(BF)
        msg[pair_rows(h, 1), :] = in1.astype(BF)
        emit_active(h, act, core, x, keep, sends)

    run_block(sbuf, (lt_out, r_out, bd_out, d_out), scratch, emit, prepare)
    dens[...] = density_of(scratch[6][...])
    for copy in ahead:
        copy.wait()


def second_kernel(
    where, sbuf, lt_ref, r_ref, bd_ref, d_ref, keep_in, keep, sends, dens, *scratch
):
    core, x = where[0], where[1]
    def emit(h, in0, in1, act):
        keep_in[pair_rows(h, 0), :] = in0
        keep_in[pair_rows(h, 1), :] = in1
        emit_active(h, act, core, x, keep, sends)

    run_block(sbuf, (lt_ref, r_ref, bd_ref, d_ref), scratch, emit)
    dens[...] = density_of(scratch[6][...])


def third_kernel(
    where, sbuf, lt_ref, r_ref, bd_ref, d_ref, sends1, sends2, dens1, dens2,
    near, far, cross, keep, dens, sends, *scratch
):
    core, x = where[0], where[1]
    def emit(h, in0, in1, act):
        near[pair_rows(h, 0), :] = in0.astype(BF)
        near[pair_rows(h, 1), :] = in1.astype(BF)
        emit_active(h, act, core, x, keep, sends)

    run_block(sbuf, (lt_ref, r_ref, bd_ref, d_ref), scratch, emit)
    dens[...] = density_of(scratch[6][...])
    wires = [split_wire(d[...]) for d in (dens1, dens2, dens)]
    for k, (msg, base) in enumerate(((near, INROWS), (far, 0), (cross, 0))):
        for n, source in enumerate((sends1, sends2, sends)):
            msg[pl.ds(base + n * PER, PER), :] = source[k]
            msg[pl.ds(base + 3 * PER + n * NBQ, NBQ), :] = wires[n]


def fourth_kernel(
    where, sbuf, lt_ref, r_ref, bd_ref, d_ref, keep_in, keep, sends, dens, *scratch
):
    core, x = where[0], where[1]

    def emit(h, in0, in1, act):
        keep_in[pair_rows(h, 0), :] = in0
        keep_in[pair_rows(h, 1), :] = in1
        emit_active(h, act, core, x, keep, sends)

    run_block(sbuf, (lt_ref, r_ref, bd_ref, d_ref), scratch, emit)
    dens[...] = density_of(scratch[6][...])


def exchange_kernel(
    where, mine, near3, far1a, far1b, sends, dens, near, far, cross, keep, whole
):
    parts = []
    for q in range(NBQ):
        rows = pl.ds(q * NACT, NACT)
        at = q * NACT - far1a.shape[0]
        other = far1a[rows, :] if at < 0 else far1b[pl.ds(at, NACT), :]
        parts.append(mine[rows, :] + near3[rows, :].astype(F32) + other.astype(F32))
    v = jnp.concatenate(parts, axis=1)
    v = v.astype(BF)
    total = lax.dot_general(v, v, (((1,), (1,)), ((), ())), preferred_element_type=F32)
    whole[...] = jnp.concatenate([total, total], axis=1)
    index = 2 * where[1] + where[0]
    keep[...] = whole[pl.ds(pl.multiple_of(index * QUARTER, QUARTER), QUARTER), :]
    wire = split_wire(dens[...])
    for k, msg in enumerate((near, far, cross)):
        msg[pl.ds(0, PER), :] = sends[k]
        msg[pl.ds(PER, NBQ), :] = wire
        at = pl.multiple_of((index ^ (k + 1)) * QUARTER, QUARTER)
        msg[pl.ds(PER + NBQ, QUARTER), :] = split_wire(whole[pl.ds(at, QUARTER), :])


def coulomb_kernel(
    keep1, keep2, keep3, keep4, dens1, dens2, dens3, dens4, exch,
    near3, far3, cross3, near4, far4, cross4, act, partial,
):
    first = low_half(QUARTER)
    early, late = (near3, far3, cross3), (near4, far4, cross4)
    total = jnp.zeros((QUARTER, LANES), F32)
    for m, (keep, dens) in enumerate(
        ((keep1, dens1), (keep2, dens2), (keep3, dens3), (keep4, dens4))
    ):
        rows, d = keep[...], dens[...]
        for k in (1, 2, 3):
            n = m ^ k
            msg = late[k - 1] if n == 3 else early[k - 1]
            base = INROWS if n < 3 and k == 1 else 0
            at, dens_at = (0, PER) if n == 3 else (base + n * PER, base + 3 * PER + n * NBQ)
            rows = rows + msg[pl.ds(at, PER), :].astype(F32)
            d = d + joined(msg[pl.ds(dens_at, NBQ), :])
        act[pl.ds(m * PER, PER), :] = rows
        for h in range(NBQ // 2):
            total = total + rows[h * QUARTER : (h + 1) * QUARTER] * jnp.where(
                first, d[2 * h : 2 * h + 1], d[2 * h + 1 : 2 * h + 2]
            )
    total = 2.0 * (total + pltpu.roll(total, BS, 1)) - exch[...]
    for msg in late:
        total = total - joined(msg[pl.ds(PER + NBQ, QUARTER), :])
    partial[...] = total[:, :BS]


def active_kernel(where, act, out):
    core, x = where[0], where[1]
    for n in range(4):
        xx = (1 - x) if n < 2 else x
        cc = (1 - core) if n % 2 == 0 else core
        base = NBQ * (2 * xx + cc)
        for h in range(NBQ // 2):
            a = act[pl.ds(n * PER + h * QUARTER, QUARTER), :]
            out[base + 2 * h] = a[:, :BS]
            out[base + 2 * h + 1] = a[:, BS:]


VM = pl.BlockSpec(memory_space=pltpu.VMEM)
SM = pl.BlockSpec(memory_space=pltpu.SMEM)
HB = pl.BlockSpec(memory_space=pltpu.HBM)

PARAMS = pltpu.CompilerParams(vmem_limit_bytes=32 * 1024 * 1024)


def in_hbm(array):
    return pltpu.with_memory_space_constraint(array, pltpu.HBM)


def shape(dims, dtype):
    return jax.ShapeDtypeStruct(dims, dtype)


def sum_over_aux(part):
    n = lax.axis_size("aux")
    if n != 4:
        return lax.psum(part, "aux")
    for k in (1, 2):
        part = part + lax.ppermute(part, "aux", [(z, z ^ k) for z in range(n)])
    return part


def call(kernel, name, inputs, out_shape, scratch, args, work=0):
    return pl.pallas_call(
        kernel,
        name=name,
        in_specs=inputs,
        out_specs=[VM] * len(out_shape),
        out_shape=out_shape,
        scratch_shapes=scratch,
        compiler_params=PARAMS,
        cost_estimate=pl.CostEstimate(flops=work, bytes_accessed=10**5, transcendentals=0),
    )(*args)


def paired_body(slabs, block_row, block_col, live_count, orbitals, hcore):
    nslab, batch, width = slabs.shape
    index = lax.axis_index("pair")
    where = jnp.stack([lax.rem(index, 2), index // 2])
    aos = nslab * BS
    slabs = in_hbm(slabs)

    def to_peer(k, array):
        return lax.ppermute(array, "pair", [(p, p ^ k) for p in range(4)])

    loaded = shape((nslab // 2, 2, NBQ, width), BF)
    scratch = [pltpu.VMEM((MSTEP * BS, LANES), F32)] * 4 + [
        pltpu.VMEM((NBQ, NACT, aos), BF),
        pltpu.VMEM((aos, NBQ * BS), BF),
        pltpu.VMEM((NBQ, 8, LANES), F32),
    ]
    weights = (
        shape((NCOL, aos), BF),
        shape((aos, 2 * LANES), BF),
        shape((nslab // 4, 2 * PAIRED, 2 * PAIRED), BF),
        shape((nslab // 2, BS, PAIRED), F32),
    )
    kept = (
        shape((PER, LANES), F32), shape((3, PER, LANES), BF), shape((NBQ, LANES), F32),
    )
    work = 5 * 10**9
    lt, r, bd, d, msg1, keep1, sends1, dens1, slabs2, slabs3, slabs4 = call(
        first_kernel,
        "slabs_first",
        [SM, HB, HB, SM, HB, HB],
        weights + (shape((INROWS, LANES), BF),) + kept + (loaded,) * 3,
        [
            pltpu.SMEM((nslab,), jnp.int32), pltpu.SMEM((nslab,), jnp.int32),
            pltpu.VMEM(orbitals.T.shape, BF), pltpu.SemaphoreType.DMA((8,)),
            pltpu.VMEM(loaded.shape, BF), pltpu.SemaphoreType.DMA((4, nslab // 2)),
        ] + scratch,
        (
            where, in_hbm(block_row), in_hbm(block_col), live_count, slabs,
            in_hbm(orbitals.T),
        ),
        work,
    )
    near1 = to_peer(1, msg1)
    keep_in2, keep2, sends2, dens2 = call(
        second_kernel,
        "slabs_second",
        [SM] + [VM] * 5,
        (shape((INROWS, LANES), F32),) + kept,
        scratch,
        (where, slabs2, lt, r, bd, d),
        work,
    )
    out2 = (keep_in2 + near1.astype(F32)).astype(BF)
    out2, lt = lax.optimization_barrier((out2, lt))
    cut = INROWS // 4
    far1a = to_peer(2, out2[:cut])
    news = 3 * PER + 3 * NBQ
    msg3, msg3x, msg3c, keep3, dens3 = call(
        third_kernel,
        "slabs_third",
        [SM] + [VM] * 9,
        (
            shape((INROWS + news, LANES), BF), shape((news, LANES), BF),
            shape((news, LANES), BF), kept[0], kept[2],
        ),
        [pltpu.VMEM((3, PER, LANES), BF)] + scratch,
        (where, slabs3, lt, r, bd, d, sends1, sends2, dens1, dens2),
        work,
    )
    near3 = to_peer(1, msg3)
    far1b = to_peer(2, out2[cut:])
    far3, cross3 = to_peer(2, msg3x), to_peer(3, msg3c)
    far1a, lt = lax.optimization_barrier((far1a, lt))
    keep_in4, keep4, sends4, dens4 = call(
        fourth_kernel,
        "slabs_fourth",
        [SM] + [VM] * 5,
        (shape((INROWS, LANES), F32),) + kept,
        scratch,
        (where, slabs4, lt, r, bd, d),
        work,
    )
    last = shape((PER + NBQ + QUARTER, LANES), BF)
    near4, far4, cross4, exch = call(
        exchange_kernel,
        "exchange",
        [SM] + [VM] * 6,
        (last,) * 3 + (shape((QUARTER, LANES), F32),),
        [pltpu.VMEM((NACT, LANES), F32)],
        (where, keep_in4, near3, far1a, far1b, sends4, dens4),
    )
    far4, cross4, near4 = to_peer(2, far4), to_peer(3, cross4), to_peer(1, near4)
    act, partial = call(
        coulomb_kernel,
        "coulomb",
        [VM] * 15,
        (shape((4 * PER, LANES), F32), shape((QUARTER, NACT), F32)),
        [],
        (
            keep1, keep2, keep3, keep4, dens1, dens2, dens3, dens4, exch,
            near3, far3, cross3, near4, far4, cross4,
        ),
    )
    (active,) = call(
        active_kernel,
        "own_active",
        [SM, VM],
        (shape((batch, QUARTER, NACT), F32),),
        [],
        (where, act),
        10**6,
    )
    return (active, hcore + sum_over_aux(partial))


def slab_terms(values, left, right):
    half = jnp.einsum("mc,qmn->qnc", left, values, preferred_element_type=F32).astype(BF)
    first = jnp.einsum("qnt,nc->qtc", half[:, :, :NACT], right, preferred_element_type=F32)
    second = jnp.einsum("qnc,nt->qtc", half, right[:, :NACT], preferred_element_type=F32)
    trace = 2.0 * jnp.einsum(
        "qni,ni->q", half[:, :, NACT:], right[:, NACT:], preferred_element_type=F32
    )
    return (first + second, trace)


def general_body(slabs, block_row, block_col, live_count, orbitals, hcore):
    batch = slabs.shape[1]
    init = (jnp.zeros((batch, NACT, NCOL), F32), jnp.zeros((batch,), F32))

    def visit(k, state):
        values = lax.dynamic_index_in_dim(slabs, k, 0, keepdims=False)
        left = lax.dynamic_slice_in_dim(orbitals, block_row[k] * BS, BS, 0)
        right = lax.dynamic_slice_in_dim(orbitals, block_col[k] * BS, BS, 0)
        terms, trace = slab_terms(values.reshape(batch, BS, BS), left, right)
        return (state[0] + terms, state[1] + trace)

    vectors, density = lax.fori_loop(0, live_count[0], visit, init)
    density = lax.psum(density, "pair")
    owned = lax.psum_scatter(vectors, "pair", scatter_dimension=1, tiled=True)
    own_active, own_inactive = owned[:, :, :NACT], owned[:, :, NACT:]
    gathered = lax.all_gather(own_inactive.astype(BF), "pair", axis=1, tiled=True)
    exchange = jnp.einsum(
        "qti,qui->tu", own_inactive, gathered.astype(F32), precision=lax.Precision.HIGHEST
    )
    coulomb = jnp.einsum("qtu,q->tu", own_active, density, precision=lax.Precision.HIGHEST)
    return (own_active, hcore + lax.psum(2.0 * coulomb - exchange, "aux"))


def solution(mesh):
    placed = (
        P(("frag", "pair"), "aux", None),
        P(("frag", "pair")),
        P(("frag", "pair")),
        P(("frag", "pair")),
        P("frag", None),
        P(("frag", "pair"), None),
    )

    def body(slabs, *rest):
        fits = mesh.shape["pair"] == 4 and slabs.shape[1] == 4 * NBQ and slabs.shape[0] % 4 == 0
        return (paired_body if fits else general_body)(slabs, *rest)

    return jax.shard_map(
        body,
        mesh=mesh,
        in_specs=placed,
        out_specs=(P(("frag", "aux"), "pair", None), P(("frag", "pair"), None)),
        check_vma=False,
    )
```

```python
import jax
import jax.numpy as jnp
from jax import lax
from jax.experimental import pallas as pl
from jax.experimental.pallas import tpu as pltpu
from jax.sharding import PartitionSpec as P

BS = 64
NACT = 64
NCOL = 192
NIN = NCOL - NACT
LANES = 128
NBQ = 16
PAIRED = 2 * BS
QSTEP, MSTEP = 3, 49
BF = jnp.bfloat16
F32 = jnp.float32


def low_half(rows):
    return lax.broadcasted_iota(jnp.int32, (rows, LANES), 1) < BS


def orbital_pair(k, blocks, live, orbitals):
    halves = []
    for n in range(2):
        slot = 2 * k + n
        base = pl.multiple_of((blocks[slot] // 2) * PAIRED, PAIRED)
        w = orbitals[:, pl.ds(base, PAIRED)]
        w = jnp.concatenate([w[NACT:], w[:NACT]], axis=0)
        w = jnp.where(lax.rem(blocks[slot], 2) != n, pltpu.roll(w, BS, 1), w)
        halves.append(jnp.where(slot < live, w, jnp.zeros_like(w)))
    return jnp.where(low_half(NCOL), halves[0], halves[1])


def slab_copies(slabs_ref, sbuf, sem, block):
    return [
        pltpu.make_async_copy(
            slabs_ref.at[pl.ds(2 * k, 2), pl.ds(pl.multiple_of(block * NBQ, NBQ), NBQ), :],
            sbuf.at[k],
            sem.at[k],
        )
        for k in range(slabs_ref.shape[0] // 2)
    ]


def lanes_of(k):
    return pl.ds(k * PAIRED if isinstance(k, int) else pl.multiple_of(k * PAIRED, PAIRED), PAIRED)


def run_block(sbuf, weights, scratch, emit, prepare=None):
    lt_ref, r_ref, bd_ref, d_ref = weights
    pt_ref, q_ref, diag = scratch[4:]
    quads = sbuf.shape[0] // 2
    first = low_half(NBQ)
    first_s = low_half(BS)
    zero = jnp.zeros((BS, LANES), BF)
    group = 8

    def relayout(k, out):
        for j in range(sbuf.shape[3] // LANES):
            lanes = slice(j * LANES, (j + 1) * LANES)
            a = sbuf[k, 0, :, lanes]
            b = sbuf[k, 1, :, lanes]
            out[pl.ds(MSTEP * 2 * j, NBQ, stride=QSTEP), :] = jnp.where(
                first, a, pltpu.roll(b, BS, 1)
            ).astype(F32)
            out[pl.ds(MSTEP * (2 * j + 1), NBQ, stride=QSTEP), :] = jnp.where(
                first, pltpu.roll(a, BS, 1), b
            ).astype(F32)

    def transform(g, bufs):
        dens = [d_ref[2 * g + n] for n in range(2)]
        left = [lt_ref[NIN:, lanes_of(2 * g + n)] for n in range(2)]
        for q in range(0, NBQ, group):
            slabs = [[], []]
            for u in range(q, q + group):
                total = diag[u]
                for n in range(2):
                    s = bufs[n][pl.ds(u * QSTEP, BS, stride=MSTEP), :]
                    total = total + jnp.sum((s * dens[n]).reshape(BS // 8, 8, LANES), axis=0)
                    slabs[n].append(s.astype(BF))
                diag[u] = total
            for n in range(2):
                at = lanes_of(2 * g + n)
                cols = [
                    jnp.concatenate(
                        [jnp.where(first_s, s, zero), jnp.where(first_s, zero, s)], axis=0
                    )
                    for s in slabs[n]
                ]
                p = jnp.dot(
                    left[n], jnp.concatenate(cols, axis=1), preferred_element_type=F32
                ).astype(BF)
                for u in range(group):
                    pt_ref[q + u, :, at] = p[:, u * LANES : (u + 1) * LANES]
            rows = jnp.concatenate(
                [jnp.concatenate([s0, s1], axis=1) for s0, s1 in zip(*slabs)], axis=0
            )
            out = jnp.dot(rows, bd_ref[g], preferred_element_type=F32).astype(BF)
            for u in range(0, group, 2):
                for n in range(2):
                    lanes = slice(n * LANES, (n + 1) * LANES)
                    q0 = out[u * BS : (u + 1) * BS, lanes]
                    q1 = out[(u + 1) * BS : (u + 2) * BS, lanes]
                    at = slice((q + u) * BS, (q + u + 2) * BS)
                    row = lanes_of(2 * g + n).start
                    q_ref[pl.ds(row, BS), at] = jnp.where(first_s, q0, pltpu.roll(q1, BS, 1))
                    q_ref[pl.ds(row + BS, BS), at] = jnp.where(
                        first_s, pltpu.roll(q0, BS, 1), q1
                    )

    def second_transform(g):
        rows = pt_ref[4 * g : 4 * g + 4].reshape(4 * NACT, pt_ref.shape[2])
        one = jnp.dot(rows, r_ref[...], preferred_element_type=F32)
        two = jnp.dot(
            lt_ref[...], q_ref[:, 4 * g * BS : (4 * g + 4) * BS], preferred_element_type=F32
        )
        return one, two

    def assemble(g, both):
        one, two = both
        for p in range(2):
            w0 = one[2 * p * NACT : (2 * p + 1) * NACT]
            w1 = one[(2 * p + 1) * NACT : (2 * p + 2) * NACT]
            turned = two[:, p * LANES : (p + 1) * LANES]
            across = turned[:NIN].T
            square = jnp.concatenate([turned[NIN:], turned[NIN:]], axis=0).T
            emit(
                2 * g + p,
                w0[:, :NIN] + across[:NACT],
                w1[:, :NIN] + across[NACT:],
                jnp.where(first_s, w0[:, NIN:] + square[:NACT], w1[:, NIN:] + square[NACT:]),
            )

    def load(g, bufs):
        for n in range(2):
            relayout(2 * g + n, bufs[n])

    def two_quads(i, carry):
        one, two = scratch[:2], scratch[2:4]
        after = jnp.minimum(2 * i + 2, quads - 1)
        prepare(2 * i + 1)
        load(2 * i + 1, two)
        transform(2 * i, one)
        prepare(after)
        load(after, one)
        transform(2 * i + 1, two)
        return carry

    diag[...] = jnp.zeros_like(diag)
    load(0, scratch[:2])
    if prepare is not None:
        prepare(0)
        lax.fori_loop(0, quads // 2, two_quads, 0)
    else:
        for g in range(quads):
            if g + 1 < quads:
                load(g + 1, scratch[2 * ((g + 1) % 2) : 2 * ((g + 1) % 2) + 2])
            transform(g, scratch[2 * (g % 2) : 2 * (g % 2) + 2])
    whole = second_transform(0)
    for g in range(NBQ // 4):
        following = second_transform(g + 1) if g + 1 < NBQ // 4 else None
        assemble(g, whole)
        whole = following


def split_wire(d):
    hi = d.astype(BF).astype(F32)
    return jnp.where(low_half(d.shape[0]), hi, d - hi).astype(BF)


def joined(wire):
    w = wire.astype(F32)
    return w + pltpu.roll(w, BS, 1)


def density_of(diag):
    d = 2.0 * jnp.sum(jnp.sum(diag, axis=1), axis=1, keepdims=True)
    return jnp.broadcast_to(d, (NBQ, LANES))


QUARTER = NACT // 4
PER = NBQ // 2 * QUARTER
INROWS = NBQ * NACT


def emit_active(h, act, core, x, keep, sends):
    upper, lower = act[: 2 * QUARTER], act[2 * QUARTER :]
    near, far = jnp.where(x == 0, upper, lower), jnp.where(x == 0, lower, upper)
    at = pl.ds(h * QUARTER, QUARTER)
    for part, own, other in ((near, keep, sends.at[0]), (far, sends.at[1], sends.at[2])):
        one, two = part[:QUARTER], part[QUARTER:]
        own[at, :] = jnp.where(core == 0, one, two).astype(own.dtype)
        other[at, :] = jnp.where(core == 0, two, one).astype(BF)


def pair_rows(h, n):
    return pl.ds((2 * h + n) * NACT, NACT)


def first_kernel(
    where, rows_ref, cols_ref, live, slabs_ref, ot_ref,
    lt_out, r_out, bd_out, d_out, msg, keep, sends, dens, after2, after3, after4,
    rows, cols, orbitals, ssem, sbuf, sem, *scratch
):
    core, x = where[0], where[1]
    part = NACT // 2
    small = [
        pltpu.make_async_copy(src, dst, ssem.at[n])
        for n, (src, dst) in enumerate(((rows_ref, rows), (cols_ref, cols)))
    ] + [
        pltpu.make_async_copy(
            ot_ref.at[pl.ds(n * part, part)], orbitals.at[pl.ds(n * part, part)], ssem.at[2 + n]
        )
        for n in range(NCOL // part)
    ]
    blocks = (2 * (1 - x) + (1 - core), 2 * (1 - x) + core, 2 * x + (1 - core), 2 * x + core)
    now, *later = [
        slab_copies(slabs_ref, ref, sem.at[n], block)
        for n, (ref, block) in enumerate(zip((sbuf, after2, after3, after4), blocks))
    ]
    ahead = [copy for copies in later for copy in copies]
    for copy in now[:2] + small + now[2:]:
        copy.start()
    bd_out[...] = jnp.zeros_like(bd_out)
    for copy in now[:2]:
        copy.wait()

    def prepare(g):
        if isinstance(g, int):
            for copy in small + now[2:]:
                copy.wait()
            for copy in ahead:
                copy.start()
        for n in range(2):
            k = 2 * g + n
            left = orbital_pair(k, rows, live[0], orbitals)
            right = orbital_pair(k, cols, live[0], orbitals)
            at = lanes_of(k)
            lt_out[:, at] = left
            turned = jnp.concatenate([right, right[NIN:]], axis=0).astype(F32).T.astype(BF)
            r_out[at, :] = turned
            inner = (lax.broadcasted_iota(jnp.int32, (PAIRED, LANES), 0) < BS) == low_half(PAIRED)
            place = slice(n * PAIRED, (n + 1) * PAIRED)
            bd_out[g, place, place] = jnp.where(
                inner, turned[:, NIN:], jnp.zeros((PAIRED, LANES), BF)
            )
            both = jnp.dot(
                left[:NIN].astype(F32).T.astype(BF), right[:NIN], preferred_element_type=F32
            )
            d_out[k] = jnp.where(low_half(BS), both[:BS], both[BS:])

    def emit(h, in0, in1, act):
        msg[pair_rows(h, 0), :] = in0.astype(BF)
        msg[pair_rows(h, 1), :] = in1.astype(BF)
        emit_active(h, act, core, x, keep, sends)

    run_block(sbuf, (lt_out, r_out, bd_out, d_out), scratch, emit, prepare)
    dens[...] = density_of(scratch[6][...])
    for copy in ahead:
        copy.wait()


def second_kernel(
    where, sbuf, lt_ref, r_ref, bd_ref, d_ref, keep_in, keep, sends, dens, *scratch
):
    core, x = where[0], where[1]
    def emit(h, in0, in1, act):
        keep_in[pair_rows(h, 0), :] = in0
        keep_in[pair_rows(h, 1), :] = in1
        emit_active(h, act, core, x, keep, sends)

    run_block(sbuf, (lt_ref, r_ref, bd_ref, d_ref), scratch, emit)
    dens[...] = density_of(scratch[6][...])


def third_kernel(
    where, sbuf, lt_ref, r_ref, bd_ref, d_ref, sends1, sends2, dens1, dens2,
    near, near_more, far, cross, keep, dens, sends, *scratch
):
    core, x = where[0], where[1]
    def emit(h, in0, in1, act):
        place, at = (near, h) if h < NBQ // 4 else (near_more, h - NBQ // 4)
        place[pair_rows(at, 0), :] = in0.astype(BF)
        place[pair_rows(at, 1), :] = in1.astype(BF)
        emit_active(h, act, core, x, keep, sends)

    run_block(sbuf, (lt_ref, r_ref, bd_ref, d_ref), scratch, emit)
    dens[...] = density_of(scratch[6][...])
    wires = [split_wire(d[...]) for d in (dens1, dens2, dens)]
    for k, (msg, base) in enumerate(((near, INROWS // 2), (far, 0), (cross, 0))):
        for n, source in enumerate((sends1, sends2, sends)):
            msg[pl.ds(base + n * PER, PER), :] = source[k]
            msg[pl.ds(base + 3 * PER + n * NBQ, NBQ), :] = wires[n]


def fourth_kernel(
    where, sbuf, lt_ref, r_ref, bd_ref, d_ref, keep_in, keep, sends, dens, *scratch
):
    core, x = where[0], where[1]

    def emit(h, in0, in1, act):
        keep_in[pair_rows(h, 0), :] = in0
        keep_in[pair_rows(h, 1), :] = in1
        emit_active(h, act, core, x, keep, sends)

    run_block(sbuf, (lt_ref, r_ref, bd_ref, d_ref), scratch, emit)
    dens[...] = density_of(scratch[6][...])


def exchange_kernel(
    where, mine, near3, near3b, far1, sends, dens, near, far, cross, keep, whole
):
    parts = []
    for q in range(NBQ):
        rows = pl.ds(q * NACT, NACT)
        other = (near3 if q < NBQ // 2 else near3b)[pl.ds(q % (NBQ // 2) * NACT, NACT), :]
        parts.append(mine[rows, :] + other.astype(F32) + far1[rows, :].astype(F32))
    v = jnp.concatenate(parts, axis=1)
    v = v.astype(BF)
    total = lax.dot_general(v, v, (((1,), (1,)), ((), ())), preferred_element_type=F32)
    whole[...] = jnp.concatenate([total, total], axis=1)
    index = 2 * where[1] + where[0]
    keep[...] = whole[pl.ds(pl.multiple_of(index * QUARTER, QUARTER), QUARTER), :]
    wire = split_wire(dens[...])
    for k, msg in enumerate((near, far, cross)):
        msg[pl.ds(0, PER), :] = sends[k]
        msg[pl.ds(PER, NBQ), :] = wire
        at = pl.multiple_of((index ^ (k + 1)) * QUARTER, QUARTER)
        msg[pl.ds(PER + NBQ, QUARTER), :] = split_wire(whole[pl.ds(at, QUARTER), :])


def coulomb_kernel(
    keep1, keep2, keep3, keep4, dens1, dens2, dens3, dens4, exch,
    near3, far3, cross3, near4, far4, cross4, act, partial,
):
    first = low_half(QUARTER)
    early, late = (near3, far3, cross3), (near4, far4, cross4)
    total = jnp.zeros((QUARTER, LANES), F32)
    for m, (keep, dens) in enumerate(
        ((keep1, dens1), (keep2, dens2), (keep3, dens3), (keep4, dens4))
    ):
        rows, d = keep[...], dens[...]
        for k in (1, 2, 3):
            n = m ^ k
            msg = late[k - 1] if n == 3 else early[k - 1]
            base = INROWS // 2 if n < 3 and k == 1 else 0
            at, dens_at = (0, PER) if n == 3 else (base + n * PER, base + 3 * PER + n * NBQ)
            rows = rows + msg[pl.ds(at, PER), :].astype(F32)
            d = d + joined(msg[pl.ds(dens_at, NBQ), :])
        act[pl.ds(m * PER, PER), :] = rows
        for h in range(NBQ // 2):
            total = total + rows[h * QUARTER : (h + 1) * QUARTER] * jnp.where(
                first, d[2 * h : 2 * h + 1], d[2 * h + 1 : 2 * h + 2]
            )
    total = 2.0 * (total + pltpu.roll(total, BS, 1)) - exch[...]
    for msg in late:
        total = total - joined(msg[pl.ds(PER + NBQ, QUARTER), :])
    partial[...] = total[:, :BS]


def active_kernel(where, act, out):
    core, x = where[0], where[1]
    for n in range(4):
        xx = (1 - x) if n < 2 else x
        cc = (1 - core) if n % 2 == 0 else core
        base = NBQ * (2 * xx + cc)
        for h in range(NBQ // 2):
            a = act[pl.ds(n * PER + h * QUARTER, QUARTER), :]
            out[base + 2 * h] = a[:, :BS]
            out[base + 2 * h + 1] = a[:, BS:]


VM = pl.BlockSpec(memory_space=pltpu.VMEM)
SM = pl.BlockSpec(memory_space=pltpu.SMEM)
HB = pl.BlockSpec(memory_space=pltpu.HBM)

LAST_WORK = 10**9
PARAMS = pltpu.CompilerParams(vmem_limit_bytes=32 * 1024 * 1024)


def in_hbm(array):
    return pltpu.with_memory_space_constraint(array, pltpu.HBM)


def shape(dims, dtype):
    return jax.ShapeDtypeStruct(dims, dtype)


def sum_over_aux(part):
    n = lax.axis_size("aux")
    if n != 4:
        return lax.psum(part, "aux")
    for k in (1, 2):
        part = part + lax.ppermute(part, "aux", [(z, z ^ k) for z in range(n)])
    return part


def call(kernel, name, inputs, out_shape, scratch, args, work=0):
    return pl.pallas_call(
        kernel,
        name=name,
        in_specs=inputs,
        out_specs=[VM] * len(out_shape),
        out_shape=out_shape,
        scratch_shapes=scratch,
        compiler_params=PARAMS,
        cost_estimate=pl.CostEstimate(flops=work, bytes_accessed=10**5, transcendentals=0),
    )(*args)


def paired_body(slabs, block_row, block_col, live_count, orbitals, hcore):
    nslab, batch, width = slabs.shape
    index = lax.axis_index("pair")
    where = jnp.stack([lax.rem(index, 2), index // 2])
    aos = nslab * BS
    slabs = in_hbm(slabs)

    def to_peer(k, array):
        return lax.ppermute(array, "pair", [(p, p ^ k) for p in range(4)])

    loaded = shape((nslab // 2, 2, NBQ, width), BF)
    scratch = [pltpu.VMEM((MSTEP * BS, LANES), F32)] * 4 + [
        pltpu.VMEM((NBQ, NACT, aos), BF),
        pltpu.VMEM((aos, NBQ * BS), BF),
        pltpu.VMEM((NBQ, 8, LANES), F32),
    ]
    weights = (
        shape((NCOL, aos), BF),
        shape((aos, 2 * LANES), BF),
        shape((nslab // 4, 2 * PAIRED, 2 * PAIRED), BF),
        shape((nslab // 2, BS, PAIRED), F32),
    )
    kept = (
        shape((PER, LANES), F32), shape((3, PER, LANES), BF), shape((NBQ, LANES), F32),
    )
    work = 5 * 10**9
    lt, r, bd, d, msg1, keep1, sends1, dens1, slabs2, slabs3, slabs4 = call(
        first_kernel,
        "slabs_first",
        [SM, HB, HB, SM, HB, HB],
        weights + (shape((INROWS, LANES), BF),) + kept + (loaded,) * 3,
        [
            pltpu.SMEM((nslab,), jnp.int32), pltpu.SMEM((nslab,), jnp.int32),
            pltpu.VMEM(orbitals.T.shape, BF), pltpu.SemaphoreType.DMA((8,)),
            pltpu.VMEM(loaded.shape, BF), pltpu.SemaphoreType.DMA((4, nslab // 2)),
        ] + scratch,
        (
            where, in_hbm(block_row), in_hbm(block_col), live_count, slabs,
            in_hbm(orbitals.T),
        ),
        work,
    )
    near1 = to_peer(1, msg1)
    keep_in2, keep2, sends2, dens2 = call(
        second_kernel,
        "slabs_second",
        [SM] + [VM] * 5,
        (shape((INROWS, LANES), F32),) + kept,
        scratch,
        (where, slabs2, lt, r, bd, d),
        work,
    )
    out2 = (keep_in2 + near1.astype(F32)).astype(BF)
    out2, lt = lax.optimization_barrier((out2, lt))
    far1 = to_peer(2, out2)
    news = 3 * PER + 3 * NBQ
    msg3, msg3b, msg3x, msg3c, keep3, dens3 = call(
        third_kernel,
        "slabs_third",
        [SM] + [VM] * 9,
        (
            shape((INROWS // 2 + news, LANES), BF), shape((INROWS // 2, LANES), BF),
            shape((news, LANES), BF), shape((news, LANES), BF), kept[0], kept[2],
        ),
        [pltpu.VMEM((3, PER, LANES), BF)] + scratch,
        (where, slabs3, lt, r, bd, d, sends1, sends2, dens1, dens2),
        work,
    )
    near3, near3b = to_peer(1, msg3), to_peer(1, msg3b)
    far3, cross3 = to_peer(2, msg3x), to_peer(3, msg3c)
    keep_in4, keep4, sends4, dens4 = call(
        fourth_kernel,
        "slabs_fourth",
        [SM] + [VM] * 5,
        (shape((INROWS, LANES), F32),) + kept,
        scratch,
        (where, slabs4, lt, r, bd, d),
        LAST_WORK,
    )
    last = shape((PER + NBQ + QUARTER, LANES), BF)
    near4, far4, cross4, exch = call(
        exchange_kernel,
        "exchange",
        [SM] + [VM] * 6,
        (last,) * 3 + (shape((QUARTER, LANES), F32),),
        [pltpu.VMEM((NACT, LANES), F32)],
        (where, keep_in4, near3, near3b, far1, sends4, dens4),
    )
    far4, cross4, near4 = to_peer(2, far4), to_peer(3, cross4), to_peer(1, near4)
    act, partial = call(
        coulomb_kernel,
        "coulomb",
        [VM] * 15,
        (shape((4 * PER, LANES), F32), shape((QUARTER, NACT), F32)),
        [],
        (
            keep1, keep2, keep3, keep4, dens1, dens2, dens3, dens4, exch,
            near3, far3, cross3, near4, far4, cross4,
        ),
    )
    (active,) = call(
        active_kernel,
        "own_active",
        [SM, VM],
        (shape((batch, QUARTER, NACT), F32),),
        [],
        (where, act),
        10**6,
    )
    return (active, hcore + sum_over_aux(partial))


def slab_terms(values, left, right):
    half = jnp.einsum("mc,qmn->qnc", left, values, preferred_element_type=F32).astype(BF)
    first = jnp.einsum("qnt,nc->qtc", half[:, :, :NACT], right, preferred_element_type=F32)
    second = jnp.einsum("qnc,nt->qtc", half, right[:, :NACT], preferred_element_type=F32)
    trace = 2.0 * jnp.einsum(
        "qni,ni->q", half[:, :, NACT:], right[:, NACT:], preferred_element_type=F32
    )
    return (first + second, trace)


def general_body(slabs, block_row, block_col, live_count, orbitals, hcore):
    batch = slabs.shape[1]
    init = (jnp.zeros((batch, NACT, NCOL), F32), jnp.zeros((batch,), F32))

    def visit(k, state):
        values = lax.dynamic_index_in_dim(slabs, k, 0, keepdims=False)
        left = lax.dynamic_slice_in_dim(orbitals, block_row[k] * BS, BS, 0)
        right = lax.dynamic_slice_in_dim(orbitals, block_col[k] * BS, BS, 0)
        terms, trace = slab_terms(values.reshape(batch, BS, BS), left, right)
        return (state[0] + terms, state[1] + trace)

    vectors, density = lax.fori_loop(0, live_count[0], visit, init)
    density = lax.psum(density, "pair")
    owned = lax.psum_scatter(vectors, "pair", scatter_dimension=1, tiled=True)
    own_active, own_inactive = owned[:, :, :NACT], owned[:, :, NACT:]
    gathered = lax.all_gather(own_inactive.astype(BF), "pair", axis=1, tiled=True)
    exchange = jnp.einsum(
        "qti,qui->tu", own_inactive, gathered.astype(F32), precision=lax.Precision.HIGHEST
    )
    coulomb = jnp.einsum("qtu,q->tu", own_active, density, precision=lax.Precision.HIGHEST)
    return (own_active, hcore + lax.psum(2.0 * coulomb - exchange, "aux"))


def solution(mesh):
    placed = (
        P(("frag", "pair"), "aux", None),
        P(("frag", "pair")),
        P(("frag", "pair")),
        P(("frag", "pair")),
        P("frag", None),
        P(("frag", "pair"), None),
    )

    def body(slabs, *rest):
        fits = mesh.shape["pair"] == 4 and slabs.shape[1] == 4 * NBQ and slabs.shape[0] % 4 == 0
        return (paired_body if fits else general_body)(slabs, *rest)

    return jax.shard_map(
        body,
        mesh=mesh,
        in_specs=placed,
        out_specs=(P(("frag", "aux"), "pair", None), P(("frag", "pair"), None)),
        check_vma=False,
    )
```

```python
import jax
import jax.numpy as jnp
from jax import lax
from jax.experimental import pallas as pl
from jax.experimental.pallas import tpu as pltpu
from jax.sharding import PartitionSpec as P

BS = 64
NACT = 64
NCOL = 192
NIN = NCOL - NACT
LANES = 128
NBQ = 16
PAIRED = 2 * BS
QSTEP, MSTEP = 3, 49
BF = jnp.bfloat16
F32 = jnp.float32


def low_half(rows):
    return lax.broadcasted_iota(jnp.int32, (rows, LANES), 1) < BS


def orbital_pair(k, blocks, live, orbitals):
    halves = []
    for n in range(2):
        slot = 2 * k + n
        base = pl.multiple_of((blocks[slot] // 2) * PAIRED, PAIRED)
        w = orbitals[:, pl.ds(base, PAIRED)]
        w = jnp.concatenate([w[NACT:], w[:NACT]], axis=0)
        w = jnp.where(lax.rem(blocks[slot], 2) != n, pltpu.roll(w, BS, 1), w)
        halves.append(jnp.where(slot < live, w, jnp.zeros_like(w)))
    return jnp.where(low_half(NCOL), halves[0], halves[1])


def slab_copies(slabs_ref, sbuf, sem, block):
    return [
        pltpu.make_async_copy(
            slabs_ref.at[pl.ds(2 * k, 2), pl.ds(pl.multiple_of(block * NBQ, NBQ), NBQ), :],
            sbuf.at[k],
            sem.at[k],
        )
        for k in range(slabs_ref.shape[0] // 2)
    ]


def lanes_of(k):
    return pl.ds(k * PAIRED if isinstance(k, int) else pl.multiple_of(k * PAIRED, PAIRED), PAIRED)


def run_block(sbuf, weights, scratch, emit, prepare=None):
    lt_ref, r_ref, bd_ref, d_ref = weights
    pt_ref, q_ref, diag = scratch[4:]
    quads = sbuf.shape[0] // 2
    first = low_half(NBQ)
    first_s = low_half(BS)
    zero = jnp.zeros((BS, LANES), BF)
    group = 8

    def relayout(k, out):
        for j in range(sbuf.shape[3] // LANES):
            lanes = slice(j * LANES, (j + 1) * LANES)
            a = sbuf[k, 0, :, lanes]
            b = sbuf[k, 1, :, lanes]
            out[pl.ds(MSTEP * 2 * j, NBQ, stride=QSTEP), :] = jnp.where(
                first, a, pltpu.roll(b, BS, 1)
            ).astype(F32)
            out[pl.ds(MSTEP * (2 * j + 1), NBQ, stride=QSTEP), :] = jnp.where(
                first, pltpu.roll(a, BS, 1), b
            ).astype(F32)

    def transform(g, bufs):
        dens = [d_ref[2 * g + n] for n in range(2)]
        left = [lt_ref[NIN:, lanes_of(2 * g + n)] for n in range(2)]
        for q in range(0, NBQ, group):
            slabs = [[], []]
            for u in range(q, q + group):
                total = diag[u]
                for n in range(2):
                    s = bufs[n][pl.ds(u * QSTEP, BS, stride=MSTEP), :]
                    total = total + jnp.sum((s * dens[n]).reshape(BS // 8, 8, LANES), axis=0)
                    slabs[n].append(s.astype(BF))
                diag[u] = total
            for n in range(2):
                at = lanes_of(2 * g + n)
                cols = [
                    jnp.concatenate(
                        [jnp.where(first_s, s, zero), jnp.where(first_s, zero, s)], axis=0
                    )
                    for s in slabs[n]
                ]
                p = jnp.dot(
                    left[n], jnp.concatenate(cols, axis=1), preferred_element_type=F32
                ).astype(BF)
                for u in range(group):
                    pt_ref[q + u, :, at] = p[:, u * LANES : (u + 1) * LANES]
            rows = jnp.concatenate(
                [jnp.concatenate([s0, s1], axis=1) for s0, s1 in zip(*slabs)], axis=0
            )
            out = jnp.dot(rows, bd_ref[g], preferred_element_type=F32).astype(BF)
            for u in range(0, group, 2):
                for n in range(2):
                    lanes = slice(n * LANES, (n + 1) * LANES)
                    q0 = out[u * BS : (u + 1) * BS, lanes]
                    q1 = out[(u + 1) * BS : (u + 2) * BS, lanes]
                    at = slice((q + u) * BS, (q + u + 2) * BS)
                    row = lanes_of(2 * g + n).start
                    q_ref[pl.ds(row, BS), at] = jnp.where(first_s, q0, pltpu.roll(q1, BS, 1))
                    q_ref[pl.ds(row + BS, BS), at] = jnp.where(
                        first_s, pltpu.roll(q0, BS, 1), q1
                    )

    def second_transform(g):
        rows = pt_ref[4 * g : 4 * g + 4].reshape(4 * NACT, pt_ref.shape[2])
        one = jnp.dot(rows, r_ref[...], preferred_element_type=F32)
        two = jnp.dot(
            lt_ref[...], q_ref[:, 4 * g * BS : (4 * g + 4) * BS], preferred_element_type=F32
        )
        return one, two

    def assemble(g, both):
        one, two = both
        for p in range(2):
            w0 = one[2 * p * NACT : (2 * p + 1) * NACT]
            w1 = one[(2 * p + 1) * NACT : (2 * p + 2) * NACT]
            turned = two[:, p * LANES : (p + 1) * LANES]
            across = turned[:NIN].T
            square = jnp.concatenate([turned[NIN:], turned[NIN:]], axis=0).T
            emit(
                2 * g + p,
                w0[:, :NIN] + across[:NACT],
                w1[:, :NIN] + across[NACT:],
                jnp.where(first_s, w0[:, NIN:] + square[:NACT], w1[:, NIN:] + square[NACT:]),
            )

    def load(g, bufs):
        for n in range(2):
            relayout(2 * g + n, bufs[n])

    def two_quads(i, carry):
        one, two = scratch[:2], scratch[2:4]
        load(2 * i, one)
        prepare(2 * i)
        load(2 * i + 1, two)
        prepare(2 * i + 1)
        transform(2 * i, one)
        transform(2 * i + 1, two)
        return carry

    diag[...] = jnp.zeros_like(diag)
    if prepare is not None:
        lax.fori_loop(0, quads // 2, two_quads, 0)
    else:
        load(0, scratch[:2])
        for g in range(quads):
            if g + 1 < quads:
                load(g + 1, scratch[2 * ((g + 1) % 2) : 2 * ((g + 1) % 2) + 2])
            transform(g, scratch[2 * (g % 2) : 2 * (g % 2) + 2])
    whole = second_transform(0)
    for g in range(NBQ // 4):
        following = second_transform(g + 1) if g + 1 < NBQ // 4 else None
        assemble(g, whole)
        whole = following


def split_wire(d):
    hi = d.astype(BF).astype(F32)
    return jnp.where(low_half(d.shape[0]), hi, d - hi).astype(BF)


def joined(wire):
    w = wire.astype(F32)
    return w + pltpu.roll(w, BS, 1)


def density_of(diag):
    d = 2.0 * jnp.sum(jnp.sum(diag, axis=1), axis=1, keepdims=True)
    return jnp.broadcast_to(d, (NBQ, LANES))


QUARTER = NACT // 4
PER = NBQ // 2 * QUARTER
INROWS = NBQ * NACT


def emit_active(h, act, core, x, keep, sends):
    upper, lower = act[: 2 * QUARTER], act[2 * QUARTER :]
    near, far = jnp.where(x == 0, upper, lower), jnp.where(x == 0, lower, upper)
    at = pl.ds(h * QUARTER, QUARTER)
    for part, own, other in ((near, keep, sends.at[0]), (far, sends.at[1], sends.at[2])):
        one, two = part[:QUARTER], part[QUARTER:]
        own[at, :] = jnp.where(core == 0, one, two).astype(own.dtype)
        other[at, :] = jnp.where(core == 0, two, one).astype(BF)


def pair_rows(h, n):
    return pl.ds((2 * h + n) * NACT, NACT)


def first_kernel(
    where, rows_ref, cols_ref, live, slabs_ref, ot_ref,
    lt_out, r_out, bd_out, d_out, msg, keep, sends, dens, after2, after3, after4,
    rows, cols, orbitals, ssem, sbuf, sem, *scratch
):
    core, x = where[0], where[1]
    part = NACT // 2
    small = [
        pltpu.make_async_copy(src, dst, ssem.at[n])
        for n, (src, dst) in enumerate(((rows_ref, rows), (cols_ref, cols)))
    ] + [
        pltpu.make_async_copy(
            ot_ref.at[pl.ds(n * part, part)], orbitals.at[pl.ds(n * part, part)], ssem.at[2 + n]
        )
        for n in range(NCOL // part)
    ]
    blocks = (2 * (1 - x) + (1 - core), 2 * (1 - x) + core, 2 * x + (1 - core), 2 * x + core)
    now, *later = [
        slab_copies(slabs_ref, ref, sem.at[n], block)
        for n, (ref, block) in enumerate(zip((sbuf, after2, after3, after4), blocks))
    ]
    ahead = [copy for copies in later for copy in copies]
    for copy in small + now:
        copy.start()
    bd_out[...] = jnp.zeros_like(bd_out)
    for copy in small + now:
        copy.wait()
    for copy in ahead:
        copy.start()

    def prepare(g):
        for n in range(2):
            k = 2 * g + n
            left = orbital_pair(k, rows, live[0], orbitals)
            right = orbital_pair(k, cols, live[0], orbitals)
            at = lanes_of(k)
            lt_out[:, at] = left
            turned = jnp.concatenate([right, right[NIN:]], axis=0).astype(F32).T.astype(BF)
            r_out[at, :] = turned
            inner = (lax.broadcasted_iota(jnp.int32, (PAIRED, LANES), 0) < BS) == low_half(PAIRED)
            place = slice(n * PAIRED, (n + 1) * PAIRED)
            bd_out[g, place, place] = jnp.where(
                inner, turned[:, NIN:], jnp.zeros((PAIRED, LANES), BF)
            )
            both = jnp.dot(
                left[:NIN].astype(F32).T.astype(BF), right[:NIN], preferred_element_type=F32
            )
            d_out[k] = jnp.where(low_half(BS), both[:BS], both[BS:])

    def emit(h, in0, in1, act):
        msg[pair_rows(h, 0), :] = in0.astype(BF)
        msg[pair_rows(h, 1), :] = in1.astype(BF)
        emit_active(h, act, core, x, keep, sends)

    run_block(sbuf, (lt_out, r_out, bd_out, d_out), scratch, emit, prepare)
    dens[...] = density_of(scratch[6][...])
    for copy in ahead:
        copy.wait()


def second_kernel(
    where, sbuf, lt_ref, r_ref, bd_ref, d_ref, keep_in, keep, sends, dens, *scratch
):
    core, x = where[0], where[1]
    def emit(h, in0, in1, act):
        keep_in[pair_rows(h, 0), :] = in0
        keep_in[pair_rows(h, 1), :] = in1
        emit_active(h, act, core, x, keep, sends)

    run_block(sbuf, (lt_ref, r_ref, bd_ref, d_ref), scratch, emit)
    dens[...] = density_of(scratch[6][...])


def third_kernel(
    where, sbuf, lt_ref, r_ref, bd_ref, d_ref, sends1, sends2, dens1, dens2,
    near, near_more, far, cross, keep, dens, sends, *scratch
):
    core, x = where[0], where[1]
    def emit(h, in0, in1, act):
        place, at = (near, h) if h < NBQ // 4 else (near_more, h - NBQ // 4)
        place[pair_rows(at, 0), :] = in0.astype(BF)
        place[pair_rows(at, 1), :] = in1.astype(BF)
        emit_active(h, act, core, x, keep, sends)

    run_block(sbuf, (lt_ref, r_ref, bd_ref, d_ref), scratch, emit)
    dens[...] = density_of(scratch[6][...])
    wires = [split_wire(d[...]) for d in (dens1, dens2, dens)]
    for k, (msg, base) in enumerate(((near, INROWS // 2), (far, 0), (cross, 0))):
        for n, source in enumerate((sends1, sends2, sends)):
            msg[pl.ds(base + n * PER, PER), :] = source[k]
            msg[pl.ds(base + 3 * PER + n * NBQ, NBQ), :] = wires[n]


def fourth_kernel(
    where, sbuf, lt_ref, r_ref, bd_ref, d_ref, keep_in, keep, sends, dens, *scratch
):
    core, x = where[0], where[1]

    def emit(h, in0, in1, act):
        keep_in[pair_rows(h, 0), :] = in0
        keep_in[pair_rows(h, 1), :] = in1
        emit_active(h, act, core, x, keep, sends)

    run_block(sbuf, (lt_ref, r_ref, bd_ref, d_ref), scratch, emit)
    dens[...] = density_of(scratch[6][...])


def exchange_kernel(
    where, mine, near3, near3b, far1, sends, dens, near, far, cross, keep, whole
):
    parts = []
    for q in range(NBQ):
        rows = pl.ds(q * NACT, NACT)
        other = (near3 if q < NBQ // 2 else near3b)[pl.ds(q % (NBQ // 2) * NACT, NACT), :]
        parts.append(mine[rows, :] + other.astype(F32) + far1[rows, :].astype(F32))
    v = jnp.concatenate(parts, axis=1)
    v = v.astype(BF)
    total = lax.dot_general(v, v, (((1,), (1,)), ((), ())), preferred_element_type=F32)
    whole[...] = jnp.concatenate([total, total], axis=1)
    index = 2 * where[1] + where[0]
    keep[...] = whole[pl.ds(pl.multiple_of(index * QUARTER, QUARTER), QUARTER), :]
    wire = split_wire(dens[...])
    for k, msg in enumerate((near, far, cross)):
        msg[pl.ds(0, PER), :] = sends[k]
        msg[pl.ds(PER, NBQ), :] = wire
        at = pl.multiple_of((index ^ (k + 1)) * QUARTER, QUARTER)
        msg[pl.ds(PER + NBQ, QUARTER), :] = split_wire(whole[pl.ds(at, QUARTER), :])


def coulomb_kernel(
    keep1, keep2, keep3, keep4, dens1, dens2, dens3, dens4, exch,
    near3, far3, cross3, near4, far4, cross4, act, partial,
):
    first = low_half(QUARTER)
    early, late = (near3, far3, cross3), (near4, far4, cross4)
    total = jnp.zeros((QUARTER, LANES), F32)
    for m, (keep, dens) in enumerate(
        ((keep1, dens1), (keep2, dens2), (keep3, dens3), (keep4, dens4))
    ):
        rows, d = keep[...], dens[...]
        for k in (1, 2, 3):
            n = m ^ k
            msg = late[k - 1] if n == 3 else early[k - 1]
            base = INROWS // 2 if n < 3 and k == 1 else 0
            at, dens_at = (0, PER) if n == 3 else (base + n * PER, base + 3 * PER + n * NBQ)
            rows = rows + msg[pl.ds(at, PER), :].astype(F32)
            d = d + joined(msg[pl.ds(dens_at, NBQ), :])
        act[pl.ds(m * PER, PER), :] = rows
        for h in range(NBQ // 2):
            total = total + rows[h * QUARTER : (h + 1) * QUARTER] * jnp.where(
                first, d[2 * h : 2 * h + 1], d[2 * h + 1 : 2 * h + 2]
            )
    total = 2.0 * (total + pltpu.roll(total, BS, 1)) - exch[...]
    for msg in late:
        total = total - joined(msg[pl.ds(PER + NBQ, QUARTER), :])
    partial[...] = total[:, :BS]


def active_kernel(where, act, out):
    core, x = where[0], where[1]
    for n in range(4):
        xx = (1 - x) if n < 2 else x
        cc = (1 - core) if n % 2 == 0 else core
        base = NBQ * (2 * xx + cc)
        for h in range(NBQ // 2):
            a = act[pl.ds(n * PER + h * QUARTER, QUARTER), :]
            out[base + 2 * h] = a[:, :BS]
            out[base + 2 * h + 1] = a[:, BS:]


VM = pl.BlockSpec(memory_space=pltpu.VMEM)
SM = pl.BlockSpec(memory_space=pltpu.SMEM)
HB = pl.BlockSpec(memory_space=pltpu.HBM)

LAST_WORK = 10**9
PARAMS = pltpu.CompilerParams(vmem_limit_bytes=32 * 1024 * 1024)


def in_hbm(array):
    return pltpu.with_memory_space_constraint(array, pltpu.HBM)


def shape(dims, dtype):
    return jax.ShapeDtypeStruct(dims, dtype)


def sum_over_aux(part):
    n = lax.axis_size("aux")
    if n != 4:
        return lax.psum(part, "aux")
    for k in (1, 2):
        part = part + lax.ppermute(part, "aux", [(z, z ^ k) for z in range(n)])
    return part


def call(kernel, name, inputs, out_shape, scratch, args, work=0):
    return pl.pallas_call(
        kernel,
        name=name,
        in_specs=inputs,
        out_specs=[VM] * len(out_shape),
        out_shape=out_shape,
        scratch_shapes=scratch,
        compiler_params=PARAMS,
        cost_estimate=pl.CostEstimate(flops=work, bytes_accessed=10**5, transcendentals=0),
    )(*args)


def paired_body(slabs, block_row, block_col, live_count, orbitals, hcore):
    nslab, batch, width = slabs.shape
    index = lax.axis_index("pair")
    where = jnp.stack([lax.rem(index, 2), index // 2])
    aos = nslab * BS
    slabs = in_hbm(slabs)

    def to_peer(k, array):
        return lax.ppermute(array, "pair", [(p, p ^ k) for p in range(4)])

    loaded = shape((nslab // 2, 2, NBQ, width), BF)
    scratch = [pltpu.VMEM((MSTEP * BS, LANES), F32)] * 4 + [
        pltpu.VMEM((NBQ, NACT, aos), BF),
        pltpu.VMEM((aos, NBQ * BS), BF),
        pltpu.VMEM((NBQ, 8, LANES), F32),
    ]
    weights = (
        shape((NCOL, aos), BF),
        shape((aos, 2 * LANES), BF),
        shape((nslab // 4, 2 * PAIRED, 2 * PAIRED), BF),
        shape((nslab // 2, BS, PAIRED), F32),
    )
    kept = (
        shape((PER, LANES), F32), shape((3, PER, LANES), BF), shape((NBQ, LANES), F32),
    )
    work = 5 * 10**9
    lt, r, bd, d, msg1, keep1, sends1, dens1, slabs2, slabs3, slabs4 = call(
        first_kernel,
        "slabs_first",
        [SM, HB, HB, SM, HB, HB],
        weights + (shape((INROWS, LANES), BF),) + kept + (loaded,) * 3,
        [
            pltpu.SMEM((nslab,), jnp.int32), pltpu.SMEM((nslab,), jnp.int32),
            pltpu.VMEM(orbitals.T.shape, BF), pltpu.SemaphoreType.DMA((8,)),
            pltpu.VMEM(loaded.shape, BF), pltpu.SemaphoreType.DMA((4, nslab // 2)),
        ] + scratch,
        (
            where, in_hbm(block_row), in_hbm(block_col), live_count, slabs,
            in_hbm(orbitals.T),
        ),
        work,
    )
    near1 = to_peer(1, msg1)
    keep_in2, keep2, sends2, dens2 = call(
        second_kernel,
        "slabs_second",
        [SM] + [VM] * 5,
        (shape((INROWS, LANES), F32),) + kept,
        scratch,
        (where, slabs2, lt, r, bd, d),
        work,
    )
    out2 = (keep_in2 + near1.astype(F32)).astype(BF)
    out2, lt = lax.optimization_barrier((out2, lt))
    far1 = to_peer(2, out2)
    news = 3 * PER + 3 * NBQ
    msg3, msg3b, msg3x, msg3c, keep3, dens3 = call(
        third_kernel,
        "slabs_third",
        [SM] + [VM] * 9,
        (
            shape((INROWS // 2 + news, LANES), BF), shape((INROWS // 2, LANES), BF),
            shape((news, LANES), BF), shape((news, LANES), BF), kept[0], kept[2],
        ),
        [pltpu.VMEM((3, PER, LANES), BF)] + scratch,
        (where, slabs3, lt, r, bd, d, sends1, sends2, dens1, dens2),
        work,
    )
    near3, near3b = to_peer(1, msg3), to_peer(1, msg3b)
    far3, cross3 = to_peer(2, msg3x), to_peer(3, msg3c)
    keep_in4, keep4, sends4, dens4 = call(
        fourth_kernel,
        "slabs_fourth",
        [SM] + [VM] * 5,
        (shape((INROWS, LANES), F32),) + kept,
        scratch,
        (where, slabs4, lt, r, bd, d),
        LAST_WORK,
    )
    last = shape((PER + NBQ + QUARTER, LANES), BF)
    near4, far4, cross4, exch = call(
        exchange_kernel,
        "exchange",
        [SM] + [VM] * 6,
        (last,) * 3 + (shape((QUARTER, LANES), F32),),
        [pltpu.VMEM((NACT, LANES), F32)],
        (where, keep_in4, near3, near3b, far1, sends4, dens4),
    )
    far4, cross4, near4 = to_peer(2, far4), to_peer(3, cross4), to_peer(1, near4)
    act, partial = call(
        coulomb_kernel,
        "coulomb",
        [VM] * 15,
        (shape((4 * PER, LANES), F32), shape((QUARTER, NACT), F32)),
        [],
        (
            keep1, keep2, keep3, keep4, dens1, dens2, dens3, dens4, exch,
            near3, far3, cross3, near4, far4, cross4,
        ),
    )
    (active,) = call(
        active_kernel,
        "own_active",
        [SM, VM],
        (shape((batch, QUARTER, NACT), F32),),
        [],
        (where, act),
        10**6,
    )
    return (active, hcore + sum_over_aux(partial))


def slab_terms(values, left, right):
    half = jnp.einsum("mc,qmn->qnc", left, values, preferred_element_type=F32).astype(BF)
    first = jnp.einsum("qnt,nc->qtc", half[:, :, :NACT], right, preferred_element_type=F32)
    second = jnp.einsum("qnc,nt->qtc", half, right[:, :NACT], preferred_element_type=F32)
    trace = 2.0 * jnp.einsum(
        "qni,ni->q", half[:, :, NACT:], right[:, NACT:], preferred_element_type=F32
    )
    return (first + second, trace)


def general_body(slabs, block_row, block_col, live_count, orbitals, hcore):
    batch = slabs.shape[1]
    init = (jnp.zeros((batch, NACT, NCOL), F32), jnp.zeros((batch,), F32))

    def visit(k, state):
        values = lax.dynamic_index_in_dim(slabs, k, 0, keepdims=False)
        left = lax.dynamic_slice_in_dim(orbitals, block_row[k] * BS, BS, 0)
        right = lax.dynamic_slice_in_dim(orbitals, block_col[k] * BS, BS, 0)
        terms, trace = slab_terms(values.reshape(batch, BS, BS), left, right)
        return (state[0] + terms, state[1] + trace)

    vectors, density = lax.fori_loop(0, live_count[0], visit, init)
    density = lax.psum(density, "pair")
    owned = lax.psum_scatter(vectors, "pair", scatter_dimension=1, tiled=True)
    own_active, own_inactive = owned[:, :, :NACT], owned[:, :, NACT:]
    gathered = lax.all_gather(own_inactive.astype(BF), "pair", axis=1, tiled=True)
    exchange = jnp.einsum(
        "qti,qui->tu", own_inactive, gathered.astype(F32), precision=lax.Precision.HIGHEST
    )
    coulomb = jnp.einsum("qtu,q->tu", own_active, density, precision=lax.Precision.HIGHEST)
    return (own_active, hcore + lax.psum(2.0 * coulomb - exchange, "aux"))


def solution(mesh):
    placed = (
        P(("frag", "pair"), "aux", None),
        P(("frag", "pair")),
        P(("frag", "pair")),
        P(("frag", "pair")),
        P("frag", None),
        P(("frag", "pair"), None),
    )

    def body(slabs, *rest):
        fits = mesh.shape["pair"] == 4 and slabs.shape[1] == 4 * NBQ and slabs.shape[0] % 4 == 0
        return (paired_body if fits else general_body)(slabs, *rest)

    return jax.shard_map(
        body,
        mesh=mesh,
        in_specs=placed,
        out_specs=(P(("frag", "aux"), "pair", None), P(("frag", "pair"), None)),
        check_vma=False,
    )
```

```python
import jax
import jax.numpy as jnp
from jax import lax
from jax.experimental import pallas as pl
from jax.experimental.pallas import tpu as pltpu
from jax.sharding import PartitionSpec as P

BS = 64
NACT = 64
NCOL = 192
NIN = NCOL - NACT
LANES = 128
NBQ = 16
PAIRED = 2 * BS
QSTEP, MSTEP = 3, 49
BF = jnp.bfloat16
F32 = jnp.float32


def low_half(rows):
    return lax.broadcasted_iota(jnp.int32, (rows, LANES), 1) < BS


def orbital_pair(k, blocks, live, orbitals):
    halves = []
    for n in range(2):
        slot = 2 * k + n
        base = pl.multiple_of((blocks[slot] // 2) * PAIRED, PAIRED)
        w = orbitals[:, pl.ds(base, PAIRED)]
        w = jnp.concatenate([w[NACT:], w[:NACT]], axis=0)
        w = jnp.where(lax.rem(blocks[slot], 2) != n, pltpu.roll(w, BS, 1), w)
        halves.append(jnp.where(slot < live, w, jnp.zeros_like(w)))
    return jnp.where(low_half(NCOL), halves[0], halves[1])


def slab_copies(slabs_ref, sbuf, sem, block):
    return [
        pltpu.make_async_copy(
            slabs_ref.at[pl.ds(2 * k, 2), pl.ds(pl.multiple_of(block * NBQ, NBQ), NBQ), :],
            sbuf.at[k],
            sem.at[k],
        )
        for k in range(slabs_ref.shape[0] // 2)
    ]


def lanes_of(k):
    return pl.ds(k * PAIRED if isinstance(k, int) else pl.multiple_of(k * PAIRED, PAIRED), PAIRED)


def run_block(sbuf, weights, scratch, emit, prepare=None, arrive=None):
    lt_ref, r_ref, bd_ref, d_ref = weights
    pt_ref, q_ref, diag = scratch[4:]
    quads = sbuf.shape[0] // 2
    first = low_half(NBQ)
    first_s = low_half(BS)
    zero = jnp.zeros((BS, LANES), BF)
    group = 8

    def relayout(k, out):
        for j in range(sbuf.shape[3] // LANES):
            lanes = slice(j * LANES, (j + 1) * LANES)
            a = sbuf[k, 0, :, lanes]
            b = sbuf[k, 1, :, lanes]
            out[pl.ds(MSTEP * 2 * j, NBQ, stride=QSTEP), :] = jnp.where(
                first, a, pltpu.roll(b, BS, 1)
            ).astype(F32)
            out[pl.ds(MSTEP * (2 * j + 1), NBQ, stride=QSTEP), :] = jnp.where(
                first, pltpu.roll(a, BS, 1), b
            ).astype(F32)

    def transform(g, bufs):
        dens = [d_ref[2 * g + n] for n in range(2)]
        left = [lt_ref[NIN:, lanes_of(2 * g + n)] for n in range(2)]
        for q in range(0, NBQ, group):
            slabs = [[], []]
            for u in range(q, q + group):
                total = diag[u]
                for n in range(2):
                    s = bufs[n][pl.ds(u * QSTEP, BS, stride=MSTEP), :]
                    total = total + jnp.sum((s * dens[n]).reshape(BS // 8, 8, LANES), axis=0)
                    slabs[n].append(s.astype(BF))
                diag[u] = total
            for n in range(2):
                at = lanes_of(2 * g + n)
                cols = [
                    jnp.concatenate(
                        [jnp.where(first_s, s, zero), jnp.where(first_s, zero, s)], axis=0
                    )
                    for s in slabs[n]
                ]
                p = jnp.dot(
                    left[n], jnp.concatenate(cols, axis=1), preferred_element_type=F32
                ).astype(BF)
                for u in range(group):
                    pt_ref[q + u, :, at] = p[:, u * LANES : (u + 1) * LANES]
            rows = jnp.concatenate(
                [jnp.concatenate([s0, s1], axis=1) for s0, s1 in zip(*slabs)], axis=0
            )
            out = jnp.dot(rows, bd_ref[g], preferred_element_type=F32).astype(BF)
            for u in range(0, group, 2):
                for n in range(2):
                    lanes = slice(n * LANES, (n + 1) * LANES)
                    q0 = out[u * BS : (u + 1) * BS, lanes]
                    q1 = out[(u + 1) * BS : (u + 2) * BS, lanes]
                    at = slice((q + u) * BS, (q + u + 2) * BS)
                    row = lanes_of(2 * g + n).start
                    q_ref[pl.ds(row, BS), at] = jnp.where(first_s, q0, pltpu.roll(q1, BS, 1))
                    q_ref[pl.ds(row + BS, BS), at] = jnp.where(
                        first_s, pltpu.roll(q0, BS, 1), q1
                    )

    def second_transform(g):
        rows = pt_ref[4 * g : 4 * g + 4].reshape(4 * NACT, pt_ref.shape[2])
        one = jnp.dot(rows, r_ref[...], preferred_element_type=F32)
        two = jnp.dot(
            lt_ref[...], q_ref[:, 4 * g * BS : (4 * g + 4) * BS], preferred_element_type=F32
        )
        return one, two

    def assemble(g, both):
        one, two = both
        for p in range(2):
            w0 = one[2 * p * NACT : (2 * p + 1) * NACT]
            w1 = one[(2 * p + 1) * NACT : (2 * p + 2) * NACT]
            turned = two[:, p * LANES : (p + 1) * LANES]
            across = turned[:NIN].T
            square = jnp.concatenate([turned[NIN:], turned[NIN:]], axis=0).T
            emit(
                2 * g + p,
                w0[:, :NIN] + across[:NACT],
                w1[:, :NIN] + across[NACT:],
                jnp.where(first_s, w0[:, NIN:] + square[:NACT], w1[:, NIN:] + square[NACT:]),
            )

    def load(g, bufs):
        for n in range(2):
            relayout(2 * g + n, bufs[n])

    def two_quads(i, carry):
        one, two = scratch[:2], scratch[2:4]
        pl.when(i > 0)(arrive)
        load(2 * i, one)
        prepare(2 * i)
        load(2 * i + 1, two)
        prepare(2 * i + 1)
        transform(2 * i, one)
        transform(2 * i + 1, two)
        return carry

    diag[...] = jnp.zeros_like(diag)
    if prepare is not None:
        lax.fori_loop(0, quads // 2, two_quads, 0)
    else:
        load(0, scratch[:2])
        for g in range(quads):
            if g + 1 < quads:
                load(g + 1, scratch[2 * ((g + 1) % 2) : 2 * ((g + 1) % 2) + 2])
            transform(g, scratch[2 * (g % 2) : 2 * (g % 2) + 2])
    whole = second_transform(0)
    for g in range(NBQ // 4):
        following = second_transform(g + 1) if g + 1 < NBQ // 4 else None
        assemble(g, whole)
        whole = following


def split_wire(d):
    hi = d.astype(BF).astype(F32)
    return jnp.where(low_half(d.shape[0]), hi, d - hi).astype(BF)


def joined(wire):
    w = wire.astype(F32)
    return w + pltpu.roll(w, BS, 1)


def density_of(diag):
    d = 2.0 * jnp.sum(jnp.sum(diag, axis=1), axis=1, keepdims=True)
    return jnp.broadcast_to(d, (NBQ, LANES))


QUARTER = NACT // 4
PER = NBQ // 2 * QUARTER
INROWS = NBQ * NACT
LAST = PER + NBQ + QUARTER


def emit_active(h, act, core, x, keep, sends):
    upper, lower = act[: 2 * QUARTER], act[2 * QUARTER :]
    near, far = jnp.where(x == 0, upper, lower), jnp.where(x == 0, lower, upper)
    at = pl.ds(h * QUARTER, QUARTER)
    for part, own, other in ((near, keep, sends.at[0]), (far, sends.at[1], sends.at[2])):
        one, two = part[:QUARTER], part[QUARTER:]
        own[at, :] = jnp.where(core == 0, one, two).astype(own.dtype)
        other[at, :] = jnp.where(core == 0, two, one).astype(BF)


def pair_rows(h, n):
    return pl.ds((2 * h + n) * NACT, NACT)


def first_kernel(
    where, rows_ref, cols_ref, live, slabs_ref, ot_ref,
    lt_out, r_out, bd_out, d_out, msg, keep, sends, dens, after2, after3, after4,
    rows, cols, orbitals, ssem, sbuf, sem, *scratch
):
    core, x = where[0], where[1]
    part = NACT // 2
    small = [
        pltpu.make_async_copy(src, dst, ssem.at[n])
        for n, (src, dst) in enumerate(((rows_ref, rows), (cols_ref, cols)))
    ] + [
        pltpu.make_async_copy(
            ot_ref.at[pl.ds(n * part, part)], orbitals.at[pl.ds(n * part, part)], ssem.at[2 + n]
        )
        for n in range(NCOL // part)
    ]
    blocks = (2 * (1 - x) + (1 - core), 2 * (1 - x) + core, 2 * x + (1 - core), 2 * x + core)
    now, *later = [
        slab_copies(slabs_ref, ref, sem.at[n], block)
        for n, (ref, block) in enumerate(zip((sbuf, after2, after3, after4), blocks))
    ]
    ahead = [copy for copies in later for copy in copies]
    for copy in small + now:
        copy.start()
    bd_out[...] = jnp.zeros_like(bd_out)
    for copy in small + now[: len(now) // 2]:
        copy.wait()
    for copy in ahead:
        copy.start()

    def arrive():
        for copy in now[len(now) // 2 :]:
            copy.wait()

    def prepare(g):
        for n in range(2):
            k = 2 * g + n
            left = orbital_pair(k, rows, live[0], orbitals)
            right = orbital_pair(k, cols, live[0], orbitals)
            at = lanes_of(k)
            lt_out[:, at] = left
            turned = jnp.concatenate([right, right[NIN:]], axis=0).astype(F32).T.astype(BF)
            r_out[at, :] = turned
            inner = (lax.broadcasted_iota(jnp.int32, (PAIRED, LANES), 0) < BS) == low_half(PAIRED)
            place = slice(n * PAIRED, (n + 1) * PAIRED)
            bd_out[g, place, place] = jnp.where(
                inner, turned[:, NIN:], jnp.zeros((PAIRED, LANES), BF)
            )
            both = jnp.dot(
                left[:NIN].astype(F32).T.astype(BF), right[:NIN], preferred_element_type=F32
            )
            d_out[k] = jnp.where(low_half(BS), both[:BS], both[BS:])

    def emit(h, in0, in1, act):
        msg[pair_rows(h, 0), :] = in0.astype(BF)
        msg[pair_rows(h, 1), :] = in1.astype(BF)
        emit_active(h, act, core, x, keep, sends)

    run_block(sbuf, (lt_out, r_out, bd_out, d_out), scratch, emit, prepare, arrive)
    dens[...] = density_of(scratch[6][...])
    for copy in ahead:
        copy.wait()


def second_kernel(
    where, sbuf, lt_ref, r_ref, bd_ref, d_ref, keep_in, keep, sends, dens, *scratch
):
    core, x = where[0], where[1]
    def emit(h, in0, in1, act):
        keep_in[pair_rows(h, 0), :] = in0
        keep_in[pair_rows(h, 1), :] = in1
        emit_active(h, act, core, x, keep, sends)

    run_block(sbuf, (lt_ref, r_ref, bd_ref, d_ref), scratch, emit)
    dens[...] = density_of(scratch[6][...])


def third_kernel(
    where, sbuf, lt_ref, r_ref, bd_ref, d_ref, sends1, sends2, dens1, dens2,
    near, near_more, far, keep, dens, sends, *scratch
):
    core, x = where[0], where[1]
    def emit(h, in0, in1, act):
        place, at = (near, h) if h < NBQ // 4 else (near_more, h - NBQ // 4)
        place[pair_rows(at, 0), :] = in0.astype(BF)
        place[pair_rows(at, 1), :] = in1.astype(BF)
        emit_active(h, act, core, x, keep, sends)

    run_block(sbuf, (lt_ref, r_ref, bd_ref, d_ref), scratch, emit)
    dens[...] = density_of(scratch[6][...])
    wires = [split_wire(d[...]) for d in (dens1, dens2, dens)]
    for n, source in enumerate((sends1, sends2, sends)):
        near_more[pl.ds(INROWS // 2 + n * PER, PER), :] = source[2]
    for k, (msg, base) in enumerate(((near, INROWS // 2), (far, 0))):
        for n, source in enumerate((sends1, sends2, sends)):
            msg[pl.ds(base + n * PER, PER), :] = source[k]
            msg[pl.ds(base + 3 * PER + n * NBQ, NBQ), :] = wires[n]


def fourth_kernel(
    where, sbuf, lt_ref, r_ref, bd_ref, d_ref, keep_in, keep, sends, dens, *scratch
):
    core, x = where[0], where[1]

    def emit(h, in0, in1, act):
        keep_in[pair_rows(h, 0), :] = in0
        keep_in[pair_rows(h, 1), :] = in1
        emit_active(h, act, core, x, keep, sends)

    run_block(sbuf, (lt_ref, r_ref, bd_ref, d_ref), scratch, emit)
    dens[...] = density_of(scratch[6][...])


def exchange_kernel(
    where, mine, near3, near3b, far1, sends, dens, near, far, cross, keep, whole
):
    parts = []
    for q in range(NBQ):
        rows = pl.ds(q * NACT, NACT)
        other = (near3 if q < NBQ // 2 else near3b)[pl.ds(q % (NBQ // 2) * NACT, NACT), :]
        parts.append(mine[rows, :] + other.astype(F32) + far1[rows, :].astype(F32))
    v = jnp.concatenate(parts, axis=1)
    v = v.astype(BF)
    total = lax.dot_general(v, v, (((1,), (1,)), ((), ())), preferred_element_type=F32)
    whole[...] = jnp.concatenate([total, total], axis=1)
    index = 2 * where[1] + where[0]
    keep[...] = whole[pl.ds(pl.multiple_of(index * QUARTER, QUARTER), QUARTER), :]
    wire = split_wire(dens[...])
    for k, msg in enumerate((near, far, cross)):
        rows = sends[k]
        if k == 1:
            passed = near3b[pl.ds(INROWS // 2 + 2 * PER, PER), :]
            rows = (rows.astype(F32) + passed.astype(F32)).astype(BF)
        msg[pl.ds(0, PER), :] = rows
        msg[pl.ds(PER, NBQ), :] = wire
        at = pl.multiple_of((index ^ (k + 1)) * QUARTER, QUARTER)
        msg[pl.ds(PER + NBQ, QUARTER), :] = split_wire(whole[pl.ds(at, QUARTER), :])
    far[pl.ds(LAST, 2 * PER), :] = near3b[pl.ds(INROWS // 2, 2 * PER), :]
    far[pl.ds(LAST + 2 * PER, 3 * NBQ), :] = near3[pl.ds(INROWS // 2 + 3 * PER, 3 * NBQ), :]


def coulomb_kernel(
    keep1, keep2, keep3, keep4, dens1, dens2, dens3, dens4, exch,
    near3, far3, near4, far4, cross4, act, partial,
):
    first = low_half(QUARTER)
    early, late = (near3, far3, far4), (near4, far4, cross4)
    total = jnp.zeros((QUARTER, LANES), F32)
    for m, (keep, dens) in enumerate(
        ((keep1, dens1), (keep2, dens2), (keep3, dens3), (keep4, dens4))
    ):
        rows, d = keep[...], dens[...]
        for k in (1, 2, 3):
            n = m ^ k
            msg = late[k - 1] if n == 3 else early[k - 1]
            if n == 3:
                at, dens_at = 0, PER
            elif k == 3:
                at, dens_at = LAST + n * PER, LAST + 2 * PER + n * NBQ
            else:
                base = INROWS // 2 if k == 1 else 0
                at, dens_at = base + n * PER, base + 3 * PER + n * NBQ
            if not (k == 3 and n == 2):
                rows = rows + msg[pl.ds(at, PER), :].astype(F32)
            d = d + joined(msg[pl.ds(dens_at, NBQ), :])
        act[pl.ds(m * PER, PER), :] = rows
        for h in range(NBQ // 2):
            total = total + rows[h * QUARTER : (h + 1) * QUARTER] * jnp.where(
                first, d[2 * h : 2 * h + 1], d[2 * h + 1 : 2 * h + 2]
            )
    total = 2.0 * (total + pltpu.roll(total, BS, 1)) - exch[...]
    for msg in late:
        total = total - joined(msg[pl.ds(PER + NBQ, QUARTER), :])
    partial[...] = total[:, :BS]


def active_kernel(where, act, out):
    core, x = where[0], where[1]
    for n in range(4):
        xx = (1 - x) if n < 2 else x
        cc = (1 - core) if n % 2 == 0 else core
        base = NBQ * (2 * xx + cc)
        for h in range(NBQ // 2):
            a = act[pl.ds(n * PER + h * QUARTER, QUARTER), :]
            out[base + 2 * h] = a[:, :BS]
            out[base + 2 * h + 1] = a[:, BS:]


VM = pl.BlockSpec(memory_space=pltpu.VMEM)
SM = pl.BlockSpec(memory_space=pltpu.SMEM)
HB = pl.BlockSpec(memory_space=pltpu.HBM)

LAST_WORK = 10**9
PARAMS = pltpu.CompilerParams(vmem_limit_bytes=32 * 1024 * 1024)


def in_hbm(array):
    return pltpu.with_memory_space_constraint(array, pltpu.HBM)


def shape(dims, dtype):
    return jax.ShapeDtypeStruct(dims, dtype)


def sum_over_aux(part):
    n = lax.axis_size("aux")
    if n != 4:
        return lax.psum(part, "aux")
    for k in (1, 2):
        part = part + lax.ppermute(part, "aux", [(z, z ^ k) for z in range(n)])
    return part


def call(kernel, name, inputs, out_shape, scratch, args, work=0):
    return pl.pallas_call(
        kernel,
        name=name,
        in_specs=inputs,
        out_specs=[VM] * len(out_shape),
        out_shape=out_shape,
        scratch_shapes=scratch,
        compiler_params=PARAMS,
        cost_estimate=pl.CostEstimate(flops=work, bytes_accessed=10**5, transcendentals=0),
    )(*args)


def paired_body(slabs, block_row, block_col, live_count, orbitals, hcore):
    nslab, batch, width = slabs.shape
    index = lax.axis_index("pair")
    where = jnp.stack([lax.rem(index, 2), index // 2])
    aos = nslab * BS
    slabs = in_hbm(slabs)

    def to_peer(k, array):
        return lax.ppermute(array, "pair", [(p, p ^ k) for p in range(4)])

    loaded = shape((nslab // 2, 2, NBQ, width), BF)
    scratch = [pltpu.VMEM((MSTEP * BS, LANES), F32)] * 4 + [
        pltpu.VMEM((NBQ, NACT, aos), BF),
        pltpu.VMEM((aos, NBQ * BS), BF),
        pltpu.VMEM((NBQ, 8, LANES), F32),
    ]
    weights = (
        shape((NCOL, aos), BF),
        shape((aos, 2 * LANES), BF),
        shape((nslab // 4, 2 * PAIRED, 2 * PAIRED), BF),
        shape((nslab // 2, BS, PAIRED), F32),
    )
    kept = (
        shape((PER, LANES), F32), shape((3, PER, LANES), BF), shape((NBQ, LANES), F32),
    )
    work = 5 * 10**9
    lt, r, bd, d, msg1, keep1, sends1, dens1, slabs2, slabs3, slabs4 = call(
        first_kernel,
        "slabs_first",
        [SM, HB, HB, SM, HB, HB],
        weights + (shape((INROWS, LANES), BF),) + kept + (loaded,) * 3,
        [
            pltpu.SMEM((nslab,), jnp.int32), pltpu.SMEM((nslab,), jnp.int32),
            pltpu.VMEM(orbitals.T.shape, BF), pltpu.SemaphoreType.DMA((8,)),
            pltpu.VMEM(loaded.shape, BF), pltpu.SemaphoreType.DMA((4, nslab // 2)),
        ] + scratch,
        (
            where, in_hbm(block_row), in_hbm(block_col), live_count, slabs,
            in_hbm(orbitals.T),
        ),
        work,
    )
    near1 = to_peer(1, msg1)
    keep_in2, keep2, sends2, dens2 = call(
        second_kernel,
        "slabs_second",
        [SM] + [VM] * 5,
        (shape((INROWS, LANES), F32),) + kept,
        scratch,
        (where, slabs2, lt, r, bd, d),
        work,
    )
    out2 = (keep_in2 + near1.astype(F32)).astype(BF)
    out2, lt = lax.optimization_barrier((out2, lt))
    far1 = to_peer(2, out2)
    news = 3 * PER + 3 * NBQ
    msg3, msg3b, msg3x, keep3, dens3 = call(
        third_kernel,
        "slabs_third",
        [SM] + [VM] * 9,
        (
            shape((INROWS // 2 + news, LANES), BF), shape((INROWS // 2 + 3 * PER, LANES), BF),
            shape((news, LANES), BF), kept[0], kept[2],
        ),
        [pltpu.VMEM((3, PER, LANES), BF)] + scratch,
        (where, slabs3, lt, r, bd, d, sends1, sends2, dens1, dens2),
        work,
    )
    near3, near3b = to_peer(1, msg3), to_peer(1, msg3b)
    far3 = to_peer(2, msg3x)
    keep_in4, keep4, sends4, dens4 = call(
        fourth_kernel,
        "slabs_fourth",
        [SM] + [VM] * 5,
        (shape((INROWS, LANES), F32),) + kept,
        scratch,
        (where, slabs4, lt, r, bd, d),
        LAST_WORK,
    )
    last = shape((LAST, LANES), BF)
    last_far = shape((LAST + 2 * PER + 3 * NBQ, LANES), BF)
    far3, keep_in4 = lax.optimization_barrier((far3, keep_in4))
    near4, far4, cross4, exch = call(
        exchange_kernel,
        "exchange",
        [SM] + [VM] * 6,
        (last, last_far, last, shape((QUARTER, LANES), F32)),
        [pltpu.VMEM((NACT, LANES), F32)],
        (where, keep_in4, near3, near3b, far1, sends4, dens4),
    )
    far4, cross4, near4 = to_peer(2, far4), to_peer(3, cross4), to_peer(1, near4)
    act, partial = call(
        coulomb_kernel,
        "coulomb",
        [VM] * 14,
        (shape((4 * PER, LANES), F32), shape((QUARTER, NACT), F32)),
        [],
        (
            keep1, keep2, keep3, keep4, dens1, dens2, dens3, dens4, exch,
            near3, far3, near4, far4, cross4,
        ),
    )
    (active,) = call(
        active_kernel,
        "own_active",
        [SM, VM],
        (shape((batch, QUARTER, NACT), F32),),
        [],
        (where, act),
        10**6,
    )
    return (active, hcore + sum_over_aux(partial))


def slab_terms(values, left, right):
    half = jnp.einsum("mc,qmn->qnc", left, values, preferred_element_type=F32).astype(BF)
    first = jnp.einsum("qnt,nc->qtc", half[:, :, :NACT], right, preferred_element_type=F32)
    second = jnp.einsum("qnc,nt->qtc", half, right[:, :NACT], preferred_element_type=F32)
    trace = 2.0 * jnp.einsum(
        "qni,ni->q", half[:, :, NACT:], right[:, NACT:], preferred_element_type=F32
    )
    return (first + second, trace)


def general_body(slabs, block_row, block_col, live_count, orbitals, hcore):
    batch = slabs.shape[1]
    init = (jnp.zeros((batch, NACT, NCOL), F32), jnp.zeros((batch,), F32))

    def visit(k, state):
        values = lax.dynamic_index_in_dim(slabs, k, 0, keepdims=False)
        left = lax.dynamic_slice_in_dim(orbitals, block_row[k] * BS, BS, 0)
        right = lax.dynamic_slice_in_dim(orbitals, block_col[k] * BS, BS, 0)
        terms, trace = slab_terms(values.reshape(batch, BS, BS), left, right)
        return (state[0] + terms, state[1] + trace)

    vectors, density = lax.fori_loop(0, live_count[0], visit, init)
    density = lax.psum(density, "pair")
    owned = lax.psum_scatter(vectors, "pair", scatter_dimension=1, tiled=True)
    own_active, own_inactive = owned[:, :, :NACT], owned[:, :, NACT:]
    gathered = lax.all_gather(own_inactive.astype(BF), "pair", axis=1, tiled=True)
    exchange = jnp.einsum(
        "qti,qui->tu", own_inactive, gathered.astype(F32), precision=lax.Precision.HIGHEST
    )
    coulomb = jnp.einsum("qtu,q->tu", own_active, density, precision=lax.Precision.HIGHEST)
    return (own_active, hcore + lax.psum(2.0 * coulomb - exchange, "aux"))


def solution(mesh):
    placed = (
        P(("frag", "pair"), "aux", None),
        P(("frag", "pair")),
        P(("frag", "pair")),
        P(("frag", "pair")),
        P("frag", None),
        P(("frag", "pair"), None),
    )

    def body(slabs, *rest):
        fits = mesh.shape["pair"] == 4 and slabs.shape[1] == 4 * NBQ and slabs.shape[0] % 8 == 0
        return (paired_body if fits else general_body)(slabs, *rest)

    return jax.shard_map(
        body,
        mesh=mesh,
        in_specs=placed,
        out_specs=(P(("frag", "aux"), "pair", None), P(("frag", "pair"), None)),
        check_vma=False,
    )
```

```python
import jax
import jax.numpy as jnp
from jax import lax
from jax.experimental import pallas as pl
from jax.experimental.pallas import tpu as pltpu
from jax.sharding import PartitionSpec as P

BS = 64
NACT = 64
NCOL = 192
NIN = NCOL - NACT
LANES = 128
NBQ = 16
PAIRED = 2 * BS
QSTEP, MSTEP = 3, 49
BF = jnp.bfloat16
F32 = jnp.float32


def low_half(rows):
    return lax.broadcasted_iota(jnp.int32, (rows, LANES), 1) < BS


def orbital_pair(k, blocks, live, orbitals):
    halves = []
    for n in range(2):
        slot = 2 * k + n
        base = pl.multiple_of((blocks[slot] // 2) * PAIRED, PAIRED)
        w = orbitals[:, pl.ds(base, PAIRED)]
        w = jnp.concatenate([w[NACT:], w[:NACT]], axis=0)
        w = jnp.where(lax.rem(blocks[slot], 2) != n, pltpu.roll(w, BS, 1), w)
        halves.append(jnp.where(slot < live, w, jnp.zeros_like(w)))
    return jnp.where(low_half(NCOL), halves[0], halves[1])


def slab_copies(slabs_ref, sbuf, sem, block):
    return [
        pltpu.make_async_copy(
            slabs_ref.at[pl.ds(2 * k, 2), pl.ds(pl.multiple_of(block * NBQ, NBQ), NBQ), :],
            sbuf.at[k],
            sem.at[k],
        )
        for k in range(slabs_ref.shape[0] // 2)
    ]


def lanes_of(k):
    return pl.ds(k * PAIRED if isinstance(k, int) else pl.multiple_of(k * PAIRED, PAIRED), PAIRED)


def run_block(sbuf, weights, scratch, emit, prepare=None, arrive=None):
    lt_ref, r_ref, bd_ref, d_ref = weights
    pt_ref, q_ref, diag = scratch[4:]
    quads = sbuf.shape[0] // 2
    first = low_half(NBQ)
    first_s = low_half(BS)
    zero = jnp.zeros((BS, LANES), BF)
    group = 8

    def relayout(k, out):
        for j in range(sbuf.shape[3] // LANES):
            lanes = slice(j * LANES, (j + 1) * LANES)
            a = sbuf[k, 0, :, lanes]
            b = sbuf[k, 1, :, lanes]
            out[pl.ds(MSTEP * 2 * j, NBQ, stride=QSTEP), :] = jnp.where(
                first, a, pltpu.roll(b, BS, 1)
            ).astype(F32)
            out[pl.ds(MSTEP * (2 * j + 1), NBQ, stride=QSTEP), :] = jnp.where(
                first, pltpu.roll(a, BS, 1), b
            ).astype(F32)

    def transform(g, bufs):
        dens = [d_ref[2 * g + n] for n in range(2)]
        left = [lt_ref[NIN:, lanes_of(2 * g + n)] for n in range(2)]
        for q in range(0, NBQ, group):
            slabs = [[], []]
            for u in range(q, q + group):
                total = diag[u]
                for n in range(2):
                    s = bufs[n][pl.ds(u * QSTEP, BS, stride=MSTEP), :]
                    total = total + jnp.sum((s * dens[n]).reshape(BS // 8, 8, LANES), axis=0)
                    slabs[n].append(s.astype(BF))
                diag[u] = total
            for n in range(2):
                at = lanes_of(2 * g + n)
                cols = [
                    jnp.concatenate(
                        [jnp.where(first_s, s, zero), jnp.where(first_s, zero, s)], axis=0
                    )
                    for s in slabs[n]
                ]
                p = jnp.dot(
                    left[n], jnp.concatenate(cols, axis=1), preferred_element_type=F32
                ).astype(BF)
                for u in range(group):
                    pt_ref[q + u, :, at] = p[:, u * LANES : (u + 1) * LANES]
            rows = jnp.concatenate(
                [jnp.concatenate([s0, s1], axis=1) for s0, s1 in zip(*slabs)], axis=0
            )
            out = jnp.dot(rows, bd_ref[g], preferred_element_type=F32).astype(BF)
            for u in range(0, group, 2):
                for n in range(2):
                    lanes = slice(n * LANES, (n + 1) * LANES)
                    q0 = out[u * BS : (u + 1) * BS, lanes]
                    q1 = out[(u + 1) * BS : (u + 2) * BS, lanes]
                    at = slice((q + u) * BS, (q + u + 2) * BS)
                    row = lanes_of(2 * g + n).start
                    q_ref[pl.ds(row, BS), at] = jnp.where(first_s, q0, pltpu.roll(q1, BS, 1))
                    q_ref[pl.ds(row + BS, BS), at] = jnp.where(
                        first_s, pltpu.roll(q0, BS, 1), q1
                    )

    def second_transform(g):
        rows = pt_ref[4 * g : 4 * g + 4].reshape(4 * NACT, pt_ref.shape[2])
        one = jnp.dot(rows, r_ref[...], preferred_element_type=F32)
        two = jnp.dot(
            lt_ref[...], q_ref[:, 4 * g * BS : (4 * g + 4) * BS], preferred_element_type=F32
        )
        return one, two

    def assemble(g, both):
        one, two = both
        for p in range(2):
            w0 = one[2 * p * NACT : (2 * p + 1) * NACT]
            w1 = one[(2 * p + 1) * NACT : (2 * p + 2) * NACT]
            turned = two[:, p * LANES : (p + 1) * LANES]
            across = turned[:NIN].T
            square = jnp.concatenate([turned[NIN:], turned[NIN:]], axis=0).T
            emit(
                2 * g + p,
                w0[:, :NIN] + across[:NACT],
                w1[:, :NIN] + across[NACT:],
                jnp.where(first_s, w0[:, NIN:] + square[:NACT], w1[:, NIN:] + square[NACT:]),
            )

    def load(g, bufs):
        for n in range(2):
            relayout(2 * g + n, bufs[n])

    def two_quads(i, carry):
        one, two = scratch[:2], scratch[2:4]
        pl.when(i > 0)(arrive)
        load(2 * i, one)
        prepare(2 * i)
        load(2 * i + 1, two)
        prepare(2 * i + 1)
        transform(2 * i, one)
        transform(2 * i + 1, two)
        return carry

    diag[...] = jnp.zeros_like(diag)
    if prepare is not None:
        lax.fori_loop(0, quads // 2, two_quads, 0)
    else:
        load(0, scratch[:2])
        for g in range(quads):
            if g + 1 < quads:
                load(g + 1, scratch[2 * ((g + 1) % 2) : 2 * ((g + 1) % 2) + 2])
            transform(g, scratch[2 * (g % 2) : 2 * (g % 2) + 2])
    whole = second_transform(0)
    for g in range(NBQ // 4):
        following = second_transform(g + 1) if g + 1 < NBQ // 4 else None
        assemble(g, whole)
        whole = following


def split_wire(d):
    hi = d.astype(BF).astype(F32)
    return jnp.where(low_half(d.shape[0]), hi, d - hi).astype(BF)


def joined(wire):
    w = wire.astype(F32)
    return w + pltpu.roll(w, BS, 1)


def density_of(diag):
    d = 2.0 * jnp.sum(jnp.sum(diag, axis=1), axis=1, keepdims=True)
    return jnp.broadcast_to(d, (NBQ, LANES))


QUARTER = NACT // 4
PER = NBQ // 2 * QUARTER
INROWS = NBQ * NACT
LAST = PER + NBQ + QUARTER


def emit_active(h, act, core, x, keep, sends):
    upper, lower = act[: 2 * QUARTER], act[2 * QUARTER :]
    near, far = jnp.where(x == 0, upper, lower), jnp.where(x == 0, lower, upper)
    at = pl.ds(h * QUARTER, QUARTER)
    for part, own, other in ((near, keep, sends.at[0]), (far, sends.at[1], sends.at[2])):
        one, two = part[:QUARTER], part[QUARTER:]
        own[at, :] = jnp.where(core == 0, one, two).astype(own.dtype)
        other[at, :] = jnp.where(core == 0, two, one).astype(BF)


def pair_rows(h, n):
    return pl.ds((2 * h + n) * NACT, NACT)


def first_kernel(
    where, rows_ref, cols_ref, live, slabs_ref, ot_ref,
    lt_out, r_out, bd_out, d_out, msg, keep, sends, dens, after2, after3, after4,
    rows, cols, orbitals, ssem, sbuf, sem, *scratch
):
    core, x = where[0], where[1]
    part = NACT // 2
    small = [
        pltpu.make_async_copy(src, dst, ssem.at[n])
        for n, (src, dst) in enumerate(((rows_ref, rows), (cols_ref, cols)))
    ] + [
        pltpu.make_async_copy(
            ot_ref.at[pl.ds(n * part, part)], orbitals.at[pl.ds(n * part, part)], ssem.at[2 + n]
        )
        for n in range(NCOL // part)
    ]
    blocks = (2 * (1 - x) + (1 - core), 2 * (1 - x) + core, 2 * x + (1 - core), 2 * x + core)
    now, *later = [
        slab_copies(slabs_ref, ref, sem.at[n], block)
        for n, (ref, block) in enumerate(zip((sbuf, after2, after3, after4), blocks))
    ]
    ahead = [copy for copies in later for copy in copies]
    for copy in small + now:
        copy.start()
    bd_out[...] = jnp.zeros_like(bd_out)
    for copy in small + now[: len(now) // 2]:
        copy.wait()
    for copy in ahead:
        copy.start()

    def arrive():
        for copy in now[len(now) // 2 :]:
            copy.wait()

    def prepare(g):
        for n in range(2):
            k = 2 * g + n
            left = orbital_pair(k, rows, live[0], orbitals)
            right = orbital_pair(k, cols, live[0], orbitals)
            at = lanes_of(k)
            lt_out[:, at] = left
            turned = jnp.concatenate([right, right[NIN:]], axis=0).astype(F32).T.astype(BF)
            r_out[at, :] = turned
            inner = (lax.broadcasted_iota(jnp.int32, (PAIRED, LANES), 0) < BS) == low_half(PAIRED)
            place = slice(n * PAIRED, (n + 1) * PAIRED)
            bd_out[g, place, place] = jnp.where(
                inner, turned[:, NIN:], jnp.zeros((PAIRED, LANES), BF)
            )
            both = jnp.dot(
                left[:NIN].astype(F32).T.astype(BF), right[:NIN], preferred_element_type=F32
            )
            d_out[k] = jnp.where(low_half(BS), both[:BS], both[BS:])

    def emit(h, in0, in1, act):
        msg[pair_rows(h, 0), :] = in0.astype(BF)
        msg[pair_rows(h, 1), :] = in1.astype(BF)
        emit_active(h, act, core, x, keep, sends)

    run_block(sbuf, (lt_out, r_out, bd_out, d_out), scratch, emit, prepare, arrive)
    dens[...] = density_of(scratch[6][...])
    for copy in ahead:
        copy.wait()


def second_kernel(
    where, sbuf, lt_ref, r_ref, bd_ref, d_ref, keep_in, keep, sends, dens, *scratch
):
    core, x = where[0], where[1]
    def emit(h, in0, in1, act):
        keep_in[pair_rows(h, 0), :] = in0
        keep_in[pair_rows(h, 1), :] = in1
        emit_active(h, act, core, x, keep, sends)

    run_block(sbuf, (lt_ref, r_ref, bd_ref, d_ref), scratch, emit)
    dens[...] = density_of(scratch[6][...])


def third_kernel(
    where, sbuf, lt_ref, r_ref, bd_ref, d_ref, sends1, sends2, dens1, dens2,
    near, near_more, far, keep, dens, sends, *scratch
):
    core, x = where[0], where[1]
    def emit(h, in0, in1, act):
        place, at = (near, h) if h < NBQ // 4 else (near_more, h - NBQ // 4)
        place[pair_rows(at, 0), :] = in0.astype(BF)
        place[pair_rows(at, 1), :] = in1.astype(BF)
        emit_active(h, act, core, x, keep, sends)

    run_block(sbuf, (lt_ref, r_ref, bd_ref, d_ref), scratch, emit)
    dens[...] = density_of(scratch[6][...])
    wires = [split_wire(d[...]) for d in (dens1, dens2, dens)]
    for n, source in enumerate((sends1, sends2, sends)):
        near_more[pl.ds(INROWS // 2 + n * PER, PER), :] = source[2]
    for k, (msg, base) in enumerate(((near, INROWS // 2), (far, 0))):
        for n, source in enumerate((sends1, sends2, sends)):
            msg[pl.ds(base + n * PER, PER), :] = source[k]
            msg[pl.ds(base + 3 * PER + n * NBQ, NBQ), :] = wires[n]


def fourth_kernel(
    where, sbuf, lt_ref, r_ref, bd_ref, d_ref, keep_in, keep, sends, dens, *scratch
):
    core, x = where[0], where[1]

    def emit(h, in0, in1, act):
        keep_in[pair_rows(h, 0), :] = in0
        keep_in[pair_rows(h, 1), :] = in1
        emit_active(h, act, core, x, keep, sends)

    run_block(sbuf, (lt_ref, r_ref, bd_ref, d_ref), scratch, emit)
    dens[...] = density_of(scratch[6][...])


def exchange_kernel(
    where, mine, near3, near3b, far1, sends, dens, near, far, cross, keep, whole
):
    parts = []
    for q in range(NBQ):
        rows = pl.ds(q * NACT, NACT)
        other = (near3 if q < NBQ // 2 else near3b)[pl.ds(q % (NBQ // 2) * NACT, NACT), :]
        parts.append(mine[rows, :] + other.astype(F32) + far1[rows, :].astype(F32))
    v = jnp.concatenate(parts, axis=1)
    v = v.astype(BF)
    total = lax.dot_general(v, v, (((1,), (1,)), ((), ())), preferred_element_type=F32)
    whole[...] = jnp.concatenate([total, total], axis=1)
    index = 2 * where[1] + where[0]
    keep[...] = whole[pl.ds(pl.multiple_of(index * QUARTER, QUARTER), QUARTER), :]
    wire = split_wire(dens[...])
    for k, msg in enumerate((near, far, cross)):
        rows = sends[k]
        if k == 1:
            passed = near3b[pl.ds(INROWS // 2 + 2 * PER, PER), :]
            rows = (rows.astype(F32) + passed.astype(F32)).astype(BF)
        msg[pl.ds(0, PER), :] = rows
        msg[pl.ds(PER, NBQ), :] = wire
        at = pl.multiple_of((index ^ (k + 1)) * QUARTER, QUARTER)
        msg[pl.ds(PER + NBQ, QUARTER), :] = split_wire(whole[pl.ds(at, QUARTER), :])
    far[pl.ds(LAST, 2 * PER), :] = near3b[pl.ds(INROWS // 2, 2 * PER), :]
    far[pl.ds(LAST + 2 * PER, 3 * NBQ), :] = near3[pl.ds(INROWS // 2 + 3 * PER, 3 * NBQ), :]


def coulomb_kernel(
    keep1, keep2, keep3, keep4, dens1, dens2, dens3, dens4, exch,
    near3, far3, near4, far4, cross4, act, partial,
):
    first = low_half(QUARTER)
    early, late = (near3, far3, far4), (near4, far4, cross4)
    total = jnp.zeros((QUARTER, LANES), F32)
    for m, (keep, dens) in enumerate(
        ((keep1, dens1), (keep2, dens2), (keep3, dens3), (keep4, dens4))
    ):
        rows, d = keep[...], dens[...]
        for k in (1, 2, 3):
            n = m ^ k
            msg = late[k - 1] if n == 3 else early[k - 1]
            if n == 3:
                at, dens_at = 0, PER
            elif k == 3:
                at, dens_at = LAST + n * PER, LAST + 2 * PER + n * NBQ
            else:
                base = INROWS // 2 if k == 1 else 0
                at, dens_at = base + n * PER, base + 3 * PER + n * NBQ
            if not (k == 3 and n == 2):
                rows = rows + msg[pl.ds(at, PER), :].astype(F32)
            d = d + joined(msg[pl.ds(dens_at, NBQ), :])
        act[pl.ds(m * PER, PER), :] = rows
        for h in range(NBQ // 2):
            total = total + rows[h * QUARTER : (h + 1) * QUARTER] * jnp.where(
                first, d[2 * h : 2 * h + 1], d[2 * h + 1 : 2 * h + 2]
            )
    total = 2.0 * (total + pltpu.roll(total, BS, 1)) - exch[...]
    for msg in late:
        total = total - joined(msg[pl.ds(PER + NBQ, QUARTER), :])
    partial[...] = total[:, :BS]


def active_kernel(where, act, out):
    core, x = where[0], where[1]
    for n in range(4):
        xx = (1 - x) if n < 2 else x
        cc = (1 - core) if n % 2 == 0 else core
        base = NBQ * (2 * xx + cc)
        for h in range(NBQ // 2):
            a = act[pl.ds(n * PER + h * QUARTER, QUARTER), :]
            out[base + 2 * h] = a[:, :BS]
            out[base + 2 * h + 1] = a[:, BS:]


VM = pl.BlockSpec(memory_space=pltpu.VMEM)
SM = pl.BlockSpec(memory_space=pltpu.SMEM)
HB = pl.BlockSpec(memory_space=pltpu.HBM)

LAST_WORK = 10**9
PARAMS = pltpu.CompilerParams(vmem_limit_bytes=32 * 1024 * 1024)


def in_hbm(array):
    return pltpu.with_memory_space_constraint(array, pltpu.HBM)


def shape(dims, dtype):
    return jax.ShapeDtypeStruct(dims, dtype)


def sum_over_aux(part):
    n = lax.axis_size("aux")
    if n != 4:
        return lax.psum(part, "aux")
    for k in (1, 2):
        part = part + lax.ppermute(part, "aux", [(z, z ^ k) for z in range(n)])
    return part


def call(kernel, name, inputs, out_shape, scratch, args, work=0):
    return pl.pallas_call(
        kernel,
        name=name,
        in_specs=inputs,
        out_specs=[VM] * len(out_shape),
        out_shape=out_shape,
        scratch_shapes=scratch,
        compiler_params=PARAMS,
        cost_estimate=pl.CostEstimate(flops=work, bytes_accessed=10**5, transcendentals=0),
    )(*args)


def paired_body(slabs, block_row, block_col, live_count, orbitals, hcore):
    nslab, batch, width = slabs.shape
    index = lax.axis_index("pair")
    where = jnp.stack([lax.rem(index, 2), index // 2])
    aos = nslab * BS
    slabs = in_hbm(slabs)

    def to_peer(k, array):
        return lax.ppermute(array, "pair", [(p, p ^ k) for p in range(4)])

    loaded = shape((nslab // 2, 2, NBQ, width), BF)
    scratch = [pltpu.VMEM((MSTEP * BS, LANES), F32)] * 4 + [
        pltpu.VMEM((NBQ, NACT, aos), BF),
        pltpu.VMEM((aos, NBQ * BS), BF),
        pltpu.VMEM((NBQ, 8, LANES), F32),
    ]
    weights = (
        shape((NCOL, aos), BF),
        shape((aos, 2 * LANES), BF),
        shape((nslab // 4, 2 * PAIRED, 2 * PAIRED), BF),
        shape((nslab // 2, BS, PAIRED), F32),
    )
    kept = (
        shape((PER, LANES), F32), shape((3, PER, LANES), BF), shape((NBQ, LANES), F32),
    )
    work = 5 * 10**9
    lt, r, bd, d, msg1, keep1, sends1, dens1, slabs2, slabs3, slabs4 = call(
        first_kernel,
        "slabs_first",
        [SM, HB, HB, SM, HB, HB],
        weights + (shape((INROWS, LANES), BF),) + kept + (loaded,) * 3,
        [
            pltpu.SMEM((nslab,), jnp.int32), pltpu.SMEM((nslab,), jnp.int32),
            pltpu.VMEM(orbitals.T.shape, BF), pltpu.SemaphoreType.DMA((8,)),
            pltpu.VMEM(loaded.shape, BF), pltpu.SemaphoreType.DMA((4, nslab // 2)),
        ] + scratch,
        (
            where, in_hbm(block_row), in_hbm(block_col), live_count, slabs,
            in_hbm(orbitals.T),
        ),
        work,
    )
    near1 = to_peer(1, msg1)
    keep_in2, keep2, sends2, dens2 = call(
        second_kernel,
        "slabs_second",
        [SM] + [VM] * 5,
        (shape((INROWS, LANES), F32),) + kept,
        scratch,
        (where, slabs2, lt, r, bd, d),
        work,
    )
    out2 = (keep_in2 + near1.astype(F32)).astype(BF)
    out2, lt = lax.optimization_barrier((out2, lt))
    far1 = to_peer(2, out2)
    news = 3 * PER + 3 * NBQ
    msg3, msg3b, msg3x, keep3, dens3 = call(
        third_kernel,
        "slabs_third",
        [SM] + [VM] * 9,
        (
            shape((INROWS // 2 + news, LANES), BF), shape((INROWS // 2 + 3 * PER, LANES), BF),
            shape((news, LANES), BF), kept[0], kept[2],
        ),
        [pltpu.VMEM((3, PER, LANES), BF)] + scratch,
        (where, slabs3, lt, r, bd, d, sends1, sends2, dens1, dens2),
        work,
    )
    near3, near3b = to_peer(1, msg3), to_peer(1, msg3b)
    far3 = to_peer(2, msg3x)
    keep_in4, keep4, sends4, dens4 = call(
        fourth_kernel,
        "slabs_fourth",
        [SM] + [VM] * 5,
        (shape((INROWS, LANES), F32),) + kept,
        scratch,
        (where, slabs4, lt, r, bd, d),
        LAST_WORK,
    )
    last = shape((LAST, LANES), BF)
    last_far = shape((LAST + 2 * PER + 3 * NBQ, LANES), BF)
    near4, far4, cross4, exch = call(
        exchange_kernel,
        "exchange",
        [SM] + [VM] * 6,
        (last, last_far, last, shape((QUARTER, LANES), F32)),
        [pltpu.VMEM((NACT, LANES), F32)],
        (where, keep_in4, near3, near3b, far1, sends4, dens4),
    )
    far3, far4 = lax.optimization_barrier((far3, far4))
    far4, cross4, near4 = to_peer(2, far4), to_peer(3, cross4), to_peer(1, near4)
    act, partial = call(
        coulomb_kernel,
        "coulomb",
        [VM] * 14,
        (shape((4 * PER, LANES), F32), shape((QUARTER, NACT), F32)),
        [],
        (
            keep1, keep2, keep3, keep4, dens1, dens2, dens3, dens4, exch,
            near3, far3, near4, far4, cross4,
        ),
    )
    (active,) = call(
        active_kernel,
        "own_active",
        [SM, VM],
        (shape((batch, QUARTER, NACT), F32),),
        [],
        (where, act),
        10**6,
    )
    return (active, hcore + sum_over_aux(partial))


def slab_terms(values, left, right):
    half = jnp.einsum("mc,qmn->qnc", left, values, preferred_element_type=F32).astype(BF)
    first = jnp.einsum("qnt,nc->qtc", half[:, :, :NACT], right, preferred_element_type=F32)
    second = jnp.einsum("qnc,nt->qtc", half, right[:, :NACT], preferred_element_type=F32)
    trace = 2.0 * jnp.einsum(
        "qni,ni->q", half[:, :, NACT:], right[:, NACT:], preferred_element_type=F32
    )
    return (first + second, trace)


def general_body(slabs, block_row, block_col, live_count, orbitals, hcore):
    batch = slabs.shape[1]
    init = (jnp.zeros((batch, NACT, NCOL), F32), jnp.zeros((batch,), F32))

    def visit(k, state):
        values = lax.dynamic_index_in_dim(slabs, k, 0, keepdims=False)
        left = lax.dynamic_slice_in_dim(orbitals, block_row[k] * BS, BS, 0)
        right = lax.dynamic_slice_in_dim(orbitals, block_col[k] * BS, BS, 0)
        terms, trace = slab_terms(values.reshape(batch, BS, BS), left, right)
        return (state[0] + terms, state[1] + trace)

    vectors, density = lax.fori_loop(0, live_count[0], visit, init)
    density = lax.psum(density, "pair")
    owned = lax.psum_scatter(vectors, "pair", scatter_dimension=1, tiled=True)
    own_active, own_inactive = owned[:, :, :NACT], owned[:, :, NACT:]
    gathered = lax.all_gather(own_inactive.astype(BF), "pair", axis=1, tiled=True)
    exchange = jnp.einsum(
        "qti,qui->tu", own_inactive, gathered.astype(F32), precision=lax.Precision.HIGHEST
    )
    coulomb = jnp.einsum("qtu,q->tu", own_active, density, precision=lax.Precision.HIGHEST)
    return (own_active, hcore + lax.psum(2.0 * coulomb - exchange, "aux"))


def solution(mesh):
    placed = (
        P(("frag", "pair"), "aux", None),
        P(("frag", "pair")),
        P(("frag", "pair")),
        P(("frag", "pair")),
        P("frag", None),
        P(("frag", "pair"), None),
    )

    def body(slabs, *rest):
        fits = mesh.shape["pair"] == 4 and slabs.shape[1] == 4 * NBQ and slabs.shape[0] % 8 == 0
        return (paired_body if fits else general_body)(slabs, *rest)

    return jax.shard_map(
        body,
        mesh=mesh,
        in_specs=placed,
        out_specs=(P(("frag", "aux"), "pair", None), P(("frag", "pair"), None)),
        check_vma=False,
    )
```

```python
import jax
import jax.numpy as jnp
from jax import lax
from jax.experimental import pallas as pl
from jax.experimental.pallas import tpu as pltpu
from jax.sharding import PartitionSpec as P

BS = 64
NACT = 64
NCOL = 192
NIN = NCOL - NACT
LANES = 128
NBQ = 16
PAIRED = 2 * BS
QSTEP, MSTEP = 3, 49
BF = jnp.bfloat16
F32 = jnp.float32


def low_half(rows):
    return lax.broadcasted_iota(jnp.int32, (rows, LANES), 1) < BS


def orbital_pair(k, blocks, live, orbitals):
    halves = []
    for n in range(2):
        slot = 2 * k + n
        base = pl.multiple_of((blocks[slot] // 2) * PAIRED, PAIRED)
        w = orbitals[:, pl.ds(base, PAIRED)]
        w = jnp.concatenate([w[NACT:], w[:NACT]], axis=0)
        w = jnp.where(lax.rem(blocks[slot], 2) != n, pltpu.roll(w, BS, 1), w)
        halves.append(jnp.where(slot < live, w, jnp.zeros_like(w)))
    return jnp.where(low_half(NCOL), halves[0], halves[1])


def slab_copies(slabs_ref, sbuf, sem, block):
    return [
        pltpu.make_async_copy(
            slabs_ref.at[pl.ds(2 * k, 2), pl.ds(pl.multiple_of(block * NBQ, NBQ), NBQ), :],
            sbuf.at[k],
            sem.at[k],
        )
        for k in range(slabs_ref.shape[0] // 2)
    ]


def lanes_of(k):
    return pl.ds(k * PAIRED if isinstance(k, int) else pl.multiple_of(k * PAIRED, PAIRED), PAIRED)


def run_block(sbuf, weights, scratch, emit, prepare=None, arrive=None):
    lt_ref, r_ref, bd_ref, d_ref = weights
    pt_ref, q_ref, diag = scratch[4:]
    quads = sbuf.shape[0] // 2
    first = low_half(NBQ)
    first_s = low_half(BS)
    zero = jnp.zeros((BS, LANES), BF)
    group = 8

    def relayout(k, out):
        for j in range(sbuf.shape[3] // LANES):
            lanes = slice(j * LANES, (j + 1) * LANES)
            a = sbuf[k, 0, :, lanes]
            b = sbuf[k, 1, :, lanes]
            out[pl.ds(MSTEP * 2 * j, NBQ, stride=QSTEP), :] = jnp.where(
                first, a, pltpu.roll(b, BS, 1)
            ).astype(F32)
            out[pl.ds(MSTEP * (2 * j + 1), NBQ, stride=QSTEP), :] = jnp.where(
                first, pltpu.roll(a, BS, 1), b
            ).astype(F32)

    def transform(g, bufs):
        dens = [d_ref[2 * g + n] for n in range(2)]
        left = [lt_ref[NIN:, lanes_of(2 * g + n)] for n in range(2)]
        for q in range(0, NBQ, group):
            slabs = [[], []]
            for u in range(q, q + group):
                total = diag[u]
                for n in range(2):
                    s = bufs[n][pl.ds(u * QSTEP, BS, stride=MSTEP), :]
                    total = total + jnp.sum((s * dens[n]).reshape(BS // 8, 8, LANES), axis=0)
                    slabs[n].append(s.astype(BF))
                diag[u] = total
            for n in range(2):
                at = lanes_of(2 * g + n)
                cols = [
                    jnp.concatenate(
                        [jnp.where(first_s, s, zero), jnp.where(first_s, zero, s)], axis=0
                    )
                    for s in slabs[n]
                ]
                p = jnp.dot(
                    left[n], jnp.concatenate(cols, axis=1), preferred_element_type=F32
                ).astype(BF)
                for u in range(group):
                    pt_ref[q + u, :, at] = p[:, u * LANES : (u + 1) * LANES]
            rows = jnp.concatenate(
                [jnp.concatenate([s0, s1], axis=1) for s0, s1 in zip(*slabs)], axis=0
            )
            out = jnp.dot(rows, bd_ref[g], preferred_element_type=F32).astype(BF)
            for u in range(0, group, 2):
                for n in range(2):
                    lanes = slice(n * LANES, (n + 1) * LANES)
                    q0 = out[u * BS : (u + 1) * BS, lanes]
                    q1 = out[(u + 1) * BS : (u + 2) * BS, lanes]
                    at = slice((q + u) * BS, (q + u + 2) * BS)
                    row = lanes_of(2 * g + n).start
                    q_ref[pl.ds(row, BS), at] = jnp.where(first_s, q0, pltpu.roll(q1, BS, 1))
                    q_ref[pl.ds(row + BS, BS), at] = jnp.where(
                        first_s, pltpu.roll(q0, BS, 1), q1
                    )

    def second_transform(g):
        rows = pt_ref[4 * g : 4 * g + 4].reshape(4 * NACT, pt_ref.shape[2])
        one = jnp.dot(rows, r_ref[...], preferred_element_type=F32)
        two = jnp.dot(
            lt_ref[...], q_ref[:, 4 * g * BS : (4 * g + 4) * BS], preferred_element_type=F32
        )
        return one, two

    def assemble(g, both):
        one, two = both
        for p in range(2):
            w0 = one[2 * p * NACT : (2 * p + 1) * NACT]
            w1 = one[(2 * p + 1) * NACT : (2 * p + 2) * NACT]
            turned = two[:, p * LANES : (p + 1) * LANES]
            across = turned[:NIN].T
            square = jnp.concatenate([turned[NIN:], turned[NIN:]], axis=0).T
            emit(
                2 * g + p,
                w0[:, :NIN] + across[:NACT],
                w1[:, :NIN] + across[NACT:],
                jnp.where(first_s, w0[:, NIN:] + square[:NACT], w1[:, NIN:] + square[NACT:]),
            )

    def load(g, bufs):
        for n in range(2):
            relayout(2 * g + n, bufs[n])

    def two_quads(i, carry):
        one, two = scratch[:2], scratch[2:4]
        pl.when(i > 0)(arrive)
        load(2 * i, one)
        prepare(2 * i)
        load(2 * i + 1, two)
        prepare(2 * i + 1)
        transform(2 * i, one)
        transform(2 * i + 1, two)
        return carry

    diag[...] = jnp.zeros_like(diag)
    if prepare is not None:
        lax.fori_loop(0, quads // 2, two_quads, 0)
    else:
        load(0, scratch[:2])
        for g in range(quads):
            if g + 1 < quads:
                load(g + 1, scratch[2 * ((g + 1) % 2) : 2 * ((g + 1) % 2) + 2])
            transform(g, scratch[2 * (g % 2) : 2 * (g % 2) + 2])
    whole = second_transform(0)
    for g in range(NBQ // 4):
        following = second_transform(g + 1) if g + 1 < NBQ // 4 else None
        assemble(g, whole)
        whole = following


def split_wire(d):
    hi = d.astype(BF).astype(F32)
    return jnp.where(low_half(d.shape[0]), hi, d - hi).astype(BF)


def joined(wire):
    w = wire.astype(F32)
    return w + pltpu.roll(w, BS, 1)


def density_of(diag):
    d = 2.0 * jnp.sum(jnp.sum(diag, axis=1), axis=1, keepdims=True)
    return jnp.broadcast_to(d, (NBQ, LANES))


QUARTER = NACT // 4
PER = NBQ // 2 * QUARTER
INROWS = NBQ * NACT
LAST = PER + NBQ + QUARTER


def emit_active(h, act, core, x, keep, sends):
    upper, lower = act[: 2 * QUARTER], act[2 * QUARTER :]
    near, far = jnp.where(x == 0, upper, lower), jnp.where(x == 0, lower, upper)
    at = pl.ds(h * QUARTER, QUARTER)
    for part, own, other in ((near, keep, sends.at[0]), (far, sends.at[1], sends.at[2])):
        one, two = part[:QUARTER], part[QUARTER:]
        own[at, :] = jnp.where(core == 0, one, two).astype(own.dtype)
        other[at, :] = jnp.where(core == 0, two, one).astype(BF)


def pair_rows(h, n):
    return pl.ds((2 * h + n) * NACT, NACT)


def first_kernel(
    where, rows_ref, cols_ref, live, slabs_ref, ot_ref,
    lt_out, r_out, bd_out, d_out, msg, keep, sends, dens, after2, after3, after4,
    rows, cols, orbitals, ssem, sbuf, sem, *scratch
):
    core, x = where[0], where[1]
    part = NACT // 2
    small = [
        pltpu.make_async_copy(src, dst, ssem.at[n])
        for n, (src, dst) in enumerate(((rows_ref, rows), (cols_ref, cols)))
    ] + [
        pltpu.make_async_copy(
            ot_ref.at[pl.ds(n * part, part)], orbitals.at[pl.ds(n * part, part)], ssem.at[2 + n]
        )
        for n in range(NCOL // part)
    ]
    blocks = (2 * (1 - x) + (1 - core), 2 * (1 - x) + core, 2 * x + (1 - core), 2 * x + core)
    now, *later = [
        slab_copies(slabs_ref, ref, sem.at[n], block)
        for n, (ref, block) in enumerate(zip((sbuf, after2, after3, after4), blocks))
    ]
    ahead = [copy for copies in later for copy in copies]
    for copy in small + now:
        copy.start()
    bd_out[...] = jnp.zeros_like(bd_out)
    for copy in small + now[: len(now) // 2]:
        copy.wait()
    for copy in ahead:
        copy.start()

    def arrive():
        for copy in now[len(now) // 2 :]:
            copy.wait()

    def prepare(g):
        for n in range(2):
            k = 2 * g + n
            left = orbital_pair(k, rows, live[0], orbitals)
            right = orbital_pair(k, cols, live[0], orbitals)
            at = lanes_of(k)
            lt_out[:, at] = left
            turned = jnp.concatenate([right, right[NIN:]], axis=0).astype(F32).T.astype(BF)
            r_out[at, :] = turned
            inner = (lax.broadcasted_iota(jnp.int32, (PAIRED, LANES), 0) < BS) == low_half(PAIRED)
            place = slice(n * PAIRED, (n + 1) * PAIRED)
            bd_out[g, place, place] = jnp.where(
                inner, turned[:, NIN:], jnp.zeros((PAIRED, LANES), BF)
            )
            both = jnp.dot(
                left[:NIN].astype(F32).T.astype(BF), right[:NIN], preferred_element_type=F32
            )
            d_out[k] = jnp.where(low_half(BS), both[:BS], both[BS:])

    def emit(h, in0, in1, act):
        msg[pair_rows(h, 0), :] = in0.astype(BF)
        msg[pair_rows(h, 1), :] = in1.astype(BF)
        emit_active(h, act, core, x, keep, sends)

    run_block(sbuf, (lt_out, r_out, bd_out, d_out), scratch, emit, prepare, arrive)
    msg[pl.ds(INROWS, PER), :] = sends[2]
    dens[...] = density_of(scratch[6][...])
    for copy in ahead:
        copy.wait()


def second_kernel(
    where, sbuf, lt_ref, r_ref, bd_ref, d_ref, keep_in, keep, sends, dens, *scratch
):
    core, x = where[0], where[1]
    def emit(h, in0, in1, act):
        keep_in[pair_rows(h, 0), :] = in0
        keep_in[pair_rows(h, 1), :] = in1
        emit_active(h, act, core, x, keep, sends)

    run_block(sbuf, (lt_ref, r_ref, bd_ref, d_ref), scratch, emit)
    dens[...] = density_of(scratch[6][...])


def third_kernel(
    where, sbuf, lt_ref, r_ref, bd_ref, d_ref, sends1, sends2, dens1, dens2, near1,
    near, near_more, far, keep, dens, sends, *scratch
):
    core, x = where[0], where[1]
    def emit(h, in0, in1, act):
        place, at = (near, h) if h < NBQ // 4 else (near_more, h - NBQ // 4)
        place[pair_rows(at, 0), :] = in0.astype(BF)
        place[pair_rows(at, 1), :] = in1.astype(BF)
        emit_active(h, act, core, x, keep, sends)

    run_block(sbuf, (lt_ref, r_ref, bd_ref, d_ref), scratch, emit)
    dens[...] = density_of(scratch[6][...])
    wires = [split_wire(d[...]) for d in (dens1, dens2, dens)]
    for n, source in enumerate((sends2, sends)):
        near_more[pl.ds(INROWS // 2 + n * PER, PER), :] = source[2]
    passed = near1[pl.ds(INROWS, PER), :]
    for k, (msg, base) in enumerate(((near, INROWS // 2), (far, 0))):
        for n, source in enumerate((sends1, sends2, sends)):
            rows = source[k]
            if (k, n) == (1, 1):
                rows = (rows.astype(F32) + passed.astype(F32)).astype(BF)
            msg[pl.ds(base + n * PER, PER), :] = rows
            msg[pl.ds(base + 3 * PER + n * NBQ, NBQ), :] = wires[n]


def fourth_kernel(
    where, sbuf, lt_ref, r_ref, bd_ref, d_ref, keep_in, keep, sends, dens, *scratch
):
    core, x = where[0], where[1]

    def emit(h, in0, in1, act):
        keep_in[pair_rows(h, 0), :] = in0
        keep_in[pair_rows(h, 1), :] = in1
        emit_active(h, act, core, x, keep, sends)

    run_block(sbuf, (lt_ref, r_ref, bd_ref, d_ref), scratch, emit)
    dens[...] = density_of(scratch[6][...])


def exchange_kernel(
    where, mine, near3, near3b, far1, sends, dens, near, far, cross, keep, whole
):
    parts = []
    for q in range(NBQ):
        rows = pl.ds(q * NACT, NACT)
        other = (near3 if q < NBQ // 2 else near3b)[pl.ds(q % (NBQ // 2) * NACT, NACT), :]
        parts.append(mine[rows, :] + other.astype(F32) + far1[rows, :].astype(F32))
    v = jnp.concatenate(parts, axis=1)
    v = v.astype(BF)
    total = lax.dot_general(v, v, (((1,), (1,)), ((), ())), preferred_element_type=F32)
    whole[...] = jnp.concatenate([total, total], axis=1)
    index = 2 * where[1] + where[0]
    keep[...] = whole[pl.ds(pl.multiple_of(index * QUARTER, QUARTER), QUARTER), :]
    wire = split_wire(dens[...])
    for k, msg in enumerate((near, far, cross)):
        rows = sends[k]
        if k == 1:
            passed = near3b[pl.ds(INROWS // 2 + PER, PER), :]
            rows = (rows.astype(F32) + passed.astype(F32)).astype(BF)
        msg[pl.ds(0, PER), :] = rows
        msg[pl.ds(PER, NBQ), :] = wire
        at = pl.multiple_of((index ^ (k + 1)) * QUARTER, QUARTER)
        msg[pl.ds(PER + NBQ, QUARTER), :] = split_wire(whole[pl.ds(at, QUARTER), :])
    far[pl.ds(LAST, PER), :] = near3b[pl.ds(INROWS // 2, PER), :]
    far[pl.ds(LAST + PER, 3 * NBQ), :] = near3[pl.ds(INROWS // 2 + 3 * PER, 3 * NBQ), :]


def coulomb_kernel(
    keep1, keep2, keep3, keep4, dens1, dens2, dens3, dens4, exch,
    near3, far3, near4, far4, cross4, act, partial,
):
    first = low_half(QUARTER)
    early, late = (near3, far3, far4), (near4, far4, cross4)
    total = jnp.zeros((QUARTER, LANES), F32)
    for m, (keep, dens) in enumerate(
        ((keep1, dens1), (keep2, dens2), (keep3, dens3), (keep4, dens4))
    ):
        rows, d = keep[...], dens[...]
        for k in (1, 2, 3):
            n = m ^ k
            msg = late[k - 1] if n == 3 else early[k - 1]
            if n == 3:
                at, dens_at = 0, PER
            elif k == 3:
                at, dens_at = LAST, LAST + PER + n * NBQ
            else:
                base = INROWS // 2 if k == 1 else 0
                at, dens_at = base + n * PER, base + 3 * PER + n * NBQ
            if not (k == 3 and n in (0, 2)):
                rows = rows + msg[pl.ds(at, PER), :].astype(F32)
            d = d + joined(msg[pl.ds(dens_at, NBQ), :])
        act[pl.ds(m * PER, PER), :] = rows
        for h in range(NBQ // 2):
            total = total + rows[h * QUARTER : (h + 1) * QUARTER] * jnp.where(
                first, d[2 * h : 2 * h + 1], d[2 * h + 1 : 2 * h + 2]
            )
    total = 2.0 * (total + pltpu.roll(total, BS, 1)) - exch[...]
    for msg in late:
        total = total - joined(msg[pl.ds(PER + NBQ, QUARTER), :])
    partial[...] = total[:, :BS]


def active_kernel(where, act, out):
    core, x = where[0], where[1]
    for n in range(4):
        xx = (1 - x) if n < 2 else x
        cc = (1 - core) if n % 2 == 0 else core
        base = NBQ * (2 * xx + cc)
        for h in range(NBQ // 2):
            a = act[pl.ds(n * PER + h * QUARTER, QUARTER), :]
            out[base + 2 * h] = a[:, :BS]
            out[base + 2 * h + 1] = a[:, BS:]


VM = pl.BlockSpec(memory_space=pltpu.VMEM)
SM = pl.BlockSpec(memory_space=pltpu.SMEM)
HB = pl.BlockSpec(memory_space=pltpu.HBM)

LAST_WORK = 10**9
PARAMS = pltpu.CompilerParams(vmem_limit_bytes=32 * 1024 * 1024)


def in_hbm(array):
    return pltpu.with_memory_space_constraint(array, pltpu.HBM)


def shape(dims, dtype):
    return jax.ShapeDtypeStruct(dims, dtype)


def sum_over_aux(part):
    n = lax.axis_size("aux")
    if n != 4:
        return lax.psum(part, "aux")
    for k in (1, 2):
        part = part + lax.ppermute(part, "aux", [(z, z ^ k) for z in range(n)])
    return part


def call(kernel, name, inputs, out_shape, scratch, args, work=0):
    return pl.pallas_call(
        kernel,
        name=name,
        in_specs=inputs,
        out_specs=[VM] * len(out_shape),
        out_shape=out_shape,
        scratch_shapes=scratch,
        compiler_params=PARAMS,
        cost_estimate=pl.CostEstimate(flops=work, bytes_accessed=10**5, transcendentals=0),
    )(*args)


def paired_body(slabs, block_row, block_col, live_count, orbitals, hcore):
    nslab, batch, width = slabs.shape
    index = lax.axis_index("pair")
    where = jnp.stack([lax.rem(index, 2), index // 2])
    aos = nslab * BS
    slabs = in_hbm(slabs)

    def to_peer(k, array):
        return lax.ppermute(array, "pair", [(p, p ^ k) for p in range(4)])

    loaded = shape((nslab // 2, 2, NBQ, width), BF)
    scratch = [pltpu.VMEM((MSTEP * BS, LANES), F32)] * 4 + [
        pltpu.VMEM((NBQ, NACT, aos), BF),
        pltpu.VMEM((aos, NBQ * BS), BF),
        pltpu.VMEM((NBQ, 8, LANES), F32),
    ]
    weights = (
        shape((NCOL, aos), BF),
        shape((aos, 2 * LANES), BF),
        shape((nslab // 4, 2 * PAIRED, 2 * PAIRED), BF),
        shape((nslab // 2, BS, PAIRED), F32),
    )
    kept = (
        shape((PER, LANES), F32), shape((3, PER, LANES), BF), shape((NBQ, LANES), F32),
    )
    work = 5 * 10**9
    lt, r, bd, d, msg1, keep1, sends1, dens1, slabs2, slabs3, slabs4 = call(
        first_kernel,
        "slabs_first",
        [SM, HB, HB, SM, HB, HB],
        weights + (shape((INROWS + PER, LANES), BF),) + kept + (loaded,) * 3,
        [
            pltpu.SMEM((nslab,), jnp.int32), pltpu.SMEM((nslab,), jnp.int32),
            pltpu.VMEM(orbitals.T.shape, BF), pltpu.SemaphoreType.DMA((8,)),
            pltpu.VMEM(loaded.shape, BF), pltpu.SemaphoreType.DMA((4, nslab // 2)),
        ] + scratch,
        (
            where, in_hbm(block_row), in_hbm(block_col), live_count, slabs,
            in_hbm(orbitals.T),
        ),
        work,
    )
    near1 = to_peer(1, msg1)
    keep_in2, keep2, sends2, dens2 = call(
        second_kernel,
        "slabs_second",
        [SM] + [VM] * 5,
        (shape((INROWS, LANES), F32),) + kept,
        scratch,
        (where, slabs2, lt, r, bd, d),
        work,
    )
    out2 = (keep_in2 + near1[:INROWS].astype(F32)).astype(BF)
    out2, lt = lax.optimization_barrier((out2, lt))
    far1 = to_peer(2, out2)
    news = 3 * PER + 3 * NBQ
    msg3, msg3b, msg3x, keep3, dens3 = call(
        third_kernel,
        "slabs_third",
        [SM] + [VM] * 10,
        (
            shape((INROWS // 2 + news, LANES), BF), shape((INROWS // 2 + 2 * PER, LANES), BF),
            shape((news, LANES), BF), kept[0], kept[2],
        ),
        [pltpu.VMEM((3, PER, LANES), BF)] + scratch,
        (where, slabs3, lt, r, bd, d, sends1, sends2, dens1, dens2, near1),
        work,
    )
    near3, near3b = to_peer(1, msg3), to_peer(1, msg3b)
    far3 = to_peer(2, msg3x)
    keep_in4, keep4, sends4, dens4 = call(
        fourth_kernel,
        "slabs_fourth",
        [SM] + [VM] * 5,
        (shape((INROWS, LANES), F32),) + kept,
        scratch,
        (where, slabs4, lt, r, bd, d),
        LAST_WORK,
    )
    last = shape((LAST, LANES), BF)
    last_far = shape((LAST + PER + 3 * NBQ, LANES), BF)
    near4, far4, cross4, exch = call(
        exchange_kernel,
        "exchange",
        [SM] + [VM] * 6,
        (last, last_far, last, shape((QUARTER, LANES), F32)),
        [pltpu.VMEM((NACT, LANES), F32)],
        (where, keep_in4, near3, near3b, far1, sends4, dens4),
    )
    far3, far4 = lax.optimization_barrier((far3, far4))
    far4, cross4, near4 = to_peer(2, far4), to_peer(3, cross4), to_peer(1, near4)
    act, partial = call(
        coulomb_kernel,
        "coulomb",
        [VM] * 14,
        (shape((4 * PER, LANES), F32), shape((QUARTER, NACT), F32)),
        [],
        (
            keep1, keep2, keep3, keep4, dens1, dens2, dens3, dens4, exch,
            near3, far3, near4, far4, cross4,
        ),
    )
    (active,) = call(
        active_kernel,
        "own_active",
        [SM, VM],
        (shape((batch, QUARTER, NACT), F32),),
        [],
        (where, act),
        10**6,
    )
    return (active, hcore + sum_over_aux(partial))


def slab_terms(values, left, right):
    half = jnp.einsum("mc,qmn->qnc", left, values, preferred_element_type=F32).astype(BF)
    first = jnp.einsum("qnt,nc->qtc", half[:, :, :NACT], right, preferred_element_type=F32)
    second = jnp.einsum("qnc,nt->qtc", half, right[:, :NACT], preferred_element_type=F32)
    trace = 2.0 * jnp.einsum(
        "qni,ni->q", half[:, :, NACT:], right[:, NACT:], preferred_element_type=F32
    )
    return (first + second, trace)


def general_body(slabs, block_row, block_col, live_count, orbitals, hcore):
    batch = slabs.shape[1]
    init = (jnp.zeros((batch, NACT, NCOL), F32), jnp.zeros((batch,), F32))

    def visit(k, state):
        values = lax.dynamic_index_in_dim(slabs, k, 0, keepdims=False)
        left = lax.dynamic_slice_in_dim(orbitals, block_row[k] * BS, BS, 0)
        right = lax.dynamic_slice_in_dim(orbitals, block_col[k] * BS, BS, 0)
        terms, trace = slab_terms(values.reshape(batch, BS, BS), left, right)
        return (state[0] + terms, state[1] + trace)

    vectors, density = lax.fori_loop(0, live_count[0], visit, init)
    density = lax.psum(density, "pair")
    owned = lax.psum_scatter(vectors, "pair", scatter_dimension=1, tiled=True)
    own_active, own_inactive = owned[:, :, :NACT], owned[:, :, NACT:]
    gathered = lax.all_gather(own_inactive.astype(BF), "pair", axis=1, tiled=True)
    exchange = jnp.einsum(
        "qti,qui->tu", own_inactive, gathered.astype(F32), precision=lax.Precision.HIGHEST
    )
    coulomb = jnp.einsum("qtu,q->tu", own_active, density, precision=lax.Precision.HIGHEST)
    return (own_active, hcore + lax.psum(2.0 * coulomb - exchange, "aux"))


def solution(mesh):
    placed = (
        P(("frag", "pair"), "aux", None),
        P(("frag", "pair")),
        P(("frag", "pair")),
        P(("frag", "pair")),
        P("frag", None),
        P(("frag", "pair"), None),
    )

    def body(slabs, *rest):
        fits = mesh.shape["pair"] == 4 and slabs.shape[1] == 4 * NBQ and slabs.shape[0] % 8 == 0
        return (paired_body if fits else general_body)(slabs, *rest)

    return jax.shard_map(
        body,
        mesh=mesh,
        in_specs=placed,
        out_specs=(P(("frag", "aux"), "pair", None), P(("frag", "pair"), None)),
        check_vma=False,
    )
```

```python
import jax
import jax.numpy as jnp
from jax import lax
from jax.experimental import pallas as pl
from jax.experimental.pallas import tpu as pltpu
from jax.sharding import PartitionSpec as P

BS = 64
NACT = 64
NCOL = 192
NIN = NCOL - NACT
LANES = 128
NBQ = 16
PAIRED = 2 * BS
QSTEP, MSTEP = 3, 49
BF = jnp.bfloat16
F32 = jnp.float32


def low_half(rows):
    return lax.broadcasted_iota(jnp.int32, (rows, LANES), 1) < BS


def orbital_pair(k, blocks, live, orbitals):
    halves = []
    for n in range(2):
        slot = 2 * k + n
        base = pl.multiple_of((blocks[slot] // 2) * PAIRED, PAIRED)
        w = orbitals[:, pl.ds(base, PAIRED)]
        w = jnp.concatenate([w[NACT:], w[:NACT]], axis=0)
        w = jnp.where(lax.rem(blocks[slot], 2) != n, pltpu.roll(w, BS, 1), w)
        halves.append(jnp.where(slot < live, w, jnp.zeros_like(w)))
    return jnp.where(low_half(NCOL), halves[0], halves[1])


def slab_copies(slabs_ref, sbuf, sem, block):
    return [
        pltpu.make_async_copy(
            slabs_ref.at[pl.ds(2 * k, 2), pl.ds(pl.multiple_of(block * NBQ, NBQ), NBQ), :],
            sbuf.at[k],
            sem.at[k],
        )
        for k in range(slabs_ref.shape[0] // 2)
    ]


def lanes_of(k):
    return pl.ds(k * PAIRED if isinstance(k, int) else pl.multiple_of(k * PAIRED, PAIRED), PAIRED)


def run_block(sbuf, weights, scratch, emit, prepare=None, arrive=None):
    lt_ref, r_ref, bd_ref, d_ref = weights
    pt_ref, q_ref, diag = scratch[4:]
    quads = sbuf.shape[0] // 2
    first = low_half(NBQ)
    first_s = low_half(BS)
    zero = jnp.zeros((BS, LANES), BF)
    group = 8

    def relayout(k, out):
        for j in range(sbuf.shape[3] // LANES):
            lanes = slice(j * LANES, (j + 1) * LANES)
            a = sbuf[k, 0, :, lanes]
            b = sbuf[k, 1, :, lanes]
            out[pl.ds(MSTEP * 2 * j, NBQ, stride=QSTEP), :] = jnp.where(
                first, a, pltpu.roll(b, BS, 1)
            ).astype(F32)
            out[pl.ds(MSTEP * (2 * j + 1), NBQ, stride=QSTEP), :] = jnp.where(
                first, pltpu.roll(a, BS, 1), b
            ).astype(F32)

    def transform(g, bufs):
        dens = [d_ref[2 * g + n] for n in range(2)]
        left = [lt_ref[NIN:, lanes_of(2 * g + n)] for n in range(2)]
        for q in range(0, NBQ, group):
            slabs = [[], []]
            for u in range(q, q + group):
                total = diag[u]
                for n in range(2):
                    s = bufs[n][pl.ds(u * QSTEP, BS, stride=MSTEP), :]
                    total = total + jnp.sum((s * dens[n]).reshape(BS // 8, 8, LANES), axis=0)
                    slabs[n].append(s.astype(BF))
                diag[u] = total
            for n in range(2):
                at = lanes_of(2 * g + n)
                cols = [
                    jnp.concatenate(
                        [jnp.where(first_s, s, zero), jnp.where(first_s, zero, s)], axis=0
                    )
                    for s in slabs[n]
                ]
                p = jnp.dot(
                    left[n], jnp.concatenate(cols, axis=1), preferred_element_type=F32
                ).astype(BF)
                for u in range(group):
                    pt_ref[q + u, :, at] = p[:, u * LANES : (u + 1) * LANES]
            rows = jnp.concatenate(
                [jnp.concatenate([s0, s1], axis=1) for s0, s1 in zip(*slabs)], axis=0
            )
            out = jnp.dot(rows, bd_ref[g], preferred_element_type=F32).astype(BF)
            for u in range(0, group, 2):
                for n in range(2):
                    lanes = slice(n * LANES, (n + 1) * LANES)
                    q0 = out[u * BS : (u + 1) * BS, lanes]
                    q1 = out[(u + 1) * BS : (u + 2) * BS, lanes]
                    at = slice((q + u) * BS, (q + u + 2) * BS)
                    row = lanes_of(2 * g + n).start
                    q_ref[pl.ds(row, BS), at] = jnp.where(first_s, q0, pltpu.roll(q1, BS, 1))
                    q_ref[pl.ds(row + BS, BS), at] = jnp.where(
                        first_s, pltpu.roll(q0, BS, 1), q1
                    )

    def second_transform(g):
        rows = pt_ref[4 * g : 4 * g + 4].reshape(4 * NACT, pt_ref.shape[2])
        one = jnp.dot(rows, r_ref[...], preferred_element_type=F32)
        two = jnp.dot(
            lt_ref[...], q_ref[:, 4 * g * BS : (4 * g + 4) * BS], preferred_element_type=F32
        )
        return one, two

    def assemble(g, both):
        one, two = both
        for p in range(2):
            w0 = one[2 * p * NACT : (2 * p + 1) * NACT]
            w1 = one[(2 * p + 1) * NACT : (2 * p + 2) * NACT]
            turned = two[:, p * LANES : (p + 1) * LANES]
            across = turned[:NIN].T
            square = jnp.concatenate([turned[NIN:], turned[NIN:]], axis=0).T
            emit(
                2 * g + p,
                w0[:, :NIN] + across[:NACT],
                w1[:, :NIN] + across[NACT:],
                jnp.where(first_s, w0[:, NIN:] + square[:NACT], w1[:, NIN:] + square[NACT:]),
            )

    def load(g, bufs):
        for n in range(2):
            relayout(2 * g + n, bufs[n])

    def two_quads(i, carry):
        one, two = scratch[:2], scratch[2:4]
        pl.when(i > 0)(arrive)
        load(2 * i, one)
        prepare(2 * i)
        load(2 * i + 1, two)
        prepare(2 * i + 1)
        transform(2 * i, one)
        transform(2 * i + 1, two)
        return carry

    diag[...] = jnp.zeros_like(diag)
    if prepare is not None:
        lax.fori_loop(0, quads // 2, two_quads, 0)
    else:
        load(0, scratch[:2])
        for g in range(quads):
            if g + 1 < quads:
                load(g + 1, scratch[2 * ((g + 1) % 2) : 2 * ((g + 1) % 2) + 2])
            transform(g, scratch[2 * (g % 2) : 2 * (g % 2) + 2])
    whole = second_transform(0)
    for g in range(NBQ // 4):
        following = second_transform(g + 1) if g + 1 < NBQ // 4 else None
        assemble(g, whole)
        whole = following


def split_wire(d):
    hi = d.astype(BF).astype(F32)
    return jnp.where(low_half(d.shape[0]), hi, d - hi).astype(BF)


def joined(wire):
    w = wire.astype(F32)
    return w + pltpu.roll(w, BS, 1)


def density_of(diag):
    d = 2.0 * jnp.sum(jnp.sum(diag, axis=1), axis=1, keepdims=True)
    return jnp.broadcast_to(d, (NBQ, LANES))


QUARTER = NACT // 4
PER = NBQ // 2 * QUARTER
INROWS = NBQ * NACT
LAST = PER + NBQ + QUARTER


def emit_active(h, act, core, x, keep, sends):
    upper, lower = act[: 2 * QUARTER], act[2 * QUARTER :]
    near, far = jnp.where(x == 0, upper, lower), jnp.where(x == 0, lower, upper)
    at = pl.ds(h * QUARTER, QUARTER)
    for part, own, other in ((near, keep, sends.at[0]), (far, sends.at[1], sends.at[2])):
        one, two = part[:QUARTER], part[QUARTER:]
        own[at, :] = jnp.where(core == 0, one, two).astype(own.dtype)
        other[at, :] = jnp.where(core == 0, two, one).astype(BF)


def pair_rows(h, n):
    return pl.ds((2 * h + n) * NACT, NACT)


def first_kernel(
    where, rows_ref, cols_ref, live, slabs_ref, ot_ref,
    lt_out, r_out, bd_out, d_out, msg, keep, sends, dens, after2, after3, after4,
    rows, cols, orbitals, ssem, sbuf, sem, *scratch
):
    core, x = where[0], where[1]
    part = NACT // 2
    small = [
        pltpu.make_async_copy(src, dst, ssem.at[n])
        for n, (src, dst) in enumerate(((rows_ref, rows), (cols_ref, cols)))
    ] + [
        pltpu.make_async_copy(
            ot_ref.at[pl.ds(n * part, part)], orbitals.at[pl.ds(n * part, part)], ssem.at[2 + n]
        )
        for n in range(NCOL // part)
    ]
    blocks = (2 * (1 - x) + (1 - core), 2 * (1 - x) + core, 2 * x + (1 - core), 2 * x + core)
    now, *later = [
        slab_copies(slabs_ref, ref, sem.at[n], block)
        for n, (ref, block) in enumerate(zip((sbuf, after2, after3, after4), blocks))
    ]
    ahead = [copy for copies in later for copy in copies]
    for copy in small + now:
        copy.start()
    bd_out[...] = jnp.zeros_like(bd_out)
    for copy in small + now[: len(now) // 2]:
        copy.wait()
    for copy in ahead:
        copy.start()

    def arrive():
        for copy in now[len(now) // 2 :]:
            copy.wait()

    def prepare(g):
        for n in range(2):
            k = 2 * g + n
            left = orbital_pair(k, rows, live[0], orbitals)
            right = orbital_pair(k, cols, live[0], orbitals)
            at = lanes_of(k)
            lt_out[:, at] = left
            turned = jnp.concatenate([right, right[NIN:]], axis=0).astype(F32).T.astype(BF)
            r_out[at, :] = turned
            inner = (lax.broadcasted_iota(jnp.int32, (PAIRED, LANES), 0) < BS) == low_half(PAIRED)
            place = slice(n * PAIRED, (n + 1) * PAIRED)
            bd_out[g, place, place] = jnp.where(
                inner, turned[:, NIN:], jnp.zeros((PAIRED, LANES), BF)
            )
            both = jnp.dot(
                left[:NIN].astype(F32).T.astype(BF), right[:NIN], preferred_element_type=F32
            )
            d_out[k] = jnp.where(low_half(BS), both[:BS], both[BS:])

    def emit(h, in0, in1, act):
        msg[pair_rows(h, 0), :] = in0.astype(BF)
        msg[pair_rows(h, 1), :] = in1.astype(BF)
        emit_active(h, act, core, x, keep, sends)

    run_block(sbuf, (lt_out, r_out, bd_out, d_out), scratch, emit, prepare, arrive)
    msg[pl.ds(INROWS, PER), :] = sends[2]
    dens[...] = density_of(scratch[6][...])
    for copy in ahead:
        copy.wait()


def second_kernel(
    where, sbuf, lt_ref, r_ref, bd_ref, d_ref, keep_in, keep, sends, dens, *scratch
):
    core, x = where[0], where[1]
    def emit(h, in0, in1, act):
        keep_in[pair_rows(h, 0), :] = in0
        keep_in[pair_rows(h, 1), :] = in1
        emit_active(h, act, core, x, keep, sends)

    run_block(sbuf, (lt_ref, r_ref, bd_ref, d_ref), scratch, emit)
    dens[...] = density_of(scratch[6][...])


def third_kernel(
    where, sbuf, lt_ref, r_ref, bd_ref, d_ref, sends1, sends2, dens1, dens2, near1,
    near, near_more, far, keep, dens, sends, *scratch
):
    core, x = where[0], where[1]
    def emit(h, in0, in1, act):
        place, at = (near, h) if h < NBQ // 4 else (near_more, h - NBQ // 4)
        place[pair_rows(at, 0), :] = in0.astype(BF)
        place[pair_rows(at, 1), :] = in1.astype(BF)
        emit_active(h, act, core, x, keep, sends)

    run_block(sbuf, (lt_ref, r_ref, bd_ref, d_ref), scratch, emit)
    dens[...] = density_of(scratch[6][...])
    wires = [split_wire(d[...]) for d in (dens1, dens2, dens)]
    for n, source in enumerate((sends2, sends)):
        near_more[pl.ds(INROWS // 2 + n * PER, PER), :] = source[2]
    passed = near1[pl.ds(INROWS, PER), :]
    for k, (msg, base) in enumerate(((near, INROWS // 2), (far, 0))):
        for n, source in enumerate((sends1, sends2, sends)):
            rows = source[k]
            if (k, n) == (1, 1):
                rows = (rows.astype(F32) + passed.astype(F32)).astype(BF)
            msg[pl.ds(base + n * PER, PER), :] = rows
            msg[pl.ds(base + 3 * PER + n * NBQ, NBQ), :] = wires[n]


def fourth_kernel(
    where, sbuf, lt_ref, r_ref, bd_ref, d_ref, keep_in, keep, sends, dens, *scratch
):
    core, x = where[0], where[1]

    def emit(h, in0, in1, act):
        keep_in[pair_rows(h, 0), :] = in0
        keep_in[pair_rows(h, 1), :] = in1
        emit_active(h, act, core, x, keep, sends)

    run_block(sbuf, (lt_ref, r_ref, bd_ref, d_ref), scratch, emit)
    dens[...] = density_of(scratch[6][...])


def exchange_kernel(
    where, mine, near3, near3b, far1, sends, dens, near, far, cross, keep, whole
):
    parts = []
    for q in range(NBQ):
        rows = pl.ds(q * NACT, NACT)
        other = (near3 if q < NBQ // 2 else near3b)[pl.ds(q % (NBQ // 2) * NACT, NACT), :]
        parts.append(mine[rows, :] + other.astype(F32) + far1[rows, :].astype(F32))
    v = jnp.concatenate(parts, axis=1)
    v = v.astype(BF)
    total = lax.dot_general(v, v, (((1,), (1,)), ((), ())), preferred_element_type=F32)
    whole[...] = jnp.concatenate([total, total], axis=1)
    index = 2 * where[1] + where[0]
    keep[...] = whole[pl.ds(pl.multiple_of(index * QUARTER, QUARTER), QUARTER), :]
    wire = split_wire(dens[...])
    for k, msg in enumerate((near, far, cross)):
        rows = sends[k]
        if k == 1:
            passed = near3b[pl.ds(INROWS // 2 + PER, PER), :]
            rows = (rows.astype(F32) + passed.astype(F32)).astype(BF)
        msg[pl.ds(0, PER), :] = rows
        msg[pl.ds(PER, NBQ), :] = wire
        at = pl.multiple_of((index ^ (k + 1)) * QUARTER, QUARTER)
        msg[pl.ds(PER + NBQ, QUARTER), :] = split_wire(whole[pl.ds(at, QUARTER), :])
    far[pl.ds(LAST, PER), :] = near3b[pl.ds(INROWS // 2, PER), :]
    far[pl.ds(LAST + PER, 3 * NBQ), :] = near3[pl.ds(INROWS // 2 + 3 * PER, 3 * NBQ), :]


def coulomb_kernel(
    keep1, keep2, keep3, keep4, dens1, dens2, dens3, dens4, exch,
    near3, far3, cross4, far4, near4, act, partial,
):
    first = low_half(QUARTER)
    early, late = (near3, far3, far4), (near4, far4, cross4)
    total = jnp.zeros((QUARTER, LANES), F32)
    for m, (keep, dens) in enumerate(
        ((keep1, dens1), (keep2, dens2), (keep3, dens3), (keep4, dens4))
    ):
        rows, d = keep[...], dens[...]
        for k in (1, 2, 3):
            n = m ^ k
            msg = late[k - 1] if n == 3 else early[k - 1]
            if n == 3:
                at, dens_at = 0, PER
            elif k == 3:
                at, dens_at = LAST, LAST + PER + n * NBQ
            else:
                base = INROWS // 2 if k == 1 else 0
                at, dens_at = base + n * PER, base + 3 * PER + n * NBQ
            if not (k == 3 and n in (0, 2)):
                rows = rows + msg[pl.ds(at, PER), :].astype(F32)
            d = d + joined(msg[pl.ds(dens_at, NBQ), :])
        act[pl.ds(m * PER, PER), :] = rows
        for h in range(NBQ // 2):
            total = total + rows[h * QUARTER : (h + 1) * QUARTER] * jnp.where(
                first, d[2 * h : 2 * h + 1], d[2 * h + 1 : 2 * h + 2]
            )
    total = 2.0 * (total + pltpu.roll(total, BS, 1)) - exch[...]
    for msg in late:
        total = total - joined(msg[pl.ds(PER + NBQ, QUARTER), :])
    partial[...] = total[:, :BS]


def active_kernel(where, act, out):
    core, x = where[0], where[1]
    for n in range(4):
        xx = (1 - x) if n < 2 else x
        cc = (1 - core) if n % 2 == 0 else core
        base = NBQ * (2 * xx + cc)
        for h in range(NBQ // 2):
            a = act[pl.ds(n * PER + h * QUARTER, QUARTER), :]
            out[base + 2 * h] = a[:, :BS]
            out[base + 2 * h + 1] = a[:, BS:]


VM = pl.BlockSpec(memory_space=pltpu.VMEM)
SM = pl.BlockSpec(memory_space=pltpu.SMEM)
HB = pl.BlockSpec(memory_space=pltpu.HBM)

LAST_WORK = 10**9
PARAMS = pltpu.CompilerParams(vmem_limit_bytes=32 * 1024 * 1024)


def in_hbm(array):
    return pltpu.with_memory_space_constraint(array, pltpu.HBM)


def shape(dims, dtype):
    return jax.ShapeDtypeStruct(dims, dtype)


def sum_over_aux(part):
    n = lax.axis_size("aux")
    if n != 4:
        return lax.psum(part, "aux")
    for k in (1, 2):
        part = part + lax.ppermute(part, "aux", [(z, z ^ k) for z in range(n)])
    return part


def call(kernel, name, inputs, out_shape, scratch, args, work=0):
    return pl.pallas_call(
        kernel,
        name=name,
        in_specs=inputs,
        out_specs=[VM] * len(out_shape),
        out_shape=out_shape,
        scratch_shapes=scratch,
        compiler_params=PARAMS,
        cost_estimate=pl.CostEstimate(flops=work, bytes_accessed=10**5, transcendentals=0),
    )(*args)


def paired_body(slabs, block_row, block_col, live_count, orbitals, hcore):
    nslab, batch, width = slabs.shape
    index = lax.axis_index("pair")
    where = jnp.stack([lax.rem(index, 2), index // 2])
    aos = nslab * BS
    slabs = in_hbm(slabs)

    def to_peer(k, array):
        return lax.ppermute(array, "pair", [(p, p ^ k) for p in range(4)])

    loaded = shape((nslab // 2, 2, NBQ, width), BF)
    scratch = [pltpu.VMEM((MSTEP * BS, LANES), F32)] * 4 + [
        pltpu.VMEM((NBQ, NACT, aos), BF),
        pltpu.VMEM((aos, NBQ * BS), BF),
        pltpu.VMEM((NBQ, 8, LANES), F32),
    ]
    weights = (
        shape((NCOL, aos), BF),
        shape((aos, 2 * LANES), BF),
        shape((nslab // 4, 2 * PAIRED, 2 * PAIRED), BF),
        shape((nslab // 2, BS, PAIRED), F32),
    )
    kept = (
        shape((PER, LANES), F32), shape((3, PER, LANES), BF), shape((NBQ, LANES), F32),
    )
    work = 5 * 10**9
    lt, r, bd, d, msg1, keep1, sends1, dens1, slabs2, slabs3, slabs4 = call(
        first_kernel,
        "slabs_first",
        [SM, HB, HB, SM, HB, HB],
        weights + (shape((INROWS + PER, LANES), BF),) + kept + (loaded,) * 3,
        [
            pltpu.SMEM((nslab,), jnp.int32), pltpu.SMEM((nslab,), jnp.int32),
            pltpu.VMEM(orbitals.T.shape, BF), pltpu.SemaphoreType.DMA((8,)),
            pltpu.VMEM(loaded.shape, BF), pltpu.SemaphoreType.DMA((4, nslab // 2)),
        ] + scratch,
        (
            where, in_hbm(block_row), in_hbm(block_col), live_count, slabs,
            in_hbm(orbitals.T),
        ),
        work,
    )
    near1 = to_peer(1, msg1)
    keep_in2, keep2, sends2, dens2 = call(
        second_kernel,
        "slabs_second",
        [SM] + [VM] * 5,
        (shape((INROWS, LANES), F32),) + kept,
        scratch,
        (where, slabs2, lt, r, bd, d),
        work,
    )
    out2 = (keep_in2 + near1[:INROWS].astype(F32)).astype(BF)
    out2, lt = lax.optimization_barrier((out2, lt))
    far1 = to_peer(2, out2)
    news = 3 * PER + 3 * NBQ
    msg3, msg3b, msg3x, keep3, dens3 = call(
        third_kernel,
        "slabs_third",
        [SM] + [VM] * 10,
        (
            shape((INROWS // 2 + news, LANES), BF), shape((INROWS // 2 + 2 * PER, LANES), BF),
            shape((news, LANES), BF), kept[0], kept[2],
        ),
        [pltpu.VMEM((3, PER, LANES), BF)] + scratch,
        (where, slabs3, lt, r, bd, d, sends1, sends2, dens1, dens2, near1),
        work,
    )
    near3, near3b = to_peer(1, msg3), to_peer(1, msg3b)
    far3 = to_peer(2, msg3x)
    keep_in4, keep4, sends4, dens4 = call(
        fourth_kernel,
        "slabs_fourth",
        [SM] + [VM] * 5,
        (shape((INROWS, LANES), F32),) + kept,
        scratch,
        (where, slabs4, lt, r, bd, d),
        LAST_WORK,
    )
    last = shape((LAST, LANES), BF)
    last_far = shape((LAST + PER + 3 * NBQ, LANES), BF)
    near4, far4, cross4, exch = call(
        exchange_kernel,
        "exchange",
        [SM] + [VM] * 6,
        (last, last_far, last, shape((QUARTER, LANES), F32)),
        [pltpu.VMEM((NACT, LANES), F32)],
        (where, keep_in4, near3, near3b, far1, sends4, dens4),
    )
    far3, cross4 = lax.optimization_barrier((far3, cross4))
    cross4, far4, near4 = to_peer(3, cross4), to_peer(2, far4), to_peer(1, near4)
    act, partial = call(
        coulomb_kernel,
        "coulomb",
        [VM] * 14,
        (shape((4 * PER, LANES), F32), shape((QUARTER, NACT), F32)),
        [],
        (
            keep1, keep2, keep3, keep4, dens1, dens2, dens3, dens4, exch,
            near3, far3, cross4, far4, near4,
        ),
    )
    (active,) = call(
        active_kernel,
        "own_active",
        [SM, VM],
        (shape((batch, QUARTER, NACT), F32),),
        [],
        (where, act),
        10**6,
    )
    return (active, hcore + sum_over_aux(partial))


def slab_terms(values, left, right):
    half = jnp.einsum("mc,qmn->qnc", left, values, preferred_element_type=F32).astype(BF)
    first = jnp.einsum("qnt,nc->qtc", half[:, :, :NACT], right, preferred_element_type=F32)
    second = jnp.einsum("qnc,nt->qtc", half, right[:, :NACT], preferred_element_type=F32)
    trace = 2.0 * jnp.einsum(
        "qni,ni->q", half[:, :, NACT:], right[:, NACT:], preferred_element_type=F32
    )
    return (first + second, trace)


def general_body(slabs, block_row, block_col, live_count, orbitals, hcore):
    batch = slabs.shape[1]
    init = (jnp.zeros((batch, NACT, NCOL), F32), jnp.zeros((batch,), F32))

    def visit(k, state):
        values = lax.dynamic_index_in_dim(slabs, k, 0, keepdims=False)
        left = lax.dynamic_slice_in_dim(orbitals, block_row[k] * BS, BS, 0)
        right = lax.dynamic_slice_in_dim(orbitals, block_col[k] * BS, BS, 0)
        terms, trace = slab_terms(values.reshape(batch, BS, BS), left, right)
        return (state[0] + terms, state[1] + trace)

    vectors, density = lax.fori_loop(0, live_count[0], visit, init)
    density = lax.psum(density, "pair")
    owned = lax.psum_scatter(vectors, "pair", scatter_dimension=1, tiled=True)
    own_active, own_inactive = owned[:, :, :NACT], owned[:, :, NACT:]
    gathered = lax.all_gather(own_inactive.astype(BF), "pair", axis=1, tiled=True)
    exchange = jnp.einsum(
        "qti,qui->tu", own_inactive, gathered.astype(F32), precision=lax.Precision.HIGHEST
    )
    coulomb = jnp.einsum("qtu,q->tu", own_active, density, precision=lax.Precision.HIGHEST)
    return (own_active, hcore + lax.psum(2.0 * coulomb - exchange, "aux"))


def solution(mesh):
    placed = (
        P(("frag", "pair"), "aux", None),
        P(("frag", "pair")),
        P(("frag", "pair")),
        P(("frag", "pair")),
        P("frag", None),
        P(("frag", "pair"), None),
    )

    def body(slabs, *rest):
        fits = mesh.shape["pair"] == 4 and slabs.shape[1] == 4 * NBQ and slabs.shape[0] % 8 == 0
        return (paired_body if fits else general_body)(slabs, *rest)

    return jax.shard_map(
        body,
        mesh=mesh,
        in_specs=placed,
        out_specs=(P(("frag", "aux"), "pair", None), P(("frag", "pair"), None)),
        check_vma=False,
    )
```

```python
import jax
import jax.numpy as jnp
from jax import lax
from jax.experimental import pallas as pl
from jax.experimental.pallas import tpu as pltpu
from jax.sharding import PartitionSpec as P

BS = 64
NACT = 64
NCOL = 192
NIN = NCOL - NACT
LANES = 128
NBQ = 16
PAIRED = 2 * BS
QSTEP, MSTEP = 3, 49
BF = jnp.bfloat16
F32 = jnp.float32


def low_half(rows):
    return lax.broadcasted_iota(jnp.int32, (rows, LANES), 1) < BS


def orbital_pair(k, blocks, live, orbitals):
    halves = []
    for n in range(2):
        slot = 2 * k + n
        base = pl.multiple_of((blocks[slot] // 2) * PAIRED, PAIRED)
        w = orbitals[:, pl.ds(base, PAIRED)]
        w = jnp.concatenate([w[NACT:], w[:NACT]], axis=0)
        w = jnp.where(lax.rem(blocks[slot], 2) != n, pltpu.roll(w, BS, 1), w)
        halves.append(jnp.where(slot < live, w, jnp.zeros_like(w)))
    return jnp.where(low_half(NCOL), halves[0], halves[1])


def slab_copies(slabs_ref, sbuf, sem, block):
    return [
        pltpu.make_async_copy(
            slabs_ref.at[pl.ds(2 * k, 2), pl.ds(pl.multiple_of(block * NBQ, NBQ), NBQ), :],
            sbuf.at[k],
            sem.at[k],
        )
        for k in range(slabs_ref.shape[0] // 2)
    ]


def lanes_of(k):
    return pl.ds(k * PAIRED if isinstance(k, int) else pl.multiple_of(k * PAIRED, PAIRED), PAIRED)


def run_block(sbuf, weights, scratch, emit, prepare=None, arrive=None):
    lt_ref, r_ref, bd_ref, d_ref = weights
    pt_ref, q_ref, diag = scratch[4:]
    quads = sbuf.shape[0] // 2
    first = low_half(NBQ)
    first_s = low_half(BS)
    zero = jnp.zeros((BS, LANES), BF)
    group = 8

    def relayout(k, out):
        for j in range(sbuf.shape[3] // LANES):
            lanes = slice(j * LANES, (j + 1) * LANES)
            a = sbuf[k, 0, :, lanes]
            b = sbuf[k, 1, :, lanes]
            out[pl.ds(MSTEP * 2 * j, NBQ, stride=QSTEP), :] = jnp.where(
                first, a, pltpu.roll(b, BS, 1)
            ).astype(F32)
            out[pl.ds(MSTEP * (2 * j + 1), NBQ, stride=QSTEP), :] = jnp.where(
                first, pltpu.roll(a, BS, 1), b
            ).astype(F32)

    def transform(g, bufs):
        dens = [d_ref[2 * g + n] for n in range(2)]
        left = [lt_ref[NIN:, lanes_of(2 * g + n)] for n in range(2)]
        for q in range(0, NBQ, group):
            slabs = [[], []]
            for u in range(q, q + group):
                total = diag[u]
                for n in range(2):
                    s = bufs[n][pl.ds(u * QSTEP, BS, stride=MSTEP), :]
                    total = total + jnp.sum((s * dens[n]).reshape(BS // 8, 8, LANES), axis=0)
                    slabs[n].append(s.astype(BF))
                diag[u] = total
            for n in range(2):
                at = lanes_of(2 * g + n)
                cols = [
                    jnp.concatenate(
                        [jnp.where(first_s, s, zero), jnp.where(first_s, zero, s)], axis=0
                    )
                    for s in slabs[n]
                ]
                p = jnp.dot(
                    left[n], jnp.concatenate(cols, axis=1), preferred_element_type=F32
                ).astype(BF)
                for u in range(group):
                    pt_ref[q + u, :, at] = p[:, u * LANES : (u + 1) * LANES]
            rows = jnp.concatenate(
                [jnp.concatenate([s0, s1], axis=1) for s0, s1 in zip(*slabs)], axis=0
            )
            out = jnp.dot(rows, bd_ref[g], preferred_element_type=F32).astype(BF)
            for u in range(0, group, 2):
                for n in range(2):
                    lanes = slice(n * LANES, (n + 1) * LANES)
                    q0 = out[u * BS : (u + 1) * BS, lanes]
                    q1 = out[(u + 1) * BS : (u + 2) * BS, lanes]
                    at = slice((q + u) * BS, (q + u + 2) * BS)
                    row = lanes_of(2 * g + n).start
                    q_ref[pl.ds(row, BS), at] = jnp.where(first_s, q0, pltpu.roll(q1, BS, 1))
                    q_ref[pl.ds(row + BS, BS), at] = jnp.where(
                        first_s, pltpu.roll(q0, BS, 1), q1
                    )

    def second_transform(g):
        rows = pt_ref[group * g : group * (g + 1)].reshape(group * NACT, pt_ref.shape[2])
        one = jnp.dot(rows, r_ref[...], preferred_element_type=F32)
        two = jnp.dot(
            lt_ref[...], q_ref[:, group * g * BS : group * (g + 1) * BS], preferred_element_type=F32
        )
        return one, two

    def assemble(g, both):
        one, two = both
        for p in range(group // 2):
            w0 = one[2 * p * NACT : (2 * p + 1) * NACT]
            w1 = one[(2 * p + 1) * NACT : (2 * p + 2) * NACT]
            turned = two[:, p * LANES : (p + 1) * LANES]
            across = turned[:NIN].T
            square = jnp.concatenate([turned[NIN:], turned[NIN:]], axis=0).T
            emit(
                group // 2 * g + p,
                w0[:, :NIN] + across[:NACT],
                w1[:, :NIN] + across[NACT:],
                jnp.where(first_s, w0[:, NIN:] + square[:NACT], w1[:, NIN:] + square[NACT:]),
            )

    def load(g, bufs):
        for n in range(2):
            relayout(2 * g + n, bufs[n])

    def two_quads(i, carry):
        one, two = scratch[:2], scratch[2:4]
        pl.when(i > 0)(arrive)
        load(2 * i, one)
        prepare(2 * i)
        load(2 * i + 1, two)
        prepare(2 * i + 1)
        transform(2 * i, one)
        transform(2 * i + 1, two)
        return carry

    diag[...] = jnp.zeros_like(diag)
    if prepare is not None:
        lax.fori_loop(0, quads // 2, two_quads, 0)
    else:
        load(0, scratch[:2])
        for g in range(quads):
            if g + 1 < quads:
                load(g + 1, scratch[2 * ((g + 1) % 2) : 2 * ((g + 1) % 2) + 2])
            transform(g, scratch[2 * (g % 2) : 2 * (g % 2) + 2])
    whole = second_transform(0)
    for g in range(NBQ // group):
        following = second_transform(g + 1) if g + 1 < NBQ // group else None
        assemble(g, whole)
        whole = following


def split_wire(d):
    hi = d.astype(BF).astype(F32)
    return jnp.where(low_half(d.shape[0]), hi, d - hi).astype(BF)


def joined(wire):
    w = wire.astype(F32)
    return w + pltpu.roll(w, BS, 1)


def density_of(diag):
    d = 2.0 * jnp.sum(jnp.sum(diag, axis=1), axis=1, keepdims=True)
    return jnp.broadcast_to(d, (NBQ, LANES))


QUARTER = NACT // 4
PER = NBQ // 2 * QUARTER
INROWS = NBQ * NACT
LAST = PER + NBQ + QUARTER


def emit_active(h, act, core, x, keep, sends):
    upper, lower = act[: 2 * QUARTER], act[2 * QUARTER :]
    near, far = jnp.where(x == 0, upper, lower), jnp.where(x == 0, lower, upper)
    at = pl.ds(h * QUARTER, QUARTER)
    for part, own, other in ((near, keep, sends.at[0]), (far, sends.at[1], sends.at[2])):
        one, two = part[:QUARTER], part[QUARTER:]
        own[at, :] = jnp.where(core == 0, one, two).astype(own.dtype)
        other[at, :] = jnp.where(core == 0, two, one).astype(BF)


def pair_rows(h, n):
    return pl.ds((2 * h + n) * NACT, NACT)


def first_kernel(
    where, rows_ref, cols_ref, live, slabs_ref, ot_ref,
    lt_out, r_out, bd_out, d_out, msg, keep, sends, dens, after2, after3, after4,
    rows, cols, orbitals, ssem, sbuf, sem, *scratch
):
    core, x = where[0], where[1]
    part = NACT // 2
    small = [
        pltpu.make_async_copy(src, dst, ssem.at[n])
        for n, (src, dst) in enumerate(((rows_ref, rows), (cols_ref, cols)))
    ] + [
        pltpu.make_async_copy(
            ot_ref.at[pl.ds(n * part, part)], orbitals.at[pl.ds(n * part, part)], ssem.at[2 + n]
        )
        for n in range(NCOL // part)
    ]
    blocks = (2 * (1 - x) + (1 - core), 2 * (1 - x) + core, 2 * x + (1 - core), 2 * x + core)
    now, *later = [
        slab_copies(slabs_ref, ref, sem.at[n], block)
        for n, (ref, block) in enumerate(zip((sbuf, after2, after3, after4), blocks))
    ]
    ahead = [copy for copies in later for copy in copies]
    for copy in small + now:
        copy.start()
    bd_out[...] = jnp.zeros_like(bd_out)
    for copy in small + now[: len(now) // 2]:
        copy.wait()
    for copy in ahead:
        copy.start()

    def arrive():
        for copy in now[len(now) // 2 :]:
            copy.wait()

    def prepare(g):
        for n in range(2):
            k = 2 * g + n
            left = orbital_pair(k, rows, live[0], orbitals)
            right = orbital_pair(k, cols, live[0], orbitals)
            at = lanes_of(k)
            lt_out[:, at] = left
            turned = jnp.concatenate([right, right[NIN:]], axis=0).astype(F32).T.astype(BF)
            r_out[at, :] = turned
            inner = (lax.broadcasted_iota(jnp.int32, (PAIRED, LANES), 0) < BS) == low_half(PAIRED)
            place = slice(n * PAIRED, (n + 1) * PAIRED)
            bd_out[g, place, place] = jnp.where(
                inner, turned[:, NIN:], jnp.zeros((PAIRED, LANES), BF)
            )
            both = jnp.dot(
                left[:NIN].astype(F32).T.astype(BF), right[:NIN], preferred_element_type=F32
            )
            d_out[k] = jnp.where(low_half(BS), both[:BS], both[BS:])

    def emit(h, in0, in1, act):
        msg[pair_rows(h, 0), :] = in0.astype(BF)
        msg[pair_rows(h, 1), :] = in1.astype(BF)
        emit_active(h, act, core, x, keep, sends)

    run_block(sbuf, (lt_out, r_out, bd_out, d_out), scratch, emit, prepare, arrive)
    msg[pl.ds(INROWS, PER), :] = sends[2]
    dens[...] = density_of(scratch[6][...])
    for copy in ahead:
        copy.wait()


def second_kernel(
    where, sbuf, lt_ref, r_ref, bd_ref, d_ref, keep_in, keep, sends, dens, *scratch
):
    core, x = where[0], where[1]
    def emit(h, in0, in1, act):
        keep_in[pair_rows(h, 0), :] = in0
        keep_in[pair_rows(h, 1), :] = in1
        emit_active(h, act, core, x, keep, sends)

    run_block(sbuf, (lt_ref, r_ref, bd_ref, d_ref), scratch, emit)
    dens[...] = density_of(scratch[6][...])


def third_kernel(
    where, sbuf, lt_ref, r_ref, bd_ref, d_ref, sends1, sends2, dens1, dens2, near1,
    near, near_more, far, keep, dens, sends, *scratch
):
    core, x = where[0], where[1]
    def emit(h, in0, in1, act):
        place, at = (near, h) if h < NBQ // 4 else (near_more, h - NBQ // 4)
        place[pair_rows(at, 0), :] = in0.astype(BF)
        place[pair_rows(at, 1), :] = in1.astype(BF)
        emit_active(h, act, core, x, keep, sends)

    run_block(sbuf, (lt_ref, r_ref, bd_ref, d_ref), scratch, emit)
    dens[...] = density_of(scratch[6][...])
    wires = [split_wire(d[...]) for d in (dens1, dens2, dens)]
    for n, source in enumerate((sends2, sends)):
        near_more[pl.ds(INROWS // 2 + n * PER, PER), :] = source[2]
    passed = near1[pl.ds(INROWS, PER), :]
    for k, (msg, base) in enumerate(((near, INROWS // 2), (far, 0))):
        for n, source in enumerate((sends1, sends2, sends)):
            rows = source[k]
            if (k, n) == (1, 1):
                rows = (rows.astype(F32) + passed.astype(F32)).astype(BF)
            msg[pl.ds(base + n * PER, PER), :] = rows
            msg[pl.ds(base + 3 * PER + n * NBQ, NBQ), :] = wires[n]


def fourth_kernel(
    where, sbuf, lt_ref, r_ref, bd_ref, d_ref, keep_in, keep, sends, dens, *scratch
):
    core, x = where[0], where[1]

    def emit(h, in0, in1, act):
        keep_in[pair_rows(h, 0), :] = in0
        keep_in[pair_rows(h, 1), :] = in1
        emit_active(h, act, core, x, keep, sends)

    run_block(sbuf, (lt_ref, r_ref, bd_ref, d_ref), scratch, emit)
    dens[...] = density_of(scratch[6][...])


def exchange_kernel(
    where, mine, near3, near3b, far1, sends, dens, near, far, cross, keep, whole
):
    parts = []
    for q in range(NBQ):
        rows = pl.ds(q * NACT, NACT)
        other = (near3 if q < NBQ // 2 else near3b)[pl.ds(q % (NBQ // 2) * NACT, NACT), :]
        parts.append(mine[rows, :] + other.astype(F32) + far1[rows, :].astype(F32))
    v = jnp.concatenate(parts, axis=1)
    v = v.astype(BF)
    total = lax.dot_general(v, v, (((1,), (1,)), ((), ())), preferred_element_type=F32)
    whole[...] = jnp.concatenate([total, total], axis=1)
    index = 2 * where[1] + where[0]
    keep[...] = whole[pl.ds(pl.multiple_of(index * QUARTER, QUARTER), QUARTER), :]
    wire = split_wire(dens[...])
    for k, msg in enumerate((near, far, cross)):
        rows = sends[k]
        if k == 1:
            passed = near3b[pl.ds(INROWS // 2 + PER, PER), :]
            rows = (rows.astype(F32) + passed.astype(F32)).astype(BF)
        msg[pl.ds(0, PER), :] = rows
        msg[pl.ds(PER, NBQ), :] = wire
        at = pl.multiple_of((index ^ (k + 1)) * QUARTER, QUARTER)
        msg[pl.ds(PER + NBQ, QUARTER), :] = split_wire(whole[pl.ds(at, QUARTER), :])
    far[pl.ds(LAST, PER), :] = near3b[pl.ds(INROWS // 2, PER), :]
    far[pl.ds(LAST + PER, 3 * NBQ), :] = near3[pl.ds(INROWS // 2 + 3 * PER, 3 * NBQ), :]


def coulomb_kernel(
    keep1, keep2, keep3, keep4, dens1, dens2, dens3, dens4, exch,
    near3, far3, near4, far4, cross4, act, partial,
):
    first = low_half(QUARTER)
    early, late = (near3, far3, far4), (near4, far4, cross4)
    total = jnp.zeros((QUARTER, LANES), F32)
    for m, (keep, dens) in enumerate(
        ((keep1, dens1), (keep2, dens2), (keep3, dens3), (keep4, dens4))
    ):
        rows, d = keep[...], dens[...]
        for k in (1, 2, 3):
            n = m ^ k
            msg = late[k - 1] if n == 3 else early[k - 1]
            if n == 3:
                at, dens_at = 0, PER
            elif k == 3:
                at, dens_at = LAST, LAST + PER + n * NBQ
            else:
                base = INROWS // 2 if k == 1 else 0
                at, dens_at = base + n * PER, base + 3 * PER + n * NBQ
            if not (k == 3 and n in (0, 2)):
                rows = rows + msg[pl.ds(at, PER), :].astype(F32)
            d = d + joined(msg[pl.ds(dens_at, NBQ), :])
        act[pl.ds(m * PER, PER), :] = rows
        for h in range(NBQ // 2):
            total = total + rows[h * QUARTER : (h + 1) * QUARTER] * jnp.where(
                first, d[2 * h : 2 * h + 1], d[2 * h + 1 : 2 * h + 2]
            )
    total = 2.0 * (total + pltpu.roll(total, BS, 1)) - exch[...]
    for msg in late:
        total = total - joined(msg[pl.ds(PER + NBQ, QUARTER), :])
    partial[...] = total[:, :BS]


def active_kernel(where, act, out):
    core, x = where[0], where[1]
    for n in range(4):
        xx = (1 - x) if n < 2 else x
        cc = (1 - core) if n % 2 == 0 else core
        base = NBQ * (2 * xx + cc)
        for h in range(NBQ // 2):
            a = act[pl.ds(n * PER + h * QUARTER, QUARTER), :]
            out[base + 2 * h] = a[:, :BS]
            out[base + 2 * h + 1] = a[:, BS:]


VM = pl.BlockSpec(memory_space=pltpu.VMEM)
SM = pl.BlockSpec(memory_space=pltpu.SMEM)
HB = pl.BlockSpec(memory_space=pltpu.HBM)

LAST_WORK = 10**9
PARAMS = pltpu.CompilerParams(vmem_limit_bytes=32 * 1024 * 1024)


def in_hbm(array):
    return pltpu.with_memory_space_constraint(array, pltpu.HBM)


def shape(dims, dtype):
    return jax.ShapeDtypeStruct(dims, dtype)


def sum_over_aux(part):
    n = lax.axis_size("aux")
    if n != 4:
        return lax.psum(part, "aux")
    for k in (1, 2):
        part = part + lax.ppermute(part, "aux", [(z, z ^ k) for z in range(n)])
    return part


def call(kernel, name, inputs, out_shape, scratch, args, work=0):
    return pl.pallas_call(
        kernel,
        name=name,
        in_specs=inputs,
        out_specs=[VM] * len(out_shape),
        out_shape=out_shape,
        scratch_shapes=scratch,
        compiler_params=PARAMS,
        cost_estimate=pl.CostEstimate(flops=work, bytes_accessed=10**5, transcendentals=0),
    )(*args)


def paired_body(slabs, block_row, block_col, live_count, orbitals, hcore):
    nslab, batch, width = slabs.shape
    index = lax.axis_index("pair")
    where = jnp.stack([lax.rem(index, 2), index // 2])
    aos = nslab * BS
    slabs = in_hbm(slabs)

    def to_peer(k, array):
        return lax.ppermute(array, "pair", [(p, p ^ k) for p in range(4)])

    loaded = shape((nslab // 2, 2, NBQ, width), BF)
    scratch = [pltpu.VMEM((MSTEP * BS, LANES), F32)] * 4 + [
        pltpu.VMEM((NBQ, NACT, aos), BF),
        pltpu.VMEM((aos, NBQ * BS), BF),
        pltpu.VMEM((NBQ, 8, LANES), F32),
    ]
    weights = (
        shape((NCOL, aos), BF),
        shape((aos, 2 * LANES), BF),
        shape((nslab // 4, 2 * PAIRED, 2 * PAIRED), BF),
        shape((nslab // 2, BS, PAIRED), F32),
    )
    kept = (
        shape((PER, LANES), F32), shape((3, PER, LANES), BF), shape((NBQ, LANES), F32),
    )
    work = 5 * 10**9
    lt, r, bd, d, msg1, keep1, sends1, dens1, slabs2, slabs3, slabs4 = call(
        first_kernel,
        "slabs_first",
        [SM, HB, HB, SM, HB, HB],
        weights + (shape((INROWS + PER, LANES), BF),) + kept + (loaded,) * 3,
        [
            pltpu.SMEM((nslab,), jnp.int32), pltpu.SMEM((nslab,), jnp.int32),
            pltpu.VMEM(orbitals.T.shape, BF), pltpu.SemaphoreType.DMA((8,)),
            pltpu.VMEM(loaded.shape, BF), pltpu.SemaphoreType.DMA((4, nslab // 2)),
        ] + scratch,
        (
            where, in_hbm(block_row), in_hbm(block_col), live_count, slabs,
            in_hbm(orbitals.T),
        ),
        work,
    )
    near1 = to_peer(1, msg1)
    keep_in2, keep2, sends2, dens2 = call(
        second_kernel,
        "slabs_second",
        [SM] + [VM] * 5,
        (shape((INROWS, LANES), F32),) + kept,
        scratch,
        (where, slabs2, lt, r, bd, d),
        work,
    )
    out2 = (keep_in2 + near1[:INROWS].astype(F32)).astype(BF)
    out2, lt = lax.optimization_barrier((out2, lt))
    far1 = to_peer(2, out2)
    news = 3 * PER + 3 * NBQ
    msg3, msg3b, msg3x, keep3, dens3 = call(
        third_kernel,
        "slabs_third",
        [SM] + [VM] * 10,
        (
            shape((INROWS // 2 + news, LANES), BF), shape((INROWS // 2 + 2 * PER, LANES), BF),
            shape((news, LANES), BF), kept[0], kept[2],
        ),
        [pltpu.VMEM((3, PER, LANES), BF)] + scratch,
        (where, slabs3, lt, r, bd, d, sends1, sends2, dens1, dens2, near1),
        work,
    )
    near3, near3b = to_peer(1, msg3), to_peer(1, msg3b)
    far3 = to_peer(2, msg3x)
    keep_in4, keep4, sends4, dens4 = call(
        fourth_kernel,
        "slabs_fourth",
        [SM] + [VM] * 5,
        (shape((INROWS, LANES), F32),) + kept,
        scratch,
        (where, slabs4, lt, r, bd, d),
        LAST_WORK,
    )
    last = shape((LAST, LANES), BF)
    last_far = shape((LAST + PER + 3 * NBQ, LANES), BF)
    near4, far4, cross4, exch = call(
        exchange_kernel,
        "exchange",
        [SM] + [VM] * 6,
        (last, last_far, last, shape((QUARTER, LANES), F32)),
        [pltpu.VMEM((NACT, LANES), F32)],
        (where, keep_in4, near3, near3b, far1, sends4, dens4),
    )
    far3, far4 = lax.optimization_barrier((far3, far4))
    far4, cross4, near4 = to_peer(2, far4), to_peer(3, cross4), to_peer(1, near4)
    act, partial = call(
        coulomb_kernel,
        "coulomb",
        [VM] * 14,
        (shape((4 * PER, LANES), F32), shape((QUARTER, NACT), F32)),
        [],
        (
            keep1, keep2, keep3, keep4, dens1, dens2, dens3, dens4, exch,
            near3, far3, near4, far4, cross4,
        ),
    )
    (active,) = call(
        active_kernel,
        "own_active",
        [SM, VM],
        (shape((batch, QUARTER, NACT), F32),),
        [],
        (where, act),
        10**6,
    )
    return (active, hcore + sum_over_aux(partial))


def slab_terms(values, left, right):
    half = jnp.einsum("mc,qmn->qnc", left, values, preferred_element_type=F32).astype(BF)
    first = jnp.einsum("qnt,nc->qtc", half[:, :, :NACT], right, preferred_element_type=F32)
    second = jnp.einsum("qnc,nt->qtc", half, right[:, :NACT], preferred_element_type=F32)
    trace = 2.0 * jnp.einsum(
        "qni,ni->q", half[:, :, NACT:], right[:, NACT:], preferred_element_type=F32
    )
    return (first + second, trace)


def general_body(slabs, block_row, block_col, live_count, orbitals, hcore):
    batch = slabs.shape[1]
    init = (jnp.zeros((batch, NACT, NCOL), F32), jnp.zeros((batch,), F32))

    def visit(k, state):
        values = lax.dynamic_index_in_dim(slabs, k, 0, keepdims=False)
        left = lax.dynamic_slice_in_dim(orbitals, block_row[k] * BS, BS, 0)
        right = lax.dynamic_slice_in_dim(orbitals, block_col[k] * BS, BS, 0)
        terms, trace = slab_terms(values.reshape(batch, BS, BS), left, right)
        return (state[0] + terms, state[1] + trace)

    vectors, density = lax.fori_loop(0, live_count[0], visit, init)
    density = lax.psum(density, "pair")
    owned = lax.psum_scatter(vectors, "pair", scatter_dimension=1, tiled=True)
    own_active, own_inactive = owned[:, :, :NACT], owned[:, :, NACT:]
    gathered = lax.all_gather(own_inactive.astype(BF), "pair", axis=1, tiled=True)
    exchange = jnp.einsum(
        "qti,qui->tu", own_inactive, gathered.astype(F32), precision=lax.Precision.HIGHEST
    )
    coulomb = jnp.einsum("qtu,q->tu", own_active, density, precision=lax.Precision.HIGHEST)
    return (own_active, hcore + lax.psum(2.0 * coulomb - exchange, "aux"))


def solution(mesh):
    placed = (
        P(("frag", "pair"), "aux", None),
        P(("frag", "pair")),
        P(("frag", "pair")),
        P(("frag", "pair")),
        P("frag", None),
        P(("frag", "pair"), None),
    )

    def body(slabs, *rest):
        fits = mesh.shape["pair"] == 4 and slabs.shape[1] == 4 * NBQ and slabs.shape[0] % 8 == 0
        return (paired_body if fits else general_body)(slabs, *rest)

    return jax.shard_map(
        body,
        mesh=mesh,
        in_specs=placed,
        out_specs=(P(("frag", "aux"), "pair", None), P(("frag", "pair"), None)),
        check_vma=False,
    )
```
